32 devices in a mesh: batch: 4 (over z), rows: 8 (over y, x, core).
Axes of the slice: x: 2, y: 2, z: 4, core: 2. Of those that a mesh axis runs over, the one named last changes fastest.
Arguments:
- tokens: bfloat16 [4, 4, 32, 64, 384], P('batch', None, 'rows'), may hold values from -6 to 6
- norm1_gain: float32 [384], replicated, may hold values from 0.5 to 1.5
- norm1_bias: float32 [384], replicated, may hold values from -1.5 to 1.5
- query_taps: float32 [3, 3, 384], replicated, may hold values from -2 to 2
- query_weight: bfloat16 [384, 384], replicated, may hold values from -1.25 to 1.25
- key_weight: bfloat16 [384, 384], replicated, may hold values from -0.3125 to 0.3125
- value_weight: bfloat16 [384, 384], replicated, may hold values from -0.3125 to 0.3125
- out_weight: bfloat16 [384, 384], replicated, may hold values from -6 to 6
- out_bias: float32 [384], replicated, may hold values from -1.5 to 1.5
- norm2_gain: float32 [384], replicated, may hold values from 0.5 to 1.5
- norm2_bias: float32 [384], replicated, may hold values from -1.5 to 1.5
- up_weight: bfloat16 [384, 1536], replicated, may hold values from -0.3125 to 0.3125
- up_bias: float32 [1536], replicated, may hold values from -1.5 to 1.5
- hidden_taps: float32 [3, 3, 1536], replicated, may hold values from -2 to 2
- down_weight: bfloat16 [1536, 384], replicated, may hold values from -0.15625 to 0.15625
- down_bias: float32 [384], replicated, may hold values from -1.5 to 1.5
- cotangent: bfloat16 [4, 4, 32, 64, 384], P('batch', None, 'rows'), may hold values from -6 to 6
- heights: int32 [4], P('batch'), may hold values from 16 to 32, as said below
- widths: int32 [4], P('batch'), may hold values from 32 to 64, as said below
Outputs:
- layer_out: bfloat16 [4, 4, 32, 64, 384], P('batch', None, 'rows')
- input_grad: float32 [4, 4, 32, 64, 384], P('batch', None, 'rows')
- grad_norm1_gain: float32 [384], replicated
- grad_norm1_bias: float32 [384], replicated
- grad_query_taps: float32 [3, 3, 384], replicated
- grad_query_weight: float32 [384, 384], replicated
- grad_key_weight: float32 [384, 384], replicated
- grad_value_weight: float32 [384, 384], replicated
- grad_out_weight: float32 [384, 384], replicated
- grad_out_bias: float32 [384], replicated
- grad_norm2_gain: float32 [384], replicated
- grad_norm2_bias: float32 [384], replicated
- grad_up_weight: float32 [384, 1536], replicated
- grad_up_bias: float32 [1536], replicated
- grad_hidden_taps: float32 [3, 3, 1536], replicated
- grad_down_weight: float32 [1536, 384], replicated
- grad_down_bias: float32 [384], replicated
- stats: float32 [3], replicated
The draws below stay inside these ranges and needn't reach their ends.
Inputs may be any that keep to these rules, and one draw needn't show every extreme that they name: `heights`: every height is even; one image drawn from the seed has all 32 rows. `widths`: every width is even; one image drawn from the seed has all 64 columns.
All inputs are finite; a program needn't handle non-finite values.
Results may differ from the reference program's by a relative error of at most 0.03.
Values may be sent and summed in bfloat16 or wider, within the bound.
No kernel may reach another device: no remote copies, remote signals or barrier semaphores. Data moves between devices by JAX's collectives and lax.ppermute only.
A program may use at most 256 MiB of HBM per device.

```python
import jax
import jax.numpy as jnp
from jax import lax

D = 384
HEADS = 6
HDIM = 64
FF = 1536
TASKS = 4
W = 64
H = 32
IMAGES = 4


def draw_heights(key, part):
    key = jax.random.fold_in(key, 7)
    halves = jax.random.randint(key, (IMAGES,), H // 4, H // 2 + 1)
    chosen = jax.random.randint(jax.random.fold_in(key, 1), (), 0, IMAGES)
    return jnp.where(jnp.arange(IMAGES) == chosen, H, 2 * halves).astype(jnp.int32)


def draw_widths(key, part):
    key = jax.random.fold_in(key, 9)
    halves = jax.random.randint(key, (IMAGES,), W // 4, W // 2 + 1)
    chosen = jax.random.randint(jax.random.fold_in(key, 1), (), 0, IMAGES)
    return jnp.where(jnp.arange(IMAGES) == chosen, W, 2 * halves).astype(jnp.int32)


def block_scale(rng, extent, split, low, top_value):
    def one(position, blocks):
        steps = jax.random.uniform(jax.random.fold_in(jax.random.fold_in(rng, 6), position), (blocks,), jnp.float32, low / len(split), top_value / len(split))
        return jnp.repeat(jnp.exp(steps), extent[position] // blocks).reshape((-1,) + (1,) * (len(extent) - position - 1))

    level = one(*split[0])
    for cut in split[1:]:
        level = level * one(*cut)
    return level


def normal_values(key, dims, scale, reach, cuts=(), kind=jnp.bfloat16):
    array = jax.random.normal(key, dims, jnp.float32) * scale
    if len(cuts) > 0:
        array = block_scale(key, dims, cuts, -0.22, 0.18) * array
    return jnp.clip(array, min=-reach, max=reach).astype(kind)


def setup_inputs(seed: int = 0) -> dict:
    seeds = jax.random.split(jax.random.key(seed), 20)
    tokens = normal_values(seeds[0], (IMAGES, TASKS, H, W, D), 1.0, 6.0, ((0, 4), (2, 8)))
    norm1_gain = jnp.clip(1.0 + 0.1 * jax.random.normal(seeds[1], (D,), jnp.float32), 0.5, 1.5)
    norm1_bias = normal_values(seeds[2], (D,), 0.3, 1.5, (), jnp.float32)
    query_taps = normal_values(seeds[3], (3, 3, D), 9 ** -0.5, 2.0, (), jnp.float32)
    query_weight = normal_values(seeds[4], (D, D), (D // 16) ** -0.5, 1.25)
    key_weight = normal_values(seeds[5], (D, D), D ** -0.5, 0.3125)
    value_weight = normal_values(seeds[6], (D, D), D ** -0.5, 0.3125)
    out_weight = normal_values(seeds[7], (D, D), (max(1, D // 256)) ** -0.5, 6.0)
    out_bias = normal_values(seeds[8], (D,), 0.3, 1.5, (), jnp.float32)
    norm2_gain = jnp.clip(1.0 + 0.1 * jax.random.normal(seeds[9], (D,), jnp.float32), 0.5, 1.5)
    norm2_bias = normal_values(seeds[10], (D,), 0.3, 1.5, (), jnp.float32)
    up_weight = normal_values(seeds[11], (D, FF), D ** -0.5, 0.3125)
    up_bias = normal_values(seeds[12], (FF,), 0.3, 1.5, (), jnp.float32)
    hidden_taps = normal_values(seeds[13], (3, 3, FF), 9 ** -0.5, 2.0, (), jnp.float32)
    down_weight = normal_values(seeds[14], (FF, D), FF ** -0.5, 0.15625)
    down_bias = normal_values(seeds[15], (D,), 0.3, 1.5, (), jnp.float32)
    cotangent = normal_values(seeds[16], (IMAGES, TASKS, H, W, D), 1.0, 6.0, ((0, 4), (2, 8)))
    heights = draw_heights(jax.random.fold_in(seeds[19], 71), 0)
    widths = draw_widths(jax.random.fold_in(seeds[19], 71), 0)
    return {"tokens": tokens, "norm1_gain": norm1_gain, "norm1_bias": norm1_bias, "query_taps": query_taps, "query_weight": query_weight, "key_weight": key_weight, "value_weight": value_weight, "out_weight": out_weight, "out_bias": out_bias, "norm2_gain": norm2_gain, "norm2_bias": norm2_bias, "up_weight": up_weight, "up_bias": up_bias, "hidden_taps": hidden_taps, "down_weight": down_weight, "down_bias": down_bias, "cotangent": cotangent, "heights": heights, "widths": widths}


@jax.custom_vjp
def low(v):
    return lax.optimization_barrier(v.astype(jnp.bfloat16)).astype(jnp.float32)

@jax.custom_vjp
def low_back(v):
    return v

def low_keep(v):
    return (low(v), None)

def low_pass(kept, grad):
    return (grad,)

def back_keep(v):
    return (v, None)

def back_low(kept, grad):
    return (low(grad),)
low.defvjp(low_keep, low_pass)
low_back.defvjp(back_keep, back_low)
highest = lax.Precision.HIGHEST

def multiply(left, right):
    return jnp.einsum('...d,de->...e', left, right, precision=highest)

def layer_norm(values, gain, shift):
    center = lax.optimization_barrier(jnp.mean(values, axis=-1, keepdims=True))
    centered = values - center
    return centered * lax.rsqrt(lax.optimization_barrier(jnp.mean(centered * centered, axis=-1, keepdims=True)) + 1e-05) * gain + shift

def convolve(field, taps):
    row_count = field.shape[2]
    column_count = field.shape[3]
    padded = jnp.pad(field, ((0, 0), (0, 0), (1, 1), (1, 1), (0, 0)))
    total_sum = jnp.zeros_like(field)
    for row_tap in range(3):
        for col_tap in range(3):
            total_sum = total_sum + taps[row_tap, col_tap] * padded[:, :, row_tap:row_tap + row_count, col_tap:col_tap + column_count]
    return total_sum

def attend_block(query_block, image_keys, image_values, image_mask):
    scores = low_back(jnp.einsum('qhd,khd->hqk', query_block, image_keys, precision=highest) * HDIM ** (-0.5))
    scores = jnp.where(image_mask[None, None, :], scores, -1e+30)
    peak = lax.optimization_barrier(jnp.max(scores, axis=-1, keepdims=True))
    exponent = jnp.exp(scores - peak)
    probability = exponent / lax.optimization_barrier(jnp.sum(exponent, axis=-1, keepdims=True))
    mixture = jnp.einsum('hqk,khd->qhd', low(probability), image_values, precision=highest)
    return low(low_back(mixture))
attend_saved = jax.checkpoint(attend_block)

def reference(tokens, norm1_gain, norm1_bias, query_taps, query_weight, key_weight, value_weight, out_weight, out_bias, norm2_gain, norm2_bias, up_weight, up_bias, hidden_taps, down_weight, down_bias, cotangent, heights, widths):
    row_index = jnp.arange(H)
    col_index = jnp.arange(W)
    valid_cells = (row_index[None, :, None] < heights[:, None, None]) & (col_index[None, None, :] < widths[:, None, None])
    pooled_rows = 2 * jnp.arange(H // 2)
    pooled_cols = 2 * jnp.arange(W // 2)
    pooled_valid = (pooled_rows[None, :, None] < heights[:, None, None]) & (pooled_cols[None, None, :] < widths[:, None, None])
    key_mask = jnp.broadcast_to(pooled_valid[:, None], (IMAGES, TASKS, H // 2, W // 2)).reshape(IMAGES, TASKS * (H // 2) * (W // 2))

    def forward(stream, norm1_gain, norm1_bias, query_taps, query_weight, key_weight, value_weight, out_weight, out_bias, norm2_gain, norm2_bias, up_weight, up_bias, hidden_taps, down_weight, down_bias):
        normal_one = low(layer_norm(stream, norm1_gain, norm1_bias))
        conv_query = low(low_back(convolve(normal_one, query_taps)))
        queries = low(low_back(multiply(conv_query, query_weight)))
        pooled = low(lax.optimization_barrier(jnp.mean(normal_one.reshape(IMAGES, TASKS, H // 2, 2, W // 2, 2, D), axis=(3, 5))))
        keys = low(multiply(pooled, key_weight))
        values = low(multiply(pooled, value_weight))
        query_rows = TASKS * H * W
        block_rows = 512 if query_rows % 512 == 0 else query_rows
        pieces = []
        for image in range(IMAGES):
            image_queries = queries[image].reshape(query_rows // block_rows, block_rows, HEADS, HDIM)
            image_keys = keys[image].reshape(-1, HEADS, HDIM)
            image_values = values[image].reshape(-1, HEADS, HDIM)
            image_mask = key_mask[image]
            mixed_blocks = lax.map(lambda query_block: attend_saved(query_block, image_keys, image_values, image_mask), image_queries)
            pieces.append(mixed_blocks.reshape(TASKS, H, W, D))
        attended = jnp.stack(pieces)
        branch_attn = low_back(multiply(attended, out_weight)) + out_bias
        middle = stream + branch_attn
        normal_two = low(layer_norm(middle, norm2_gain, norm2_bias))
        lifted = low(low_back(multiply(normal_two, up_weight) + up_bias))
        spread = low_back(convolve(lifted, hidden_taps))
        activated = low(jax.nn.gelu(spread))
        branch_mlp = multiply(activated, down_weight) + down_bias
        final_stream = middle + branch_mlp
        return (final_stream, (branch_attn, branch_mlp, final_stream))
    inputs = (tokens.astype(jnp.float32), norm1_gain, norm1_bias, query_taps, query_weight.astype(jnp.float32), key_weight.astype(jnp.float32), value_weight.astype(jnp.float32), out_weight.astype(jnp.float32), out_bias, norm2_gain, norm2_bias, up_weight.astype(jnp.float32), up_bias, hidden_taps, down_weight.astype(jnp.float32), down_bias)
    final_stream, backward, extras = jax.vjp(forward, *inputs, has_aux=True)
    grads = backward(cotangent.astype(jnp.float32))
    weighting = jnp.broadcast_to(valid_cells[:, None, :, :, None], (IMAGES, TASKS, H, W, 1)).astype(jnp.float32)
    token_total = jnp.sum(weighting) * D
    stat_list = [jnp.sqrt(jnp.sum(piece * piece * weighting) / token_total) for piece in extras]
    stats = jnp.stack(stat_list)
    return (final_stream.astype(jnp.bfloat16), grads[0], grads[1], grads[2], grads[3], grads[4], grads[5], grads[6], grads[7], grads[8], grads[9], grads[10], grads[11], grads[12], grads[13], grads[14], grads[15], stats)
```

```python
import jax
import jax.numpy as jnp
from jax import lax
from jax.experimental import pallas as pl
from jax.experimental.pallas import tpu as pltpu
from jax.sharding import PartitionSpec as P

HEADS = 6
LANES = 128
HALF = 64
GUARD = 8
SMALL = 64
epsilon = 1e-05
f32 = jnp.float32
bf16 = jnp.bfloat16
NN = (((1,), (0,)), ((), ()))
NT = (((1,), (1,)), ((), ()))
TN = (((0,), (0,)), ((), ()))


def dot(left, right, form=NN):
    return lax.dot_general(left, right, form, preferred_element_type=f32)


def call(kernel, outs, args, smem=0, scratch=(), us=5, limit=48):
    specs = [pl.BlockSpec(memory_space=pltpu.SMEM)] * smem
    specs += [pl.BlockSpec(memory_space=pltpu.VMEM)] * (len(args) - smem)
    return pl.pallas_call(
        kernel,
        out_shape=tuple(jax.ShapeDtypeStruct(s, d) for s, d in outs),
        in_specs=specs,
        out_specs=tuple(pl.BlockSpec(memory_space=pltpu.VMEM) for _ in outs),
        scratch_shapes=list(scratch),
        compiler_params=pltpu.CompilerParams(vmem_limit_bytes=limit << 20),
        cost_estimate=pl.CostEstimate(
            flops=int(us * 1e9), bytes_accessed=int(us * 1e6), transcendentals=0
        ),
    )(*args)


def normalize(values):
    center = jnp.mean(values, axis=-1, keepdims=True)
    centered = values - center
    inverse = lax.rsqrt(jnp.mean(centered * centered, axis=-1, keepdims=True) + epsilon)
    return centered * inverse, inverse


def normalize_back(grad_output, gain, normed, inverse):
    scaled = grad_output * gain
    return inverse * (
        scaled
        - jnp.mean(scaled, axis=-1, keepdims=True)
        - normed * jnp.mean(scaled * normed, axis=-1, keepdims=True)
    )


def column_sum(values):
    return jnp.sum(values, axis=0, keepdims=True)


def flat(ref):
    value = ref[...]
    return value.reshape(-1, value.shape[-1])


def band_flags():
    me = lax.axis_index("rows")
    count = lax.axis_size("rows")
    return me, (me > 0).astype(f32), (me < count - 1).astype(f32)


def pool_matrix(width):
    rows = lax.broadcasted_iota(jnp.int32, (width // 2, 2 * width), 0)
    cols = lax.broadcasted_iota(jnp.int32, (width // 2, 2 * width), 1)
    cols = jnp.where(cols >= width, cols - width, cols)
    return jnp.where((cols >> 1) == rows, 0.25, 0.0).astype(bf16)


def first_norm_kernel(tokens, gain, bias, normal, pooled):
    tasks, rows, width, model = tokens.shape
    matrix = pool_matrix(width)
    scale = gain[...].reshape(1, model)
    shift = bias[...].reshape(1, model)
    for task in range(tasks):
        for row in range(0, rows, 2):
            value = tokens[task, row : row + 2].astype(f32).reshape(2 * width, model)
            low = (normalize(value)[0] * scale + shift).astype(bf16)
            normal[task, row : row + 2] = low.reshape(2, width, model)
            start = (task * (rows // 2) + row // 2) * (width // 2)
            pooled[start : start + width // 2, :] = dot(matrix, low).astype(bf16)


def clear_guards(wide):
    lines, length, model = wide.shape
    zero = jnp.zeros((lines, GUARD, model), wide.dtype)
    wide[:, 0:GUARD, :] = zero
    wide[:, length - GUARD : length, :] = zero


def query_kernel(normal, before, after, gain, bias, taps, weight, extended, conv, queries, wide):
    tasks, rows, width, model = normal.shape
    _, has_before, has_after = band_flags()
    scale = gain[...].reshape(1, model)
    shift = bias[...].reshape(1, model)
    clear_guards(wide)
    lines = rows + 2
    for task in range(tasks):
        top = (normalize(before[task, 0].astype(f32))[0] * scale + shift) * has_before
        low = (normalize(after[task, 0].astype(f32))[0] * scale + shift) * has_after
        extended[task, 0] = top.astype(bf16)
        extended[task, lines - 1] = low.astype(bf16)
        for row in range(rows):
            extended[task, row + 1] = normal[task, row]
        for line in range(lines):
            wide[task * lines + line, GUARD : GUARD + width, :] = extended[task, line].astype(f32)

    def body(step, carry):
        task = step // (model // LANES)
        lanes = pl.ds(pl.multiple_of((step % (model // LANES)) * LANES, LANES), LANES)
        for row in range(rows):
            for start in range(0, width, 16):
                total = jnp.zeros((16, LANES), f32)
                for a in range(3):
                    for b in range(3):
                        at = GUARD - 1 + b + start
                        total = total + taps[a, b, lanes][None, :] * wide[
                            task * lines + row + a, at : at + 16, lanes
                        ]
                conv[task, row, start : start + 16, lanes] = total.astype(bf16)
        return carry

    lax.fori_loop(0, tasks * (model // LANES), body, 0)
    product = dot(flat(conv), weight[...]).astype(bf16)
    scaled = product * jnp.asarray(HALF**-0.5, bf16)
    queries[...] = scaled.reshape(queries.shape)


def half_mask(shape, side):
    lane = lax.broadcasted_iota(jnp.int32, shape, 1)
    return (lane < HALF) if side == 0 else (lane >= HALF)


def small_lane(shape):
    return lax.broadcasted_iota(jnp.int32, shape, 1) & (HALF - 1)


def pieces(value):
    high = value.astype(bf16).astype(f32)
    middle = (value - high).astype(bf16).astype(f32)
    return high, middle, value - high - middle


def marked(lead, value, shape):
    lane = small_lane(shape)
    high, middle, low = pieces(value)
    rest = jnp.where(lane == 1, high, jnp.where(lane == 2, middle, jnp.where(lane == 3, low, 0.0)))
    return jnp.where(lane == 0, lead, rest).astype(bf16)


def token_weight(lines, tasks, width, first_row, height, valid_width):
    count = tasks * len(lines) * width
    index = lax.broadcasted_iota(jnp.int32, (count, 1), 0)
    col = index & (width - 1)
    place = (index // width) % len(lines)
    row = jnp.zeros_like(place)
    for position, line in enumerate(lines):
        row = jnp.where(place == position, line, row)
    return ((first_row + row < height) & (col < valid_width)).astype(f32)


def attend_kernel(lines, order, *refs):
    refs = list(refs)
    heights, widths = refs[:2]
    del refs[:2]
    if order is not None:
        pooled = refs[: len(order)]
        del refs[: len(order)]
        key_weight, value_weight = refs[:2]
        del refs[:2]
    else:
        keys, values, extra = refs[:3]
        del refs[:3]
    queries, tokens, out_weight, out_bias, gain, bias = refs[:6]
    del refs[:6]
    if order is not None:
        keys, values, extra = refs[:3]
        del refs[:3]
    attended, middle, normal, marks, square, held = refs
    tasks, rows, width, model = tokens.shape
    me = lax.axis_index("rows")
    height, valid_width = heights[0], widths[0]
    if order is not None:
        cells = pooled[0].shape[0]
        pooled_rows = rows // 2
        for position, offset in enumerate(order):
            part = slice(position * cells, (position + 1) * cells)
            block = pooled[position][...]
            keys[part, :] = dot(block, key_weight[...]).astype(bf16)
            values[part, :] = dot(block, value_weight[...]).astype(bf16)
            cell = lax.broadcasted_iota(jnp.int32, (cells, LANES), 0)
            col = cell & (width // 2 - 1)
            row = (cell // (width // 2)) % pooled_rows + (me ^ offset) * pooled_rows
            good = (2 * row < height) & (2 * col < valid_width)
            lane = small_lane((cells, LANES))
            ones = jnp.where(lane < 4, 1.0, 0.0)
            extra[part, :] = jnp.where(
                lane == 0, jnp.where(good, 0.0, -1e30), ones
            ).astype(bf16)
    held[...] = jnp.concatenate(
        [queries[task, line] for task in range(tasks) for line in lines], axis=0
    )
    query_count = held.shape[0]
    key_count = keys.shape[0]
    chunk = query_count if key_count <= 2048 else LANES
    chunk_count = query_count // chunk

    def body(step, carry):
        pair = step // chunk_count
        lanes = pl.ds(pl.multiple_of(pair * LANES, LANES), LANES)
        part = pl.ds(pl.multiple_of((step % chunk_count) * chunk, chunk), chunk)
        key_pair, value_pair, extras = keys[:, lanes], values[:, lanes], extra[...]
        query_pair = held[part, lanes]
        mixtures = []
        for side in range(2):
            key_half = half_mask(key_pair.shape, side)
            query_half = half_mask(query_pair.shape, side)
            lead = jnp.where(small_lane(query_pair.shape) == 0, 1.0, 0.0).astype(bf16)
            scores = dot(
                jnp.where(query_half, query_pair, lead), jnp.where(key_half, key_pair, extras), NT
            )
            peak = jnp.max(scores, axis=-1, keepdims=True)
            weights = jnp.exp(scores - peak).astype(bf16)
            mixture = dot(weights, jnp.where(key_half, value_pair, extras))
            at = (1 - side) * HALF + 1
            total = mixture[:, at : at + 1]
            mark = marked(1.0, -(peak + jnp.log(total)), query_pair.shape)
            marks[2 * pair + side, part, :] = jnp.where(query_half, query_pair, mark)
            mixtures.append(mixture / total)
        chosen = jnp.where(half_mask(query_pair.shape, 0), mixtures[0], mixtures[1])
        attended[part, lanes] = chosen.astype(bf16)
        return carry

    lax.fori_loop(0, HEADS // 2 * chunk_count, body, 0)
    branch = dot(attended[...], out_weight[...]) + out_bias[...].reshape(1, model)
    stream = jnp.concatenate(
        [tokens[task, line] for task in range(tasks) for line in lines], axis=0
    ).astype(f32)
    total = stream + branch
    middle[...] = total.reshape(middle.shape)
    normed, _ = normalize(total)
    normal[...] = (
        (normed * gain[...].reshape(1, model) + bias[...].reshape(1, model))
        .astype(bf16)
        .reshape(normal.shape)
    )
    weight = token_weight(lines, tasks, width, me * rows, height, valid_width)
    square[...] = column_sum(branch * branch * weight)


def store_piece(owner, me, keep, send, start, piece):
    place = owner ^ me
    size = piece.shape[0]

    @pl.when((place & 1) == 0)
    def _():
        keep[place >> 1, start : start + size, :] = piece

    @pl.when((place & 1) == 1)
    def _():
        send[place >> 1, start : start + size, :] = piece


def feed_kernel(
    heights, widths, edge, inner, before, after, up_weight, up_bias, taps, down_weight, down_bias,
    cotangent, edge_middle, inner_middle,
    layer_out, grad_edge, grad_inner, to_before, to_after, keep, send, grad_taps, grad_up_bias, sums,
    normal, wide, grad_act, wide_back, active, grad_lifted, branch, grad_normal,
):
    tasks, rows, width, model = cotangent.shape
    part = up_weight.shape[1]
    step = pl.program_id(0)
    last = pl.num_programs(0) - 1
    me, has_before, has_after = band_flags()
    count = lax.axis_size("rows")
    lines = rows + 2

    @pl.when(step == 0)
    def _():
        clear_guards(wide)
        clear_guards(wide_back)
        branch[...] = jnp.zeros_like(branch)
        grad_normal[...] = jnp.zeros_like(grad_normal)
        for task in range(tasks):
            normal[task, 0] = before[task, 0]
            normal[task, 1] = edge[task, 0]
            for row in range(rows - 2):
                normal[task, row + 2] = inner[task, row]
            normal[task, rows] = edge[task, 1]
            normal[task, rows + 1] = after[task, 0]

    fed = flat(normal)
    lifted = dot(fed, up_weight[...]) + up_bias[...].reshape(1, part)
    lifted = lifted.astype(bf16).astype(f32).reshape(tasks, lines, width, part)
    for task in range(tasks):
        for line in range(lines):
            value = lifted[task, line]
            if line == 0:
                value = value * has_before
            if line == lines - 1:
                value = value * has_after
            wide[task * lines + line, GUARD : GUARD + width, :] = value
    grad_output = flat(cotangent)
    grad_act[...] = dot(grad_output, down_weight[...], NT).reshape(grad_act.shape)

    c1 = 0.7978845608028654
    c2 = c1 * 0.044715
    blocks = part // LANES

    def across(block, carry):
        lanes = pl.ds(pl.multiple_of(block * LANES, LANES), LANES)
        tap = [[taps[a, b, lanes][None, :] for b in range(3)] for a in range(3)]

        def one_task(task, sums9):
            sums9 = list(sums9)
            for row in range(rows):
                for start in range(0, width, 16):
                    near = []
                    spread = None
                    for a in range(3):
                        for b in range(3):
                            at = GUARD - 1 + b + start
                            value = wide[task * lines + row + a, at : at + 16, lanes]
                            near.append(value)
                            term = tap[a][b] * value
                            spread = term if spread is None else spread + term
                    squared = spread * spread
                    gate = 0.5 + 0.5 * jnp.tanh(spread * (c1 + c2 * squared))
                    active[task * rows + row, start : start + 16, lanes] = (spread * gate).astype(
                        bf16
                    )
                    slope = gate + spread * (gate - gate * gate) * (2 * c1 + 6 * c2 * squared)
                    grad = grad_act[task * rows + row, start : start + 16, lanes] * slope
                    grad = grad.astype(bf16).astype(f32)
                    wide_back[
                        task * rows + row, GUARD + start : GUARD + start + 16, lanes
                    ] = grad
                    for k in range(9):
                        both = near[k] * grad
                        sums9[k] = sums9[k] + (both[0:8] + both[8:16])
            return tuple(sums9)

        sums9 = lax.fori_loop(
            0, tasks, one_task, tuple(jnp.zeros((8, LANES), f32) for _ in range(9))
        )
        for k in range(9):
            grad_taps[k // 3, k % 3, lanes] = jnp.sum(sums9[k], axis=0)

        def back_task(task, total):
            for line in range(lines):
                for start in range(0, width, 16):
                    value = None
                    for a in range(3):
                        if not 0 <= line - a < rows:
                            continue
                        for b in range(3):
                            at = GUARD + 1 - b + start
                            term = tap[a][b] * wide_back[
                                task * rows + line - a, at : at + 16, lanes
                            ]
                            value = term if value is None else value + term
                    if line == 0:
                        value = value * has_before
                    if line == lines - 1:
                        value = value * has_after
                    low = value.astype(bf16)
                    grad_lifted[task * lines + line, start : start + 16, lanes] = low
                    low = low.astype(f32)
                    total = total + (low[0:8] + low[8:16])
            return total

        total = lax.fori_loop(0, tasks, back_task, jnp.zeros((8, LANES), f32))
        grad_up_bias[0, :, lanes] = column_sum(total)
        return carry

    lax.fori_loop(0, blocks, across, 0)

    act = flat(active)
    branch[...] += dot(act, down_weight[...])
    grad_down = dot(act, grad_output, TN).astype(bf16)
    grad_low = flat(grad_lifted)
    grad_up = dot(fed, grad_low, TN).astype(bf16)
    grad_normal[...] += dot(grad_low, up_weight[...], NT)
    size = keep.shape[1] // 2
    groups = part // size
    for group in range(groups):
        rows_of = slice(group * size, (group + 1) * size)
        store_piece(group * (count // groups) + step, me, keep, send, 0, grad_up[rows_of])
        store_piece(step * groups + group, me, keep, send, size, grad_down[rows_of])

    @pl.when(step == last)
    def _():
        shift = down_bias[...].reshape(1, model)
        height, valid_width = heights[0], widths[0]
        whole = branch[...].reshape(tasks, rows, width, model)
        grads = grad_normal[...].reshape(tasks, lines, width, model)
        first = jnp.zeros((1, model), f32)
        second = jnp.zeros((1, model), f32)
        col = lax.broadcasted_iota(jnp.int32, (width, 1), 0)
        for task in range(tasks):
            for row in range(rows):
                if row == 0 or row == rows - 1:
                    stream = edge_middle[task, 0 if row == 0 else 1]
                else:
                    stream = inner_middle[task, row - 1]
                mlp = whole[task, row] + shift
                final = stream + mlp
                layer_out[task, row] = final.astype(bf16)
                inside = (col < valid_width) & (me * rows + row < height)
                weight = inside.astype(f32)
                first = first + column_sum(mlp * mlp * weight)
                second = second + column_sum(final * final * weight)
            to_before[task, 0] = grads[task, 0].astype(bf16)
            grad_edge[task, 0] = grads[task, 1]
            for row in range(rows - 2):
                grad_inner[task, row] = grads[task, row + 2]
            grad_edge[task, 1] = grads[task, rows]
            to_after[task, 0] = grads[task, rows + 1].astype(bf16)
        bias_sum = column_sum(grad_output.astype(f32))
        sums[...] = jnp.concatenate(
            [bias_sum, first, second, jnp.zeros((5, model), f32)], axis=0
        )


def feed(heights, widths, edge, inner, before, after, up_weight, up_bias, taps, down_weight,
         down_bias, cotangent, edge_middle, inner_middle, count):
    tasks, rows, width, model = cotangent.shape
    hidden = up_weight.shape[1]
    part = model
    lines = rows + 2
    size = hidden // count
    smem = pl.BlockSpec(memory_space=pltpu.SMEM)

    def whole(shape):
        return pl.BlockSpec(shape, lambda i, k=len(shape): (0,) * k)

    ins = [
        smem, smem, whole(edge.shape), whole(inner.shape), whole(before.shape), whole(after.shape),
        pl.BlockSpec((model, part), lambda i: (0, i)),
        pl.BlockSpec((1, 1, part), lambda i: (i, 0, 0)),
        pl.BlockSpec((3, 3, part), lambda i: (0, 0, i)),
        pl.BlockSpec((part, model), lambda i: (i, 0)),
        whole(down_bias.shape), whole(cotangent.shape), whole(edge_middle.shape), whole(inner_middle.shape),
    ]
    line_shape = (tasks, 1, width, model)
    outs = [
        (cotangent.shape, bf16), (edge.shape, f32), (inner.shape, f32), (line_shape, bf16), (line_shape, bf16),
        ((count // 2, 2 * size, model), bf16), ((count // 2, 2 * size, model), bf16),
        ((3, 3, hidden), f32), ((hidden // part, 1, part), f32), ((8, model), f32),
    ]
    out_specs = [whole(s) for s, _ in outs]
    out_specs[7] = pl.BlockSpec((3, 3, part), lambda i: (0, 0, i))
    out_specs[8] = pl.BlockSpec((1, 1, part), lambda i: (i, 0, 0))
    return pl.pallas_call(
        feed_kernel,
        grid=(hidden // part,),
        out_shape=tuple(jax.ShapeDtypeStruct(s, d) for s, d in outs),
        in_specs=ins,
        out_specs=tuple(out_specs),
        scratch_shapes=[
            pltpu.VMEM((tasks, lines, width, model), bf16),
            pltpu.VMEM((tasks * lines, width + 2 * GUARD, part), f32),
            pltpu.VMEM((tasks * rows, width, part), f32),
            pltpu.VMEM((tasks * rows, width + 2 * GUARD, part), f32),
            pltpu.VMEM((tasks * rows, width, part), bf16),
            pltpu.VMEM((tasks * lines, width, part), bf16),
            pltpu.VMEM((tasks * rows * width, model), f32),
            pltpu.VMEM((tasks * lines * width, model), f32),
        ],
        compiler_params=pltpu.CompilerParams(
            vmem_limit_bytes=52 << 20, dimension_semantics=("arbitrary",)
        ),
        cost_estimate=pl.CostEstimate(flops=int(30e9), bytes_accessed=int(30e6), transcendentals=0),
    )(heights, widths, edge, inner, before, after, up_weight, up_bias, taps, down_weight, down_bias,
      cotangent, edge_middle, inner_middle)


def attend_back_kernel(lines, edge, *refs):
    refs = list(refs)
    grad_normal, middle, cotangent, gain, out_weight, attended, marks, keys, values, extra = refs[:10]
    del refs[:10]
    if edge:
        from_before, from_after, more_keys, more_values, more_out, more_sums = refs[:6]
        del refs[:6]
    grad_middle, grad_queries, grad_keys, grad_values, grad_out, sums = refs[:6]
    grad_marks, grad_pair, query_total = refs[6:]
    tasks, rows, width, model = cotangent.shape
    scale = gain[...].reshape(1, model)
    query_count = attended.shape[0]
    key_count = keys.shape[0]

    if edge:
        pieces_of = []
        for task in range(tasks):
            pieces_of.append(grad_normal[task, 0] + from_before[task, 0].astype(f32))
            pieces_of.append(grad_normal[task, 1] + from_after[task, 0].astype(f32))
        grad_input = jnp.concatenate(pieces_of, axis=0)
    else:
        grad_input = flat(grad_normal)
    normed, inverse = normalize(flat(middle))
    gain_sum = column_sum(grad_input * normed)
    bias_sum = column_sum(grad_input)
    grad_final = jnp.concatenate(
        [cotangent[task, line] for task in range(tasks) for line in lines], axis=0
    ).astype(f32)
    total = grad_final + normalize_back(grad_input, scale, normed, inverse)
    grad_middle[...] = total.reshape(grad_middle.shape)
    out_sum = column_sum(total)
    sums_now = jnp.concatenate([gain_sum, bias_sum, out_sum, jnp.zeros((5, model), f32)], axis=0)
    grad_branch = total.astype(bf16)
    grad_out_now = dot(attended[...], grad_branch, TN)
    if edge:
        sums_now = sums_now + more_sums[...]
        grad_out_now = grad_out_now + more_out[...]
    sums[...] = sums_now
    grad_out[...] = grad_out_now
    grad_attended = dot(grad_branch, out_weight[...], NT).astype(bf16)
    shape = (query_count, LANES)
    for pair in range(HEADS // 2):
        lanes = slice(pair * LANES, (pair + 1) * LANES)
        grad_two = grad_attended[:, lanes]
        both = grad_two.astype(f32) * attended[:, lanes].astype(f32)
        for side in range(2):
            half = half_mask(shape, side)
            inner = jnp.sum(jnp.where(half, both, 0.0), axis=-1, keepdims=True)
            grad_marks[2 * pair + side] = jnp.where(half, grad_two, marked(0.0, -inner, shape))
    block = 512

    def body(step, carry):
        pair = step // (key_count // block)
        place = step % (key_count // block)
        lanes = pl.ds(pl.multiple_of(pair * LANES, LANES), LANES)
        part = pl.ds(pl.multiple_of(place * block, block), block)
        key_pair, value_pair, extras = keys[part, lanes], values[part, lanes], extra[part, :]
        lows, grads, query_rows, grad_rows, key_rows = [], [], [], [], []
        for side in range(2):
            key_half = half_mask((block, LANES), side)
            query_half = half_mask(shape, side)
            query = marks[2 * pair + side]
            grad = grad_marks[2 * pair + side]
            scores = dot(jnp.where(key_half, key_pair, extras), query, NT)
            grad_prob = dot(jnp.where(key_half, value_pair, extras), grad, NT)
            probability = jnp.exp(scores)
            grads.append((probability * grad_prob).astype(bf16))
            lows.append(probability.astype(bf16))
            zero = jnp.zeros(shape, bf16)
            query_rows.append(jnp.where(query_half, query, zero))
            grad_rows.append(jnp.where(query_half, grad, zero))
            key_rows.append(jnp.where(key_half, key_pair, jnp.zeros((block, LANES), bf16)))
        value_part = dot(jnp.concatenate(lows, axis=1), jnp.concatenate(grad_rows, axis=0))
        key_part = dot(jnp.concatenate(grads, axis=1), jnp.concatenate(query_rows, axis=0))
        query_part = dot(
            jnp.concatenate(grads, axis=0), jnp.concatenate(key_rows, axis=0), TN
        )
        if edge:
            value_part = value_part + more_values[part, lanes].astype(f32)
            key_part = key_part + more_keys[part, lanes].astype(f32)
        grad_values[part, lanes] = value_part.astype(bf16)
        grad_keys[part, lanes] = key_part.astype(bf16)

        @pl.when(place == 0)
        def _():
            query_total[:, lanes] = query_part

        @pl.when(place > 0)
        def _():
            query_total[:, lanes] += query_part

        return carry

    lax.fori_loop(0, HEADS // 2 * (key_count // block), body, 0)
    grad_queries[...] = (
        (query_total[...] * HALF**-0.5).astype(bf16).reshape(grad_queries.shape)
    )


def pool_back_kernel(order, *refs):
    (grad_keys, grad_values, key_weight, value_weight, edge_queries, inner_queries, query_weight,
     keep, send, grad_conv, first, last) = refs
    tasks, rows, width, model = grad_conv.shape
    cells = keep.shape[1]
    for position, offset in enumerate(order):
        part = slice(position * cells, (position + 1) * cells)
        total = dot(grad_keys[part, :], key_weight[...], NT) + dot(
            grad_values[part, :], value_weight[...], NT
        )
        target = send if offset & 1 else keep
        target[offset >> 1] = total.astype(bf16)
    edge = dot(flat(edge_queries), query_weight[...], NT).astype(bf16)
    inner = dot(flat(inner_queries), query_weight[...], NT).astype(bf16)
    edge = edge.reshape(edge_queries.shape)
    inner = inner.reshape(inner_queries.shape)
    for task in range(tasks):
        grad_conv[task, 0] = edge[task, 0]
        grad_conv[task, rows - 1] = edge[task, 1]
        first[task, 0] = edge[task, 0]
        last[task, 0] = edge[task, 1]
        for row in range(rows - 2):
            grad_conv[task, row + 1] = inner[task, row]


def weight_kernel(order, *refs):
    refs = list(refs)
    heights, widths = refs[:2]
    del refs[:2]
    pooled = refs[: len(order)]
    del refs[: len(order)]
    (grad_keys, grad_values, pool_keep, pool_send, conv, edge_queries, inner_queries, extended,
     grad_conv, taps, gain, bias, grad_out, edge_square, inner_square, back_sums, feed_sums,
     hidden_taps, up_bias, keep, send, wide, rows_of) = refs
    tasks, rows, width, model = grad_conv.shape
    count = len(order)
    cells = pooled[0].shape[0]
    lines = rows + 2
    me, has_before, has_after = band_flags()
    size = keep.shape[1] - 16

    def put(which, grad):
        groups = model // size
        low = grad.astype(bf16)
        for group in range(groups):
            store_piece(
                which * groups + group, me, keep, send, 0, low[group * size : (group + 1) * size]
            )

    grad_key = jnp.zeros((model, model), f32)
    grad_value = jnp.zeros((model, model), f32)
    pool_sum = jnp.zeros((1, model), f32)
    pool_dot = jnp.zeros((1, model), f32)
    for position, offset in enumerate(order):
        part = slice(position * cells, (position + 1) * cells)
        block = pooled[position][...]
        grad_key = grad_key + dot(block, grad_keys[part, :], TN)
        grad_value = grad_value + dot(block, grad_values[part, :], TN)
        source = pool_send if offset & 1 else pool_keep
        grad = source[offset >> 1].astype(f32)
        pool_sum = pool_sum + column_sum(grad)
        pool_dot = pool_dot + column_sum(grad * block.astype(f32))
    put(1, grad_key)
    put(2, grad_value)
    put(3, grad_out[...])
    edge_conv = jnp.concatenate(
        [conv[task, line] for task in range(tasks) for line in (0, rows - 1)], axis=0
    )
    inner_conv = jnp.concatenate(
        [conv[task, line] for task in range(tasks) for line in range(1, rows - 1)], axis=0
    )
    put(0, dot(edge_conv, flat(edge_queries), TN) + dot(inner_conv, flat(inner_queries), TN))

    clear_guards(wide)
    for task in range(tasks):
        for line in range(lines):
            wide[task * lines + line, GUARD : GUARD + width, :] = extended[task, line].astype(f32)

    def across(block, carry):
        lanes = pl.ds(pl.multiple_of(block * LANES, LANES), LANES)

        def one_task(task, sums9):
            sums9 = list(sums9)
            for row in range(rows):
                for start in range(0, width, 16):
                    grad = grad_conv[task, row, start : start + 16, lanes].astype(f32)
                    for k in range(9):
                        at = GUARD - 1 + k % 3 + start
                        both = grad * wide[task * lines + row + k // 3, at : at + 16, lanes]
                        sums9[k] = sums9[k] + (both[0:8] + both[8:16])
            return tuple(sums9)

        sums9 = lax.fori_loop(
            0, tasks, one_task, tuple(jnp.zeros((8, LANES), f32) for _ in range(9))
        )
        for k in range(9):
            rows_of[2 + k : 3 + k, lanes] = column_sum(sums9[k])
        return carry

    lax.fori_loop(0, model // LANES, across, 0)

    shift = bias[...].reshape(1, model)
    zero = jnp.zeros((1, model), f32)
    conv_dot, conv_sum = zero, zero
    for row in range(rows):
        line = grad_conv[0, row].astype(f32)
        for task in range(1, tasks):
            line = line + grad_conv[task, row].astype(f32)
        full = column_sum(line)
        by_col = (full - line[0:1], full, full - line[width - 1 : width])
        for a in range(3):
            for b in range(3):
                value = by_col[b]
                if a == 0 and row == 0:
                    value = value * has_before
                if a == 2 and row == rows - 1:
                    value = value * has_after
                conv_sum = conv_sum + taps[a, b].reshape(1, model) * value
    for k in range(9):
        conv_dot = conv_dot + taps[k // 3, k % 3].reshape(1, model) * rows_of[2 + k : 3 + k, :]
    grad_bias = conv_sum + pool_sum
    grad_gain = (conv_dot + pool_dot - shift * grad_bias) / gain[...].reshape(1, model)
    rows_of[0:1, :] = grad_gain
    rows_of[1:2, :] = grad_bias
    rows_of[11:12, :] = back_sums[2:3, :]
    rows_of[12:14, :] = back_sums[0:2, :]
    rows_of[14:15, :] = feed_sums[0:1, :]
    rows_of[15:16, :] = edge_square[...] + inner_square[...]
    rows_of[16:18, :] = feed_sums[1:3, :]
    in_rows = jnp.clip(heights[0] - me * rows, 0, rows)
    in_cols = jnp.clip(widths[0], 0, width)
    cells_in = (tasks * in_rows * in_cols).astype(f32)
    rows_of[18:19, :] = jnp.full((1, model), cells_in, f32)
    parts = up_bias.shape[0]
    for part in range(parts):
        rows_of[19 + part : 20 + part, :] = up_bias[part]
        for k in range(9):
            rows_of[19 + parts * (k + 1) + part : 20 + parts * (k + 1) + part, :] = hidden_taps[
                k // 3, k % 3, part * model : (part + 1) * model
            ].reshape(1, model)
    used = 19 + 10 * parts
    rows_of[used:SMALL, :] = jnp.zeros((SMALL - used, model), f32)
    group = SMALL // count
    for owner in range(count):
        value = rows_of[owner * group : (owner + 1) * group, :]
        if group < 8:
            value = jnp.concatenate([value, jnp.zeros((8 - group, model), f32)], axis=0)
        high = value.astype(bf16)
        low = (value - high.astype(f32)).astype(bf16)
        store_piece(owner, me, keep, send, size, jnp.concatenate([high, low], axis=0))


def last_kernel(grad_conv, before, after, taps, tokens, gain, edge_middle, inner_middle, *refs):
    parts = refs[:-2]
    input_grad, wide = refs[-2:]
    tasks, rows, width, model = tokens.shape
    lines = rows + 2
    pooled_rows = rows // 2
    clear_guards(wide)
    span = slice(GUARD, GUARD + width)
    for task in range(tasks):
        wide[task * lines, span, :] = before[task, 0].astype(f32)
        wide[task * lines + lines - 1, span, :] = after[task, 0].astype(f32)
        for row in range(rows):
            wide[task * lines + row + 1, span, :] = grad_conv[task, row].astype(f32)
    pooled = parts[0][...].astype(f32)
    for part in parts[1:]:
        pooled = pooled + part[...].astype(f32)
    pooled = pooled.astype(bf16).reshape(tasks, pooled_rows, width // 2, model)
    spread_matrix = pool_matrix(width)[:, 0:width]

    def body(step, carry):
        task = step // (model // LANES)
        lanes = pl.ds(pl.multiple_of((step % (model // LANES)) * LANES, LANES), LANES)
        for row in range(rows):
            for start in range(0, width, 16):
                total = jnp.zeros((16, LANES), f32)
                for a in range(3):
                    for b in range(3):
                        at = GUARD + 1 - b + start
                        total = total + taps[a, b, lanes][None, :] * wide[
                            task * lines + row + 2 - a, at : at + 16, lanes
                        ]
                input_grad[task, row, start : start + 16, lanes] = total
        return carry

    lax.fori_loop(0, tasks * (model // LANES), body, 0)
    scale = gain[...].reshape(1, model)
    for task in range(tasks):
        for row in range(rows):
            grad = input_grad[task, row] + dot(spread_matrix, pooled[task, row // 2], TN)
            normed, inverse = normalize(tokens[task, row].astype(f32))
            if row == 0 or row == rows - 1:
                stream = edge_middle[task, 0 if row == 0 else 1]
            else:
                stream = inner_middle[task, row - 1]
            input_grad[task, row] = stream + normalize_back(grad, scale, normed, inverse)


def combine_kernel(parts, small, *refs):
    ins, outs = refs[:parts], refs[parts:]
    for block, out in enumerate(outs):
        total = ins[0][block].astype(f32)
        for other in ins[1:]:
            total = total + other[block].astype(f32)
        if small:
            size = total.shape[0] - 16
            value = total[size : size + 8] + total[size + 8 : size + 16]
            high = value.astype(bf16)
            low = (value - high.astype(f32)).astype(bf16)
            out[0:size, :] = total[0:size].astype(bf16)
            out[size : size + 16, :] = jnp.concatenate([high, low], axis=0)
        else:
            out[...] = total.astype(bf16)


def combine(arrays, small):
    blocks, size, model = arrays[0].shape
    return call(
        lambda *refs: combine_kernel(len(arrays), small, *refs),
        [((size, model), bf16)] * blocks,
        list(arrays),
        us=1,
        limit=24,
    )


def exchange(value, axis, mask):
    count = lax.axis_size(axis)
    return lax.ppermute(value, axis, [(i, i ^ mask) for i in range(count)])


def far_masks():
    return list(range(2, lax.axis_size("rows"), 2))


def sum_over_devices(keep, send, small):
    swapped = exchange(send, "rows", 1)
    blocks = combine([keep, swapped], small)
    arrived = [exchange(blocks[mask >> 1], "rows", mask) for mask in far_masks()]
    (own,) = combine([x[None] for x in [blocks[0], *arrived]], small)
    arrived = [exchange(own, "batch", mask) for mask in range(1, lax.axis_size("batch"))]
    (own,) = combine([x[None] for x in [own, *arrived]], small)
    even = [own] + [exchange(own, "rows", mask) for mask in far_masks()]
    odd = [exchange(x, "rows", 1) for x in even]
    return even, odd


def unpack_feed_kernel(count, *refs):
    blocks, (grad_up, grad_down) = refs[:count], refs[count:]
    me = lax.axis_index("rows")
    model = grad_up.shape[0]
    size = blocks[0].shape[0] // 2
    groups = model // size
    columns = grad_up.shape[1] // model
    for j in range(count):
        owner = blocks_owner(j, count, me)
        block = blocks[j]
        up = block[0:size, :].astype(f32)
        place = owner // columns
        col = owner % columns
        grad_up[
            pl.ds(pl.multiple_of(place * size, size), size),
            pl.ds(pl.multiple_of(col * model, model), model),
        ] = up
        grad_down[pl.ds(pl.multiple_of(owner * size, size), size), :] = block[
            size : 2 * size, :
        ].astype(f32)


def blocks_owner(j, count, me):
    half = count // 2
    offset = 2 * j if j < half else 2 * (j - half) + 1
    return me ^ offset


def unpack_late_kernel(count, *refs):
    blocks = refs[:count]
    (grad_query, grad_key, grad_value, grad_out, norm1_gain, norm1_bias, query_taps, out_bias,
     norm2_gain, norm2_bias, up_bias, hidden_taps, down_bias, stats, weights, rows_of) = refs[count:]
    me = lax.axis_index("rows")
    model = grad_query.shape[0]
    size = blocks[0].shape[0] - 16
    group = SMALL // count
    for j in range(count):
        owner = blocks_owner(j, count, me)
        block = blocks[j][...].astype(f32)
        weights[pl.ds(pl.multiple_of(owner * size, size), size), :] = block[0:size]
        small = block[size : size + 8] + block[size + 8 : size + 16]
        rows_of[owner] = small
    for which, out in enumerate((grad_query, grad_key, grad_value, grad_out)):
        out[...] = weights[which * model : (which + 1) * model, :]

    def line(k):
        return rows_of[k // group, k % group, :]

    norm1_gain[...] = line(0)
    norm1_bias[...] = line(1)
    for k in range(9):
        query_taps[k // 3, k % 3, :] = line(2 + k)
    out_bias[...] = line(11)
    norm2_gain[...] = line(12)
    norm2_bias[...] = line(13)
    down_bias[...] = line(14)
    parts = up_bias.shape[0] // model
    for part in range(parts):
        lanes = slice(part * model, (part + 1) * model)
        up_bias[lanes] = line(19 + part)
        for k in range(9):
            hidden_taps[k // 3, k % 3, lanes] = line(19 + parts * (k + 1) + part)
    cells = line(18).reshape(1, model)[:, 0:1]
    row = lax.broadcasted_iota(jnp.int32, (1, LANES), 1)
    value = jnp.zeros((1, LANES), f32)
    for k in range(3):
        total = jnp.sum(line(15 + k).reshape(1, model), axis=-1, keepdims=True)
        value = jnp.where(row == k, jnp.sqrt(total / (cells * model)), value)
    stats[...] = value


def local(
    tokens,
    norm1_gain,
    norm1_bias,
    query_taps,
    query_weight,
    key_weight,
    value_weight,
    out_weight,
    out_bias,
    norm2_gain,
    norm2_bias,
    up_weight,
    up_bias,
    hidden_taps,
    down_weight,
    down_bias,
    cotangent,
    heights,
    widths,
):
    shape = tokens.shape
    tokens, cotangent = tokens[0], cotangent[0]
    tasks, rows, width, model = tokens.shape
    hidden = up_weight.shape[1]
    count = lax.axis_size("rows")
    cells = tasks * (rows // 2) * (width // 2)
    key_count = count * cells
    forward = [(i, i + 1) for i in range(count - 1)]
    backward = [(i + 1, i) for i in range(count - 1)]
    edge_lines = (0, rows - 1)
    inner_lines = tuple(range(1, rows - 1))
    lines = rows + 2

    def down_rows(line):
        return lax.ppermute(line, "rows", forward)

    def up_rows(line):
        return lax.ppermute(line, "rows", backward)

    before = down_rows(tokens[:, rows - 1 : rows])
    after = up_rows(tokens[:, 0:1])
    normal_one, pooled = call(
        first_norm_kernel,
        [(tokens.shape, bf16), ((cells, model), bf16)],
        [tokens, norm1_gain, norm1_bias],
        us=3,
        limit=24,
    )
    far = far_masks()
    order = [0, 1, *far, *[mask + 1 for mask in far]]
    swapped = exchange(pooled, "rows", 1)
    arrived = [exchange(pooled, "rows", mask) for mask in far]
    blocks = [pooled, swapped, *arrived, *[exchange(x, "rows", 1) for x in arrived]]

    line_shape = (tasks, lines, width, model)
    extended, conv, queries = call(
        query_kernel,
        [(line_shape, bf16), (tokens.shape, bf16), (tokens.shape, bf16)],
        [normal_one, before, after, norm1_gain, norm1_bias, query_taps, query_weight],
        scratch=[pltpu.VMEM((tasks * lines, width + 2 * GUARD, model), f32)],
        us=6,
        limit=24,
    )

    def attend(which, made, first):
        band = (tasks, len(which), width, model)
        query_count = tasks * len(which) * width
        outs = [
            ((query_count, model), bf16), (band, f32), (band, bf16),
            ((HEADS, query_count, LANES), bf16), ((1, model), f32),
        ]
        if first:
            outs = [((key_count, model), bf16)] * 2 + [((key_count, LANES), bf16)] + outs
        return call(
            lambda *refs: attend_kernel(which, order if first else None, *refs),
            outs,
            [heights, widths, *made, queries, tokens, out_weight, out_bias, norm2_gain, norm2_bias],
            smem=2,
            scratch=[pltpu.VMEM((query_count, model), bf16)],
            us=12,
            limit=56,
        )

    keys, values, extra, edge_att, edge_middle, edge_normal, edge_marks, edge_square = attend(
        edge_lines, [*blocks, key_weight, value_weight], True
    )
    before = down_rows(edge_normal[:, 1:2])
    after = up_rows(edge_normal[:, 0:1])
    inner_att, inner_middle, inner_normal, inner_marks, inner_square = attend(
        inner_lines, [keys, values, extra], False
    )
    (layer_out, grad_edge, grad_inner, to_before, to_after, feed_keep, feed_send, grad_hidden_taps,
     grad_up_bias, feed_sums) = feed(
        heights, widths, edge_normal, inner_normal, before, after, up_weight,
        up_bias.reshape(hidden // model, 1, model), hidden_taps, down_weight, down_bias, cotangent,
        edge_middle, inner_middle, count,
    )
    from_after = up_rows(to_before)
    from_before = down_rows(to_after)

    def attend_back(which, edge, grad_normal, middle, attended, marks, more):
        band = (tasks, len(which), width, model)
        query_count = tasks * len(which) * width
        return call(
            lambda *refs: attend_back_kernel(which, edge, *refs),
            [
                (band, f32), (band, bf16), ((key_count, model), bf16), ((key_count, model), bf16),
                ((model, model), f32), ((8, model), f32),
            ],
            [grad_normal, middle, cotangent, norm2_gain, out_weight, attended, marks, keys, values,
             extra, *more],
            scratch=[
                pltpu.VMEM((HEADS, query_count, LANES), bf16),
                pltpu.VMEM((8, LANES), f32),
                pltpu.VMEM((query_count, model), f32),
            ],
            us=22,
            limit=56,
        )

    inner_grad, inner_queries, some_keys, some_values, some_out, some_sums = attend_back(
        inner_lines, False, grad_inner, inner_middle, inner_att, inner_marks, []
    )
    edge_grad, edge_queries, grad_keys, grad_values, grad_out, back_sums = attend_back(
        edge_lines, True, grad_edge, edge_middle, edge_att, edge_marks,
        [from_before, from_after, some_keys, some_values, some_out, some_sums],
    )
    feed_even, feed_odd = sum_over_devices(feed_keep, feed_send, False)

    line = (tasks, 1, width, model)
    pool_keep, pool_send, grad_conv, first_line, last_line = call(
        lambda *refs: pool_back_kernel(order, *refs),
        [((count // 2, cells, model), bf16)] * 2 + [(tokens.shape, bf16), (line, bf16), (line, bf16)],
        [grad_keys, grad_values, key_weight, value_weight, edge_queries, inner_queries, query_weight],
        us=3,
        limit=40,
    )
    swapped = exchange(pool_send, "rows", 1)
    before = down_rows(last_line)
    after = up_rows(first_line)
    keep, send = call(
        lambda *refs: weight_kernel(order, *refs),
        [((count // 2, hidden // count + 16, model), bf16)] * 2,
        [
            heights, widths, *blocks, grad_keys, grad_values, pool_keep, pool_send, conv,
            edge_queries, inner_queries, extended, grad_conv, query_taps, norm1_gain, norm1_bias,
            grad_out, edge_square, inner_square, back_sums, feed_sums, grad_hidden_taps,
            grad_up_bias,
        ],
        smem=2,
        scratch=[
            pltpu.VMEM((tasks * lines, width + 2 * GUARD, model), f32),
            pltpu.VMEM((SMALL, model), f32),
        ],
        us=5,
        limit=48,
    )
    mine = combine([pool_keep, swapped], False)
    pool_parts = [mine[0], *[exchange(mine[mask >> 1], "rows", mask) for mask in far]]
    even, odd = sum_over_devices(keep, send, True)
    (input_grad,) = call(
        last_kernel,
        [(tokens.shape, f32)],
        [grad_conv, before, after, query_taps, tokens, norm1_gain, edge_grad, inner_grad, *pool_parts],
        scratch=[pltpu.VMEM((tasks * lines, width + 2 * GUARD, model), f32)],
        us=6,
        limit=40,
    )
    grad_up, grad_down = call(
        lambda *refs: unpack_feed_kernel(count, *refs),
        [((model, hidden), f32), ((hidden, model), f32)],
        [*feed_even, *feed_odd],
        us=2,
        limit=40,
    )
    square = ((model, model), f32)
    vector = ((model,), f32)
    late = call(
        lambda *refs: unpack_late_kernel(count, *refs),
        [square] * 4
        + [vector, vector, ((3, 3, model), f32), vector, vector, vector, ((hidden,), f32),
           ((3, 3, hidden), f32), vector, ((1, LANES), f32)],
        [*even, *odd],
        scratch=[
            pltpu.VMEM((4 * model, model), f32),
            pltpu.VMEM((count, 8, model), f32),
        ],
        us=2,
        limit=40,
    )
    (grad_query, grad_key, grad_value, grad_out, gain1, bias1, taps1, out_sum, gain2, bias2, up_sum,
     taps2, down_sum, stats) = late
    return (
        layer_out.reshape(shape),
        input_grad.reshape(shape),
        gain1,
        bias1,
        taps1,
        grad_query,
        grad_key,
        grad_value,
        grad_out,
        out_sum,
        gain2,
        bias2,
        grad_up,
        up_sum,
        taps2,
        grad_down,
        down_sum,
        stats[0, 0:3],
    )


def solution(mesh):
    band = P("batch", None, "rows", None, None)
    placed = (band, *[P()] * 15, band, P("batch"), P("batch"))
    return jax.shard_map(
        local,
        mesh=mesh,
        in_specs=placed,
        out_specs=(band, band, *[P()] * 16),
        check_vma=False,
    )
```

```python
import jax
import jax.numpy as jnp
from jax import lax
from jax.experimental import pallas as pl
from jax.experimental.pallas import tpu as pltpu
from jax.sharding import PartitionSpec as P

HEADS = 6
LANES = 128
HALF = 64
GUARD = 8
SMALL = 64
PIECES = 8
FEED_PART = 2
epsilon = 1e-05
f32 = jnp.float32
bf16 = jnp.bfloat16
NN = (((1,), (0,)), ((), ()))
NT = (((1,), (1,)), ((), ()))
TN = (((0,), (0,)), ((), ()))


def dot(left, right, form=NN):
    return lax.dot_general(left, right, form, preferred_element_type=f32)


def cost():
    return pl.CostEstimate(flops=100000, bytes_accessed=100000, transcendentals=0)


def call(name, kernel, outs, args, smem=0, scratch=(), limit=48):
    specs = [pl.BlockSpec(memory_space=pltpu.SMEM)] * smem
    specs += [pl.BlockSpec(memory_space=pltpu.VMEM)] * (len(args) - smem)
    return pl.pallas_call(
        kernel,
        out_shape=tuple(jax.ShapeDtypeStruct(s, d) for s, d in outs),
        in_specs=specs,
        out_specs=tuple(pl.BlockSpec(memory_space=pltpu.VMEM) for _ in outs),
        scratch_shapes=list(scratch),
        name=name,
        compiler_params=pltpu.CompilerParams(vmem_limit_bytes=limit << 20),
        cost_estimate=cost(),
    )(*args)


def normalize(values):
    center = jnp.mean(values, axis=-1, keepdims=True)
    centered = values - center
    inverse = lax.rsqrt(jnp.mean(centered * centered, axis=-1, keepdims=True) + epsilon)
    return centered * inverse, inverse


def normalize_back(grad_output, gain, normed, inverse):
    scaled = grad_output * gain
    return inverse * (
        scaled
        - jnp.mean(scaled, axis=-1, keepdims=True)
        - normed * jnp.mean(scaled * normed, axis=-1, keepdims=True)
    )


def column_sum(values):
    return jnp.sum(values, axis=0, keepdims=True)


def flat(ref):
    value = ref[...]
    return value.reshape(-1, value.shape[-1])


def band_flags():
    me = lax.axis_index("rows")
    count = lax.axis_size("rows")
    return me, (me > 0).astype(f32), (me < count - 1).astype(f32)


def pool_matrix(width):
    rows = lax.broadcasted_iota(jnp.int32, (width // 2, 2 * width), 0)
    cols = lax.broadcasted_iota(jnp.int32, (width // 2, 2 * width), 1)
    cols = jnp.where(cols >= width, cols - width, cols)
    return jnp.where((cols >> 1) == rows, 0.25, 0.0).astype(bf16)


def first_norm_kernel(tokens, gain, bias, normal, pooled, first, last):
    tasks, rows, width, model = tokens.shape
    matrix = pool_matrix(width)
    scale = gain[...].reshape(1, model)
    shift = bias[...].reshape(1, model)
    for task in range(tasks):
        for row in range(0, rows, 2):
            value = tokens[task, row : row + 2].astype(f32).reshape(2 * width, model)
            low = (normalize(value)[0] * scale + shift).astype(bf16)
            normal[task, row : row + 2] = low.reshape(2, width, model)
            start = (task * (rows // 2) + row // 2) * (width // 2)
            pooled[start : start + width // 2, :] = dot(matrix, low).astype(bf16)
        first[task, 0] = normal[task, 0]
        last[task, 0] = normal[task, rows - 1]


def clear_guards(wide):
    blocks, lines, length, lanes = wide.shape
    zero = jnp.zeros((blocks, lines, GUARD, lanes), wide.dtype)
    wide[:, :, 0:GUARD, :] = zero
    wide[:, :, length - GUARD : length, :] = zero


def put_line(wide, line, value):
    for block in range(wide.shape[0]):
        wide[block, line, GUARD : GUARD + value.shape[0], :] = value[
            :, block * LANES : (block + 1) * LANES
        ]


def wide_scratch(lines, width, model):
    return pltpu.VMEM((model // LANES, lines, width + 2 * GUARD, LANES), f32)


def query_kernel(normal, before, after, taps, weight, extended, conv, queries, wide):
    tasks, rows, width, model = normal.shape
    clear_guards(wide)
    lines = rows + 2
    for task in range(tasks):
        extended[task, 0] = before[task, 0]
        extended[task, lines - 1] = after[task, 0]
        for row in range(rows):
            extended[task, row + 1] = normal[task, row]
        for line in range(lines):
            put_line(wide, task * lines + line, extended[task, line].astype(f32))

    def body(step, carry):
        task = step // (model // LANES)
        block = step % (model // LANES)
        lanes = pl.ds(pl.multiple_of(block * LANES, LANES), LANES)
        for row in range(rows):
            for start in range(0, width, 16):
                total = jnp.zeros((16, LANES), f32)
                for a in range(3):
                    for b in range(3):
                        at = GUARD - 1 + b + start
                        total = total + taps[a, b, lanes][None, :] * wide[
                            block, task * lines + row + a, at : at + 16, :
                        ]
                conv[task, row, start : start + 16, lanes] = total.astype(bf16)
        return carry

    lax.fori_loop(0, tasks * (model // LANES), body, 0)
    product = dot(flat(conv), weight[...]).astype(bf16)
    scaled = product * jnp.asarray(HALF**-0.5, bf16)
    queries[...] = scaled.reshape(queries.shape)


def half_mask(shape, side):
    lane = lax.broadcasted_iota(jnp.int32, shape, 1)
    return (lane < HALF) if side == 0 else (lane >= HALF)


def small_lane(shape):
    return lax.broadcasted_iota(jnp.int32, shape, 1) & (HALF - 1)


def pieces(value):
    high = value.astype(bf16).astype(f32)
    middle = (value - high).astype(bf16).astype(f32)
    return high, middle, value - high - middle


def marked(lead, value, shape):
    lane = small_lane(shape)
    high, middle, low = pieces(value)
    rest = jnp.where(lane == 1, high, jnp.where(lane == 2, middle, jnp.where(lane == 3, low, 0.0)))
    return jnp.where(lane == 0, lead, rest).astype(bf16)


def attend_kernel(order, *refs):
    refs = list(refs)
    heights, widths = refs[:2]
    del refs[:2]
    pooled = refs[: len(order)]
    del refs[: len(order)]
    (key_weight, value_weight, queries, tokens, out_weight, out_bias, gain, bias,
     keys, values, extra, attended, middle, normal, first_line, last_line, marks, square,
     sums, totals) = refs
    tasks, rows, width, model = tokens.shape
    me = lax.axis_index("rows")
    height, valid_width = heights[0], widths[0]
    cells = pooled[0].shape[0]
    pooled_rows = rows // 2
    for position, offset in enumerate(order):
        part = slice(position * cells, (position + 1) * cells)
        block = pooled[position][...]
        keys[part, :] = dot(block, key_weight[...]).astype(bf16)
        values[part, :] = dot(block, value_weight[...]).astype(bf16)
        cell = lax.broadcasted_iota(jnp.int32, (cells, LANES), 0)
        col = cell & (width // 2 - 1)
        row = (cell // (width // 2)) % pooled_rows + (me ^ offset) * pooled_rows
        good = (2 * row < height) & (2 * col < valid_width)
        lane = small_lane((cells, LANES))
        ones = jnp.where(lane < 4, 1.0, 0.0)
        extra[part, :] = jnp.where(
            lane == 0, jnp.where(good, 0.0, -1e30), ones
        ).astype(bf16)
    query_count = queries.shape[0]
    key_count = keys.shape[0]
    block = min(512, key_count)
    together = min(4, key_count // block)
    steps = key_count // (block * together)

    def body(pair, carry):
        lanes = pl.ds(pl.multiple_of(pair * LANES, LANES), LANES)
        query_pair = queries[:, lanes]
        shape = query_pair.shape
        across = lax.broadcasted_iota(jnp.int32, (LANES, LANES), 0) < HALF
        over = lax.broadcasted_iota(jnp.int32, (LANES, LANES), 1) >= HALF
        swap = jnp.where(across == over, 1.0, 0.0).astype(bf16)
        key_all = keys[:, lanes].astype(f32)
        key_norms = dot((key_all * key_all).astype(bf16), swap)
        largest = jnp.max(key_norms, axis=0, keepdims=True)
        query_all = query_pair.astype(f32)
        query_norms = dot((query_all * query_all).astype(bf16), swap)
        bound = 1.02 * jnp.sqrt(query_norms * largest)
        small = small_lane(shape)
        mark = jnp.where(small == 0, 1.0, jnp.where(small == 1, -bound, 0.0)).astype(bf16)
        bounded = []
        bounds = []
        for side in range(2):
            query = jnp.where(half_mask(shape, side), query_pair, mark)
            bounded.append(query)
            lane = lax.broadcasted_iota(jnp.int32, (8, LANES), 1)
            chosen = jnp.where(lane == (1 - side) * HALF + 1, 1.0, 0.0).astype(bf16)
            bounds.append(-dot(chosen, query, NT)[0:1])

        def some(step, first):
            results = []
            for side in range(2):
                total = None
                for k in range(together):
                    start = pl.multiple_of((step * together + k) * block, block)
                    part = pl.ds(start, block)
                    half = half_mask((block, LANES), side)
                    extras = extra[part, :]
                    scores = dot(jnp.where(half, keys[part, lanes], extras), bounded[side], NT)
                    weights = jnp.exp(scores).astype(bf16)
                    mixture = dot(jnp.where(half, values[part, lanes], extras), weights, TN)
                    total = mixture if total is None else total + mixture
                results.append(total)
            return results

        first = some(0, True)
        for side in range(2):
            sums[side] = first[side]
        if steps > 1:

            def more(step, carry):
                for side, total in enumerate(some(step, False)):
                    sums[side] += total
                return carry

            lax.fori_loop(1, steps, more, 0)
        for side in range(2):
            totals[side : side + 1, :] = bounds[side]
        at = [(1 - side) * HALF + 1 for side in range(2)]
        least = jnp.minimum(
            jnp.min(sums[0, at[0] : at[0] + 1, :]), jnp.min(sums[1, at[1] : at[1] + 1, :])
        )

        @pl.when(jnp.logical_not(least > 1e-25))
        def _():
            lead = jnp.where(small_lane(shape) == 0, 1.0, 0.0).astype(bf16)
            for side in range(2):
                query = jnp.where(half_mask(shape, side), query_pair, lead)

                def scores_of(step):
                    part = pl.ds(pl.multiple_of(step * LANES, LANES), LANES)
                    half = half_mask((LANES, LANES), side)
                    extras = extra[part, :]
                    value = jnp.where(half, values[part, lanes], extras)
                    return dot(jnp.where(half, keys[part, lanes], extras), query, NT), value

                def highest(step, peak):
                    scores, _ = scores_of(step)
                    return jnp.maximum(peak, jnp.max(scores, axis=0, keepdims=True))

                start = jnp.full((1, query_count), -jnp.inf, f32)
                peak = lax.fori_loop(0, key_count // LANES, highest, start)
                totals[side : side + 1, :] = peak
                sums[side] = jnp.zeros((LANES, query_count), f32)

                def add(step, carry):
                    scores, value = scores_of(step)
                    weights = jnp.exp(scores - totals[side : side + 1, :]).astype(bf16)
                    sums[side] += dot(value, weights, TN)
                    return carry

                lax.fori_loop(0, key_count // LANES, add, 0)

        both = []
        row = lax.broadcasted_iota(jnp.int32, (LANES, query_count), 0)
        small = row & (HALF - 1)
        for side in range(2):
            mixture = sums[side]
            total = mixture[at[side] : at[side] + 1]
            high, middle_part, low = pieces(-(totals[side : side + 1, :] + jnp.log(total)))
            mark = jnp.where(
                small == 0,
                1.0,
                jnp.where(
                    small == 1,
                    high,
                    jnp.where(small == 2, middle_part, jnp.where(small == 3, low, 0.0)),
                ),
            )
            inside = (row < HALF) if side == 0 else (row >= HALF)
            across = jnp.where(inside, mixture / total, mark).T
            marks[2 * pair + side] = jnp.where(
                half_mask(shape, side), query_pair, across.astype(bf16)
            )
            both.append(across)
        chosen = jnp.where(half_mask(shape, 0), both[0], both[1])
        attended[:, lanes] = chosen.astype(bf16)
        return carry

    lax.fori_loop(0, HEADS // 2, body, 0)
    branch = dot(attended[...], out_weight[...]) + out_bias[...].reshape(1, model)
    total = flat(tokens).astype(f32) + branch
    middle[...] = total.reshape(middle.shape)
    normed, _ = normalize(total)
    low = normed * gain[...].reshape(1, model) + bias[...].reshape(1, model)
    normal[...] = low.astype(bf16).reshape(normal.shape)
    for task in range(tasks):
        first_line[task, 0] = normal[task, 0]
        last_line[task, 0] = normal[task, rows - 1]
    index = lax.broadcasted_iota(jnp.int32, (query_count, 1), 0)
    inside = (me * rows + (index // width) % rows < height) & ((index & (width - 1)) < valid_width)
    square[...] = column_sum(branch * branch * inside.astype(f32))


def put_pieces(grad, first, count, me, keep, send):
    size = grad.shape[0] // PIECES
    for group in range(PIECES):
        piece = grad[group * size : (group + 1) * size]
        slot, owner = divmod(first + group, count)
        store_piece(owner, me, keep, send, slot * size, piece)


def store_piece(owner, me, keep, send, start, piece):
    place = owner ^ me
    size = piece.shape[0]

    @pl.when((place & 1) == 0)
    def _():
        keep[place >> 1, start : start + size, :] = piece

    @pl.when((place & 1) == 1)
    def _():
        send[place >> 1, start : start + size, :] = piece


def feed_kernel(
    heights, widths, middle_normal, before, after, up_weight, up_bias, taps, down_weight, down_bias,
    cotangent, middle,
    layer_out, grad_band, to_before, to_after, keep, send, grad_taps, grad_up_bias, sums,
    normal, wide, grad_act, wide_back, active, grad_lifted, branch, grad_normal,
):
    tasks, rows, width, model = cotangent.shape
    part = up_weight.shape[1]
    step = pl.program_id(0)
    last = pl.num_programs(0) - 1
    me, has_before, has_after = band_flags()
    count = lax.axis_size("rows")
    lines = rows + 2

    @pl.when(step == 0)
    def _():
        clear_guards(wide)
        clear_guards(wide_back)
        branch[...] = jnp.zeros_like(branch)
        grad_normal[...] = jnp.zeros_like(grad_normal)
        for task in range(tasks):
            normal[task, 0] = before[task, 0]
            for row in range(rows):
                normal[task, row + 1] = middle_normal[task, row]
            normal[task, rows + 1] = after[task, 0]

    fed = flat(normal)
    shift_up = jnp.concatenate([up_bias[k] for k in range(up_bias.shape[0])], axis=1)
    lifted = dot(fed, up_weight[...]) + shift_up
    lifted = lifted.astype(bf16).astype(f32).reshape(tasks, lines, width, part)
    for task in range(tasks):
        for line in range(lines):
            value = lifted[task, line]
            if line == 0:
                value = value * has_before
            if line == lines - 1:
                value = value * has_after
            put_line(wide, task * lines + line, value)
    grad_output = flat(cotangent)
    grad_act[...] = dot(grad_output, down_weight[...], NT).reshape(grad_act.shape)

    c1 = 0.7978845608028654
    c2 = c1 * 0.044715
    blocks = part // LANES

    def across(block, carry):
        lanes = pl.ds(pl.multiple_of(block * LANES, LANES), LANES)
        tap = [[taps[a, b, lanes][None, :] for b in range(3)] for a in range(3)]

        def one_task(task, sums9):
            sums9 = list(sums9)
            for row in range(rows):
                for start in range(0, width, 16):
                    near = []
                    spread = None
                    for a in range(3):
                        for b in range(3):
                            at = GUARD - 1 + b + start
                            value = wide[block, task * lines + row + a, at : at + 16, :]
                            near.append(value)
                            term = tap[a][b] * value
                            spread = term if spread is None else spread + term
                    squared = spread * spread
                    gate = 0.5 + 0.5 * jnp.tanh(spread * (c1 + c2 * squared))
                    active[task * rows + row, start : start + 16, lanes] = (spread * gate).astype(
                        bf16
                    )
                    slope = gate + spread * (gate - gate * gate) * (2 * c1 + 6 * c2 * squared)
                    grad = grad_act[task * rows + row, start : start + 16, lanes] * slope
                    grad = grad.astype(bf16).astype(f32)
                    wide_back[
                        block, task * rows + row, GUARD + start : GUARD + start + 16, :
                    ] = grad
                    for k in range(9):
                        both = near[k] * grad
                        sums9[k] = sums9[k] + (both[0:8] + both[8:16])
            return tuple(sums9)

        sums9 = lax.fori_loop(
            0, tasks, one_task, tuple(jnp.zeros((8, LANES), f32) for _ in range(9))
        )
        for k in range(9):
            grad_taps[k // 3, k % 3, lanes] = jnp.sum(sums9[k], axis=0)

        def back_task(task, total):
            for line in range(lines):
                for start in range(0, width, 16):
                    value = None
                    for a in range(3):
                        if not 0 <= line - a < rows:
                            continue
                        for b in range(3):
                            at = GUARD + 1 - b + start
                            term = tap[a][b] * wide_back[
                                block, task * rows + line - a, at : at + 16, :
                            ]
                            value = term if value is None else value + term
                    if line == 0:
                        value = value * has_before
                    if line == lines - 1:
                        value = value * has_after
                    low = value.astype(bf16)
                    grad_lifted[task * lines + line, start : start + 16, lanes] = low
                    low = low.astype(f32)
                    total = total + (low[0:8] + low[8:16])
            return total

        total = lax.fori_loop(0, tasks, back_task, jnp.zeros((8, LANES), f32))
        per = model // LANES
        inside = pl.ds(pl.multiple_of((block % per) * LANES, LANES), LANES)
        grad_up_bias[block // per, :, inside] = column_sum(total)
        return carry

    lax.fori_loop(0, blocks, across, 0)

    act = flat(active)
    branch[...] += dot(act, down_weight[...])
    grad_down = dot(act, grad_output, TN).astype(bf16)
    grad_low = flat(grad_lifted)
    grad_up = dot(fed, grad_low, TN).astype(bf16)
    grad_normal[...] += dot(grad_low, up_weight[...], NT)
    size = keep.shape[1] // 2
    groups = model // size
    for sub in range(part // model):
        column = step * (part // model) + sub
        columns = slice(sub * model, (sub + 1) * model)
        for group in range(groups):
            rows_of = slice(group * size, (group + 1) * size)
            store_piece(
                group * (count // groups) + column, me, keep, send, 0, grad_up[rows_of, columns]
            )
    for group in range(part // size):
        rows_of = slice(group * size, (group + 1) * size)
        owner = step * (part // size) + group
        store_piece(owner, me, keep, send, size, grad_down[rows_of])

    @pl.when(step == last)
    def _():
        shift = down_bias[...].reshape(1, model)
        height, valid_width = heights[0], widths[0]
        whole = branch[...].reshape(tasks, rows, width, model)
        grads = grad_normal[...].reshape(tasks, lines, width, model)
        first = jnp.zeros((1, model), f32)
        second = jnp.zeros((1, model), f32)
        col = lax.broadcasted_iota(jnp.int32, (width, 1), 0)
        for task in range(tasks):
            for row in range(rows):
                mlp = whole[task, row] + shift
                final = middle[task, row] + mlp
                layer_out[task, row] = final.astype(bf16)
                inside = (col < valid_width) & (me * rows + row < height)
                weight = inside.astype(f32)
                first = first + column_sum(mlp * mlp * weight)
                second = second + column_sum(final * final * weight)
            to_before[task, 0] = grads[task, 0].astype(bf16)
            grad_band[task] = grads[task, 1 : rows + 1]
            to_after[task, 0] = grads[task, rows + 1].astype(bf16)
        bias_sum = column_sum(grad_output.astype(f32))
        sums[...] = jnp.concatenate(
            [bias_sum, first, second, jnp.zeros((5, model), f32)], axis=0
        )


def feed(heights, widths, normal, before, after, up_weight, up_bias, taps, down_weight,
         down_bias, cotangent, middle, count):
    tasks, rows, width, model = cotangent.shape
    hidden = up_weight.shape[1]
    part = FEED_PART * model
    lines = rows + 2
    size = hidden // count
    smem = pl.BlockSpec(memory_space=pltpu.SMEM)

    def whole(shape):
        return pl.BlockSpec(shape, lambda i, k=len(shape): (0,) * k)

    ins = [
        smem, smem, whole(normal.shape), whole(before.shape), whole(after.shape),
        pl.BlockSpec((model, part), lambda i: (0, i)),
        pl.BlockSpec((FEED_PART, 1, model), lambda i: (i, 0, 0)),
        pl.BlockSpec((3, 3, part), lambda i: (0, 0, i)),
        pl.BlockSpec((part, model), lambda i: (i, 0)),
        whole(down_bias.shape), whole(cotangent.shape), whole(middle.shape),
    ]
    line_shape = (tasks, 1, width, model)
    outs = [
        (cotangent.shape, bf16), (cotangent.shape, f32), (line_shape, bf16), (line_shape, bf16),
        ((count // 2, 2 * size, model), bf16), ((count // 2, 2 * size, model), bf16),
        ((3, 3, hidden), f32), ((hidden // model, 1, model), f32), ((8, model), f32),
    ]
    out_specs = [whole(s) for s, _ in outs]
    out_specs[6] = pl.BlockSpec((3, 3, part), lambda i: (0, 0, i))
    out_specs[7] = pl.BlockSpec((FEED_PART, 1, model), lambda i: (i, 0, 0))
    return pl.pallas_call(
        feed_kernel,
        name="feed",
        grid=(hidden // part,),
        out_shape=tuple(jax.ShapeDtypeStruct(s, d) for s, d in outs),
        in_specs=ins,
        out_specs=tuple(out_specs),
        scratch_shapes=[
            pltpu.VMEM((tasks, lines, width, model), bf16),
            wide_scratch(tasks * lines, width, part),
            pltpu.VMEM((tasks * rows, width, part), f32),
            wide_scratch(tasks * rows, width, part),
            pltpu.VMEM((tasks * rows, width, part), bf16),
            pltpu.VMEM((tasks * lines, width, part), bf16),
            pltpu.VMEM((tasks * rows * width, model), f32),
            pltpu.VMEM((tasks * lines * width, model), f32),
        ],
        compiler_params=pltpu.CompilerParams(
            vmem_limit_bytes=52 << 20, dimension_semantics=("arbitrary",)
        ),
        cost_estimate=cost(),
    )(heights, widths, normal, before, after, up_weight, up_bias, taps, down_weight, down_bias,
      cotangent, middle)


def norm_back_kernel(
    grad_band, from_before, from_after, middle, cotangent, gain, out_weight, attended,
    grad_middle, grad_marks, keep, send, sums,
):
    tasks, rows, width, model = cotangent.shape
    scale = gain[...].reshape(1, model)
    parts = []
    for task in range(tasks):
        for row in range(rows):
            grad = grad_band[task, row]
            if row == 0:
                grad = grad + from_before[task, 0].astype(f32)
            if row == rows - 1:
                grad = grad + from_after[task, 0].astype(f32)
            parts.append(grad)
    grad_input = jnp.concatenate(parts, axis=0)
    normed, inverse = normalize(flat(middle))
    total = flat(cotangent).astype(f32) + normalize_back(grad_input, scale, normed, inverse)
    grad_middle[...] = total.reshape(grad_middle.shape)
    sums[0:1, :] = column_sum(grad_input * normed)
    sums[1:2, :] = column_sum(grad_input)
    sums[2:3, :] = column_sum(total)
    sums[3:8, :] = jnp.zeros((5, model), f32)
    grad_branch = total.astype(bf16)
    mixture = attended[...]
    grad_out = dot(mixture, grad_branch, TN).astype(bf16)
    me = lax.axis_index("rows")
    put_pieces(grad_out, 0, lax.axis_size("rows"), me, keep, send)
    grad_attended = dot(grad_branch, out_weight[...], NT).astype(bf16)
    shape = (mixture.shape[0], LANES)
    for pair in range(HEADS // 2):
        lanes = slice(pair * LANES, (pair + 1) * LANES)
        grad_two = grad_attended[:, lanes]
        both = grad_two.astype(f32) * mixture[:, lanes].astype(f32)
        for side in range(2):
            half = half_mask(shape, side)
            inner = jnp.sum(jnp.where(half, both, 0.0), axis=-1, keepdims=True)
            grad_marks[2 * pair + side] = jnp.where(half, grad_two, marked(0.0, -inner, shape))


def attend_back_kernel(
    marks, grad_marks, keys, values, extra, grad_queries, grad_keys, grad_values,
    total, query_zero, grad_zero,
):
    key_count = keys.shape[0]
    query_count = grad_marks.shape[1]
    block = min(512, key_count)
    shape = (query_count, LANES)
    for side in range(2):
        half = half_mask(shape, side)
        zero = jnp.zeros(shape, bf16)
        part = slice(side * query_count, (side + 1) * query_count)
        query_zero[part, :] = jnp.where(half, marks[side], zero)
        grad_zero[part, :] = jnp.where(half, grad_marks[side], zero)

    def body(place, carry):
        part = pl.ds(pl.multiple_of(place * block, block), block)
        key_pair, value_pair, extras = keys[part, :], values[part, :], extra[part, :]
        lows, grads = [], []
        query_part = None
        for side in range(2):
            half = half_mask((block, LANES), side)
            scores = dot(jnp.where(half, key_pair, extras), marks[side], NT)
            grad_prob = dot(jnp.where(half, value_pair, extras), grad_marks[side], NT)
            probability = jnp.exp(scores)
            grad = (probability * grad_prob).astype(bf16)
            grads.append(grad)
            lows.append(probability.astype(bf16))
            one = dot(jnp.where(half, key_pair, jnp.zeros((block, LANES), bf16)), grad, TN)
            query_part = one if query_part is None else query_part + one
        grad_values[part, :] = dot(jnp.concatenate(lows, axis=1), grad_zero[...]).astype(bf16)
        grad_keys[part, :] = dot(jnp.concatenate(grads, axis=1), query_zero[...]).astype(bf16)

        @pl.when(place == 0)
        def _():
            total[...] = query_part

        @pl.when(place > 0)
        def _():
            total[...] += query_part

        return carry

    lax.fori_loop(0, key_count // block, body, 0)
    grad_queries[...] = (total[...] * HALF**-0.5).T.astype(bf16)


def side_by_side(refs):
    return jnp.concatenate([ref[...] for ref in refs], axis=1)


def pool_back_kernel(order, *refs):
    pairs = HEADS // 2
    refs = list(refs)
    grad_queries, grad_keys, grad_values = refs[:pairs], refs[pairs : 2 * pairs], refs[2 * pairs : 3 * pairs]
    del refs[: 3 * pairs]
    key_weight, value_weight, query_weight, keep, send, grad_conv, first, last = refs
    tasks, rows, width, model = grad_conv.shape
    cells = keep.shape[1]
    both = jnp.concatenate([key_weight[...], value_weight[...]], axis=1)
    for position, offset in enumerate(order):
        part = slice(position * cells, (position + 1) * cells)
        grads = jnp.concatenate([ref[part, :] for ref in (*grad_keys, *grad_values)], axis=1)
        target = send if offset & 1 else keep
        target[offset >> 1] = dot(grads, both, NT).astype(bf16)
    grad = dot(side_by_side(grad_queries), query_weight[...], NT).astype(bf16)
    grad_conv[...] = grad.reshape(grad_conv.shape)
    for task in range(tasks):
        first[task, 0] = grad_conv[task, 0]
        last[task, 0] = grad_conv[task, rows - 1]


def weight_kernel(order, *refs):
    refs = list(refs)
    heights, widths = refs[:2]
    del refs[:2]
    pooled = refs[: len(order)]
    del refs[: len(order)]
    pairs = HEADS // 2
    grad_queries, grad_keys, grad_values = refs[:pairs], refs[pairs : 2 * pairs], refs[2 * pairs : 3 * pairs]
    del refs[: 3 * pairs]
    (pool_keep, pool_send, conv, extended, grad_conv, taps, gain, bias, square, back_sums, feed_sums,
     hidden_taps, up_bias, keep, send, wide, rows_of) = refs
    tasks, rows, width, model = grad_conv.shape
    count = len(order)
    cells = pooled[0].shape[0]
    lines = rows + 2
    me, has_before, has_after = band_flags()
    size = keep.shape[1] - 16

    grad_both = jnp.zeros((model, 2 * model), f32)
    pool_sum = jnp.zeros((1, model), f32)
    pool_dot = jnp.zeros((1, model), f32)
    for position, offset in enumerate(order):
        part = slice(position * cells, (position + 1) * cells)
        block = pooled[position][...]
        grads = jnp.concatenate([ref[part, :] for ref in (*grad_keys, *grad_values)], axis=1)
        grad_both = grad_both + dot(block, grads, TN)
        source = pool_send if offset & 1 else pool_keep
        grad = source[offset >> 1].astype(f32)
        pool_sum = pool_sum + column_sum(grad)
        pool_dot = pool_dot + column_sum(grad * block.astype(f32))
    put_pieces(grad_both[:, 0:model].astype(bf16), PIECES, count, me, keep, send)
    put_pieces(grad_both[:, model:].astype(bf16), 2 * PIECES, count, me, keep, send)
    grad_query = dot(flat(conv), side_by_side(grad_queries), TN)
    put_pieces(grad_query.astype(bf16), 0, count, me, keep, send)

    clear_guards(wide)
    for task in range(tasks):
        for line in range(lines):
            put_line(wide, task * lines + line, extended[task, line].astype(f32))

    def across(block, carry):
        lanes = pl.ds(pl.multiple_of(block * LANES, LANES), LANES)

        def one_task(task, sums9):
            sums9 = list(sums9)
            for row in range(rows):
                for start in range(0, width, 16):
                    grad = grad_conv[task, row, start : start + 16, lanes].astype(f32)
                    for k in range(9):
                        at = GUARD - 1 + k % 3 + start
                        both = grad * wide[block, task * lines + row + k // 3, at : at + 16, :]
                        sums9[k] = sums9[k] + (both[0:8] + both[8:16])
            return tuple(sums9)

        sums9 = lax.fori_loop(
            0, tasks, one_task, tuple(jnp.zeros((8, LANES), f32) for _ in range(9))
        )
        for k in range(9):
            rows_of[2 + k : 3 + k, lanes] = column_sum(sums9[k])
        return carry

    lax.fori_loop(0, model // LANES, across, 0)

    shift = bias[...].reshape(1, model)
    zero = jnp.zeros((1, model), f32)
    conv_dot, conv_sum = zero, zero
    for row in range(rows):
        line = grad_conv[0, row].astype(f32)
        for task in range(1, tasks):
            line = line + grad_conv[task, row].astype(f32)
        full = column_sum(line)
        by_col = (full - line[0:1], full, full - line[width - 1 : width])
        for a in range(3):
            for b in range(3):
                value = by_col[b]
                if a == 0 and row == 0:
                    value = value * has_before
                if a == 2 and row == rows - 1:
                    value = value * has_after
                conv_sum = conv_sum + taps[a, b].reshape(1, model) * value
    for k in range(9):
        conv_dot = conv_dot + taps[k // 3, k % 3].reshape(1, model) * rows_of[2 + k : 3 + k, :]
    grad_bias = conv_sum + pool_sum
    grad_gain = (conv_dot + pool_dot - shift * grad_bias) / gain[...].reshape(1, model)
    rows_of[0:1, :] = grad_gain
    rows_of[1:2, :] = grad_bias
    rows_of[11:12, :] = back_sums[2:3, :]
    rows_of[12:14, :] = back_sums[0:2, :]
    rows_of[14:15, :] = feed_sums[0:1, :]
    rows_of[15:16, :] = square[...]
    rows_of[16:18, :] = feed_sums[1:3, :]
    in_rows = jnp.clip(heights[0] - me * rows, 0, rows)
    in_cols = jnp.clip(widths[0], 0, width)
    cells_in = (tasks * in_rows * in_cols).astype(f32)
    rows_of[18:19, :] = jnp.full((1, model), cells_in, f32)
    parts = up_bias.shape[0]
    for part in range(parts):
        rows_of[19 + part : 20 + part, :] = up_bias[part]
        for k in range(9):
            rows_of[19 + parts * (k + 1) + part : 20 + parts * (k + 1) + part, :] = hidden_taps[
                k // 3, k % 3, part * model : (part + 1) * model
            ].reshape(1, model)
    used = 19 + 10 * parts
    rows_of[used:SMALL, :] = jnp.zeros((SMALL - used, model), f32)
    group = SMALL // count
    for owner in range(count):
        value = rows_of[owner * group : (owner + 1) * group, :]
        if group < 8:
            value = jnp.concatenate([value, jnp.zeros((8 - group, model), f32)], axis=0)
        high = value.astype(bf16)
        low = (value - high.astype(f32)).astype(bf16)
        store_piece(owner, me, keep, send, size, jnp.concatenate([high, low], axis=0))


def last_kernel(
    grad_conv, before, after, taps, tokens, gain, grad_middle, pool, input_grad, wide
):
    tasks, rows, width, model = tokens.shape
    lines = rows + 2
    pooled_rows = rows // 2
    clear_guards(wide)
    for task in range(tasks):
        put_line(wide, task * lines, before[task, 0].astype(f32))
        put_line(wide, task * lines + lines - 1, after[task, 0].astype(f32))
        for row in range(rows):
            put_line(wide, task * lines + row + 1, grad_conv[task, row].astype(f32))
    pooled = pool[...].reshape(tasks, pooled_rows, width // 2, model)
    spread_matrix = pool_matrix(width)[:, 0:width]

    def body(step, carry):
        task = step // (model // LANES)
        block = step % (model // LANES)
        lanes = pl.ds(pl.multiple_of(block * LANES, LANES), LANES)
        for row in range(rows):
            for start in range(0, width, 16):
                total = jnp.zeros((16, LANES), f32)
                for a in range(3):
                    for b in range(3):
                        at = GUARD + 1 - b + start
                        total = total + taps[a, b, lanes][None, :] * wide[
                            block, task * lines + row + 2 - a, at : at + 16, :
                        ]
                input_grad[task, row, start : start + 16, lanes] = total
        return carry

    lax.fori_loop(0, tasks * (model // LANES), body, 0)
    scale = gain[...].reshape(1, model)
    for task in range(tasks):
        for row in range(rows):
            grad = input_grad[task, row] + dot(spread_matrix, pooled[task, row // 2], TN)
            normed, inverse = normalize(tokens[task, row].astype(f32))
            input_grad[task, row] = grad_middle[task, row] + normalize_back(grad, scale, normed, inverse)


def add_blocks(values):
    total = values[0].astype(f32)
    for other in values[1:]:
        total = total + other.astype(f32)
    return total


def put_sum(out, start, values, small):
    total = add_blocks(values)
    size = total.shape[0]
    if not small:
        out[start : start + size, :] = total.astype(bf16)
        return
    size -= 16
    value = total[size : size + 8] + total[size + 8 : size + 16]
    high = value.astype(bf16)
    low = (value - high.astype(f32)).astype(bf16)
    out[start : start + size, :] = total[0:size].astype(bf16)
    out[start + size : start + size + 16, :] = jnp.concatenate([high, low], axis=0)


def combine(arrays, small):
    blocks, size, model = arrays[0].shape

    def kernel(*refs):
        ins, outs = refs[: len(arrays)], refs[len(arrays) :]
        for block, out in enumerate(outs):
            put_sum(out, 0, [x[block] for x in ins], small)

    return call("combine", kernel, [((size, model), bf16)] * blocks, list(arrays), limit=24)


def combine_two(ones, others, small):
    blocks, above, model = ones[0].shape
    below = others[0].shape[1]

    def kernel(*refs):
        for block, out in enumerate(refs[4:]):
            put_sum(out, 0, [x[block] for x in refs[0:2]], False)
            put_sum(out, above, [x[block] for x in refs[2:4]], small)

    outs = [((above + below, model), bf16)] * blocks
    return call("combine_two", kernel, outs, [*ones, *others], limit=24)


def split_late(parts, cells):
    size, model = parts[0].shape

    def kernel(*refs):
        ins, (pool, weights) = refs[: len(parts)], refs[len(parts) :]
        put_sum(pool, 0, [x[0:cells, :] for x in ins], False)
        put_sum(weights, 0, [x[cells:size, :] for x in ins], True)

    outs = [((cells, model), bf16), ((size - cells, model), bf16)]
    return call("split_late", kernel, outs, list(parts), limit=24)


def exchange(value, axis, mask):
    count = lax.axis_size(axis)
    return lax.ppermute(value, axis, [(i, i ^ mask) for i in range(count)])


def far_masks():
    return list(range(2, lax.axis_size("rows"), 2))


def once(value, *earlier):
    return lax.optimization_barrier((value, earlier))[0]


def far_rows(value):
    return [exchange(value, "rows", mask) for mask in far_masks()]


def all_images(value):
    return [exchange(value, "batch", mask) for mask in range(1, lax.axis_size("batch"))]


def add_images(own, arrived, small):
    (total,) = combine([x[None] for x in [own, *arrived]], small)
    return total


def unpack_feed_kernel(count, *refs):
    blocks, (grad_up, grad_down, grad_out, pieces_of) = refs[:count], refs[count:]
    me = lax.axis_index("rows")
    model, hidden = grad_up.shape
    size = hidden // count
    columns = hidden // model
    piece = model // PIECES
    for j in range(count):
        owner = blocks_owner(j, count, me)
        block = blocks[j]
        up = block[0:size, :].astype(f32)
        place = owner // columns
        col = owner % columns
        grad_up[
            pl.ds(pl.multiple_of(place * size, size), size),
            pl.ds(pl.multiple_of(col * model, model), model),
        ] = up
        grad_down[pl.ds(pl.multiple_of(owner * size, size), size), :] = block[
            size : 2 * size, :
        ].astype(f32)
        pieces_of[pl.ds(pl.multiple_of(owner * piece, piece), piece), :] = block[
            2 * size : 2 * size + piece, :
        ].astype(f32)
    grad_out[...] = pieces_of[0:model, :]


def blocks_owner(j, count, me):
    half = count // 2
    offset = 2 * j if j < half else 2 * (j - half) + 1
    return me ^ offset


def unpack_late_kernel(count, *refs):
    blocks = refs[:count]
    (grad_query, grad_key, grad_value, norm1_gain, norm1_bias, query_taps, out_bias,
     norm2_gain, norm2_bias, up_bias, hidden_taps, down_bias, stats, weights, rows_of) = refs[count:]
    me = lax.axis_index("rows")
    model = grad_query.shape[0]
    size = blocks[0].shape[0] - 16
    piece = model // PIECES
    group = SMALL // count
    for j in range(count):
        owner = blocks_owner(j, count, me)
        block = blocks[j][...].astype(f32)
        for slot in range(size // piece):
            start = pl.multiple_of((slot * count + owner) * piece, piece)
            weights[pl.ds(start, piece), :] = block[slot * piece : (slot + 1) * piece]
        small = block[size : size + 8] + block[size + 8 : size + 16]
        rows_of[owner] = small
    for which, out in enumerate((grad_query, grad_key, grad_value)):
        out[...] = weights[which * model : (which + 1) * model, :]

    def line(k):
        return rows_of[k // group, k % group, :]

    norm1_gain[...] = line(0)
    norm1_bias[...] = line(1)
    for k in range(9):
        query_taps[k // 3, k % 3, :] = line(2 + k)
    out_bias[...] = line(11)
    norm2_gain[...] = line(12)
    norm2_bias[...] = line(13)
    down_bias[...] = line(14)
    parts = up_bias.shape[0] // model
    for part in range(parts):
        lanes = slice(part * model, (part + 1) * model)
        up_bias[lanes] = line(19 + part)
        for k in range(9):
            hidden_taps[k // 3, k % 3, lanes] = line(19 + parts * (k + 1) + part)
    cells = line(18).reshape(1, model)[:, 0:1]
    row = lax.broadcasted_iota(jnp.int32, (1, LANES), 1)
    value = jnp.zeros((1, LANES), f32)
    for k in range(3):
        total = jnp.sum(line(15 + k).reshape(1, model), axis=-1, keepdims=True)
        value = jnp.where(row == k, jnp.sqrt(total / (cells * model)), value)
    stats[...] = value


def local(
    tokens,
    norm1_gain,
    norm1_bias,
    query_taps,
    query_weight,
    key_weight,
    value_weight,
    out_weight,
    out_bias,
    norm2_gain,
    norm2_bias,
    up_weight,
    up_bias,
    hidden_taps,
    down_weight,
    down_bias,
    cotangent,
    heights,
    widths,
):
    shape = tokens.shape
    tokens, cotangent = tokens[0], cotangent[0]
    tasks, rows, width, model = tokens.shape
    hidden = up_weight.shape[1]
    count = lax.axis_size("rows")
    cells = tasks * (rows // 2) * (width // 2)
    key_count = count * cells
    forward = [(i, i + 1) for i in range(count - 1)]
    backward = [(i + 1, i) for i in range(count - 1)]
    lines = rows + 2
    token_count = tasks * rows * width
    line = (tasks, 1, width, model)

    def down_rows(value):
        return lax.ppermute(value, "rows", forward)

    def up_rows(value):
        return lax.ppermute(value, "rows", backward)

    normal_one, pooled, first_line, last_line = call(
        "first_norm",
        first_norm_kernel,
        [(tokens.shape, bf16), ((cells, model), bf16), (line, bf16), (line, bf16)],
        [tokens, norm1_gain, norm1_bias],
        limit=16,
    )
    far = far_masks()
    order = [0, 1, *far, *[mask + 1 for mask in far]]
    before = down_rows(last_line)
    after = up_rows(first_line)
    swapped = exchange(pooled, "rows", 1)
    arrived = far_rows(pooled)
    blocks = [pooled, swapped, *arrived, *[exchange(x, "rows", 1) for x in arrived]]

    extended, conv, queries = call(
        "query_conv",
        query_kernel,
        [((tasks, lines, width, model), bf16), (tokens.shape, bf16), ((token_count, model), bf16)],
        [normal_one, before, after, query_taps, query_weight],
        scratch=[wide_scratch(tasks * lines, width, model)],
        limit=24,
    )
    (keys, values, extra, attended, middle, normal_two, first_line, last_line, marks, square) = call(
        "attend",
        lambda *refs: attend_kernel(order, *refs),
        [
            ((key_count, model), bf16), ((key_count, model), bf16), ((key_count, LANES), bf16),
            ((token_count, model), bf16), (tokens.shape, f32), (tokens.shape, bf16), (line, bf16),
            (line, bf16), ((HEADS, token_count, LANES), bf16), ((1, model), f32),
        ],
        [heights, widths, *blocks, key_weight, value_weight, queries, tokens, out_weight, out_bias,
         norm2_gain, norm2_bias],
        smem=2,
        scratch=[pltpu.VMEM((2, LANES, token_count), f32), pltpu.VMEM((8, token_count), f32)],
        limit=56,
    )
    before = down_rows(last_line)
    after = up_rows(first_line)
    (layer_out, grad_band, to_before, to_after, feed_keep, feed_send, grad_hidden_taps,
     grad_up_bias, feed_sums) = feed(
        heights, widths, normal_two, before, after, up_weight,
        up_bias.reshape(hidden // model, 1, model), hidden_taps, down_weight, down_bias, cotangent,
        middle, count,
    )
    from_after = up_rows(to_before)
    from_before = down_rows(to_after)
    feed_swapped = exchange(feed_send, "rows", 1)
    piece = model // PIECES
    grad_middle, grad_marks, out_keep, out_send, back_sums = call(
        "norm_back",
        norm_back_kernel,
        [
            (tokens.shape, f32), ((HEADS, token_count, LANES), bf16),
            ((count // 2, piece, model), bf16), ((count // 2, piece, model), bf16), ((8, model), f32),
        ],
        [
            grad_band, from_before, from_after, middle, cotangent, norm2_gain, out_weight, attended,
        ],
        limit=40,
    )
    out_swapped = exchange(out_send, "rows", 1)

    def attend_back(pair, tie):
        inputs = [marks, grad_marks, keys, values, extra]
        inputs = once(inputs, *tie)

        def of_heads(x):
            return pl.BlockSpec((2, x.shape[1], LANES), lambda i: (pair, 0, 0))

        def of_lanes(x):
            return pl.BlockSpec((x.shape[0], LANES), lambda i: (0, pair))

        whole = pl.BlockSpec((key_count, LANES), lambda i: (0, 0))
        outs = [(token_count, LANES), (key_count, LANES), (key_count, LANES)]
        return pl.pallas_call(
            attend_back_kernel,
            name="attend_back",
            grid=(1,),
            out_shape=[jax.ShapeDtypeStruct(shape, bf16) for shape in outs],
            in_specs=[*[of_heads(x) for x in inputs[0:2]], *[of_lanes(x) for x in inputs[2:4]], whole],
            out_specs=[pl.BlockSpec(shape, lambda i: (0, 0)) for shape in outs],
            scratch_shapes=[
                pltpu.VMEM((LANES, token_count), f32),
                pltpu.VMEM((2 * token_count, LANES), bf16),
                pltpu.VMEM((2 * token_count, LANES), bf16),
            ],
            compiler_params=pltpu.CompilerParams(vmem_limit_bytes=40 << 20),
            cost_estimate=cost(),
        )(*inputs)

    feed_blocks = combine_two([feed_keep, feed_swapped], [out_keep, out_swapped], False)
    feed_arrived = [exchange(feed_blocks[mask >> 1], "rows", mask) for mask in far]
    back = [attend_back(0, feed_blocks)]
    feed_arrived = once(feed_arrived, *back[0])
    feed_own = add_images(feed_blocks[0], feed_arrived, False)
    feed_arrived = all_images(feed_own)
    back.append(attend_back(1, [feed_own]))
    for pair in range(2, HEADS // 2):
        back.append(attend_back(pair, back[-1]))
    feed_arrived = once(feed_arrived, *back[-1])
    feed_own = add_images(feed_own, feed_arrived, False)
    feed_even = [feed_own, *far_rows(feed_own)]
    grads = [part for which in range(3) for part in [x[which] for x in back]]
    grads = once(grads, feed_own)

    pool_keep, pool_send, grad_conv, first_line, last_line = call(
        "pool_back",
        lambda *refs: pool_back_kernel(order, *refs),
        [((count // 2, cells, model), bf16)] * 2 + [(tokens.shape, bf16), (line, bf16), (line, bf16)],
        [*grads, key_weight, value_weight, query_weight],
        limit=40,
    )
    pool_swapped = exchange(pool_send, "rows", 1)
    before = down_rows(last_line)
    after = up_rows(first_line)
    keep, send = call(
        "weights",
        lambda *refs: weight_kernel(order, *refs),
        [((count // 2, -(-3 * PIECES // count) * piece + 16, model), bf16)] * 2,
        [
            heights, widths, *blocks, *grads, pool_keep, pool_send, conv, extended, grad_conv,
            query_taps, norm1_gain, norm1_bias, square, back_sums, feed_sums, grad_hidden_taps,
            grad_up_bias,
        ],
        smem=2,
        scratch=[
            wide_scratch(tasks * lines, width, model),
            pltpu.VMEM((SMALL, model), f32),
        ],
        limit=48,
    )
    feed_odd = [exchange(x, "rows", 1) for x in once(feed_even, keep)]
    late_swapped = exchange(send, "rows", 1)
    late_blocks = combine_two([pool_keep, pool_swapped], [keep, late_swapped], True)
    late_arrived = [exchange(late_blocks[mask >> 1], "rows", mask) for mask in far]
    pool_total, late_own = split_late([late_blocks[0], *late_arrived], cells)
    late_arrived = all_images(late_own)
    (input_grad,) = call(
        "last_norm",
        last_kernel,
        [(tokens.shape, f32)],
        [grad_conv, before, after, query_taps, tokens, norm1_gain, grad_middle, pool_total],
        scratch=[wide_scratch(tasks * lines, width, model)],
        limit=40,
    )
    late_own = add_images(late_own, late_arrived, True)
    even = [late_own, *far_rows(late_own)]
    odd = [exchange(x, "rows", 1) for x in even]
    grad_up, grad_down, grad_out = call(
        "unpack_feed",
        lambda *refs: unpack_feed_kernel(count, *refs),
        [((model, hidden), f32), ((hidden, model), f32), ((model, model), f32)],
        [*feed_even, *feed_odd],
        scratch=[pltpu.VMEM((count * piece, model), f32)],
        limit=40,
    )
    vector = ((model,), f32)
    late = call(
        "unpack_late",
        lambda *refs: unpack_late_kernel(count, *refs),
        [((model, model), f32)] * 3
        + [vector, vector, ((3, 3, model), f32), vector, vector, vector, ((hidden,), f32),
           ((3, 3, hidden), f32), vector, ((1, LANES), f32)],
        [*even, *odd],
        scratch=[
            pltpu.VMEM((-(-3 * PIECES // count) * count * piece, model), f32),
            pltpu.VMEM((count, 8, model), f32),
        ],
        limit=40,
    )
    (grad_query, grad_key, grad_value, gain1, bias1, taps1, out_sum, gain2, bias2, up_sum,
     taps2, down_sum, stats) = late
    return (
        layer_out.reshape(shape),
        input_grad.reshape(shape),
        gain1,
        bias1,
        taps1,
        grad_query,
        grad_key,
        grad_value,
        grad_out,
        out_sum,
        gain2,
        bias2,
        grad_up,
        up_sum,
        taps2,
        grad_down,
        down_sum,
        stats[0, 0:3],
    )


def solution(mesh):
    band = P("batch", None, "rows", None, None)
    placed = (band, *[P()] * 15, band, P("batch"), P("batch"))
    return jax.shard_map(
        local,
        mesh=mesh,
        in_specs=placed,
        out_specs=(band, band, *[P()] * 16),
        check_vma=False,
    )
```

```python
import jax
import jax.numpy as jnp
from jax import lax
from jax.experimental import pallas as pl
from jax.experimental.pallas import tpu as pltpu
from jax.sharding import PartitionSpec as P

HEADS = 6
LANES = 128
HALF = 64
GUARD = 8
SMALL = 64
PIECES = 8
FEED_PART = 2
epsilon = 1e-05
f32 = jnp.float32
bf16 = jnp.bfloat16
NN = (((1,), (0,)), ((), ()))
NT = (((1,), (1,)), ((), ()))
TN = (((0,), (0,)), ((), ()))


def dot(left, right, form=NN):
    return lax.dot_general(left, right, form, preferred_element_type=f32)


def cost(us):
    return pl.CostEstimate(flops=int(us * 1e4), bytes_accessed=int(us * 1e4), transcendentals=0)


def hbm(value):
    return pltpu.with_memory_space_constraint(value, pltpu.HBM)


def in_hbm(shape, dtype):
    return shape, dtype, True


def out_type(shape, dtype, away=False):
    return pltpu.HBM(shape, dtype) if away else jax.ShapeDtypeStruct(shape, dtype)


def call(name, kernel, outs, args, smem=0, scratch=(), us=1, limit=12):
    def whole(shape):
        return pl.BlockSpec(shape, lambda i, k=len(shape): (0,) * k)

    return pl.pallas_call(
        kernel,
        grid=(1,),
        out_shape=tuple(out_type(*x) for x in outs),
        in_specs=[pl.BlockSpec(memory_space=pltpu.SMEM)] * smem
        + [whole(x.shape) for x in args[smem:]],
        out_specs=tuple(whole(x[0]) for x in outs),
        scratch_shapes=list(scratch),
        name=name,
        compiler_params=pltpu.CompilerParams(vmem_limit_bytes=limit << 20),
        cost_estimate=cost(us),
    )(*args)


def normalize(values):
    center = jnp.mean(values, axis=-1, keepdims=True)
    centered = values - center
    inverse = lax.rsqrt(jnp.mean(centered * centered, axis=-1, keepdims=True) + epsilon)
    return centered * inverse, inverse


def normalize_back(grad_output, gain, normed, inverse):
    scaled = grad_output * gain
    return inverse * (
        scaled
        - jnp.mean(scaled, axis=-1, keepdims=True)
        - normed * jnp.mean(scaled * normed, axis=-1, keepdims=True)
    )


def column_sum(values):
    return jnp.sum(values, axis=0, keepdims=True)


def flat(ref):
    value = ref[...]
    return value.reshape(-1, value.shape[-1])


def band_flags():
    me = lax.axis_index("rows")
    count = lax.axis_size("rows")
    return me, (me > 0).astype(f32), (me < count - 1).astype(f32)


def neighbours(rows):
    odd = lax.axis_index("rows") & 1
    even = 1 - odd
    return even * (rows - 1), odd * (rows - 1), even * (rows + 1), odd * (rows + 1)


def pool_matrix(width):
    rows = lax.broadcasted_iota(jnp.int32, (width // 2, 2 * width), 0)
    cols = lax.broadcasted_iota(jnp.int32, (width // 2, 2 * width), 1)
    cols = jnp.where(cols >= width, cols - width, cols)
    return jnp.where((cols >> 1) == rows, 0.25, 0.0).astype(bf16)


def first_norm_kernel(tokens, gain, bias, normal, pooled, to_core, to_far):
    tasks, rows, width, model = tokens.shape
    matrix = pool_matrix(width)
    core_row, far_row, _, _ = neighbours(rows)
    scale = gain[...].reshape(1, model)
    shift = bias[...].reshape(1, model)
    for task in range(tasks):
        for row in range(0, rows, 2):
            value = tokens[task, row : row + 2].astype(f32).reshape(2 * width, model)
            low = (normalize(value)[0] * scale + shift).astype(bf16)
            normal[task, row : row + 2] = low.reshape(2, width, model)
            start = (task * (rows // 2) + row // 2) * (width // 2)
            pooled[start : start + width // 2, :] = dot(matrix, low).astype(bf16)
        to_core[task, 0] = normal[task, core_row]
        to_far[task, 0] = normal[task, far_row]


def clear_guards(wide):
    blocks, lines, length, lanes = wide.shape
    zero = jnp.zeros((blocks, lines, GUARD, lanes), wide.dtype)
    wide[:, :, 0:GUARD, :] = zero
    wide[:, :, length - GUARD : length, :] = zero


def put_line(wide, line, value):
    for block in range(wide.shape[0]):
        wide[block, line, GUARD : GUARD + value.shape[0], :] = value[
            :, block * LANES : (block + 1) * LANES
        ]


def wide_scratch(lines, width, model):
    return pltpu.VMEM((model // LANES, lines, width + 2 * GUARD, LANES), f32)


def query_kernel(normal, from_core, from_far, taps, weight, extended, conv, queries, wide):
    tasks, rows, width, model = normal.shape
    clear_guards(wide)
    lines = rows + 2
    _, _, core_line, far_line = neighbours(rows)
    for task in range(tasks):
        extended[task, core_line] = from_core[task, 0]
        extended[task, far_line] = from_far[task, 0]
        for row in range(rows):
            extended[task, row + 1] = normal[task, row]
        for line in range(lines):
            put_line(wide, task * lines + line, extended[task, line].astype(f32))

    def body(step, carry):
        task = step // (model // LANES)
        block = step % (model // LANES)
        lanes = pl.ds(pl.multiple_of(block * LANES, LANES), LANES)
        for row in range(rows):
            for start in range(0, width, 16):
                total = jnp.zeros((16, LANES), f32)
                for a in range(3):
                    for b in range(3):
                        at = GUARD - 1 + b + start
                        total = total + taps[a, b, lanes][None, :] * wide[
                            block, task * lines + row + a, at : at + 16, :
                        ]
                conv[task, row, start : start + 16, lanes] = total.astype(bf16)
        return carry

    lax.fori_loop(0, tasks * (model // LANES), body, 0)
    product = dot(flat(conv), weight[...]).astype(bf16)
    scaled = product * jnp.asarray(HALF**-0.5, bf16)
    queries[...] = scaled.reshape(queries.shape)


def half_mask(shape, side):
    lane = lax.broadcasted_iota(jnp.int32, shape, 1)
    return (lane < HALF) if side == 0 else (lane >= HALF)


def small_lane(shape):
    return lax.broadcasted_iota(jnp.int32, shape, 1) & (HALF - 1)


def pieces(value):
    high = value.astype(bf16).astype(f32)
    middle = (value - high).astype(bf16).astype(f32)
    return high, middle, value - high - middle


def marked(lead, value, shape):
    lane = small_lane(shape)
    high, middle, low = pieces(value)
    rest = jnp.where(lane == 1, high, jnp.where(lane == 2, middle, jnp.where(lane == 3, low, 0.0)))
    return jnp.where(lane == 0, lead, rest).astype(bf16)


def attend_kernel(order, *refs):
    refs = list(refs)
    heights, widths = refs[:2]
    del refs[:2]
    pooled = refs[: len(order)]
    del refs[: len(order)]
    (key_weight, value_weight, queries, tokens, out_weight, out_bias, gain, bias,
     keys, values, extra, attended, middle, normal, to_core, to_far, marks, square,
     sums, totals) = refs
    tasks, rows, width, model = tokens.shape
    me = lax.axis_index("rows")
    height, valid_width = heights[0], widths[0]
    cells = pooled[0].shape[0]
    pooled_rows = rows // 2
    for position, offset in enumerate(order):
        part = slice(position * cells, (position + 1) * cells)
        block = pooled[position][...]
        keys[part, :] = dot(block, key_weight[...]).astype(bf16)
        values[part, :] = dot(block, value_weight[...]).astype(bf16)
        cell = lax.broadcasted_iota(jnp.int32, (cells, LANES), 0)
        col = cell & (width // 2 - 1)
        row = (cell // (width // 2)) % pooled_rows + (me ^ offset) * pooled_rows
        good = (2 * row < height) & (2 * col < valid_width)
        lane = small_lane((cells, LANES))
        ones = jnp.where(lane < 4, 1.0, 0.0)
        extra[part, :] = jnp.where(
            lane == 0, jnp.where(good, 0.0, -1e30), ones
        ).astype(bf16)
    query_count = queries.shape[0]
    key_count = keys.shape[0]
    block = min(512, key_count)
    together = min(4, key_count // block)
    steps = key_count // (block * together)

    def body(pair, carry):
        lanes = pl.ds(pl.multiple_of(pair * LANES, LANES), LANES)
        query_pair = queries[:, lanes]
        shape = query_pair.shape
        across = lax.broadcasted_iota(jnp.int32, (LANES, LANES), 0) < HALF
        over = lax.broadcasted_iota(jnp.int32, (LANES, LANES), 1) >= HALF
        swap = jnp.where(across == over, 1.0, 0.0).astype(bf16)
        key_all = keys[:, lanes].astype(f32)
        key_norms = dot((key_all * key_all).astype(bf16), swap)
        largest = jnp.max(key_norms, axis=0, keepdims=True)
        query_all = query_pair.astype(f32)
        query_norms = dot((query_all * query_all).astype(bf16), swap)
        bound = 1.02 * jnp.sqrt(query_norms * largest)
        small = small_lane(shape)
        mark = jnp.where(small == 0, 1.0, jnp.where(small == 1, -bound, 0.0)).astype(bf16)
        bounded = []
        bounds = []
        for side in range(2):
            query = jnp.where(half_mask(shape, side), query_pair, mark)
            bounded.append(query)
            lane = lax.broadcasted_iota(jnp.int32, (8, LANES), 1)
            chosen = jnp.where(lane == (1 - side) * HALF + 1, 1.0, 0.0).astype(bf16)
            bounds.append(-dot(chosen, query, NT)[0:1])

        def some(step, first):
            results = []
            for side in range(2):
                total = None
                for k in range(together):
                    start = pl.multiple_of((step * together + k) * block, block)
                    part = pl.ds(start, block)
                    half = half_mask((block, LANES), side)
                    extras = extra[part, :]
                    scores = dot(jnp.where(half, keys[part, lanes], extras), bounded[side], NT)
                    weights = jnp.exp(scores).astype(bf16)
                    mixture = dot(jnp.where(half, values[part, lanes], extras), weights, TN)
                    total = mixture if total is None else total + mixture
                results.append(total)
            return results

        first = some(0, True)
        for side in range(2):
            sums[side] = first[side]
        if steps > 1:

            def more(step, carry):
                for side, total in enumerate(some(step, False)):
                    sums[side] += total
                return carry

            lax.fori_loop(1, steps, more, 0)
        for side in range(2):
            totals[side : side + 1, :] = bounds[side]
        at = [(1 - side) * HALF + 1 for side in range(2)]
        least = jnp.minimum(
            jnp.min(sums[0, at[0] : at[0] + 1, :]), jnp.min(sums[1, at[1] : at[1] + 1, :])
        )

        @pl.when(jnp.logical_not(least > 1e-25))
        def _():
            lead = jnp.where(small_lane(shape) == 0, 1.0, 0.0).astype(bf16)
            for side in range(2):
                query = jnp.where(half_mask(shape, side), query_pair, lead)

                def scores_of(step):
                    part = pl.ds(pl.multiple_of(step * LANES, LANES), LANES)
                    half = half_mask((LANES, LANES), side)
                    extras = extra[part, :]
                    value = jnp.where(half, values[part, lanes], extras)
                    return dot(jnp.where(half, keys[part, lanes], extras), query, NT), value

                def highest(step, peak):
                    scores, _ = scores_of(step)
                    return jnp.maximum(peak, jnp.max(scores, axis=0, keepdims=True))

                start = jnp.full((1, query_count), -jnp.inf, f32)
                peak = lax.fori_loop(0, key_count // LANES, highest, start)
                totals[side : side + 1, :] = peak
                sums[side] = jnp.zeros((LANES, query_count), f32)

                def add(step, carry):
                    scores, value = scores_of(step)
                    weights = jnp.exp(scores - totals[side : side + 1, :]).astype(bf16)
                    sums[side] += dot(value, weights, TN)
                    return carry

                lax.fori_loop(0, key_count // LANES, add, 0)

        both = []
        row = lax.broadcasted_iota(jnp.int32, (LANES, query_count), 0)
        small = row & (HALF - 1)
        for side in range(2):
            mixture = sums[side]
            total = mixture[at[side] : at[side] + 1]
            high, middle_part, low = pieces(-(totals[side : side + 1, :] + jnp.log(total)))
            mark = jnp.where(
                small == 0,
                1.0,
                jnp.where(
                    small == 1,
                    high,
                    jnp.where(small == 2, middle_part, jnp.where(small == 3, low, 0.0)),
                ),
            )
            inside = (row < HALF) if side == 0 else (row >= HALF)
            across = jnp.where(inside, mixture / total, mark).T
            marks[2 * pair + side] = jnp.where(
                half_mask(shape, side), query_pair, across.astype(bf16)
            )
            both.append(across)
        chosen = jnp.where(half_mask(shape, 0), both[0], both[1])
        attended[:, lanes] = chosen.astype(bf16)
        return carry

    lax.fori_loop(0, HEADS // 2, body, 0)
    branch = dot(attended[...], out_weight[...]) + out_bias[...].reshape(1, model)
    total = flat(tokens).astype(f32) + branch
    middle[...] = total.reshape(middle.shape)
    normed, _ = normalize(total)
    low = normed * gain[...].reshape(1, model) + bias[...].reshape(1, model)
    normal[...] = low.astype(bf16).reshape(normal.shape)
    core_row, far_row, _, _ = neighbours(rows)
    for task in range(tasks):
        to_core[task, 0] = normal[task, core_row]
        to_far[task, 0] = normal[task, far_row]
    index = lax.broadcasted_iota(jnp.int32, (query_count, 1), 0)
    inside = (me * rows + (index // width) % rows < height) & ((index & (width - 1)) < valid_width)
    square[...] = column_sum(branch * branch * inside.astype(f32))


def put_pieces(grad, first, count, me, keep, send):
    size = grad.shape[0] // PIECES
    for group in range(PIECES):
        piece = grad[group * size : (group + 1) * size]
        slot, owner = divmod(first + group, count)
        store_piece(owner, me, keep, send, slot * size, piece)


def store_piece(owner, me, keep, send, start, piece):
    place = owner ^ me
    size = piece.shape[0]

    @pl.when((place & 1) == 0)
    def _():
        keep[place >> 1, start : start + size, :] = piece

    @pl.when((place & 1) == 1)
    def _():
        send[place >> 1, start : start + size, :] = piece


def feed_kernel(
    heights, widths, middle_normal, from_core, from_far, up_weight, up_bias, taps, down_weight, down_bias,
    cotangent, middle,
    layer_out, grad_band, to_core, to_far, keep, send, grad_taps, grad_up_bias, sums,
    normal, wide, grad_act, wide_back, active, grad_lifted, branch, grad_normal,
):
    tasks, rows, width, model = cotangent.shape
    part = up_weight.shape[1]
    step = pl.program_id(0)
    last = pl.num_programs(0) - 1
    me, has_before, has_after = band_flags()
    count = lax.axis_size("rows")
    lines = rows + 2
    _, _, core_line, far_line = neighbours(rows)

    @pl.when(step == 0)
    def _():
        clear_guards(wide)
        clear_guards(wide_back)
        branch[...] = jnp.zeros_like(branch)
        grad_normal[...] = jnp.zeros_like(grad_normal)
        for task in range(tasks):
            for row in range(rows):
                normal[task, row + 1] = middle_normal[task, row]
            normal[task, core_line] = from_core[task, 0]
            normal[task, far_line] = from_far[task, 0]

    fed = flat(normal)
    shift_up = jnp.concatenate([up_bias[k] for k in range(up_bias.shape[0])], axis=1)
    lifted = dot(fed, up_weight[...]) + shift_up
    lifted = lifted.astype(bf16).astype(f32).reshape(tasks, lines, width, part)
    for task in range(tasks):
        for line in range(lines):
            value = lifted[task, line]
            if line == 0:
                value = value * has_before
            if line == lines - 1:
                value = value * has_after
            put_line(wide, task * lines + line, value)
    grad_output = flat(cotangent)
    grad_act[...] = dot(grad_output, down_weight[...], NT).reshape(grad_act.shape)

    c1 = 0.7978845608028654
    c2 = c1 * 0.044715
    blocks = part // LANES

    def across(block, carry):
        lanes = pl.ds(pl.multiple_of(block * LANES, LANES), LANES)
        tap = [[taps[a, b, lanes][None, :] for b in range(3)] for a in range(3)]

        def one_task(task, sums9):
            sums9 = list(sums9)
            for row in range(rows):
                for start in range(0, width, 16):
                    near = []
                    spread = None
                    for a in range(3):
                        for b in range(3):
                            at = GUARD - 1 + b + start
                            value = wide[block, task * lines + row + a, at : at + 16, :]
                            near.append(value)
                            term = tap[a][b] * value
                            spread = term if spread is None else spread + term
                    squared = spread * spread
                    gate = 0.5 + 0.5 * jnp.tanh(spread * (c1 + c2 * squared))
                    active[task * rows + row, start : start + 16, lanes] = (spread * gate).astype(
                        bf16
                    )
                    slope = gate + spread * (gate - gate * gate) * (2 * c1 + 6 * c2 * squared)
                    grad = grad_act[task * rows + row, start : start + 16, lanes] * slope
                    grad = grad.astype(bf16).astype(f32)
                    wide_back[
                        block, task * rows + row, GUARD + start : GUARD + start + 16, :
                    ] = grad
                    for k in range(9):
                        both = near[k] * grad
                        sums9[k] = sums9[k] + (both[0:8] + both[8:16])
            return tuple(sums9)

        sums9 = lax.fori_loop(
            0, tasks, one_task, tuple(jnp.zeros((8, LANES), f32) for _ in range(9))
        )
        for k in range(9):
            grad_taps[k // 3, k % 3, lanes] = jnp.sum(sums9[k], axis=0)

        def back_task(task, total):
            for line in range(lines):
                for start in range(0, width, 16):
                    value = None
                    for a in range(3):
                        if not 0 <= line - a < rows:
                            continue
                        for b in range(3):
                            at = GUARD + 1 - b + start
                            term = tap[a][b] * wide_back[
                                block, task * rows + line - a, at : at + 16, :
                            ]
                            value = term if value is None else value + term
                    if line == 0:
                        value = value * has_before
                    if line == lines - 1:
                        value = value * has_after
                    low = value.astype(bf16)
                    grad_lifted[task * lines + line, start : start + 16, lanes] = low
                    low = low.astype(f32)
                    total = total + (low[0:8] + low[8:16])
            return total

        total = lax.fori_loop(0, tasks, back_task, jnp.zeros((8, LANES), f32))
        per = model // LANES
        inside = pl.ds(pl.multiple_of((block % per) * LANES, LANES), LANES)
        grad_up_bias[block // per, :, inside] = column_sum(total)
        return carry

    lax.fori_loop(0, blocks, across, 0)

    act = flat(active)
    branch[...] += dot(act, down_weight[...])
    grad_down = dot(act, grad_output, TN).astype(bf16)
    grad_low = flat(grad_lifted)
    grad_up = dot(fed, grad_low, TN).astype(bf16)
    grad_normal[...] += dot(grad_low, up_weight[...], NT).reshape(grad_normal.shape)
    size = keep.shape[1] // 2
    groups = model // size
    for sub in range(part // model):
        column = step * (part // model) + sub
        columns = slice(sub * model, (sub + 1) * model)
        for group in range(groups):
            rows_of = slice(group * size, (group + 1) * size)
            store_piece(
                group * (count // groups) + column, me, keep, send, 0, grad_up[rows_of, columns]
            )
    for group in range(part // size):
        rows_of = slice(group * size, (group + 1) * size)
        owner = step * (part // size) + group
        store_piece(owner, me, keep, send, size, grad_down[rows_of])

    @pl.when(step == last)
    def _():
        shift = down_bias[...].reshape(1, model)
        height, valid_width = heights[0], widths[0]
        whole = branch[...].reshape(tasks, rows, width, model)
        first = jnp.zeros((1, model), f32)
        second = jnp.zeros((1, model), f32)
        col = lax.broadcasted_iota(jnp.int32, (width, 1), 0)
        for task in range(tasks):
            for row in range(rows):
                mlp = whole[task, row] + shift
                final = middle[task, row] + mlp
                layer_out[task, row] = final.astype(bf16)
                inside = (col < valid_width) & (me * rows + row < height)
                weight = inside.astype(f32)
                first = first + column_sum(mlp * mlp * weight)
                second = second + column_sum(final * final * weight)
            grad_band[task] = grad_normal[task, 1 : rows + 1]
            to_core[task, 0] = grad_normal[task, core_line].astype(bf16)
            to_far[task, 0] = grad_normal[task, far_line].astype(bf16)
        bias_sum = column_sum(grad_output.astype(f32))
        sums[...] = jnp.concatenate(
            [bias_sum, first, second, jnp.zeros((5, model), f32)], axis=0
        )


def feed(heights, widths, normal, from_core, from_far, up_weight, up_bias, taps, down_weight,
         down_bias, cotangent, middle, count):
    tasks, rows, width, model = cotangent.shape
    hidden = up_weight.shape[1]
    part = FEED_PART * model
    lines = rows + 2
    size = hidden // count
    smem = pl.BlockSpec(memory_space=pltpu.SMEM)

    def whole(shape):
        return pl.BlockSpec(shape, lambda i, k=len(shape): (0,) * k)

    ins = [
        smem, smem, whole(normal.shape), whole(from_core.shape), whole(from_far.shape),
        pl.BlockSpec((model, part), lambda i: (0, i)),
        pl.BlockSpec((FEED_PART, 1, model), lambda i: (i, 0, 0)),
        pl.BlockSpec((3, 3, part), lambda i: (0, 0, i)),
        pl.BlockSpec((part, model), lambda i: (i, 0)),
        whole(down_bias.shape), whole(cotangent.shape), whole(middle.shape),
    ]
    line_shape = (tasks, 1, width, model)
    outs = [
        (cotangent.shape, bf16), (cotangent.shape, f32), (line_shape, bf16), (line_shape, bf16),
        ((count // 2, 2 * size, model), bf16), ((count // 2, 2 * size, model), bf16),
        ((3, 3, hidden), f32), ((hidden // model, 1, model), f32), ((8, model), f32),
    ]
    out_specs = [whole(s) for s, _ in outs]
    out_specs[6] = pl.BlockSpec((3, 3, part), lambda i: (0, 0, i))
    out_specs[7] = pl.BlockSpec((FEED_PART, 1, model), lambda i: (i, 0, 0))
    return pl.pallas_call(
        feed_kernel,
        name="feed",
        grid=(hidden // part,),
        out_shape=tuple(jax.ShapeDtypeStruct(s, d) for s, d in outs),
        in_specs=ins,
        out_specs=tuple(out_specs),
        scratch_shapes=[
            pltpu.VMEM((tasks, lines, width, model), bf16),
            wide_scratch(tasks * lines, width, part),
            pltpu.VMEM((tasks * rows, width, part), f32),
            wide_scratch(tasks * rows, width, part),
            pltpu.VMEM((tasks * rows, width, part), bf16),
            pltpu.VMEM((tasks * lines, width, part), bf16),
            pltpu.VMEM((tasks * rows * width, model), f32),
            pltpu.VMEM((tasks, lines, width, model), f32),
        ],
        compiler_params=pltpu.CompilerParams(
            vmem_limit_bytes=36 << 20, dimension_semantics=("arbitrary",)
        ),
        cost_estimate=cost(33),
    )(heights, widths, normal, from_core, from_far, up_weight, up_bias, taps, down_weight, down_bias,
      cotangent, middle)


def norm_back_kernel(
    grad_band, from_core, from_far, middle, cotangent, gain, out_weight, attended,
    grad_middle, grad_marks, grad_out, sums,
):
    tasks, rows, width, model = cotangent.shape
    scale = gain[...].reshape(1, model)
    parts = []
    odd = (lax.axis_index("rows") & 1).astype(f32)
    for task in range(tasks):
        core = from_core[task, 0].astype(f32)
        far = from_far[task, 0].astype(f32)
        for row in range(rows):
            grad = grad_band[task, row]
            if row == 0:
                grad = grad + core * odd + far * (1.0 - odd)
            if row == rows - 1:
                grad = grad + far * odd + core * (1.0 - odd)
            parts.append(grad)
    grad_input = jnp.concatenate(parts, axis=0)
    normed, inverse = normalize(flat(middle))
    total = flat(cotangent).astype(f32) + normalize_back(grad_input, scale, normed, inverse)
    grad_middle[...] = total.reshape(grad_middle.shape)
    sums[0:1, :] = column_sum(grad_input * normed)
    sums[1:2, :] = column_sum(grad_input)
    sums[2:3, :] = column_sum(total)
    sums[3:8, :] = jnp.zeros((5, model), f32)
    grad_branch = total.astype(bf16)
    mixture = attended[...]
    grad_out[...] = dot(mixture, grad_branch, TN).astype(bf16)
    grad_attended = dot(grad_branch, out_weight[...], NT).astype(bf16)
    shape = (mixture.shape[0], LANES)
    for pair in range(HEADS // 2):
        lanes = slice(pair * LANES, (pair + 1) * LANES)
        grad_two = grad_attended[:, lanes]
        both = grad_two.astype(f32) * mixture[:, lanes].astype(f32)
        for side in range(2):
            half = half_mask(shape, side)
            inner = jnp.sum(jnp.where(half, both, 0.0), axis=-1, keepdims=True)
            grad_marks[2 * pair + side] = jnp.where(half, grad_two, marked(0.0, -inner, shape))


def attend_back_kernel(
    marks, grad_marks, keys, values, extra, grad_queries, grad_keys, grad_values,
    total, query_zero, grad_zero,
):
    key_count = keys.shape[0]
    query_count = grad_marks.shape[1]
    block = min(512, key_count)
    shape = (query_count, LANES)
    for side in range(2):
        half = half_mask(shape, side)
        zero = jnp.zeros(shape, bf16)
        part = slice(side * query_count, (side + 1) * query_count)
        query_zero[part, :] = jnp.where(half, marks[side], zero)
        grad_zero[part, :] = jnp.where(half, grad_marks[side], zero)

    def body(place, carry):
        part = pl.ds(pl.multiple_of(place * block, block), block)
        key_pair, value_pair, extras = keys[part, :], values[part, :], extra[part, :]
        lows, grads = [], []
        query_part = None
        for side in range(2):
            half = half_mask((block, LANES), side)
            scores = dot(jnp.where(half, key_pair, extras), marks[side], NT)
            grad_prob = dot(jnp.where(half, value_pair, extras), grad_marks[side], NT)
            probability = jnp.exp(scores)
            grad = (probability * grad_prob).astype(bf16)
            grads.append(grad)
            lows.append(probability.astype(bf16))
            one = dot(jnp.where(half, key_pair, jnp.zeros((block, LANES), bf16)), grad, TN)
            query_part = one if query_part is None else query_part + one
        grad_values[part, :] = dot(jnp.concatenate(lows, axis=1), grad_zero[...]).astype(bf16)
        grad_keys[part, :] = dot(jnp.concatenate(grads, axis=1), query_zero[...]).astype(bf16)

        @pl.when(place == 0)
        def _():
            total[...] = query_part

        @pl.when(place > 0)
        def _():
            total[...] += query_part

        return carry

    lax.fori_loop(0, key_count // block, body, 0)
    grad_queries[...] = (total[...] * HALF**-0.5).T.astype(bf16)


def side_by_side(refs):
    return jnp.concatenate([ref[...] for ref in refs], axis=1)


def pool_back_kernel(order, *refs):
    pairs = HEADS // 2
    refs = list(refs)
    grad_queries, grad_keys, grad_values = refs[:pairs], refs[pairs : 2 * pairs], refs[2 * pairs : 3 * pairs]
    del refs[: 3 * pairs]
    key_weight, value_weight, query_weight, keep, send, grad_conv, to_core, to_far = refs
    tasks, rows, width, model = grad_conv.shape
    cells = keep.shape[1]
    both = jnp.concatenate([key_weight[...], value_weight[...]], axis=1)
    for position, offset in enumerate(order):
        part = slice(position * cells, (position + 1) * cells)
        grads = jnp.concatenate([ref[part, :] for ref in (*grad_keys, *grad_values)], axis=1)
        target = send if offset & 1 else keep
        target[offset >> 1] = dot(grads, both, NT).astype(bf16)
    grad = dot(side_by_side(grad_queries), query_weight[...], NT).astype(bf16)
    grad_conv[...] = grad.reshape(grad_conv.shape)
    core_row, far_row, _, _ = neighbours(rows)
    for task in range(tasks):
        to_core[task, 0] = grad_conv[task, core_row]
        to_far[task, 0] = grad_conv[task, far_row]


def pair_weights(order, pooled, conv, queries, keys, values):
    cells = pooled[0].shape[0]
    total = None
    for position in range(len(order)):
        part = slice(position * cells, (position + 1) * cells)
        grads = jnp.concatenate([ref[part, :] for ref in (*keys, *values)], axis=1)
        value = dot(pooled[position][...], grads, TN)
        total = value if total is None else total + value
    grad_query = dot(flat(conv), side_by_side(queries), TN)
    return jnp.concatenate([grad_query, total], axis=1).astype(bf16)


def early_weight_kernel(order, *refs):
    refs = list(refs)
    pooled = refs[: len(order)]
    del refs[: len(order)]
    pairs = HEADS // 2 - 1
    conv, grad_out = refs[:2]
    queries, keys, values = refs[2 : 2 + pairs], refs[2 + pairs : 2 + 2 * pairs], refs[2 + 2 * pairs : -2]
    keep, send = refs[-2:]
    me = lax.axis_index("rows")
    count = len(order)
    model = grad_out.shape[0]
    both = pair_weights(order, pooled, conv, queries, keys, values)
    put_pieces(both[:, 0:model], 0, count, me, keep, send)
    put_pieces(both[:, model:], PIECES, count, me, keep, send)
    put_pieces(grad_out[...], 2 * PIECES, count, me, keep, send)


def weight_kernel(order, *refs):
    refs = list(refs)
    heights, widths = refs[:2]
    del refs[:2]
    pooled = refs[: len(order)]
    del refs[: len(order)]
    queries, keys, values = refs[:3]
    del refs[:3]
    (pool_keep, pool_send, conv, extended, grad_conv, taps, gain, bias, square, back_sums, feed_sums,
     hidden_taps, up_bias, keep, send, wide, rows_of) = refs
    tasks, rows, width, model = grad_conv.shape
    count = len(order)
    lines = rows + 2
    me, has_before, has_after = band_flags()
    size = keep.shape[1] - 16
    put_pieces(
        pair_weights(order, pooled, conv, [queries], [keys], [values]), 0, count, me, keep, send
    )
    pool_sum = jnp.zeros((1, model), f32)
    pool_dot = jnp.zeros((1, model), f32)
    for position, offset in enumerate(order):
        source = pool_send if offset & 1 else pool_keep
        grad = source[offset >> 1].astype(f32)
        pool_sum = pool_sum + column_sum(grad)
        pool_dot = pool_dot + column_sum(grad * pooled[position][...].astype(f32))

    clear_guards(wide)
    for task in range(tasks):
        for line in range(lines):
            put_line(wide, task * lines + line, extended[task, line].astype(f32))

    def across(block, carry):
        lanes = pl.ds(pl.multiple_of(block * LANES, LANES), LANES)

        def one_task(task, sums9):
            sums9 = list(sums9)
            for row in range(rows):
                for start in range(0, width, 16):
                    grad = grad_conv[task, row, start : start + 16, lanes].astype(f32)
                    for k in range(9):
                        at = GUARD - 1 + k % 3 + start
                        both = grad * wide[block, task * lines + row + k // 3, at : at + 16, :]
                        sums9[k] = sums9[k] + (both[0:8] + both[8:16])
            return tuple(sums9)

        sums9 = lax.fori_loop(
            0, tasks, one_task, tuple(jnp.zeros((8, LANES), f32) for _ in range(9))
        )
        for k in range(9):
            rows_of[2 + k : 3 + k, lanes] = column_sum(sums9[k])
        return carry

    lax.fori_loop(0, model // LANES, across, 0)

    shift = bias[...].reshape(1, model)
    zero = jnp.zeros((1, model), f32)
    conv_dot, conv_sum = zero, zero
    for row in range(rows):
        line = grad_conv[0, row].astype(f32)
        for task in range(1, tasks):
            line = line + grad_conv[task, row].astype(f32)
        full = column_sum(line)
        by_col = (full - line[0:1], full, full - line[width - 1 : width])
        for a in range(3):
            for b in range(3):
                value = by_col[b]
                if a == 0 and row == 0:
                    value = value * has_before
                if a == 2 and row == rows - 1:
                    value = value * has_after
                conv_sum = conv_sum + taps[a, b].reshape(1, model) * value
    for k in range(9):
        conv_dot = conv_dot + taps[k // 3, k % 3].reshape(1, model) * rows_of[2 + k : 3 + k, :]
    grad_bias = conv_sum + pool_sum
    grad_gain = (conv_dot + pool_dot - shift * grad_bias) / gain[...].reshape(1, model)
    rows_of[0:1, :] = grad_gain
    rows_of[1:2, :] = grad_bias
    rows_of[11:12, :] = back_sums[2:3, :]
    rows_of[12:14, :] = back_sums[0:2, :]
    rows_of[14:15, :] = feed_sums[0:1, :]
    rows_of[15:16, :] = square[...]
    rows_of[16:18, :] = feed_sums[1:3, :]
    in_rows = jnp.clip(heights[0] - me * rows, 0, rows)
    in_cols = jnp.clip(widths[0], 0, width)
    cells_in = (tasks * in_rows * in_cols).astype(f32)
    rows_of[18:19, :] = jnp.full((1, model), cells_in, f32)
    parts = up_bias.shape[0]
    for part in range(parts):
        rows_of[19 + part : 20 + part, :] = up_bias[part]
        for k in range(9):
            rows_of[19 + parts * (k + 1) + part : 20 + parts * (k + 1) + part, :] = hidden_taps[
                k // 3, k % 3, part * model : (part + 1) * model
            ].reshape(1, model)
    used = 19 + 10 * parts
    rows_of[used:SMALL, :] = jnp.zeros((SMALL - used, model), f32)
    group = SMALL // count
    for owner in range(count):
        value = rows_of[owner * group : (owner + 1) * group, :]
        if group < 8:
            value = jnp.concatenate([value, jnp.zeros((8 - group, model), f32)], axis=0)
        high = value.astype(bf16)
        low = (value - high.astype(f32)).astype(bf16)
        store_piece(owner, me, keep, send, size, jnp.concatenate([high, low], axis=0))


def last_kernel(
    grad_conv, from_core, from_far, taps, tokens, gain, grad_middle, pool, input_grad, wide
):
    tasks, rows, width, model = tokens.shape
    lines = rows + 2
    pooled_rows = rows // 2
    clear_guards(wide)
    _, _, core_line, far_line = neighbours(rows)
    for task in range(tasks):
        put_line(wide, task * lines + core_line, from_core[task, 0].astype(f32))
        put_line(wide, task * lines + far_line, from_far[task, 0].astype(f32))
        for row in range(rows):
            put_line(wide, task * lines + row + 1, grad_conv[task, row].astype(f32))
    pooled = pool[...].reshape(tasks, pooled_rows, width // 2, model)
    spread_matrix = pool_matrix(width)[:, 0:width]

    def body(step, carry):
        task = step // (model // LANES)
        block = step % (model // LANES)
        lanes = pl.ds(pl.multiple_of(block * LANES, LANES), LANES)
        for row in range(rows):
            for start in range(0, width, 16):
                total = jnp.zeros((16, LANES), f32)
                for a in range(3):
                    for b in range(3):
                        at = GUARD + 1 - b + start
                        total = total + taps[a, b, lanes][None, :] * wide[
                            block, task * lines + row + 2 - a, at : at + 16, :
                        ]
                input_grad[task, row, start : start + 16, lanes] = total
        return carry

    lax.fori_loop(0, tasks * (model // LANES), body, 0)
    scale = gain[...].reshape(1, model)
    for task in range(tasks):
        for row in range(rows):
            grad = input_grad[task, row] + dot(spread_matrix, pooled[task, row // 2], TN)
            normed, inverse = normalize(tokens[task, row].astype(f32))
            input_grad[task, row] = grad_middle[task, row] + normalize_back(grad, scale, normed, inverse)


def add_blocks(values):
    total = values[0].astype(f32)
    for other in values[1:]:
        total = total + other.astype(f32)
    return total


def put_sum(out, start, values, small):
    total = add_blocks(values)
    size = total.shape[0]
    if not small:
        out[start : start + size, :] = total.astype(bf16)
        return
    size -= 16
    value = total[size : size + 8] + total[size + 8 : size + 16]
    high = value.astype(bf16)
    low = (value - high.astype(f32)).astype(bf16)
    out[start : start + size, :] = total[0:size].astype(bf16)
    out[start + size : start + size + 16, :] = jnp.concatenate([high, low], axis=0)


def combine(arrays, small):
    blocks, size, model = arrays[0].shape

    def kernel(*refs):
        ins, outs = refs[: len(arrays)], refs[len(arrays) :]
        for block, out in enumerate(outs):
            put_sum(out, 0, [x[block] for x in ins], small)

    return call("combine", kernel, [((size, model), bf16)] * blocks, list(arrays))


def halve(ones, others):
    blocks, size, model = ones.shape
    if blocks == 1:
        return combine([ones, others], False)

    def kernel(mine, arrived, stay, go):
        for block in range(blocks):
            total = add_blocks([mine[block], arrived[block]]).astype(bf16)
            (go if block & 1 else stay)[block >> 1] = total

    return call("halve", kernel, [((blocks // 2, size, model), bf16)] * 2, [ones, others])


def join_early(keep, swapped, sums):
    blocks, size, model = keep.shape
    below = sums[0].shape[0]

    def kernel(*refs):
        ones, others = refs[0:2], refs[2 : 2 + len(sums)]
        own, total, *outs = refs[2 + len(sums) :]
        put_sum(own, 0, [x[0] for x in ones], False)
        put_sum(total, 0, [x[...] for x in others], False)
        for block, out in enumerate(outs):
            put_sum(out, 0, [x[block + 1] for x in ones], False)
            out[size : size + below, :] = total[...]

    outs = [((size, model), bf16), ((below, model), bf16)]
    outs += [((size + below, model), bf16)] * (blocks - 1)
    own, total, *others = call("join_early", kernel, outs, [keep, swapped, *sums])
    return own, total, others


def split_early(own, below, arrived):
    size, model = own.shape
    under = below.shape[0]

    def kernel(*refs):
        mine, first, others, total, stack = refs[0], refs[1], refs[2:-2], refs[-2], refs[-1]
        put_sum(total, 0, [mine[...], *[x[0:size, :] for x in others]], False)
        stack[0] = first[...]
        for place, x in enumerate(others):
            stack[place + 1] = x[size : size + under, :]

    outs = [((size, model), bf16), ((1 + len(arrived), under, model), bf16)]
    return call("split_early", kernel, outs, [own, below, *arrived], limit=16)


def join_late(own, arrived, early, early_arrived):
    size, model = own.shape
    below = early.shape[0]
    count = 1 + len(arrived)

    def kernel(*refs):
        out = refs[-1]
        put_sum(out, 0, [x[...] for x in refs[0:count]], True)
        put_sum(out, size, [x[...] for x in refs[count:-1]], False)

    outs = [((size + below, model), bf16)]
    return call("join_late", kernel, outs, [own, *arrived, early, *early_arrived])[0]


def exchange(value, axis, mask):
    count = lax.axis_size(axis)
    return lax.ppermute(value, axis, [(i, i ^ mask) for i in range(count)])


def far_masks():
    return list(range(2, lax.axis_size("rows"), 2))


def once(value, *earlier):
    return lax.optimization_barrier((value, earlier))[0]


def far_rows(value):
    return [exchange(value, "rows", mask) for mask in far_masks()]


def all_images(value):
    return [exchange(value, "batch", mask) for mask in range(1, lax.axis_size("batch"))]


def add_images(own, arrived, small):
    (total,) = combine([x[None] for x in [own, *arrived]], small)
    return total


def unpack_feed_kernel(count, *refs):
    even, odd, grad_up, grad_down = refs
    blocks = [half.at[place] for half in (even, odd) for place in range(count // 2)]
    me = lax.axis_index("rows")
    model, hidden = grad_up.shape
    size = hidden // count
    columns = hidden // model
    for j in range(count):
        owner = blocks_owner(j, count, me)
        block = blocks[j]
        up = block[0:size, :].astype(f32)
        place = owner // columns
        col = owner % columns
        grad_up[
            pl.ds(pl.multiple_of(place * size, size), size),
            pl.ds(pl.multiple_of(col * model, model), model),
        ] = up
        grad_down[pl.ds(pl.multiple_of(owner * size, size), size), :] = block[
            size : 2 * size, :
        ].astype(f32)


def blocks_owner(j, count, me):
    half = count // 2
    offset = 2 * j if j < half else 2 * (j - half) + 1
    return me ^ offset


def unpack_late_kernel(count, *refs):
    blocks = refs[:count]
    (grad_query, grad_key, grad_value, grad_out, norm1_gain, norm1_bias, query_taps, out_bias,
     norm2_gain, norm2_bias, up_bias, hidden_taps, down_bias, stats, weights, rows_of) = refs[count:]
    me = lax.axis_index("rows")
    model = grad_query.shape[0]
    piece = model // PIECES
    size = piece + 16
    group = SMALL // count
    slots = (blocks[0].shape[0] - size) // piece
    above = slots * count * piece
    for j in range(count):
        owner = blocks_owner(j, count, me)
        block = blocks[j][...].astype(f32)
        for slot in range(slots):
            start = pl.multiple_of((slot * count + owner) * piece, piece)
            at = size + slot * piece
            weights[pl.ds(start, piece), :] = block[at : at + piece]
        start = pl.multiple_of(above + owner * piece, piece)
        weights[pl.ds(start, piece), :] = block[0:piece]
        rows_of[owner] = block[piece : piece + 8] + block[piece + 8 : piece + 16]
    grad_out[...] = weights[2 * model : 3 * model, :]
    pairs = HEADS // 2
    columns = [(which, pair) for which in range(3) for pair in range(pairs - 1)]
    outs = (grad_query, grad_key, grad_value)
    for place, (which, pair) in enumerate(columns):
        matrix, at = divmod(place * LANES, model)
        outs[which][:, pair * LANES : (pair + 1) * LANES] = weights[
            matrix * model : (matrix + 1) * model, at : at + LANES
        ]
    for which, out in enumerate(outs):
        out[:, (pairs - 1) * LANES : pairs * LANES] = weights[
            above : above + model, which * LANES : (which + 1) * LANES
        ]

    def line(k):
        return rows_of[k // group, k % group, :]

    norm1_gain[...] = line(0)
    norm1_bias[...] = line(1)
    for k in range(9):
        query_taps[k // 3, k % 3, :] = line(2 + k)
    out_bias[...] = line(11)
    norm2_gain[...] = line(12)
    norm2_bias[...] = line(13)
    down_bias[...] = line(14)
    parts = up_bias.shape[0] // model
    for part in range(parts):
        lanes = slice(part * model, (part + 1) * model)
        up_bias[lanes] = line(19 + part)
        for k in range(9):
            hidden_taps[k // 3, k % 3, lanes] = line(19 + parts * (k + 1) + part)
    cells = line(18).reshape(1, model)[:, 0:1]
    row = lax.broadcasted_iota(jnp.int32, (1, LANES), 1)
    value = jnp.zeros((1, LANES), f32)
    for k in range(3):
        total = jnp.sum(line(15 + k).reshape(1, model), axis=-1, keepdims=True)
        value = jnp.where(row == k, jnp.sqrt(total / (cells * model)), value)
    stats[...] = value


def local(
    tokens,
    norm1_gain,
    norm1_bias,
    query_taps,
    query_weight,
    key_weight,
    value_weight,
    out_weight,
    out_bias,
    norm2_gain,
    norm2_bias,
    up_weight,
    up_bias,
    hidden_taps,
    down_weight,
    down_bias,
    cotangent,
    heights,
    widths,
):
    shape = tokens.shape
    tokens, cotangent = tokens[0], cotangent[0]
    tasks, rows, width, model = tokens.shape
    hidden = up_weight.shape[1]
    count = lax.axis_size("rows")
    cells = tasks * (rows // 2) * (width // 2)
    key_count = count * cells
    lines = rows + 2
    token_count = tasks * rows * width
    line = (tasks, 1, width, model)

    def swap_lines(lines_out):
        to_core, to_far = lines_out
        across = [pair for i in range(1, count - 1, 2) for pair in ((i, i + 1), (i + 1, i))]
        return exchange(to_core, "rows", 1), lax.ppermute(to_far, "rows", across)

    normal_one, pooled, *edge = call(
        "first_norm",
        first_norm_kernel,
        [(tokens.shape, bf16), ((cells, model), bf16), (line, bf16), (line, bf16)],
        [hbm(x) for x in (tokens, norm1_gain, norm1_bias)],
        limit=8,
    )
    far = far_masks()
    order = [0, 1, *far, *[mask + 1 for mask in far]]
    edge = swap_lines(edge)
    swapped = exchange(pooled, "rows", 1)
    arrived = far_rows(pooled)
    extended, conv, queries = call(
        "query_conv",
        query_kernel,
        [
            in_hbm((tasks, lines, width, model), bf16), in_hbm(tokens.shape, bf16),
            ((token_count, model), bf16),
        ],
        [normal_one, *edge, hbm(query_taps), hbm(query_weight)],
        scratch=[wide_scratch(tasks * lines, width, model)],
        us=2,
        limit=12,
    )
    arrived = once(arrived, queries)
    blocks = [pooled, swapped, *arrived, *[exchange(x, "rows", 1) for x in arrived]]

    (keys, values, extra, attended, middle, normal_two, to_core, to_far, marks, square) = call(
        "attend",
        lambda *refs: attend_kernel(order, *refs),
        [
            ((key_count, model), bf16), ((key_count, model), bf16), in_hbm((key_count, LANES), bf16),
            in_hbm((token_count, model), bf16), in_hbm(tokens.shape, f32),
            in_hbm(tokens.shape, bf16), (line, bf16), (line, bf16), in_hbm((HEADS, token_count, LANES), bf16), ((1, model), f32),
        ],
        [heights, widths, *blocks, hbm(key_weight), hbm(value_weight), queries,
         *[hbm(x) for x in (tokens, out_weight, out_bias, norm2_gain, norm2_bias)]],
        smem=2,
        scratch=[pltpu.VMEM((2, LANES, token_count), f32), pltpu.VMEM((8, token_count), f32)],
        us=18,
        limit=24,
    )
    (layer_out, grad_band, to_core, to_far, feed_keep, feed_send, grad_hidden_taps,
     grad_up_bias, feed_sums) = feed(
        heights, widths, hbm(normal_two), *swap_lines((to_core, to_far)), hbm(up_weight),
        up_bias.reshape(hidden // model, 1, model),
        *[hbm(x) for x in (hidden_taps, down_weight, down_bias, cotangent, middle)], count,
    )
    edge = swap_lines((to_core, to_far))
    feed_swapped = exchange(feed_send, "rows", 1)
    feed_blocks = combine(once([feed_keep, feed_swapped], edge), False)
    feed_arrived = [exchange(feed_blocks[mask >> 1], "rows", mask) for mask in far]
    piece = model // PIECES
    grad_middle, grad_marks, grad_out, back_sums = call(
        "norm_back",
        norm_back_kernel,
        [
            (tokens.shape, f32), ((HEADS, token_count, LANES), bf16), ((model, model), bf16),
            ((8, model), f32),
        ],
        [
            once(grad_band, feed_blocks), *edge,
            *[hbm(x) for x in (middle, cotangent, norm2_gain, out_weight, attended)],
        ],
        us=4,
        limit=24,
    )

    def attend_back(pair, tie):
        inputs = [marks, grad_marks, keys, values, extra]
        inputs = once(inputs, *tie)

        def of_heads(x):
            return pl.BlockSpec((2, x.shape[1], LANES), lambda i: (pair, 0, 0))

        def of_lanes(x):
            return pl.BlockSpec((x.shape[0], LANES), lambda i: (0, pair))

        whole = pl.BlockSpec((key_count, LANES), lambda i: (0, 0))
        outs = [(token_count, LANES), (key_count, LANES), (key_count, LANES)]
        return pl.pallas_call(
            attend_back_kernel,
            name="attend_back",
            grid=(1,),
            out_shape=[jax.ShapeDtypeStruct(shape, bf16) for shape in outs],
            in_specs=[*[of_heads(x) for x in inputs[0:2]], *[of_lanes(x) for x in inputs[2:4]], whole],
            out_specs=[pl.BlockSpec(shape, lambda i: (0, 0)) for shape in outs],
            scratch_shapes=[
                pltpu.VMEM((LANES, token_count), f32),
                pltpu.VMEM((2 * token_count, LANES), bf16),
                pltpu.VMEM((2 * token_count, LANES), bf16),
            ],
            compiler_params=pltpu.CompilerParams(vmem_limit_bytes=16 << 20),
            cost_estimate=cost(11),
        )(*inputs)

    feed_arrived = once(feed_arrived, grad_marks)
    feed_own = add_images(feed_blocks[0], feed_arrived, False)
    feed_arrived = all_images(feed_own)
    back = [attend_back(0, [feed_own])]
    back.append(attend_back(1, back[0]))
    feed_arrived = once(feed_arrived, *back[1])
    slots = -(-3 * PIECES // count)
    early_keep, early_send = call(
        "weights_early",
        lambda *refs: early_weight_kernel(order, *refs),
        [((count // 2, slots * piece, model), bf16)] * 2,
        [*blocks, conv, once(grad_out, feed_arrived), *[x[which] for which in range(3) for x in back]],
        us=3,
        limit=12,
    )
    early_swapped = exchange(early_send, "rows", 1)
    early_own, feed_own, leaving = join_early(early_keep, early_swapped, [feed_own, *feed_arrived])
    arrived = [exchange(x, "rows", mask) for x, mask in zip(leaving, far)]
    back.append(attend_back(2, [*back[-1], *leaving]))
    early_own, feed_even = split_early(early_own, feed_own, once(arrived, *back[-1]))
    early_arrived = all_images(early_own)
    feed_odd = exchange(feed_even, "rows", 1)
    grads = [part for which in range(3) for part in [x[which] for x in back]]
    grads = once(grads, early_own)

    pool_keep, pool_send, grad_conv, *edge = call(
        "pool_back",
        lambda *refs: pool_back_kernel(order, *refs),
        [((count // 2, cells, model), bf16)] * 2 + [(tokens.shape, bf16), (line, bf16), (line, bf16)],
        [*grads, key_weight, value_weight, query_weight],
        us=3,
        limit=12,
    )
    pairs = HEADS // 2
    keep, send = call(
        "weights",
        lambda *refs: weight_kernel(order, *refs),
        [((count // 2, piece + 16, model), bf16)] * 2,
        [
            heights, widths, *blocks, *[grads[k * pairs + pairs - 1] for k in range(3)], pool_keep,
            pool_send, conv, extended, grad_conv, query_taps, norm1_gain, norm1_bias, square,
            back_sums, feed_sums, grad_hidden_taps, grad_up_bias,
        ],
        smem=2,
        scratch=[
            wide_scratch(tasks * lines, width, model),
            pltpu.VMEM((SMALL, model), f32),
        ],
        us=4,
        limit=16,
    )
    early_arrived = once(early_arrived, keep)
    feed_odd = once(feed_odd, keep)
    send, pool_send, edge = once((send, pool_send, edge), early_arrived, feed_odd)
    late_swapped = exchange(send, "rows", 1)
    pool_swapped = exchange(pool_send, "rows", 1)
    edge = swap_lines(edge)
    late_blocks = combine([keep, late_swapped], True)
    pool_blocks, pool_going = halve(pool_keep, pool_swapped)
    late_arrived = [exchange(late_blocks[mask >> 1], "rows", mask) for mask in far]
    pool_arrived = exchange(pool_going, "rows", 2)
    grad_up, grad_down = call(
        "unpack_feed",
        lambda *refs: unpack_feed_kernel(count, *refs),
        [((model, hidden), f32), ((hidden, model), f32)],
        [feed_even, once(feed_odd, late_blocks, pool_going)],
        us=3,
        limit=12,
    )
    late_arrived, pool_arrived, edge = once((late_arrived, pool_arrived, edge), grad_up)
    (late_own,) = combine([x[None] for x in [late_blocks[0], *late_arrived]], True)
    late_arrived = all_images(late_own)
    hop = 2
    while 2 * hop < count:
        pool_blocks, pool_going = halve(pool_blocks, pool_arrived)
        hop *= 2
        pool_arrived = exchange(pool_going, "rows", hop)
    (pool_total,) = halve(pool_blocks, once(pool_arrived, *late_arrived))
    late_own = join_late(late_own, late_arrived, early_own, early_arrived)
    late_others = far_rows(late_own)
    (input_grad,) = call(
        "last_norm",
        last_kernel,
        [(tokens.shape, f32)],
        [grad_conv, *edge, query_taps, tokens, norm1_gain, grad_middle, once(pool_total, late_own)],
        scratch=[wide_scratch(tasks * lines, width, model)],
        us=5,
        limit=12,
    )
    even = [late_own, *once(late_others, input_grad)]
    odd = [exchange(x, "rows", 1) for x in even]
    vector = ((model,), f32)
    late = call(
        "unpack_late",
        lambda *refs: unpack_late_kernel(count, *refs),
        [((model, model), f32)] * 4
        + [vector, vector, ((3, 3, model), f32), vector, vector, vector, ((hidden,), f32),
           ((3, 3, hidden), f32), vector, ((1, LANES), f32)],
        [*even, *odd],
        scratch=[
            pltpu.VMEM(((slots + 1) * count * piece, model), f32),
            pltpu.VMEM((count, 8, model), f32),
        ],
        us=2,
        limit=12,
    )
    (grad_query, grad_key, grad_value, grad_out, gain1, bias1, taps1, out_sum, gain2, bias2, up_sum,
     taps2, down_sum, stats) = late
    return (
        layer_out.reshape(shape),
        input_grad.reshape(shape),
        gain1,
        bias1,
        taps1,
        grad_query,
        grad_key,
        grad_value,
        grad_out,
        out_sum,
        gain2,
        bias2,
        grad_up,
        up_sum,
        taps2,
        grad_down,
        down_sum,
        stats[0, 0:3],
    )


def solution(mesh):
    band = P("batch", None, "rows", None, None)
    placed = (band, *[P()] * 15, band, P("batch"), P("batch"))
    return jax.shard_map(
        local,
        mesh=mesh,
        in_specs=placed,
        out_specs=(band, band, *[P()] * 16),
        check_vma=False,
    )
```

```python
import jax
import jax.numpy as jnp
from jax import lax
from jax.experimental import pallas as pl
from jax.experimental.pallas import tpu as pltpu
from jax.sharding import PartitionSpec as P

HEADS = 6
LANES = 128
HALF = 64
GUARD = 8
SMALL = 64
PIECES = 8
FEED_PART = 2
epsilon = 1e-05
f32 = jnp.float32
bf16 = jnp.bfloat16
NN = (((1,), (0,)), ((), ()))
NT = (((1,), (1,)), ((), ()))
TN = (((0,), (0,)), ((), ()))


def dot(left, right, form=NN):
    return lax.dot_general(left, right, form, preferred_element_type=f32)


def cost(us):
    return pl.CostEstimate(flops=int(us * 1e4), bytes_accessed=int(us * 1e4), transcendentals=0)


def hbm(value):
    return pltpu.with_memory_space_constraint(value, pltpu.HBM)


def in_hbm(shape, dtype):
    return shape, dtype, True


def out_type(shape, dtype, away=False):
    return pltpu.HBM(shape, dtype) if away else jax.ShapeDtypeStruct(shape, dtype)


def call(name, kernel, outs, args, smem=0, scratch=(), us=1, limit=12):
    def whole(shape):
        return pl.BlockSpec(shape, lambda i, k=len(shape): (0,) * k)

    return pl.pallas_call(
        kernel,
        grid=(1,),
        out_shape=tuple(out_type(*x) for x in outs),
        in_specs=[pl.BlockSpec(memory_space=pltpu.SMEM)] * smem
        + [whole(x.shape) for x in args[smem:]],
        out_specs=tuple(whole(x[0]) for x in outs),
        scratch_shapes=list(scratch),
        name=name,
        compiler_params=pltpu.CompilerParams(vmem_limit_bytes=limit << 20),
        cost_estimate=cost(us),
    )(*args)


def normalize(values):
    center = jnp.mean(values, axis=-1, keepdims=True)
    centered = values - center
    inverse = lax.rsqrt(jnp.mean(centered * centered, axis=-1, keepdims=True) + epsilon)
    return centered * inverse, inverse


def normalize_back(grad_output, gain, normed, inverse):
    scaled = grad_output * gain
    return inverse * (
        scaled
        - jnp.mean(scaled, axis=-1, keepdims=True)
        - normed * jnp.mean(scaled * normed, axis=-1, keepdims=True)
    )


def column_sum(values):
    return jnp.sum(values, axis=0, keepdims=True)


def flat(ref):
    value = ref[...]
    return value.reshape(-1, value.shape[-1])


def band_flags():
    me = lax.axis_index("rows")
    count = lax.axis_size("rows")
    return me, (me > 0).astype(f32), (me < count - 1).astype(f32)


def neighbours(rows):
    odd = lax.axis_index("rows") & 1
    even = 1 - odd
    return even * (rows - 1), odd * (rows - 1), even * (rows + 1), odd * (rows + 1)


def far_weight():
    me, has_before, has_after = band_flags()
    return jnp.where((me & 1) == 1, has_after, has_before)


def pool_matrix(width):
    rows = lax.broadcasted_iota(jnp.int32, (width // 2, 2 * width), 0)
    cols = lax.broadcasted_iota(jnp.int32, (width // 2, 2 * width), 1)
    cols = jnp.where(cols >= width, cols - width, cols)
    return jnp.where((cols >> 1) == rows, 0.25, 0.0).astype(bf16)


def first_norm_kernel(tokens, gain, bias, normal, pooled):
    tasks, rows, width, model = tokens.shape
    matrix = pool_matrix(width)
    scale = gain[...].reshape(1, model)
    shift = bias[...].reshape(1, model)
    for task in range(tasks):
        for row in range(0, rows, 2):
            value = tokens[task, row : row + 2].astype(f32).reshape(2 * width, model)
            low = (normalize(value)[0] * scale + shift).astype(bf16)
            normal[task, row : row + 2] = low.reshape(2, width, model)
            start = (task * (rows // 2) + row // 2) * (width // 2)
            pooled[start : start + width // 2, :] = dot(matrix, low).astype(bf16)


def edge_kernel(normal, to_core, to_far):
    tasks, rows = normal.shape[:2]
    core_row, far_row, _, _ = neighbours(rows)
    for task in range(tasks):
        to_core[task, 0] = normal[task, core_row]
        to_far[task, 0] = normal[task, far_row]


def clear_guards(wide):
    blocks, lines, length, lanes = wide.shape
    zero = jnp.zeros((blocks, lines, GUARD, lanes), wide.dtype)
    wide[:, :, 0:GUARD, :] = zero
    wide[:, :, length - GUARD : length, :] = zero


def put_line(wide, line, value):
    for block in range(wide.shape[0]):
        wide[block, line, GUARD : GUARD + value.shape[0], :] = value[
            :, block * LANES : (block + 1) * LANES
        ]


def wide_scratch(lines, width, model):
    return pltpu.VMEM((model // LANES, lines, width + 2 * GUARD, LANES), f32)


def query_kernel(normal, from_core, from_far, taps, weight, extended, conv, queries, wide):
    tasks, rows, width, model = normal.shape
    clear_guards(wide)
    lines = rows + 2
    _, _, core_line, far_line = neighbours(rows)
    for task in range(tasks):
        extended[task, core_line] = from_core[task, 0]
        extended[task, far_line] = (from_far[task, 0].astype(f32) * far_weight()).astype(bf16)
        for row in range(rows):
            extended[task, row + 1] = normal[task, row]
        for line in range(lines):
            put_line(wide, task * lines + line, extended[task, line].astype(f32))

    def body(step, carry):
        task = step // (model // LANES)
        block = step % (model // LANES)
        lanes = pl.ds(pl.multiple_of(block * LANES, LANES), LANES)
        for row in range(rows):
            for start in range(0, width, 16):
                total = jnp.zeros((16, LANES), f32)
                for a in range(3):
                    for b in range(3):
                        at = GUARD - 1 + b + start
                        total = total + taps[a, b, lanes][None, :] * wide[
                            block, task * lines + row + a, at : at + 16, :
                        ]
                conv[task, row, start : start + 16, lanes] = total.astype(bf16)
        return carry

    lax.fori_loop(0, tasks * (model // LANES), body, 0)
    product = dot(flat(conv), weight[...]).astype(bf16)
    scaled = product * jnp.asarray(HALF**-0.5, bf16)
    queries[...] = scaled.reshape(queries.shape)


def half_mask(shape, side):
    lane = lax.broadcasted_iota(jnp.int32, shape, 1)
    return (lane < HALF) if side == 0 else (lane >= HALF)


def small_lane(shape):
    return lax.broadcasted_iota(jnp.int32, shape, 1) & (HALF - 1)


def pieces(value):
    high = value.astype(bf16).astype(f32)
    middle = (value - high).astype(bf16).astype(f32)
    return high, middle, value - high - middle


def marked(lead, value, shape):
    lane = small_lane(shape)
    high, middle, low = pieces(value)
    rest = jnp.where(lane == 1, high, jnp.where(lane == 2, middle, jnp.where(lane == 3, low, 0.0)))
    return jnp.where(lane == 0, lead, rest).astype(bf16)


def attend_kernel(order, *refs):
    refs = list(refs)
    heights, widths = refs[:2]
    del refs[:2]
    pooled = refs[: len(order)]
    del refs[: len(order)]
    (key_weight, value_weight, queries, tokens, out_weight, out_bias, gain, bias,
     keys, values, extra, attended, middle, normal, to_core, to_far, marks, square,
     sums, totals) = refs
    tasks, rows, width, model = tokens.shape
    me = lax.axis_index("rows")
    height, valid_width = heights[0], widths[0]
    cells = pooled[0].shape[0]
    pooled_rows = rows // 2
    for position, offset in enumerate(order):
        part = slice(position * cells, (position + 1) * cells)
        block = pooled[position][...]
        keys[part, :] = dot(block, key_weight[...]).astype(bf16)
        values[part, :] = dot(block, value_weight[...]).astype(bf16)
        cell = lax.broadcasted_iota(jnp.int32, (cells, LANES), 0)
        col = cell & (width // 2 - 1)
        row = (cell // (width // 2)) % pooled_rows + (me ^ offset) * pooled_rows
        good = (2 * row < height) & (2 * col < valid_width)
        lane = small_lane((cells, LANES))
        ones = jnp.where(lane < 4, 1.0, 0.0)
        extra[part, :] = jnp.where(
            lane == 0, jnp.where(good, 0.0, -1e30), ones
        ).astype(bf16)
    query_count = queries.shape[0]
    key_count = keys.shape[0]
    block = min(512, key_count)
    together = min(4, key_count // block)
    steps = key_count // (block * together)

    def body(pair, carry):
        lanes = pl.ds(pl.multiple_of(pair * LANES, LANES), LANES)
        query_pair = queries[:, lanes]
        shape = query_pair.shape
        across = lax.broadcasted_iota(jnp.int32, (LANES, LANES), 0) < HALF
        over = lax.broadcasted_iota(jnp.int32, (LANES, LANES), 1) >= HALF
        swap = jnp.where(across == over, 1.0, 0.0).astype(bf16)
        key_all = keys[:, lanes].astype(f32)
        key_norms = dot((key_all * key_all).astype(bf16), swap)
        largest = jnp.max(key_norms, axis=0, keepdims=True)
        query_all = query_pair.astype(f32)
        query_norms = dot((query_all * query_all).astype(bf16), swap)
        bound = 1.02 * jnp.sqrt(query_norms * largest)
        small = small_lane(shape)
        mark = jnp.where(small == 0, 1.0, jnp.where(small == 1, -bound, 0.0)).astype(bf16)
        bounded = []
        bounds = []
        for side in range(2):
            query = jnp.where(half_mask(shape, side), query_pair, mark)
            bounded.append(query)
            lane = lax.broadcasted_iota(jnp.int32, (8, LANES), 1)
            chosen = jnp.where(lane == (1 - side) * HALF + 1, 1.0, 0.0).astype(bf16)
            bounds.append(-dot(chosen, query, NT)[0:1])

        def some(step, first):
            results = []
            for side in range(2):
                total = None
                for k in range(together):
                    start = pl.multiple_of((step * together + k) * block, block)
                    part = pl.ds(start, block)
                    half = half_mask((block, LANES), side)
                    extras = extra[part, :]
                    scores = dot(jnp.where(half, keys[part, lanes], extras), bounded[side], NT)
                    weights = jnp.exp(scores).astype(bf16)
                    mixture = dot(jnp.where(half, values[part, lanes], extras), weights, TN)
                    total = mixture if total is None else total + mixture
                results.append(total)
            return results

        first = some(0, True)
        for side in range(2):
            sums[side] = first[side]
        if steps > 1:

            def more(step, carry):
                for side, total in enumerate(some(step, False)):
                    sums[side] += total
                return carry

            lax.fori_loop(1, steps, more, 0)
        for side in range(2):
            totals[side : side + 1, :] = bounds[side]
        at = [(1 - side) * HALF + 1 for side in range(2)]
        least = jnp.minimum(
            jnp.min(sums[0, at[0] : at[0] + 1, :]), jnp.min(sums[1, at[1] : at[1] + 1, :])
        )

        @pl.when(jnp.logical_not(least > 1e-25))
        def _():
            lead = jnp.where(small_lane(shape) == 0, 1.0, 0.0).astype(bf16)
            for side in range(2):
                query = jnp.where(half_mask(shape, side), query_pair, lead)

                def scores_of(step):
                    part = pl.ds(pl.multiple_of(step * LANES, LANES), LANES)
                    half = half_mask((LANES, LANES), side)
                    extras = extra[part, :]
                    value = jnp.where(half, values[part, lanes], extras)
                    return dot(jnp.where(half, keys[part, lanes], extras), query, NT), value

                def highest(step, peak):
                    scores, _ = scores_of(step)
                    return jnp.maximum(peak, jnp.max(scores, axis=0, keepdims=True))

                start = jnp.full((1, query_count), -jnp.inf, f32)
                peak = lax.fori_loop(0, key_count // LANES, highest, start)
                totals[side : side + 1, :] = peak
                sums[side] = jnp.zeros((LANES, query_count), f32)

                def add(step, carry):
                    scores, value = scores_of(step)
                    weights = jnp.exp(scores - totals[side : side + 1, :]).astype(bf16)
                    sums[side] += dot(value, weights, TN)
                    return carry

                lax.fori_loop(0, key_count // LANES, add, 0)

        both = []
        row = lax.broadcasted_iota(jnp.int32, (LANES, query_count), 0)
        small = row & (HALF - 1)
        for side in range(2):
            mixture = sums[side]
            total = mixture[at[side] : at[side] + 1]
            high, middle_part, low = pieces(-(totals[side : side + 1, :] + jnp.log(total)))
            mark = jnp.where(
                small == 0,
                1.0,
                jnp.where(
                    small == 1,
                    high,
                    jnp.where(small == 2, middle_part, jnp.where(small == 3, low, 0.0)),
                ),
            )
            inside = (row < HALF) if side == 0 else (row >= HALF)
            across = jnp.where(inside, mixture / total, mark).T
            marks[2 * pair + side] = jnp.where(
                half_mask(shape, side), query_pair, across.astype(bf16)
            )
            both.append(across)
        chosen = jnp.where(half_mask(shape, 0), both[0], both[1])
        attended[:, lanes] = chosen.astype(bf16)
        return carry

    lax.fori_loop(0, HEADS // 2, body, 0)
    branch = dot(attended[...], out_weight[...]) + out_bias[...].reshape(1, model)
    total = flat(tokens).astype(f32) + branch
    middle[...] = total.reshape(middle.shape)
    normed, _ = normalize(total)
    low = normed * gain[...].reshape(1, model) + bias[...].reshape(1, model)
    normal[...] = low.astype(bf16).reshape(normal.shape)
    core_row, far_row, _, _ = neighbours(rows)
    for task in range(tasks):
        to_core[task, 0] = normal[task, core_row]
        to_far[task, 0] = normal[task, far_row]
    index = lax.broadcasted_iota(jnp.int32, (query_count, 1), 0)
    inside = (me * rows + (index // width) % rows < height) & ((index & (width - 1)) < valid_width)
    square[...] = column_sum(branch * branch * inside.astype(f32))


def put_pieces(grad, first, count, me, keep, send):
    size = grad.shape[0] // PIECES
    for group in range(PIECES):
        piece = grad[group * size : (group + 1) * size]
        slot, owner = divmod(first + group, count)
        store_piece(owner, me, keep, send, slot * size, piece)


def store_piece(owner, me, keep, send, start, piece):
    place = owner ^ me
    size = piece.shape[0]

    @pl.when((place & 1) == 0)
    def _():
        keep[place >> 1, start : start + size, :] = piece

    @pl.when((place & 1) == 1)
    def _():
        send[place >> 1, start : start + size, :] = piece


def feed_kernel(
    heights, widths, middle_normal, from_core, from_far, up_weight, up_bias, taps, down_weight, down_bias,
    cotangent, middle,
    layer_out, grad_band, to_core, to_far, keep, send, grad_taps, grad_up_bias, sums,
    normal, bias_row, wide, grad_act, wide_back, active, grad_lifted, branch, grad_normal,
):
    tasks, rows, width, model = cotangent.shape
    part = up_weight.shape[1]
    step = pl.program_id(0)
    last = pl.num_programs(0) - 1
    me, has_before, has_after = band_flags()
    count = lax.axis_size("rows")
    lines = rows + 2
    _, _, core_line, far_line = neighbours(rows)

    @pl.when(step == 0)
    def _():
        clear_guards(wide)
        clear_guards(wide_back)
        bias_row[0:1, :] = up_bias[...].reshape(1, bias_row.shape[1])
        branch[...] = jnp.zeros_like(branch)
        grad_normal[...] = jnp.zeros_like(grad_normal)
        for task in range(tasks):
            for row in range(rows):
                normal[task, row + 1] = middle_normal[task, row]
            normal[task, core_line] = from_core[task, 0]
            normal[task, far_line] = from_far[task, 0]

    fed = flat(normal)
    here = pl.ds(pl.multiple_of(step * part, part), part)
    lifted = dot(fed, up_weight[...]) + bias_row[0:1, here]
    lifted = lifted.astype(bf16).astype(f32).reshape(tasks, lines, width, part)
    for task in range(tasks):
        for line in range(lines):
            value = lifted[task, line]
            if line == 0:
                value = value * has_before
            if line == lines - 1:
                value = value * has_after
            put_line(wide, task * lines + line, value)
    grad_output = flat(cotangent)
    grad_act[...] = dot(grad_output, down_weight[...], NT).reshape(grad_act.shape)

    c1 = 0.7978845608028654
    c2 = c1 * 0.044715
    blocks = part // LANES

    def across(block, carry):
        lanes = pl.ds(pl.multiple_of(block * LANES, LANES), LANES)
        tap = [[taps[a, b, lanes][None, :] for b in range(3)] for a in range(3)]

        def one_task(task, sums9):
            sums9 = list(sums9)
            for row in range(rows):
                for start in range(0, width, 16):
                    near = []
                    spread = None
                    for a in range(3):
                        for b in range(3):
                            at = GUARD - 1 + b + start
                            value = wide[block, task * lines + row + a, at : at + 16, :]
                            near.append(value)
                            term = tap[a][b] * value
                            spread = term if spread is None else spread + term
                    squared = spread * spread
                    gate = 0.5 + 0.5 * jnp.tanh(spread * (c1 + c2 * squared))
                    active[task * rows + row, start : start + 16, lanes] = (spread * gate).astype(
                        bf16
                    )
                    slope = gate + spread * (gate - gate * gate) * (2 * c1 + 6 * c2 * squared)
                    grad = grad_act[task * rows + row, start : start + 16, lanes] * slope
                    grad = grad.astype(bf16).astype(f32)
                    wide_back[
                        block, task * rows + row, GUARD + start : GUARD + start + 16, :
                    ] = grad
                    for k in range(9):
                        both = near[k] * grad
                        sums9[k] = sums9[k] + (both[0:8] + both[8:16])
            return tuple(sums9)

        sums9 = lax.fori_loop(
            0, tasks, one_task, tuple(jnp.zeros((8, LANES), f32) for _ in range(9))
        )
        for k in range(9):
            grad_taps[k // 3, k % 3, lanes] = jnp.sum(sums9[k], axis=0)

        def back_task(task, total):
            for line in range(lines):
                for start in range(0, width, 16):
                    value = None
                    for a in range(3):
                        if not 0 <= line - a < rows:
                            continue
                        for b in range(3):
                            at = GUARD + 1 - b + start
                            term = tap[a][b] * wide_back[
                                block, task * rows + line - a, at : at + 16, :
                            ]
                            value = term if value is None else value + term
                    if line == 0:
                        value = value * has_before
                    if line == lines - 1:
                        value = value * has_after
                    low = value.astype(bf16)
                    grad_lifted[task * lines + line, start : start + 16, lanes] = low
                    low = low.astype(f32)
                    total = total + (low[0:8] + low[8:16])
            return total

        total = lax.fori_loop(0, tasks, back_task, jnp.zeros((8, LANES), f32))
        per = model // LANES
        inside = pl.ds(pl.multiple_of((block % per) * LANES, LANES), LANES)
        grad_up_bias[block // per, :, inside] = column_sum(total)
        return carry

    lax.fori_loop(0, blocks, across, 0)

    act = flat(active)
    branch[...] += dot(act, down_weight[...])
    grad_down = dot(act, grad_output, TN).astype(bf16)
    grad_low = flat(grad_lifted)
    grad_up = dot(fed, grad_low, TN).astype(bf16)
    grad_normal[...] += dot(grad_low, up_weight[...], NT).reshape(grad_normal.shape)
    size = keep.shape[1] // 2
    groups = model // size
    for sub in range(part // model):
        column = step * (part // model) + sub
        columns = slice(sub * model, (sub + 1) * model)
        for group in range(groups):
            rows_of = slice(group * size, (group + 1) * size)
            store_piece(
                group * (count // groups) + column, me, keep, send, 0, grad_up[rows_of, columns]
            )
    for group in range(part // size):
        rows_of = slice(group * size, (group + 1) * size)
        owner = step * (part // size) + group
        store_piece(owner, me, keep, send, size, grad_down[rows_of])

    @pl.when(step == last)
    def _():
        shift = down_bias[...].reshape(1, model)
        height, valid_width = heights[0], widths[0]
        whole = branch[...].reshape(tasks, rows, width, model)
        first = jnp.zeros((1, model), f32)
        second = jnp.zeros((1, model), f32)
        col = lax.broadcasted_iota(jnp.int32, (width, 1), 0)
        for task in range(tasks):
            for row in range(rows):
                mlp = whole[task, row] + shift
                final = middle[task, row] + mlp
                layer_out[task, row] = final.astype(bf16)
                inside = (col < valid_width) & (me * rows + row < height)
                weight = inside.astype(f32)
                first = first + column_sum(mlp * mlp * weight)
                second = second + column_sum(final * final * weight)
            grad_band[task] = grad_normal[task, 1 : rows + 1]
            to_core[task, 0] = grad_normal[task, core_line].astype(bf16)
            to_far[task, 0] = grad_normal[task, far_line].astype(bf16)
        bias_sum = column_sum(grad_output.astype(f32))
        sums[...] = jnp.concatenate(
            [bias_sum, first, second, jnp.zeros((5, model), f32)], axis=0
        )


def feed(heights, widths, normal, from_core, from_far, up_weight, up_bias, taps, down_weight,
         down_bias, cotangent, middle, count):
    tasks, rows, width, model = cotangent.shape
    hidden = up_weight.shape[1]
    part = FEED_PART * model
    lines = rows + 2
    size = hidden // count
    smem = pl.BlockSpec(memory_space=pltpu.SMEM)

    def whole(shape):
        return pl.BlockSpec(shape, lambda i, k=len(shape): (0,) * k)

    ins = [
        smem, smem, whole(normal.shape), whole(from_core.shape), whole(from_far.shape),
        pl.BlockSpec((model, part), lambda i: (0, i)),
        whole(up_bias.shape),
        pl.BlockSpec((3, 3, part), lambda i: (0, 0, i)),
        pl.BlockSpec((part, model), lambda i: (i, 0)),
        whole(down_bias.shape), whole(cotangent.shape), whole(middle.shape),
    ]
    line_shape = (tasks, 1, width, model)
    outs = [
        (cotangent.shape, bf16), (cotangent.shape, f32), (line_shape, bf16), (line_shape, bf16),
        ((count // 2, 2 * size, model), bf16), ((count // 2, 2 * size, model), bf16),
        ((3, 3, hidden), f32), ((hidden // model, 1, model), f32), ((8, model), f32),
    ]
    out_specs = [whole(s) for s, _ in outs]
    out_specs[6] = pl.BlockSpec((3, 3, part), lambda i: (0, 0, i))
    out_specs[7] = pl.BlockSpec((FEED_PART, 1, model), lambda i: (i, 0, 0))
    return pl.pallas_call(
        feed_kernel,
        name="feed",
        grid=(hidden // part,),
        out_shape=tuple(jax.ShapeDtypeStruct(s, d) for s, d in outs),
        in_specs=ins,
        out_specs=tuple(out_specs),
        scratch_shapes=[
            pltpu.VMEM((tasks, lines, width, model), bf16),
            pltpu.VMEM((8, hidden), f32),
            wide_scratch(tasks * lines, width, part),
            pltpu.VMEM((tasks * rows, width, part), f32),
            wide_scratch(tasks * rows, width, part),
            pltpu.VMEM((tasks * rows, width, part), bf16),
            pltpu.VMEM((tasks * lines, width, part), bf16),
            pltpu.VMEM((tasks * rows * width, model), f32),
            pltpu.VMEM((tasks, lines, width, model), f32),
        ],
        compiler_params=pltpu.CompilerParams(
            vmem_limit_bytes=36 << 20, dimension_semantics=("arbitrary",)
        ),
        cost_estimate=cost(33),
    )(heights, widths, normal, from_core, from_far, up_weight, up_bias, taps, down_weight, down_bias,
      cotangent, middle)


def norm_back_kernel(
    grad_band, from_core, from_far, middle, cotangent, gain, out_weight, attended,
    grad_middle, grad_marks, grad_out, sums,
):
    tasks, rows, width, model = cotangent.shape
    scale = gain[...].reshape(1, model)
    parts = []
    odd = (lax.axis_index("rows") & 1).astype(f32)
    for task in range(tasks):
        core = from_core[task, 0].astype(f32)
        far = from_far[task, 0].astype(f32)
        for row in range(rows):
            grad = grad_band[task, row]
            if row == 0:
                grad = grad + core * odd + far * (1.0 - odd)
            if row == rows - 1:
                grad = grad + far * odd + core * (1.0 - odd)
            parts.append(grad)
    grad_input = jnp.concatenate(parts, axis=0)
    normed, inverse = normalize(flat(middle))
    total = flat(cotangent).astype(f32) + normalize_back(grad_input, scale, normed, inverse)
    grad_middle[...] = total.reshape(grad_middle.shape)
    sums[0:1, :] = column_sum(grad_input * normed)
    sums[1:2, :] = column_sum(grad_input)
    sums[2:3, :] = column_sum(total)
    sums[3:8, :] = jnp.zeros((5, model), f32)
    grad_branch = total.astype(bf16)
    mixture = attended[...]
    grad_out[...] = dot(mixture, grad_branch, TN).astype(bf16)
    grad_attended = dot(grad_branch, out_weight[...], NT).astype(bf16)
    shape = (mixture.shape[0], LANES)
    for pair in range(HEADS // 2):
        lanes = slice(pair * LANES, (pair + 1) * LANES)
        grad_two = grad_attended[:, lanes]
        both = grad_two.astype(f32) * mixture[:, lanes].astype(f32)
        for side in range(2):
            half = half_mask(shape, side)
            inner = jnp.sum(jnp.where(half, both, 0.0), axis=-1, keepdims=True)
            grad_marks[2 * pair + side] = jnp.where(half, grad_two, marked(0.0, -inner, shape))


def attend_back_kernel(
    marks, grad_marks, keys, values, extra, grad_queries, grad_keys, grad_values,
    total, query_zero, grad_zero,
):
    key_count = keys.shape[0]
    query_count = grad_marks.shape[1]
    block = min(1024, key_count)
    shape = (query_count, LANES)
    for side in range(2):
        half = half_mask(shape, side)
        zero = jnp.zeros(shape, bf16)
        part = slice(side * query_count, (side + 1) * query_count)
        query_zero[part, :] = jnp.where(half, marks[side], zero)
        grad_zero[part, :] = jnp.where(half, grad_marks[side], zero)

    def body(place, carry):
        part = pl.ds(pl.multiple_of(place * block, block), block)
        key_pair, value_pair, extras = keys[part, :], values[part, :], extra[part, :]
        lows, grads = [], []
        query_part = None
        for side in range(2):
            half = half_mask((block, LANES), side)
            scores = dot(jnp.where(half, key_pair, extras), marks[side], NT)
            grad_prob = dot(jnp.where(half, value_pair, extras), grad_marks[side], NT)
            probability = jnp.exp(scores)
            grad = (probability * grad_prob).astype(bf16)
            grads.append(grad)
            lows.append(probability.astype(bf16))
            one = dot(jnp.where(half, key_pair, jnp.zeros((block, LANES), bf16)), grad, TN)
            query_part = one if query_part is None else query_part + one
        grad_values[part, :] = dot(jnp.concatenate(lows, axis=1), grad_zero[...]).astype(bf16)
        grad_keys[part, :] = dot(jnp.concatenate(grads, axis=1), query_zero[...]).astype(bf16)

        @pl.when(place == 0)
        def _():
            total[...] = query_part

        @pl.when(place > 0)
        def _():
            total[...] += query_part

        return carry

    lax.fori_loop(0, key_count // block, body, 0)
    grad_queries[...] = (total[...] * HALF**-0.5).T.astype(bf16)


def side_by_side(refs):
    return jnp.concatenate([ref[...] for ref in refs], axis=1)


def conv_back_kernel(*refs):
    pairs = HEADS // 2
    grad_queries = refs[:pairs]
    query_weight, grad_conv, to_core, to_far = refs[pairs:]
    tasks, rows = grad_conv.shape[:2]
    grad = dot(side_by_side(grad_queries), query_weight[...], NT).astype(bf16)
    grad_conv[...] = grad.reshape(grad_conv.shape)
    core_row, far_row, _, _ = neighbours(rows)
    for task in range(tasks):
        to_core[task, 0] = grad_conv[task, core_row]
        to_far[task, 0] = grad_conv[task, far_row]


def pool_back_kernel(order, *refs):
    pairs = HEADS // 2
    grad_keys, grad_values = refs[:pairs], refs[pairs : 2 * pairs]
    key_weight, value_weight, keep, send = refs[2 * pairs :]
    cells = keep.shape[1]
    both = jnp.concatenate([key_weight[...], value_weight[...]], axis=1)
    for position, offset in enumerate(order):
        part = slice(position * cells, (position + 1) * cells)
        grads = jnp.concatenate([ref[part, :] for ref in (*grad_keys, *grad_values)], axis=1)
        target = send if offset & 1 else keep
        target[offset >> 1] = dot(grads, both, NT).astype(bf16)


def pair_weights(order, pooled, conv, queries, keys, values):
    cells = pooled[0].shape[0]
    total = None
    for position in range(len(order)):
        part = slice(position * cells, (position + 1) * cells)
        grads = jnp.concatenate([ref[part, :] for ref in (*keys, *values)], axis=1)
        value = dot(pooled[position][...], grads, TN)
        total = value if total is None else total + value
    grad_query = dot(flat(conv), side_by_side(queries), TN)
    return jnp.concatenate([grad_query, total], axis=1).astype(bf16)


def weight_kernel(order, *refs):
    refs = list(refs)
    heights, widths = refs[:2]
    del refs[:2]
    pooled = refs[: len(order)]
    del refs[: len(order)]
    pairs = HEADS // 2
    queries, keys, values = refs[:pairs], refs[pairs : 2 * pairs], refs[2 * pairs : 3 * pairs]
    del refs[: 3 * pairs]
    (pool_keep, pool_send, conv, extended, grad_conv, taps, gain, bias, grad_out, square, back_sums,
     feed_sums, hidden_taps, up_bias, keep, send, wide, rows_of) = refs
    tasks, rows, width, model = grad_conv.shape
    count = len(order)
    lines = rows + 2
    me, has_before, has_after = band_flags()
    size = keep.shape[1] - 16
    model_grads = pair_weights(order, pooled, conv, queries, keys, values)
    for which in range(3):
        grad = model_grads[:, which * model : (which + 1) * model]
        put_pieces(grad, which * PIECES, count, me, keep, send)
    put_pieces(grad_out[...], 3 * PIECES, count, me, keep, send)
    pool_sum = jnp.zeros((1, model), f32)
    pool_dot = jnp.zeros((1, model), f32)
    for position, offset in enumerate(order):
        source = pool_send if offset & 1 else pool_keep
        grad = source[offset >> 1].astype(f32)
        pool_sum = pool_sum + column_sum(grad)
        pool_dot = pool_dot + column_sum(grad * pooled[position][...].astype(f32))

    clear_guards(wide)
    for task in range(tasks):
        for line in range(lines):
            put_line(wide, task * lines + line, extended[task, line].astype(f32))

    def across(block, carry):
        lanes = pl.ds(pl.multiple_of(block * LANES, LANES), LANES)

        def one_task(task, sums9):
            sums9 = list(sums9)
            for row in range(rows):
                for start in range(0, width, 16):
                    grad = grad_conv[task, row, start : start + 16, lanes].astype(f32)
                    for k in range(9):
                        at = GUARD - 1 + k % 3 + start
                        both = grad * wide[block, task * lines + row + k // 3, at : at + 16, :]
                        sums9[k] = sums9[k] + (both[0:8] + both[8:16])
            return tuple(sums9)

        sums9 = lax.fori_loop(
            0, tasks, one_task, tuple(jnp.zeros((8, LANES), f32) for _ in range(9))
        )
        for k in range(9):
            rows_of[2 + k : 3 + k, lanes] = column_sum(sums9[k])
        return carry

    lax.fori_loop(0, model // LANES, across, 0)

    shift = bias[...].reshape(1, model)
    zero = jnp.zeros((1, model), f32)
    conv_dot, conv_sum = zero, zero
    for row in range(rows):
        line = grad_conv[0, row].astype(f32)
        for task in range(1, tasks):
            line = line + grad_conv[task, row].astype(f32)
        full = column_sum(line)
        by_col = (full - line[0:1], full, full - line[width - 1 : width])
        for a in range(3):
            for b in range(3):
                value = by_col[b]
                if a == 0 and row == 0:
                    value = value * has_before
                if a == 2 and row == rows - 1:
                    value = value * has_after
                conv_sum = conv_sum + taps[a, b].reshape(1, model) * value
    for k in range(9):
        conv_dot = conv_dot + taps[k // 3, k % 3].reshape(1, model) * rows_of[2 + k : 3 + k, :]
    grad_bias = conv_sum + pool_sum
    grad_gain = (conv_dot + pool_dot - shift * grad_bias) / gain[...].reshape(1, model)
    rows_of[0:1, :] = grad_gain
    rows_of[1:2, :] = grad_bias
    rows_of[11:12, :] = back_sums[2:3, :]
    rows_of[12:14, :] = back_sums[0:2, :]
    rows_of[14:15, :] = feed_sums[0:1, :]
    rows_of[15:16, :] = square[...]
    rows_of[16:18, :] = feed_sums[1:3, :]
    in_rows = jnp.clip(heights[0] - me * rows, 0, rows)
    in_cols = jnp.clip(widths[0], 0, width)
    cells_in = (tasks * in_rows * in_cols).astype(f32)
    rows_of[18:19, :] = jnp.full((1, model), cells_in, f32)
    parts = up_bias.shape[0]
    for part in range(parts):
        rows_of[19 + part : 20 + part, :] = up_bias[part]
        for k in range(9):
            rows_of[19 + parts * (k + 1) + part : 20 + parts * (k + 1) + part, :] = hidden_taps[
                k // 3, k % 3, part * model : (part + 1) * model
            ].reshape(1, model)
    used = 19 + 10 * parts
    rows_of[used:SMALL, :] = jnp.zeros((SMALL - used, model), f32)
    group = SMALL // count
    for owner in range(count):
        value = rows_of[owner * group : (owner + 1) * group, :]
        if group < 8:
            value = jnp.concatenate([value, jnp.zeros((8 - group, model), f32)], axis=0)
        high = value.astype(bf16)
        low = (value - high.astype(f32)).astype(bf16)
        store_piece(owner, me, keep, send, size, jnp.concatenate([high, low], axis=0))


def last_kernel(
    grad_conv, from_core, from_far, taps, tokens, gain, grad_middle, pool, input_grad, wide
):
    tasks, rows, width, model = tokens.shape
    lines = rows + 2
    pooled_rows = rows // 2
    clear_guards(wide)
    _, _, core_line, far_line = neighbours(rows)
    for task in range(tasks):
        put_line(wide, task * lines + core_line, from_core[task, 0].astype(f32))
        put_line(wide, task * lines + far_line, from_far[task, 0].astype(f32) * far_weight())
        for row in range(rows):
            put_line(wide, task * lines + row + 1, grad_conv[task, row].astype(f32))
    pooled = pool[...].reshape(tasks, pooled_rows, width // 2, model)
    spread_matrix = pool_matrix(width)[:, 0:width]

    def body(step, carry):
        task = step // (model // LANES)
        block = step % (model // LANES)
        lanes = pl.ds(pl.multiple_of(block * LANES, LANES), LANES)
        for row in range(rows):
            for start in range(0, width, 16):
                total = jnp.zeros((16, LANES), f32)
                for a in range(3):
                    for b in range(3):
                        at = GUARD + 1 - b + start
                        total = total + taps[a, b, lanes][None, :] * wide[
                            block, task * lines + row + 2 - a, at : at + 16, :
                        ]
                input_grad[task, row, start : start + 16, lanes] = total
        return carry

    lax.fori_loop(0, tasks * (model // LANES), body, 0)
    scale = gain[...].reshape(1, model)
    for task in range(tasks):
        for row in range(rows):
            grad = input_grad[task, row] + dot(spread_matrix, pooled[task, row // 2], TN)
            normed, inverse = normalize(tokens[task, row].astype(f32))
            input_grad[task, row] = grad_middle[task, row] + normalize_back(grad, scale, normed, inverse)


def add_blocks(values):
    total = values[0].astype(f32)
    for other in values[1:]:
        total = total + other.astype(f32)
    return total


def put_sum(out, start, values, small):
    total = add_blocks(values)
    size = total.shape[0]
    if not small:
        out[start : start + size, :] = total.astype(bf16)
        return
    size -= 16
    value = total[size : size + 8] + total[size + 8 : size + 16]
    high = value.astype(bf16)
    low = (value - high.astype(f32)).astype(bf16)
    out[start : start + size, :] = total[0:size].astype(bf16)
    out[start + size : start + size + 16, :] = jnp.concatenate([high, low], axis=0)


def combine(arrays, small):
    blocks, size, model = arrays[0].shape

    def kernel(*refs):
        ins, outs = refs[: len(arrays)], refs[len(arrays) :]
        for block, out in enumerate(outs):
            put_sum(out, 0, [x[block] for x in ins], small)

    return call("combine", kernel, [((size, model), bf16)] * blocks, list(arrays))


def stack(values):
    size, model = values[0].shape

    def kernel(*refs):
        for place, value in enumerate(refs[:-1]):
            refs[-1][place] = value[...]

    return call("stack", kernel, [((len(values), size, model), bf16)], list(values))[0]


def exchange(value, axis, mask):
    count = lax.axis_size(axis)
    return lax.ppermute(value, axis, [(i, i ^ mask) for i in range(count)])


def far_masks():
    return list(range(2, lax.axis_size("rows"), 2))


def once(value, *earlier):
    return lax.optimization_barrier((value, earlier))[0]


def far_rows(value):
    return [exchange(value, "rows", mask) for mask in far_masks()]


def all_images(value):
    return [exchange(value, "batch", mask) for mask in range(1, lax.axis_size("batch"))]


def add_images(own, arrived, small):
    (total,) = combine([x[None] for x in [own, *arrived]], small)
    return total


def unpack_feed_kernel(count, *refs):
    even, odd, grad_up, grad_down = refs
    blocks = [half.at[place] for half in (even, odd) for place in range(count // 2)]
    me = lax.axis_index("rows")
    model, hidden = grad_up.shape
    size = hidden // count
    columns = hidden // model
    for j in range(count):
        owner = blocks_owner(j, count, me)
        block = blocks[j]
        up = block[0:size, :].astype(f32)
        place = owner // columns
        col = owner % columns
        grad_up[
            pl.ds(pl.multiple_of(place * size, size), size),
            pl.ds(pl.multiple_of(col * model, model), model),
        ] = up
        grad_down[pl.ds(pl.multiple_of(owner * size, size), size), :] = block[
            size : 2 * size, :
        ].astype(f32)


def blocks_owner(j, count, me):
    half = count // 2
    offset = 2 * j if j < half else 2 * (j - half) + 1
    return me ^ offset


def unpack_late_kernel(count, *refs):
    blocks = refs[:count]
    (grad_query, grad_key, grad_value, grad_out, norm1_gain, norm1_bias, query_taps, out_bias,
     norm2_gain, norm2_bias, up_bias, hidden_taps, down_bias, stats, weights, rows_of) = refs[count:]
    me = lax.axis_index("rows")
    model = grad_query.shape[0]
    piece = model // PIECES
    size = blocks[0].shape[0] - 16
    group = SMALL // count
    for j in range(count):
        owner = blocks_owner(j, count, me)
        block = blocks[j][...].astype(f32)
        for slot in range(size // piece):
            start = pl.multiple_of((slot * count + owner) * piece, piece)
            weights[pl.ds(start, piece), :] = block[slot * piece : (slot + 1) * piece]
        rows_of[owner] = block[size : size + 8] + block[size + 8 : size + 16]
    for which, out in enumerate((grad_query, grad_key, grad_value, grad_out)):
        out[...] = weights[which * model : (which + 1) * model, :]

    def line(k):
        return rows_of[k // group, k % group, :]

    norm1_gain[...] = line(0)
    norm1_bias[...] = line(1)
    for k in range(9):
        query_taps[k // 3, k % 3, :] = line(2 + k)
    out_bias[...] = line(11)
    norm2_gain[...] = line(12)
    norm2_bias[...] = line(13)
    down_bias[...] = line(14)
    parts = up_bias.shape[0] // model
    for part in range(parts):
        lanes = slice(part * model, (part + 1) * model)
        up_bias[lanes] = line(19 + part)
        for k in range(9):
            hidden_taps[k // 3, k % 3, lanes] = line(19 + parts * (k + 1) + part)
    cells = line(18).reshape(1, model)[:, 0:1]
    row = lax.broadcasted_iota(jnp.int32, (1, LANES), 1)
    value = jnp.zeros((1, LANES), f32)
    for k in range(3):
        total = jnp.sum(line(15 + k).reshape(1, model), axis=-1, keepdims=True)
        value = jnp.where(row == k, jnp.sqrt(total / (cells * model)), value)
    stats[...] = value.reshape(LANES)[0:3]


def local(
    tokens,
    norm1_gain,
    norm1_bias,
    query_taps,
    query_weight,
    key_weight,
    value_weight,
    out_weight,
    out_bias,
    norm2_gain,
    norm2_bias,
    up_weight,
    up_bias,
    hidden_taps,
    down_weight,
    down_bias,
    cotangent,
    heights,
    widths,
):
    shape = tokens.shape
    tokens, cotangent = tokens[0], cotangent[0]
    tasks, rows, width, model = tokens.shape
    hidden = up_weight.shape[1]
    count = lax.axis_size("rows")
    cells = tasks * (rows // 2) * (width // 2)
    key_count = count * cells
    lines = rows + 2
    token_count = tasks * rows * width
    line = (tasks, 1, width, model)

    def swap_lines(lines_out):
        to_core, to_far = lines_out
        across = [p for i in range(1, count, 2) for p in ((i, (i + 1) % count), ((i + 1) % count, i))]
        return exchange(to_core, "rows", 1), lax.ppermute(to_far, "rows", across)

    normal_one, pooled = call(
        "first_norm",
        first_norm_kernel,
        [(tokens.shape, bf16), ((cells, model), bf16)],
        [hbm(x) for x in (tokens, norm1_gain, norm1_bias)],
        limit=8,
    )
    far = far_masks()
    order = [0, 1, *far, *[mask + 1 for mask in far]]
    arrived = far_rows(pooled)
    edge = call("edge", edge_kernel, [(line, bf16), (line, bf16)], [normal_one])
    edge = swap_lines(edge)
    swapped = exchange(pooled, "rows", 1)
    extended, conv, queries = call(
        "query_conv",
        query_kernel,
        [
            in_hbm((tasks, lines, width, model), bf16), in_hbm(tokens.shape, bf16),
            ((token_count, model), bf16),
        ],
        [normal_one, *edge, hbm(query_taps), hbm(query_weight)],
        scratch=[wide_scratch(tasks * lines, width, model)],
        us=2,
        limit=12,
    )
    arrived = once(arrived, queries)
    blocks = [pooled, swapped, *arrived, *[exchange(x, "rows", 1) for x in arrived]]

    (keys, values, extra, attended, middle, normal_two, to_core, to_far, marks, square) = call(
        "attend",
        lambda *refs: attend_kernel(order, *refs),
        [
            ((key_count, model), bf16), ((key_count, model), bf16), in_hbm((key_count, LANES), bf16),
            in_hbm((token_count, model), bf16), in_hbm(tokens.shape, f32),
            in_hbm(tokens.shape, bf16), (line, bf16), (line, bf16), in_hbm((HEADS, token_count, LANES), bf16), ((1, model), f32),
        ],
        [heights, widths, *blocks, hbm(key_weight), hbm(value_weight), queries,
         *[hbm(x) for x in (tokens, out_weight, out_bias, norm2_gain, norm2_bias)]],
        smem=2,
        scratch=[pltpu.VMEM((2, LANES, token_count), f32), pltpu.VMEM((8, token_count), f32)],
        us=18,
        limit=24,
    )
    (layer_out, grad_band, to_core, to_far, feed_keep, feed_send, grad_hidden_taps,
     grad_up_bias, feed_sums) = feed(
        heights, widths, hbm(normal_two), *swap_lines((to_core, to_far)), hbm(up_weight),
        *[hbm(x) for x in (up_bias, hidden_taps, down_weight, down_bias, cotangent, middle)], count,
    )
    edge = swap_lines((to_core, to_far))
    feed_swapped = exchange(feed_send, "rows", 1)
    feed_blocks = combine(once([feed_keep, feed_swapped], edge), False)
    feed_arrived = [exchange(feed_blocks[mask >> 1], "rows", mask) for mask in far]
    piece = model // PIECES
    grad_middle, grad_marks, grad_out, back_sums = call(
        "norm_back",
        norm_back_kernel,
        [
            (tokens.shape, f32), ((HEADS, token_count, LANES), bf16), ((model, model), bf16),
            ((8, model), f32),
        ],
        [
            once(grad_band, feed_blocks), *edge,
            *[hbm(x) for x in (middle, cotangent, norm2_gain, out_weight, attended)],
        ],
        us=4,
        limit=24,
    )

    def attend_back(pair, tie):
        inputs = [marks, grad_marks, keys, values, extra]
        inputs = once(inputs, *tie)

        def of_heads(x):
            return pl.BlockSpec((2, x.shape[1], LANES), lambda i: (pair, 0, 0))

        def of_lanes(x):
            return pl.BlockSpec((x.shape[0], LANES), lambda i: (0, pair))

        whole = pl.BlockSpec((key_count, LANES), lambda i: (0, 0))
        outs = [(token_count, LANES), (key_count, LANES), (key_count, LANES)]
        return pl.pallas_call(
            attend_back_kernel,
            name="attend_back",
            grid=(1,),
            out_shape=[jax.ShapeDtypeStruct(shape, bf16) for shape in outs],
            in_specs=[*[of_heads(x) for x in inputs[0:2]], *[of_lanes(x) for x in inputs[2:4]], whole],
            out_specs=[pl.BlockSpec(shape, lambda i: (0, 0)) for shape in outs],
            scratch_shapes=[
                pltpu.VMEM((LANES, token_count), f32),
                pltpu.VMEM((2 * token_count, LANES), bf16),
                pltpu.VMEM((2 * token_count, LANES), bf16),
            ],
            compiler_params=pltpu.CompilerParams(vmem_limit_bytes=20 << 20),
            cost_estimate=cost(11),
        )(*inputs)

    back = [attend_back(0, [])]
    feed_arrived = once(feed_arrived, *back[0])
    feed_own = add_images(feed_blocks[0], feed_arrived, False)
    hop = 1
    while hop < lax.axis_size("batch"):
        feed_arrived = exchange(feed_own, "batch", hop)
        if len(back) < HEADS // 2:
            back.append(attend_back(len(back), [*back[-1], feed_own]))
        feed_arrived = once(feed_arrived, *back[-1])
        feed_own = add_images(feed_own, [feed_arrived], False)
        hop *= 2
    while len(back) < HEADS // 2:
        back.append(attend_back(len(back), back[-1]))
    grads = [part for which in range(3) for part in [x[which] for x in back]]
    pairs = HEADS // 2
    grad_conv, *edge = call(
        "conv_back",
        conv_back_kernel,
        [(tokens.shape, bf16), (line, bf16), (line, bf16)],
        [*once(grads[:pairs], feed_own), query_weight],
    )
    feed_arrived = far_rows(feed_own)
    edge = swap_lines(edge)
    pool_keep, pool_send = call(
        "pool_back",
        lambda *refs: pool_back_kernel(order, *refs),
        [((count // 2, cells, model), bf16)] * 2,
        [*once(grads[pairs:], grad_conv), key_weight, value_weight],
        us=3,
        limit=12,
    )
    slots = -(-4 * PIECES // count)
    keep, send = call(
        "weights",
        lambda *refs: weight_kernel(order, *refs),
        [((count // 2, slots * piece + 16, model), bf16)] * 2,
        [
            heights, widths, *blocks, *grads, pool_keep, pool_send, conv, extended, grad_conv,
            query_taps, norm1_gain, norm1_bias, grad_out, square, back_sums, feed_sums,
            grad_hidden_taps, grad_up_bias,
        ],
        smem=2,
        scratch=[
            wide_scratch(tasks * lines, width, model),
            pltpu.VMEM((SMALL, model), f32),
        ],
        us=4,
        limit=16,
    )
    feed_arrived, edge = once((feed_arrived, edge), keep)
    send, pool_send = once((send, pool_send), feed_arrived, edge)
    late_swapped = exchange(send, "rows", 1)
    pool_swapped = exchange(pool_send, "rows", 1)
    late_blocks = combine([keep, late_swapped], True)
    late_arrived = [exchange(late_blocks[mask >> 1], "rows", mask) for mask in far]
    pool_blocks = combine([pool_keep, once(pool_swapped, late_blocks)], False)
    feed_even = stack(once([feed_own, *feed_arrived], pool_blocks))
    feed_odd = exchange(feed_even, "rows", 1)
    late_arrived = once(late_arrived, feed_even)
    (late_own,) = combine([x[None] for x in [late_blocks[0], *late_arrived]], True)
    pool_arrived = [exchange(x, "rows", mask) for x, mask in zip(once(pool_blocks[1:], late_own), far)]
    arrived = exchange(late_own, "batch", 1)
    grad_up, grad_down = call(
        "unpack_feed",
        lambda *refs: unpack_feed_kernel(count, *refs),
        [((model, hidden), f32), ((hidden, model), f32)],
        [once(feed_even, late_own), feed_odd],
        us=3,
        limit=12,
    )
    arrived = once(arrived, grad_up)
    hop = 2
    while hop < lax.axis_size("batch"):
        late_own = add_images(late_own, [arrived], True)
        arrived = exchange(late_own, "batch", hop)
        hop *= 2
    pool_arrived = once(pool_arrived, late_own)
    (pool_total,) = combine([x[None] for x in [pool_blocks[0], *pool_arrived]], False)
    (input_grad,) = call(
        "last_norm",
        last_kernel,
        [(tokens.shape, f32)],
        [grad_conv, *edge, query_taps, tokens, norm1_gain, grad_middle, pool_total],
        scratch=[wide_scratch(tasks * lines, width, model)],
        us=5,
        limit=12,
    )
    late_own = add_images(late_own, [once(arrived, input_grad)], True)
    even = [late_own, *far_rows(late_own)]
    odd = [exchange(x, "rows", 1) for x in even]
    vector = ((model,), f32)
    late = call(
        "unpack_late",
        lambda *refs: unpack_late_kernel(count, *refs),
        [((model, model), f32)] * 4
        + [vector, vector, ((3, 3, model), f32), vector, vector, vector, ((hidden,), f32),
           ((3, 3, hidden), f32), vector, ((3,), f32)],
        [*even, *odd],
        scratch=[
            pltpu.VMEM((slots * count * piece, model), f32),
            pltpu.VMEM((count, 8, model), f32),
        ],
        us=2,
        limit=12,
    )
    (grad_query, grad_key, grad_value, grad_out, gain1, bias1, taps1, out_sum, gain2, bias2, up_sum,
     taps2, down_sum, stats) = late
    return (
        layer_out.reshape(shape),
        input_grad.reshape(shape),
        gain1,
        bias1,
        taps1,
        grad_query,
        grad_key,
        grad_value,
        grad_out,
        out_sum,
        gain2,
        bias2,
        grad_up,
        up_sum,
        taps2,
        grad_down,
        down_sum,
        stats,
    )


def solution(mesh):
    band = P("batch", None, "rows", None, None)
    placed = (band, *[P()] * 15, band, P("batch"), P("batch"))
    return jax.shard_map(
        local,
        mesh=mesh,
        in_specs=placed,
        out_specs=(band, band, *[P()] * 16),
        check_vma=False,
    )
```

```python
import jax
import jax.numpy as jnp
from jax import lax
from jax.experimental import pallas as pl
from jax.experimental.pallas import tpu as pltpu
from jax.sharding import PartitionSpec as P

HEADS = 6
LANES = 128
HALF = 64
GUARD = 8
SMALL = 64
PIECES = 8
epsilon = 1e-05
f32 = jnp.float32
bf16 = jnp.bfloat16
NN = (((1,), (0,)), ((), ()))
NT = (((1,), (1,)), ((), ()))
TN = (((0,), (0,)), ((), ()))


def dot(left, right, form=NN):
    return lax.dot_general(left, right, form, preferred_element_type=f32)


def cost(us):
    return pl.CostEstimate(flops=int(us * 1e4), bytes_accessed=int(us * 1e4), transcendentals=0)


def hbm(value):
    return pltpu.with_memory_space_constraint(value, pltpu.HBM)


def in_hbm(shape, dtype):
    return shape, dtype, True


def out_type(shape, dtype, away=False):
    return pltpu.HBM(shape, dtype) if away else jax.ShapeDtypeStruct(shape, dtype)


def call(name, kernel, outs, args, smem=0, scratch=(), us=1, limit=12):
    def whole(shape):
        return pl.BlockSpec(shape, lambda i, k=len(shape): (0,) * k)

    return pl.pallas_call(
        kernel,
        grid=(1,),
        out_shape=tuple(out_type(*x) for x in outs),
        in_specs=[pl.BlockSpec(memory_space=pltpu.SMEM)] * smem
        + [whole(x.shape) for x in args[smem:]],
        out_specs=tuple(whole(x[0]) for x in outs),
        scratch_shapes=list(scratch),
        name=name,
        compiler_params=pltpu.CompilerParams(vmem_limit_bytes=limit << 20),
        cost_estimate=cost(us),
    )(*args)


def normalize(values):
    center = jnp.mean(values, axis=-1, keepdims=True)
    centered = values - center
    inverse = lax.rsqrt(jnp.mean(centered * centered, axis=-1, keepdims=True) + epsilon)
    return centered * inverse, inverse


def normalize_back(grad_output, gain, normed, inverse):
    scaled = grad_output * gain
    return inverse * (
        scaled
        - jnp.mean(scaled, axis=-1, keepdims=True)
        - normed * jnp.mean(scaled * normed, axis=-1, keepdims=True)
    )


def column_sum(values):
    return jnp.sum(values, axis=0, keepdims=True)


def flat(ref):
    value = ref[...]
    return value.reshape(-1, value.shape[-1])


def band_flags():
    me = lax.axis_index("rows")
    count = lax.axis_size("rows")
    return me, (me > 0).astype(f32), (me < count - 1).astype(f32)


def neighbours(rows):
    odd = lax.axis_index("rows") & 1
    even = 1 - odd
    return even * (rows - 1), odd * (rows - 1), even * (rows + 1), odd * (rows + 1)


def far_weight():
    me, has_before, has_after = band_flags()
    return jnp.where((me & 1) == 1, has_after, has_before)


def pool_matrix(width):
    rows = lax.broadcasted_iota(jnp.int32, (width // 2, 2 * width), 0)
    cols = lax.broadcasted_iota(jnp.int32, (width // 2, 2 * width), 1)
    cols = jnp.where(cols >= width, cols - width, cols)
    return jnp.where((cols >> 1) == rows, 0.25, 0.0).astype(bf16)


def first_norm_kernel(tokens, gain, bias, normal, pooled):
    tasks, rows, width, model = tokens.shape
    matrix = pool_matrix(width)
    scale = gain[...].reshape(1, model)
    shift = bias[...].reshape(1, model)
    for task in range(tasks):
        for row in range(0, rows, 2):
            value = tokens[task, row : row + 2].astype(f32).reshape(2 * width, model)
            low = (normalize(value)[0] * scale + shift).astype(bf16)
            normal[task, row : row + 2] = low.reshape(2, width, model)
            start = (task * (rows // 2) + row // 2) * (width // 2)
            pooled[start : start + width // 2, :] = dot(matrix, low).astype(bf16)


def edge_kernel(normal, to_core, to_far):
    tasks, rows = normal.shape[:2]
    core_row, far_row, _, _ = neighbours(rows)
    for task in range(tasks):
        to_core[task, 0] = normal[task, core_row]
        to_far[task, 0] = normal[task, far_row]


def clear_guards(wide):
    blocks, lines, length, lanes = wide.shape
    zero = jnp.zeros((blocks, lines, GUARD, lanes), wide.dtype)
    wide[:, :, 0:GUARD, :] = zero
    wide[:, :, length - GUARD : length, :] = zero


def put_line(wide, line, value):
    for block in range(wide.shape[0]):
        wide[block, line, GUARD : GUARD + value.shape[0], :] = value[
            :, block * LANES : (block + 1) * LANES
        ]


def wide_scratch(lines, width, model):
    return pltpu.VMEM((model // LANES, lines, width + 2 * GUARD, LANES), f32)


def query_kernel(normal, from_core, from_far, taps, weight, extended, conv, queries, wide):
    tasks, rows, width, model = normal.shape
    clear_guards(wide)
    lines = rows + 2
    _, _, core_line, far_line = neighbours(rows)
    for task in range(tasks):
        extended[task, core_line] = from_core[task, 0]
        extended[task, far_line] = (from_far[task, 0].astype(f32) * far_weight()).astype(bf16)
        for row in range(rows):
            extended[task, row + 1] = normal[task, row]
        for line in range(lines):
            put_line(wide, task * lines + line, extended[task, line].astype(f32))

    def body(step, carry):
        task = step // (model // LANES)
        block = step % (model // LANES)
        lanes = pl.ds(pl.multiple_of(block * LANES, LANES), LANES)
        for row in range(rows):
            for start in range(0, width, 16):
                total = jnp.zeros((16, LANES), f32)
                for a in range(3):
                    for b in range(3):
                        at = GUARD - 1 + b + start
                        total = total + taps[a, b, lanes][None, :] * wide[
                            block, task * lines + row + a, at : at + 16, :
                        ]
                conv[task, row, start : start + 16, lanes] = total.astype(bf16)
        return carry

    lax.fori_loop(0, tasks * (model // LANES), body, 0)
    product = dot(flat(conv), weight[...]).astype(bf16)
    scaled = product * jnp.asarray(HALF**-0.5, bf16)
    queries[...] = scaled.reshape(queries.shape)


def half_mask(shape, side):
    lane = lax.broadcasted_iota(jnp.int32, shape, 1)
    return (lane < HALF) if side == 0 else (lane >= HALF)


def small_lane(shape):
    return lax.broadcasted_iota(jnp.int32, shape, 1) & (HALF - 1)


def pieces(value):
    high = value.astype(bf16).astype(f32)
    middle = (value - high).astype(bf16).astype(f32)
    return high, middle, value - high - middle


def marked(lead, value, shape):
    lane = small_lane(shape)
    high, middle, low = pieces(value)
    rest = jnp.where(lane == 1, high, jnp.where(lane == 2, middle, jnp.where(lane == 3, low, 0.0)))
    return jnp.where(lane == 0, lead, rest).astype(bf16)


def attend_kernel(order, *refs):
    refs = list(refs)
    heights, widths = refs[:2]
    del refs[:2]
    pooled = refs[: len(order)]
    del refs[: len(order)]
    (key_weight, value_weight, queries, tokens, out_weight, out_bias, gain, bias,
     keys, values, extra, attended, middle, normal, to_core, to_far, marks, square,
     sums, totals) = refs
    tasks, rows, width, model = tokens.shape
    me = lax.axis_index("rows")
    height, valid_width = heights[0], widths[0]
    cells = pooled[0].shape[0]
    pooled_rows = rows // 2
    for position, offset in enumerate(order):
        part = slice(position * cells, (position + 1) * cells)
        block = pooled[position][...]
        keys[part, :] = dot(block, key_weight[...]).astype(bf16)
        values[part, :] = dot(block, value_weight[...]).astype(bf16)
        cell = lax.broadcasted_iota(jnp.int32, (cells, LANES), 0)
        col = cell & (width // 2 - 1)
        row = (cell // (width // 2)) % pooled_rows + (me ^ offset) * pooled_rows
        good = (2 * row < height) & (2 * col < valid_width)
        lane = small_lane((cells, LANES))
        ones = jnp.where(lane < 4, 1.0, 0.0)
        extra[part, :] = jnp.where(
            lane == 0, jnp.where(good, 0.0, -1e30), ones
        ).astype(bf16)
    query_count = queries.shape[0]
    key_count = keys.shape[0]
    block = min(512, key_count)
    together = min(4, key_count // block)
    steps = key_count // (block * together)

    def body(pair, carry):
        lanes = pl.ds(pl.multiple_of(pair * LANES, LANES), LANES)
        query_pair = queries[:, lanes]
        shape = query_pair.shape
        across = lax.broadcasted_iota(jnp.int32, (LANES, LANES), 0) < HALF
        over = lax.broadcasted_iota(jnp.int32, (LANES, LANES), 1) >= HALF
        swap = jnp.where(across == over, 1.0, 0.0).astype(bf16)
        key_all = keys[:, lanes].astype(f32)
        key_norms = dot((key_all * key_all).astype(bf16), swap)
        largest = jnp.max(key_norms, axis=0, keepdims=True)
        query_all = query_pair.astype(f32)
        query_norms = dot((query_all * query_all).astype(bf16), swap)
        bound = 1.02 * jnp.sqrt(query_norms * largest)
        small = small_lane(shape)
        mark = jnp.where(small == 0, 1.0, jnp.where(small == 1, -bound, 0.0)).astype(bf16)
        bounded = []
        bounds = []
        for side in range(2):
            query = jnp.where(half_mask(shape, side), query_pair, mark)
            bounded.append(query)
            lane = lax.broadcasted_iota(jnp.int32, (8, LANES), 1)
            chosen = jnp.where(lane == (1 - side) * HALF + 1, 1.0, 0.0).astype(bf16)
            bounds.append(-dot(chosen, query, NT)[0:1])

        def some(step, first):
            results = []
            for side in range(2):
                total = None
                for k in range(together):
                    start = pl.multiple_of((step * together + k) * block, block)
                    part = pl.ds(start, block)
                    half = half_mask((block, LANES), side)
                    extras = extra[part, :]
                    scores = dot(jnp.where(half, keys[part, lanes], extras), bounded[side], NT)
                    weights = jnp.exp(scores).astype(bf16)
                    mixture = dot(jnp.where(half, values[part, lanes], extras), weights, TN)
                    total = mixture if total is None else total + mixture
                results.append(total)
            return results

        first = some(0, True)
        for side in range(2):
            sums[side] = first[side]
        if steps > 1:

            def more(step, carry):
                for side, total in enumerate(some(step, False)):
                    sums[side] += total
                return carry

            lax.fori_loop(1, steps, more, 0)
        for side in range(2):
            totals[side : side + 1, :] = bounds[side]
        at = [(1 - side) * HALF + 1 for side in range(2)]
        least = jnp.minimum(
            jnp.min(sums[0, at[0] : at[0] + 1, :]), jnp.min(sums[1, at[1] : at[1] + 1, :])
        )

        @pl.when(jnp.logical_not(least > 1e-25))
        def _():
            lead = jnp.where(small_lane(shape) == 0, 1.0, 0.0).astype(bf16)
            for side in range(2):
                query = jnp.where(half_mask(shape, side), query_pair, lead)

                def scores_of(step):
                    part = pl.ds(pl.multiple_of(step * LANES, LANES), LANES)
                    half = half_mask((LANES, LANES), side)
                    extras = extra[part, :]
                    value = jnp.where(half, values[part, lanes], extras)
                    return dot(jnp.where(half, keys[part, lanes], extras), query, NT), value

                def highest(step, peak):
                    scores, _ = scores_of(step)
                    return jnp.maximum(peak, jnp.max(scores, axis=0, keepdims=True))

                start = jnp.full((1, query_count), -jnp.inf, f32)
                peak = lax.fori_loop(0, key_count // LANES, highest, start)
                totals[side : side + 1, :] = peak
                sums[side] = jnp.zeros((LANES, query_count), f32)

                def add(step, carry):
                    scores, value = scores_of(step)
                    weights = jnp.exp(scores - totals[side : side + 1, :]).astype(bf16)
                    sums[side] += dot(value, weights, TN)
                    return carry

                lax.fori_loop(0, key_count // LANES, add, 0)

        both = []
        row = lax.broadcasted_iota(jnp.int32, (LANES, query_count), 0)
        small = row & (HALF - 1)
        for side in range(2):
            mixture = sums[side]
            total = mixture[at[side] : at[side] + 1]
            high, middle_part, low = pieces(-(totals[side : side + 1, :] + jnp.log(total)))
            mark = jnp.where(
                small == 0,
                1.0,
                jnp.where(
                    small == 1,
                    high,
                    jnp.where(small == 2, middle_part, jnp.where(small == 3, low, 0.0)),
                ),
            )
            inside = (row < HALF) if side == 0 else (row >= HALF)
            across = jnp.where(inside, mixture / total, mark).T
            marks[2 * pair + side] = jnp.where(
                half_mask(shape, side), query_pair, across.astype(bf16)
            )
            both.append(across)
        chosen = jnp.where(half_mask(shape, 0), both[0], both[1])
        attended[:, lanes] = chosen.astype(bf16)
        return carry

    lax.fori_loop(0, HEADS // 2, body, 0)
    branch = dot(attended[...], out_weight[...]) + out_bias[...].reshape(1, model)
    total = flat(tokens).astype(f32) + branch
    middle[...] = total.reshape(middle.shape)
    normed, _ = normalize(total)
    low = normed * gain[...].reshape(1, model) + bias[...].reshape(1, model)
    normal[...] = low.astype(bf16).reshape(normal.shape)
    core_row, far_row, _, _ = neighbours(rows)
    for task in range(tasks):
        to_core[task, 0] = normal[task, core_row]
        to_far[task, 0] = normal[task, far_row]
    index = lax.broadcasted_iota(jnp.int32, (query_count, 1), 0)
    inside = (me * rows + (index // width) % rows < height) & ((index & (width - 1)) < valid_width)
    square[...] = column_sum(branch * branch * inside.astype(f32))


def put_pieces(grad, first, count, me, held):
    size = grad.shape[0] // PIECES
    for group in range(PIECES):
        piece = grad[group * size : (group + 1) * size]
        slot, owner = divmod(first + group, count)
        store_piece(owner, me, held, slot * size, piece)


def store_piece(owner, me, held, start, piece):
    place = owner ^ me
    place = (place & 1) * (held.shape[0] // 2) + (place >> 1)
    held[place, start : start + piece.shape[0], :] = piece


def part_pieces(held, keep, send):
    half = held.shape[0] // 2
    keep[...] = held[0:half]
    send[...] = held[half:]


def feed_in_kernel(normal, cotangent, up_weight, up_bias, down_weight, lifted, grad_act):
    tasks, rows, width, model = cotangent.shape
    hidden = up_weight.shape[1]
    bias = up_bias[...].reshape(1, hidden)
    fed, grad = flat(normal), flat(cotangent)
    for start in range(0, hidden, model):
        lanes = slice(start, start + model)
        value = (dot(fed, up_weight[:, lanes]) + bias[:, lanes]).astype(bf16)
        lifted[:, :, :, lanes] = value.reshape(tasks, rows, width, model)
        value = dot(grad, down_weight[lanes, :], NT).astype(bf16)
        grad_act[:, :, :, lanes] = value.reshape(tasks, rows, width, model)


def feed_kernel(
    from_core, from_far, lifted, grad_act, up_weight, up_bias, taps,
    active, grad_lifted, grad_band, to_core, to_far, grad_taps, grad_up_bias,
    core_lifted, far_lifted, wide, wide_back, grad_normal,
):
    tasks, rows, width, hidden = lifted.shape
    model = up_weight.shape[0]
    _, has_before, has_after = band_flags()
    lines = rows + 2
    _, _, core_line, far_line = neighbours(rows)
    c1 = 0.7978845608028654
    c2 = c1 * 0.044715

    clear_guards(wide)
    clear_guards(wide_back)
    bias = up_bias[...].reshape(1, hidden)
    for source, weight, target in ((from_core, None, core_lifted), (from_far, far_weight(), far_lifted)):
        value = dot(flat(source), up_weight[...]) + bias
        if weight is not None:
            value = value * weight
        target[...] = value.astype(bf16).reshape(target.shape)

    def across(block, carry):
        lanes = pl.ds(pl.multiple_of(block * LANES, LANES), LANES)
        tap = [[taps[a, b, lanes][None, :] for b in range(3)] for a in range(3)]

        def forth(task, sums9):
            sums9 = list(sums9)
            put_line(wide, task * lines + core_line, core_lifted[task, :, lanes].astype(f32))
            put_line(wide, task * lines + far_line, far_lifted[task, :, lanes].astype(f32))
            for row in range(rows):
                put_line(wide, task * lines + row + 1, lifted[task, row, :, lanes].astype(f32))
            for row in range(rows):
                for start in range(0, width, 16):
                    near = []
                    spread = None
                    for a in range(3):
                        for b in range(3):
                            at = GUARD - 1 + b + start
                            value = wide[0, task * lines + row + a, at : at + 16, :]
                            near.append(value)
                            term = tap[a][b] * value
                            spread = term if spread is None else spread + term
                    squared = spread * spread
                    gate = 0.5 + 0.5 * jnp.tanh(spread * (c1 + c2 * squared))
                    active[task, row, start : start + 16, lanes] = (spread * gate).astype(bf16)
                    slope = gate + spread * (gate - gate * gate) * (2 * c1 + 6 * c2 * squared)
                    grad = grad_act[task, row, start : start + 16, lanes].astype(f32) * slope
                    grad = grad.astype(bf16).astype(f32)
                    wide_back[
                        0, task * rows + row, GUARD + start : GUARD + start + 16, :
                    ] = grad
                    for k in range(9):
                        both = near[k] * grad
                        sums9[k] = sums9[k] + (both[0:8] + both[8:16])
            return tuple(sums9)

        zero = jnp.zeros((8, LANES), f32)
        sums9 = lax.fori_loop(0, tasks, forth, (zero,) * 9)
        for k in range(9):
            grad_taps[k // 3, k % 3, lanes] = jnp.sum(sums9[k], axis=0)

        def back(task, total):
            for line in range(lines):
                for start in range(0, width, 16):
                    value = None
                    for a in range(3):
                        if not 0 <= line - a < rows:
                            continue
                        for b in range(3):
                            at = GUARD + 1 - b + start
                            term = tap[a][b] * wide_back[
                                0, task * rows + line - a, at : at + 16, :
                            ]
                            value = term if value is None else value + term
                    if line == 0:
                        value = value * has_before
                    if line == lines - 1:
                        value = value * has_after
                    low = value.astype(bf16)
                    grad_lifted[task, line, start : start + 16, lanes] = low
                    low = low.astype(f32)
                    total = total + (low[0:8] + low[8:16])
            return total

        grad_up_bias[0:1, lanes] = column_sum(lax.fori_loop(0, tasks, back, zero))
        return carry

    lax.fori_loop(0, hidden // LANES, across, 0)
    grad = dot(flat(grad_lifted), up_weight[...], NT)
    grad_normal[...] = grad.reshape(grad_normal.shape)
    for task in range(tasks):
        grad_band[task] = grad_normal[task, 1 : rows + 1]
        to_core[task, 0] = grad_normal[task, core_line].astype(bf16)
        to_far[task, 0] = grad_normal[task, far_line].astype(bf16)


def feed_weight_kernel(
    middle_normal, from_core, from_far, active, grad_lifted, cotangent, keep, send, normal, held
):
    tasks, rows, width, model = cotangent.shape
    hidden = active.shape[-1]
    me = lax.axis_index("rows")
    count = lax.axis_size("rows")
    _, _, core_line, far_line = neighbours(rows)
    for task in range(tasks):
        for row in range(rows):
            normal[task, row + 1] = middle_normal[task, row]
        normal[task, core_line] = from_core[task, 0]
        normal[task, far_line] = from_far[task, 0]
    size = hidden // count
    groups = model // size
    columns = hidden // model
    fed, grad_output = flat(normal), flat(cotangent)
    for column in range(columns):
        lanes = slice(column * model, (column + 1) * model)
        grad = grad_lifted[:, :, :, lanes].reshape(-1, model)
        grad_up = dot(fed, grad, TN).astype(bf16)
        act = active[:, :, :, lanes].reshape(-1, model)
        grad_down = dot(act, grad_output, TN).astype(bf16)
        for group in range(groups):
            part = slice(group * size, (group + 1) * size)
            store_piece(group * columns + column, me, held, 0, grad_up[part])
            store_piece(column * groups + group, me, held, size, grad_down[part])
    part_pieces(held, keep, send)


def layer_kernel(
    heights, widths, active, down_weight, down_bias, cotangent, middle, layer_out, sums
):
    tasks, rows, width, model = cotangent.shape
    me = lax.axis_index("rows")
    height, valid_width = heights[0], widths[0]
    zero = jnp.zeros((1, model), f32)
    totals = [zero, zero, zero]
    col = lax.broadcasted_iota(jnp.int32, (width, 1), 0)
    for task in range(tasks):
        branch = dot(flat(active.at[task]), down_weight[...]) + down_bias[...].reshape(1, model)
        for row in range(rows):
            mlp = branch[row * width : (row + 1) * width]
            final = middle[task, row] + mlp
            layer_out[task, row] = final.astype(bf16)
            inside = (col < valid_width) & (me * rows + row < height)
            weight = inside.astype(f32)
            grad = cotangent[task, row].astype(f32)
            for k, value in enumerate((grad, mlp * mlp * weight, final * final * weight)):
                totals[k] = totals[k] + column_sum(value)
    sums[...] = jnp.concatenate([*totals, jnp.zeros((5, model), f32)], axis=0)


def norm_back_kernel(
    grad_band, from_core, from_far, middle, cotangent, gain, out_weight, attended,
    grad_middle, grad_marks, grad_out, sums,
):
    tasks, rows, width, model = cotangent.shape
    scale = gain[...].reshape(1, model)
    parts = []
    odd = (lax.axis_index("rows") & 1).astype(f32)
    for task in range(tasks):
        core = from_core[task, 0].astype(f32)
        far = from_far[task, 0].astype(f32)
        for row in range(rows):
            grad = grad_band[task, row]
            if row == 0:
                grad = grad + core * odd + far * (1.0 - odd)
            if row == rows - 1:
                grad = grad + far * odd + core * (1.0 - odd)
            parts.append(grad)
    grad_input = jnp.concatenate(parts, axis=0)
    normed, inverse = normalize(flat(middle))
    total = flat(cotangent).astype(f32) + normalize_back(grad_input, scale, normed, inverse)
    grad_middle[...] = total.reshape(grad_middle.shape)
    sums[0:1, :] = column_sum(grad_input * normed)
    sums[1:2, :] = column_sum(grad_input)
    sums[2:3, :] = column_sum(total)
    sums[3:8, :] = jnp.zeros((5, model), f32)
    grad_branch = total.astype(bf16)
    mixture = attended[...]
    grad_out[...] = dot(mixture, grad_branch, TN).astype(bf16)
    grad_attended = dot(grad_branch, out_weight[...], NT).astype(bf16)
    shape = (mixture.shape[0], LANES)
    for pair in range(HEADS // 2):
        lanes = slice(pair * LANES, (pair + 1) * LANES)
        grad_two = grad_attended[:, lanes]
        both = grad_two.astype(f32) * mixture[:, lanes].astype(f32)
        for side in range(2):
            half = half_mask(shape, side)
            inner = jnp.sum(jnp.where(half, both, 0.0), axis=-1, keepdims=True)
            grad_marks[2 * pair + side] = jnp.where(half, grad_two, marked(0.0, -inner, shape))


def attend_back_kernel(
    marks, grad_marks, keys, values, extra, grad_queries, grad_keys, grad_values,
    total, query_zero, grad_zero,
):
    key_count = keys.shape[0]
    query_count = grad_marks.shape[1]
    block = min(1024, key_count)
    shape = (query_count, LANES)
    for side in range(2):
        half = half_mask(shape, side)
        zero = jnp.zeros(shape, bf16)
        part = slice(side * query_count, (side + 1) * query_count)
        query_zero[part, :] = jnp.where(half, marks[side], zero)
        grad_zero[part, :] = jnp.where(half, grad_marks[side], zero)

    def body(place, carry):
        part = pl.ds(pl.multiple_of(place * block, block), block)
        key_pair, value_pair, extras = keys[part, :], values[part, :], extra[part, :]
        lows, grads = [], []
        query_part = None
        for side in range(2):
            half = half_mask((block, LANES), side)
            scores = dot(jnp.where(half, key_pair, extras), marks[side], NT)
            grad_prob = dot(jnp.where(half, value_pair, extras), grad_marks[side], NT)
            probability = jnp.exp(scores)
            grad = (probability * grad_prob).astype(bf16)
            grads.append(grad)
            lows.append(probability.astype(bf16))
            one = dot(jnp.where(half, key_pair, jnp.zeros((block, LANES), bf16)), grad, TN)
            query_part = one if query_part is None else query_part + one
        grad_values[part, :] = dot(jnp.concatenate(lows, axis=1), grad_zero[...]).astype(bf16)
        grad_keys[part, :] = dot(jnp.concatenate(grads, axis=1), query_zero[...]).astype(bf16)

        @pl.when(place == 0)
        def _():
            total[...] = query_part

        @pl.when(place > 0)
        def _():
            total[...] += query_part

        return carry

    lax.fori_loop(0, key_count // block, body, 0)
    grad_queries[...] = (total[...] * HALF**-0.5).T.astype(bf16)


def side_by_side(refs):
    return jnp.concatenate([ref[...] for ref in refs], axis=1)


def conv_back_kernel(*refs):
    pairs = HEADS // 2
    grad_queries = refs[:pairs]
    query_weight, grad_conv, to_core, to_far = refs[pairs:]
    tasks, rows = grad_conv.shape[:2]
    grad = dot(side_by_side(grad_queries), query_weight[...], NT).astype(bf16)
    grad_conv[...] = grad.reshape(grad_conv.shape)
    core_row, far_row, _, _ = neighbours(rows)
    for task in range(tasks):
        to_core[task, 0] = grad_conv[task, core_row]
        to_far[task, 0] = grad_conv[task, far_row]


def pool_back_kernel(order, *refs):
    pairs = HEADS // 2
    grad_keys, grad_values = refs[:pairs], refs[pairs : 2 * pairs]
    key_weight, value_weight, keep, send = refs[2 * pairs :]
    cells = keep.shape[1]
    both = jnp.concatenate([key_weight[...], value_weight[...]], axis=1)
    for position, offset in enumerate(order):
        part = slice(position * cells, (position + 1) * cells)
        grads = jnp.concatenate([ref[part, :] for ref in (*grad_keys, *grad_values)], axis=1)
        target = send if offset & 1 else keep
        target[offset >> 1] = dot(grads, both, NT).astype(bf16)


def pair_weights(order, pooled, conv, queries, keys, values):
    cells = pooled[0].shape[0]
    total = None
    for position in range(len(order)):
        part = slice(position * cells, (position + 1) * cells)
        grads = jnp.concatenate([ref[part, :] for ref in (*keys, *values)], axis=1)
        value = dot(pooled[position][...], grads, TN)
        total = value if total is None else total + value
    grad_query = dot(flat(conv), side_by_side(queries), TN)
    return jnp.concatenate([grad_query, total], axis=1).astype(bf16)


def weight_kernel(order, *refs):
    refs = list(refs)
    heights, widths = refs[:2]
    del refs[:2]
    pooled = refs[: len(order)]
    del refs[: len(order)]
    pairs = HEADS // 2
    queries, keys, values = refs[:pairs], refs[pairs : 2 * pairs], refs[2 * pairs : 3 * pairs]
    del refs[: 3 * pairs]
    (pool_keep, pool_send, conv, extended, grad_conv, taps, gain, bias, grad_out, square, back_sums,
     feed_sums, hidden_taps, up_bias, keep, send, wide, rows_of, held) = refs
    tasks, rows, width, model = grad_conv.shape
    count = len(order)
    lines = rows + 2
    me, has_before, has_after = band_flags()
    size = keep.shape[1] - 16
    model_grads = pair_weights(order, pooled, conv, queries, keys, values)
    for which in range(3):
        grad = model_grads[:, which * model : (which + 1) * model]
        put_pieces(grad, which * PIECES, count, me, held)
    put_pieces(grad_out[...], 3 * PIECES, count, me, held)
    pool_sum = jnp.zeros((1, model), f32)
    pool_dot = jnp.zeros((1, model), f32)
    for position, offset in enumerate(order):
        source = pool_send if offset & 1 else pool_keep
        grad = source[offset >> 1].astype(f32)
        pool_sum = pool_sum + column_sum(grad)
        pool_dot = pool_dot + column_sum(grad * pooled[position][...].astype(f32))

    clear_guards(wide)
    for task in range(tasks):
        for line in range(lines):
            put_line(wide, task * lines + line, extended[task, line].astype(f32))

    def across(block, carry):
        lanes = pl.ds(pl.multiple_of(block * LANES, LANES), LANES)

        def one_task(task, sums9):
            sums9 = list(sums9)
            for row in range(rows):
                for start in range(0, width, 16):
                    grad = grad_conv[task, row, start : start + 16, lanes].astype(f32)
                    for k in range(9):
                        at = GUARD - 1 + k % 3 + start
                        both = grad * wide[block, task * lines + row + k // 3, at : at + 16, :]
                        sums9[k] = sums9[k] + (both[0:8] + both[8:16])
            return tuple(sums9)

        sums9 = lax.fori_loop(
            0, tasks, one_task, tuple(jnp.zeros((8, LANES), f32) for _ in range(9))
        )
        for k in range(9):
            rows_of[2 + k : 3 + k, lanes] = column_sum(sums9[k])
        return carry

    lax.fori_loop(0, model // LANES, across, 0)

    shift = bias[...].reshape(1, model)
    zero = jnp.zeros((1, model), f32)
    conv_dot, conv_sum = zero, zero
    for row in range(rows):
        line = grad_conv[0, row].astype(f32)
        for task in range(1, tasks):
            line = line + grad_conv[task, row].astype(f32)
        full = column_sum(line)
        by_col = (full - line[0:1], full, full - line[width - 1 : width])
        for a in range(3):
            for b in range(3):
                value = by_col[b]
                if a == 0 and row == 0:
                    value = value * has_before
                if a == 2 and row == rows - 1:
                    value = value * has_after
                conv_sum = conv_sum + taps[a, b].reshape(1, model) * value
    for k in range(9):
        conv_dot = conv_dot + taps[k // 3, k % 3].reshape(1, model) * rows_of[2 + k : 3 + k, :]
    grad_bias = conv_sum + pool_sum
    grad_gain = (conv_dot + pool_dot - shift * grad_bias) / gain[...].reshape(1, model)
    rows_of[0:1, :] = grad_gain
    rows_of[1:2, :] = grad_bias
    rows_of[11:12, :] = back_sums[2:3, :]
    rows_of[12:14, :] = back_sums[0:2, :]
    rows_of[14:15, :] = feed_sums[0:1, :]
    rows_of[15:16, :] = square[...]
    rows_of[16:18, :] = feed_sums[1:3, :]
    in_rows = jnp.clip(heights[0] - me * rows, 0, rows)
    in_cols = jnp.clip(widths[0], 0, width)
    cells_in = (tasks * in_rows * in_cols).astype(f32)
    rows_of[18:19, :] = jnp.full((1, model), cells_in, f32)
    parts = up_bias.shape[1] // model
    for part in range(parts):
        rows_of[19 + part : 20 + part, :] = up_bias[:, part * model : (part + 1) * model]
        for k in range(9):
            rows_of[19 + parts * (k + 1) + part : 20 + parts * (k + 1) + part, :] = hidden_taps[
                k // 3, k % 3, part * model : (part + 1) * model
            ].reshape(1, model)
    used = 19 + 10 * parts
    rows_of[used:SMALL, :] = jnp.zeros((SMALL - used, model), f32)
    group = SMALL // count
    for owner in range(count):
        value = rows_of[owner * group : (owner + 1) * group, :]
        if group < 8:
            value = jnp.concatenate([value, jnp.zeros((8 - group, model), f32)], axis=0)
        high = value.astype(bf16)
        low = (value - high.astype(f32)).astype(bf16)
        store_piece(owner, me, held, size, jnp.concatenate([high, low], axis=0))
    part_pieces(held, keep, send)


def last_kernel(
    grad_conv, from_core, from_far, taps, tokens, gain, grad_middle, pool, input_grad, wide
):
    tasks, rows, width, model = tokens.shape
    lines = rows + 2
    pooled_rows = rows // 2
    clear_guards(wide)
    _, _, core_line, far_line = neighbours(rows)
    for task in range(tasks):
        put_line(wide, task * lines + core_line, from_core[task, 0].astype(f32))
        put_line(wide, task * lines + far_line, from_far[task, 0].astype(f32) * far_weight())
        for row in range(rows):
            put_line(wide, task * lines + row + 1, grad_conv[task, row].astype(f32))
    pooled = pool[...].reshape(tasks, pooled_rows, width // 2, model)
    spread_matrix = pool_matrix(width)[:, 0:width]

    def body(step, carry):
        task = step // (model // LANES)
        block = step % (model // LANES)
        lanes = pl.ds(pl.multiple_of(block * LANES, LANES), LANES)
        for row in range(rows):
            for start in range(0, width, 16):
                total = jnp.zeros((16, LANES), f32)
                for a in range(3):
                    for b in range(3):
                        at = GUARD + 1 - b + start
                        total = total + taps[a, b, lanes][None, :] * wide[
                            block, task * lines + row + 2 - a, at : at + 16, :
                        ]
                input_grad[task, row, start : start + 16, lanes] = total
        return carry

    lax.fori_loop(0, tasks * (model // LANES), body, 0)
    scale = gain[...].reshape(1, model)
    for task in range(tasks):
        for row in range(rows):
            grad = input_grad[task, row] + dot(spread_matrix, pooled[task, row // 2], TN)
            normed, inverse = normalize(tokens[task, row].astype(f32))
            input_grad[task, row] = grad_middle[task, row] + normalize_back(grad, scale, normed, inverse)


def add_blocks(values):
    total = values[0].astype(f32)
    for other in values[1:]:
        total = total + other.astype(f32)
    return total


def put_sum(out, start, values, small):
    total = add_blocks(values)
    size = total.shape[0]
    if not small:
        out[start : start + size, :] = total.astype(bf16)
        return
    size -= 16
    value = total[size : size + 8] + total[size + 8 : size + 16]
    high = value.astype(bf16)
    low = (value - high.astype(f32)).astype(bf16)
    out[start : start + size, :] = total[0:size].astype(bf16)
    out[start + size : start + size + 16, :] = jnp.concatenate([high, low], axis=0)


def combine(arrays, small):
    blocks, size, model = arrays[0].shape

    def kernel(*refs):
        ins, outs = refs[: len(arrays)], refs[len(arrays) :]
        for block, out in enumerate(outs):
            put_sum(out, 0, [x[block] for x in ins], small)

    return call("combine", kernel, [((size, model), bf16)] * blocks, list(arrays))


def stack(values):
    size, model = values[0].shape

    def kernel(*refs):
        for place, value in enumerate(refs[:-1]):
            refs[-1][place] = value[...]

    return call("stack", kernel, [((len(values), size, model), bf16)], list(values))[0]


def exchange(value, axis, mask):
    count = lax.axis_size(axis)
    return lax.ppermute(value, axis, [(i, i ^ mask) for i in range(count)])


def far_masks():
    return list(range(2, lax.axis_size("rows"), 2))


def once(value, *earlier):
    return lax.optimization_barrier((value, earlier))[0]


def far_rows(value):
    return [exchange(value, "rows", mask) for mask in far_masks()]


def all_images(value):
    return [exchange(value, "batch", mask) for mask in range(1, lax.axis_size("batch"))]


def add_images(own, arrived, small):
    (total,) = combine([x[None] for x in [own, *arrived]], small)
    return total


def unpack_feed_kernel(count, *refs):
    even, odd, grad_up, grad_down = refs
    blocks = [half.at[place] for half in (even, odd) for place in range(count // 2)]
    me = lax.axis_index("rows")
    model, hidden = grad_up.shape
    size = hidden // count
    columns = hidden // model
    for j in range(count):
        owner = blocks_owner(j, count, me)
        block = blocks[j]
        up = block[0:size, :].astype(f32)
        place = owner // columns
        col = owner % columns
        grad_up[
            pl.ds(pl.multiple_of(place * size, size), size),
            pl.ds(pl.multiple_of(col * model, model), model),
        ] = up
        grad_down[pl.ds(pl.multiple_of(owner * size, size), size), :] = block[
            size : 2 * size, :
        ].astype(f32)


def blocks_owner(j, count, me):
    half = count // 2
    offset = 2 * j if j < half else 2 * (j - half) + 1
    return me ^ offset


def unpack_late_kernel(count, *refs):
    blocks = refs[:count]
    (grad_query, grad_key, grad_value, grad_out, norm1_gain, norm1_bias, query_taps, out_bias,
     norm2_gain, norm2_bias, up_bias, hidden_taps, down_bias, stats, weights, rows_of) = refs[count:]
    me = lax.axis_index("rows")
    model = grad_query.shape[0]
    piece = model // PIECES
    size = blocks[0].shape[0] - 16
    group = SMALL // count
    for j in range(count):
        owner = blocks_owner(j, count, me)
        block = blocks[j][...].astype(f32)
        for slot in range(size // piece):
            start = pl.multiple_of((slot * count + owner) * piece, piece)
            weights[pl.ds(start, piece), :] = block[slot * piece : (slot + 1) * piece]
        rows_of[owner] = block[size : size + 8] + block[size + 8 : size + 16]
    for which, out in enumerate((grad_query, grad_key, grad_value, grad_out)):
        out[...] = weights[which * model : (which + 1) * model, :]

    def line(k):
        return rows_of[k // group, k % group, :]

    norm1_gain[...] = line(0)
    norm1_bias[...] = line(1)
    for k in range(9):
        query_taps[k // 3, k % 3, :] = line(2 + k)
    out_bias[...] = line(11)
    norm2_gain[...] = line(12)
    norm2_bias[...] = line(13)
    down_bias[...] = line(14)
    parts = up_bias.shape[0] // model
    for part in range(parts):
        lanes = slice(part * model, (part + 1) * model)
        up_bias[lanes] = line(19 + part)
        for k in range(9):
            hidden_taps[k // 3, k % 3, lanes] = line(19 + parts * (k + 1) + part)
    cells = line(18).reshape(1, model)[:, 0:1]
    row = lax.broadcasted_iota(jnp.int32, (1, LANES), 1)
    value = jnp.zeros((1, LANES), f32)
    for k in range(3):
        total = jnp.sum(line(15 + k).reshape(1, model), axis=-1, keepdims=True)
        value = jnp.where(row == k, jnp.sqrt(total / (cells * model)), value)
    stats[...] = value.reshape(LANES)[0:3]


def local(
    tokens,
    norm1_gain,
    norm1_bias,
    query_taps,
    query_weight,
    key_weight,
    value_weight,
    out_weight,
    out_bias,
    norm2_gain,
    norm2_bias,
    up_weight,
    up_bias,
    hidden_taps,
    down_weight,
    down_bias,
    cotangent,
    heights,
    widths,
):
    shape = tokens.shape
    tokens, cotangent = tokens[0], cotangent[0]
    tasks, rows, width, model = tokens.shape
    hidden = up_weight.shape[1]
    count = lax.axis_size("rows")
    cells = tasks * (rows // 2) * (width // 2)
    key_count = count * cells
    lines = rows + 2
    token_count = tasks * rows * width
    line = (tasks, 1, width, model)

    def swap_lines(lines_out):
        to_core, to_far = lines_out
        across = [p for i in range(1, count, 2) for p in ((i, (i + 1) % count), ((i + 1) % count, i))]
        return exchange(to_core, "rows", 1), lax.ppermute(to_far, "rows", across)

    normal_one, pooled = call(
        "first_norm",
        first_norm_kernel,
        [(tokens.shape, bf16), ((cells, model), bf16)],
        [hbm(x) for x in (tokens, norm1_gain, norm1_bias)],
        limit=8,
    )
    far = far_masks()
    order = [0, 1, *far, *[mask + 1 for mask in far]]
    arrived = far_rows(pooled)
    edge = call("edge", edge_kernel, [(line, bf16), (line, bf16)], [normal_one])
    edge = swap_lines(edge)
    swapped = exchange(pooled, "rows", 1)
    extended, conv, queries = call(
        "query_conv",
        query_kernel,
        [
            in_hbm((tasks, lines, width, model), bf16), in_hbm(tokens.shape, bf16),
            ((token_count, model), bf16),
        ],
        [normal_one, *edge, hbm(query_taps), hbm(query_weight)],
        scratch=[wide_scratch(tasks * lines, width, model)],
        us=2,
        limit=12,
    )
    arrived = once(arrived, queries)
    blocks = [pooled, swapped, *arrived, *[exchange(x, "rows", 1) for x in arrived]]

    (keys, values, extra, attended, middle, normal_two, to_core, to_far, marks, square) = call(
        "attend",
        lambda *refs: attend_kernel(order, *refs),
        [
            ((key_count, model), bf16), ((key_count, model), bf16), in_hbm((key_count, LANES), bf16),
            in_hbm((token_count, model), bf16), in_hbm(tokens.shape, f32),
            (tokens.shape, bf16), (line, bf16), (line, bf16), in_hbm((HEADS, token_count, LANES), bf16), ((1, model), f32),
        ],
        [heights, widths, *blocks, hbm(key_weight), hbm(value_weight), queries,
         *[hbm(x) for x in (tokens, out_weight, out_bias, norm2_gain, norm2_bias)]],
        smem=2,
        scratch=[pltpu.VMEM((2, LANES, token_count), f32), pltpu.VMEM((8, token_count), f32)],
        us=18,
        limit=24,
    )
    next_lines = swap_lines((to_core, to_far))
    band = (tasks, rows, width, hidden)
    lifted, grad_act = call(
        "feed_in",
        feed_in_kernel,
        [(band, bf16), (band, bf16)],
        [normal_two, *[hbm(x) for x in (cotangent, up_weight, up_bias, down_weight)]],
        us=4,
        limit=28,
    )
    next_lines = once(next_lines, grad_act)
    (active, grad_lifted, grad_band, to_core, to_far, grad_hidden_taps, grad_up_bias) = call(
        "feed",
        feed_kernel,
        [
            (band, bf16), ((tasks, lines, width, hidden), bf16), (tokens.shape, f32), (line, bf16),
            (line, bf16), ((3, 3, hidden), f32), ((1, hidden), f32),
        ],
        [*next_lines, lifted, grad_act, *[hbm(x) for x in (up_weight, up_bias, hidden_taps)]],
        scratch=[
            pltpu.VMEM((tasks, width, hidden), bf16),
            pltpu.VMEM((tasks, width, hidden), bf16),
            wide_scratch(tasks * lines, width, LANES),
            wide_scratch(tasks * rows, width, LANES),
            pltpu.VMEM((tasks, lines, width, model), f32),
        ],
        us=24,
        limit=32,
    )
    edge = swap_lines((to_core, to_far))
    feed_keep, feed_send = call(
        "feed_weights",
        feed_weight_kernel,
        [((count // 2, 2 * hidden // count, model), bf16)] * 2,
        [normal_two, *next_lines, active, grad_lifted, hbm(cotangent)],
        scratch=[
            pltpu.VMEM((tasks, lines, width, model), bf16),
            pltpu.VMEM((count, 2 * hidden // count, model), bf16),
        ],
        us=5,
        limit=32,
    )
    edge = once(edge, feed_keep)
    feed_swapped = exchange(once(feed_send, edge), "rows", 1)
    feed_blocks = combine(once([feed_keep, feed_swapped], edge), False)
    feed_arrived = [exchange(feed_blocks[mask >> 1], "rows", mask) for mask in far]
    piece = model // PIECES
    grad_middle, grad_marks, grad_out, back_sums = call(
        "norm_back",
        norm_back_kernel,
        [
            (tokens.shape, f32), ((HEADS, token_count, LANES), bf16), ((model, model), bf16),
            ((8, model), f32),
        ],
        [
            once(grad_band, feed_blocks), *edge,
            *[hbm(x) for x in (middle, cotangent, norm2_gain, out_weight, attended)],
        ],
        us=4,
        limit=24,
    )

    def attend_back(pair, tie):
        inputs = [marks, grad_marks, keys, values, extra]
        inputs = once(inputs, *tie)

        def of_heads(x):
            return pl.BlockSpec((2, x.shape[1], LANES), lambda i: (pair, 0, 0))

        def of_lanes(x):
            return pl.BlockSpec((x.shape[0], LANES), lambda i: (0, pair))

        whole = pl.BlockSpec((key_count, LANES), lambda i: (0, 0))
        outs = [(token_count, LANES), (key_count, LANES), (key_count, LANES)]
        return pl.pallas_call(
            attend_back_kernel,
            name="attend_back",
            grid=(1,),
            out_shape=[jax.ShapeDtypeStruct(shape, bf16) for shape in outs],
            in_specs=[*[of_heads(x) for x in inputs[0:2]], *[of_lanes(x) for x in inputs[2:4]], whole],
            out_specs=[pl.BlockSpec(shape, lambda i: (0, 0)) for shape in outs],
            scratch_shapes=[
                pltpu.VMEM((LANES, token_count), f32),
                pltpu.VMEM((2 * token_count, LANES), bf16),
                pltpu.VMEM((2 * token_count, LANES), bf16),
            ],
            compiler_params=pltpu.CompilerParams(vmem_limit_bytes=20 << 20),
            cost_estimate=cost(11),
        )(*inputs)

    back = [attend_back(0, [])]
    feed_arrived = once(feed_arrived, *back[0])
    feed_own = add_images(feed_blocks[0], feed_arrived, False)
    hop = 1
    while hop < lax.axis_size("batch"):
        feed_arrived = exchange(feed_own, "batch", hop)
        if len(back) < HEADS // 2:
            back.append(attend_back(len(back), [*back[-1], feed_own]))
        feed_arrived = once(feed_arrived, *back[-1])
        feed_own = add_images(feed_own, [feed_arrived], False)
        hop *= 2
    while len(back) < HEADS // 2:
        back.append(attend_back(len(back), back[-1]))
    grads = [part for which in range(3) for part in [x[which] for x in back]]
    pairs = HEADS // 2
    grad_conv, *edge = call(
        "conv_back",
        conv_back_kernel,
        [(tokens.shape, bf16), (line, bf16), (line, bf16)],
        [*once(grads[:pairs], feed_own), query_weight],
    )
    feed_arrived = far_rows(feed_own)
    edge = swap_lines(edge)
    pool_keep, pool_send = call(
        "pool_back",
        lambda *refs: pool_back_kernel(order, *refs),
        [((count // 2, cells, model), bf16)] * 2,
        [*once(grads[pairs:], grad_conv), key_weight, value_weight],
        us=3,
        limit=12,
    )
    layer_out, feed_sums = call(
        "layer",
        layer_kernel,
        [(tokens.shape, bf16), ((8, model), f32)],
        [heights, widths, once(active, pool_keep), *[hbm(x) for x in (down_weight, down_bias, cotangent, middle)]],
        smem=2,
        us=3,
        limit=20,
    )
    slots = -(-4 * PIECES // count)
    keep, send = call(
        "weights",
        lambda *refs: weight_kernel(order, *refs),
        [((count // 2, slots * piece + 16, model), bf16)] * 2,
        [
            heights, widths, *blocks, *grads, pool_keep, pool_send, conv, extended, grad_conv,
            query_taps, norm1_gain, norm1_bias, grad_out, square, back_sums, feed_sums,
            grad_hidden_taps, grad_up_bias,
        ],
        smem=2,
        scratch=[
            wide_scratch(tasks * lines, width, model),
            pltpu.VMEM((SMALL, model), f32),
            pltpu.VMEM((count, slots * piece + 16, model), bf16),
        ],
        us=4,
        limit=16,
    )
    feed_arrived, edge = once((feed_arrived, edge), keep)
    send, pool_send = once((send, pool_send), feed_arrived, edge)
    late_swapped = exchange(send, "rows", 1)
    pool_swapped = exchange(pool_send, "rows", 1)
    late_blocks = combine([keep, late_swapped], True)
    late_arrived = [exchange(late_blocks[mask >> 1], "rows", mask) for mask in far]
    pool_blocks = combine([pool_keep, once(pool_swapped, late_blocks)], False)
    feed_even = stack(once([feed_own, *feed_arrived], pool_blocks))
    feed_odd = exchange(feed_even, "rows", 1)
    late_arrived = once(late_arrived, feed_even)
    (late_own,) = combine([x[None] for x in [late_blocks[0], *late_arrived]], True)
    pool_arrived = [exchange(x, "rows", mask) for x, mask in zip(once(pool_blocks[1:], late_own), far)]
    arrived = exchange(late_own, "batch", 1)
    grad_up, grad_down = call(
        "unpack_feed",
        lambda *refs: unpack_feed_kernel(count, *refs),
        [((model, hidden), f32), ((hidden, model), f32)],
        [once(feed_even, late_own), feed_odd],
        us=3,
        limit=12,
    )
    arrived = once(arrived, grad_up)
    hop = 2
    while hop < lax.axis_size("batch"):
        late_own = add_images(late_own, [arrived], True)
        arrived = exchange(late_own, "batch", hop)
        hop *= 2
    pool_arrived = once(pool_arrived, late_own)
    (pool_total,) = combine([x[None] for x in [pool_blocks[0], *pool_arrived]], False)
    (input_grad,) = call(
        "last_norm",
        last_kernel,
        [(tokens.shape, f32)],
        [grad_conv, *edge, query_taps, tokens, norm1_gain, grad_middle, pool_total],
        scratch=[wide_scratch(tasks * lines, width, model)],
        us=5,
        limit=12,
    )
    late_own = add_images(late_own, [once(arrived, input_grad)], True)
    even = [late_own, *far_rows(late_own)]
    odd = [exchange(x, "rows", 1) for x in even]
    vector = ((model,), f32)
    late = call(
        "unpack_late",
        lambda *refs: unpack_late_kernel(count, *refs),
        [((model, model), f32)] * 4
        + [vector, vector, ((3, 3, model), f32), vector, vector, vector, ((hidden,), f32),
           ((3, 3, hidden), f32), vector, ((3,), f32)],
        [*even, *odd],
        scratch=[
            pltpu.VMEM((slots * count * piece, model), f32),
            pltpu.VMEM((count, 8, model), f32),
        ],
        us=2,
        limit=12,
    )
    (grad_query, grad_key, grad_value, grad_out, gain1, bias1, taps1, out_sum, gain2, bias2, up_sum,
     taps2, down_sum, stats) = late
    return (
        layer_out.reshape(shape),
        input_grad.reshape(shape),
        gain1,
        bias1,
        taps1,
        grad_query,
        grad_key,
        grad_value,
        grad_out,
        out_sum,
        gain2,
        bias2,
        grad_up,
        up_sum,
        taps2,
        grad_down,
        down_sum,
        stats,
    )


def solution(mesh):
    band = P("batch", None, "rows", None, None)
    placed = (band, *[P()] * 15, band, P("batch"), P("batch"))
    return jax.shard_map(
        local,
        mesh=mesh,
        in_specs=placed,
        out_specs=(band, band, *[P()] * 16),
        check_vma=False,
    )
```

```python
import jax
import jax.numpy as jnp
from jax import lax
from jax.experimental import pallas as pl
from jax.experimental.pallas import tpu as pltpu
from jax.sharding import PartitionSpec as P

HEADS = 6
LANES = 128
HALF = 64
GUARD = 8
SMALL = 64
PIECES = 8
epsilon = 1e-05
f32 = jnp.float32
bf16 = jnp.bfloat16
NN = (((1,), (0,)), ((), ()))
NT = (((1,), (1,)), ((), ()))
TN = (((0,), (0,)), ((), ()))


def dot(left, right, form=NN):
    return lax.dot_general(left, right, form, preferred_element_type=f32)


def cost(us):
    return pl.CostEstimate(flops=int(us * 1e4), bytes_accessed=int(us * 1e4), transcendentals=0)


def hbm(value):
    return pltpu.with_memory_space_constraint(value, pltpu.HBM)


def in_hbm(shape, dtype):
    return shape, dtype, True


def out_type(shape, dtype, away=False):
    return pltpu.HBM(shape, dtype) if away else jax.ShapeDtypeStruct(shape, dtype)


def call(name, kernel, outs, args, smem=0, scratch=(), us=1, limit=12):
    def whole(shape):
        return pl.BlockSpec(shape, lambda i, k=len(shape): (0,) * k)

    return pl.pallas_call(
        kernel,
        grid=(1,),
        out_shape=tuple(out_type(*x) for x in outs),
        in_specs=[pl.BlockSpec(memory_space=pltpu.SMEM)] * smem
        + [whole(x.shape) for x in args[smem:]],
        out_specs=tuple(whole(x[0]) for x in outs),
        scratch_shapes=list(scratch),
        name=name,
        compiler_params=pltpu.CompilerParams(vmem_limit_bytes=limit << 20),
        cost_estimate=cost(us),
    )(*args)


def normalize(values):
    center = jnp.mean(values, axis=-1, keepdims=True)
    centered = values - center
    inverse = lax.rsqrt(jnp.mean(centered * centered, axis=-1, keepdims=True) + epsilon)
    return centered * inverse, inverse


def normalize_back(grad_output, gain, normed, inverse):
    scaled = grad_output * gain
    return inverse * (
        scaled
        - jnp.mean(scaled, axis=-1, keepdims=True)
        - normed * jnp.mean(scaled * normed, axis=-1, keepdims=True)
    )


def column_sum(values):
    return jnp.sum(values, axis=0, keepdims=True)


def flat(ref):
    value = ref[...]
    return value.reshape(-1, value.shape[-1])


def band_flags():
    me = lax.axis_index("rows")
    count = lax.axis_size("rows")
    return me, (me > 0).astype(f32), (me < count - 1).astype(f32)


def neighbours(rows):
    odd = lax.axis_index("rows") & 1
    even = 1 - odd
    return even * (rows - 1), odd * (rows - 1), even * (rows + 1), odd * (rows + 1)


def far_weight():
    me, has_before, has_after = band_flags()
    return jnp.where((me & 1) == 1, has_after, has_before)


def pool_matrix(width):
    rows = lax.broadcasted_iota(jnp.int32, (width // 2, 2 * width), 0)
    cols = lax.broadcasted_iota(jnp.int32, (width // 2, 2 * width), 1)
    cols = jnp.where(cols >= width, cols - width, cols)
    return jnp.where((cols >> 1) == rows, 0.25, 0.0).astype(bf16)


def first_norm_kernel(tokens, gain, bias, normal, pooled):
    tasks, rows, width, model = tokens.shape
    matrix = pool_matrix(width)
    scale = gain[...].reshape(1, model)
    shift = bias[...].reshape(1, model)
    for task in range(tasks):
        for row in range(0, rows, 2):
            value = tokens[task, row : row + 2].astype(f32).reshape(2 * width, model)
            low = (normalize(value)[0] * scale + shift).astype(bf16)
            normal[task, row : row + 2] = low.reshape(2, width, model)
            start = (task * (rows // 2) + row // 2) * (width // 2)
            pooled[start : start + width // 2, :] = dot(matrix, low).astype(bf16)


def edge_kernel(normal, to_core, to_far):
    tasks, rows = normal.shape[:2]
    core_row, far_row, _, _ = neighbours(rows)
    for task in range(tasks):
        to_core[task, 0] = normal[task, core_row]
        to_far[task, 0] = normal[task, far_row]


def clear_guards(wide):
    blocks, lines, length, lanes = wide.shape
    zero = jnp.zeros((blocks, lines, GUARD, lanes), wide.dtype)
    wide[:, :, 0:GUARD, :] = zero
    wide[:, :, length - GUARD : length, :] = zero


def put_line(wide, line, value):
    for block in range(wide.shape[0]):
        wide[block, line, GUARD : GUARD + value.shape[0], :] = value[
            :, block * LANES : (block + 1) * LANES
        ]


def wide_scratch(lines, width, model):
    return pltpu.VMEM((model // LANES, lines, width + 2 * GUARD, LANES), f32)


def query_kernel(normal, from_core, from_far, taps, weight, extended, conv, queries, wide):
    tasks, rows, width, model = normal.shape
    clear_guards(wide)
    lines = rows + 2
    _, _, core_line, far_line = neighbours(rows)
    for task in range(tasks):
        extended[task, core_line] = from_core[task, 0]
        extended[task, far_line] = (from_far[task, 0].astype(f32) * far_weight()).astype(bf16)
        for row in range(rows):
            extended[task, row + 1] = normal[task, row]
        for line in range(lines):
            put_line(wide, task * lines + line, extended[task, line].astype(f32))

    def body(step, carry):
        task = step // (model // LANES)
        block = step % (model // LANES)
        lanes = pl.ds(pl.multiple_of(block * LANES, LANES), LANES)
        for row in range(rows):
            for start in range(0, width, 16):
                total = jnp.zeros((16, LANES), f32)
                for a in range(3):
                    for b in range(3):
                        at = GUARD - 1 + b + start
                        total = total + taps[a, b, lanes][None, :] * wide[
                            block, task * lines + row + a, at : at + 16, :
                        ]
                conv[task, row, start : start + 16, lanes] = total.astype(bf16)
        return carry

    lax.fori_loop(0, tasks * (model // LANES), body, 0)
    product = dot(flat(conv), weight[...]).astype(bf16)
    scaled = product * jnp.asarray(HALF**-0.5, bf16)
    queries[...] = scaled.reshape(queries.shape)


def half_mask(shape, side):
    lane = lax.broadcasted_iota(jnp.int32, shape, 1)
    return (lane < HALF) if side == 0 else (lane >= HALF)


def small_lane(shape):
    return lax.broadcasted_iota(jnp.int32, shape, 1) & (HALF - 1)


def pieces(value):
    high = value.astype(bf16).astype(f32)
    middle = (value - high).astype(bf16).astype(f32)
    return high, middle, value - high - middle


def marked(lead, value, shape):
    lane = small_lane(shape)
    high, middle, low = pieces(value)
    rest = jnp.where(lane == 1, high, jnp.where(lane == 2, middle, jnp.where(lane == 3, low, 0.0)))
    return jnp.where(lane == 0, lead, rest).astype(bf16)


def project(offsets, blocks, start, shape, height, valid_width, weights, targets):
    rows, width = shape
    pooled_rows = rows // 2
    me = lax.axis_index("rows")
    key_weight, value_weight = weights
    keys, values, extra = targets
    cells = blocks[0].shape[0]
    for position, offset in enumerate(offsets):
        part = slice(start + position * cells, start + (position + 1) * cells)
        block = blocks[position][...]
        keys[part, :] = dot(block, key_weight[...]).astype(bf16)
        values[part, :] = dot(block, value_weight[...]).astype(bf16)
        cell = lax.broadcasted_iota(jnp.int32, (cells, LANES), 0)
        col = cell & (width // 2 - 1)
        row = (cell // (width // 2)) % pooled_rows + (me ^ offset) * pooled_rows
        good = (2 * row < height) & (2 * col < valid_width)
        lane = small_lane((cells, LANES))
        ones = jnp.where(lane < 4, 1.0, 0.0)
        extra[part, :] = jnp.where(lane == 0, jnp.where(good, 0.0, -1e30), ones).astype(bf16)


def bound_scores(query_pair, key_pair, known):
    shape = query_pair.shape
    across = lax.broadcasted_iota(jnp.int32, (LANES, LANES), 0) < HALF
    over = lax.broadcasted_iota(jnp.int32, (LANES, LANES), 1) >= HALF
    swap = jnp.where(across == over, 1.0, 0.0).astype(bf16)
    key_all = key_pair.astype(f32)
    largest = jnp.max(dot((key_all * key_all).astype(bf16), swap), axis=0, keepdims=True)
    if known is not None:
        largest = jnp.maximum(largest, known)
    query_all = query_pair.astype(f32)
    query_norms = dot((query_all * query_all).astype(bf16), swap)
    bound = 1.02 * jnp.sqrt(query_norms * largest)
    small = small_lane(shape)
    mark = jnp.where(small == 0, 1.0, jnp.where(small == 1, -bound, 0.0)).astype(bf16)
    bounded = []
    bounds = []
    for side in range(2):
        query = jnp.where(half_mask(shape, side), query_pair, mark)
        bounded.append(query)
        lane = lax.broadcasted_iota(jnp.int32, (8, LANES), 1)
        chosen = jnp.where(lane == (1 - side) * HALF + 1, 1.0, 0.0).astype(bf16)
        bounds.append(-dot(chosen, query, NT)[0:1])
    return bounded, bounds, largest


def mix(query, side, keys, values, extra, lanes, starts, block):
    total = None
    for start in starts:
        part = pl.ds(start, block)
        half = half_mask((block, LANES), side)
        extras = extra[part, :]
        scores = dot(jnp.where(half, keys[part, lanes], extras), query, NT)
        weights = jnp.exp(scores).astype(bf16)
        mixture = dot(jnp.where(half, values[part, lanes], extras), weights, TN)
        total = mixture if total is None else total + mixture
    return total


def near_kernel(
    offsets, shape, heights, widths, first, second, key_weight, value_weight, queries,
    keys, values, extra, sums, bounds, largest,
):
    project(
        offsets, (first, second), 0, shape, heights[0], widths[0], (key_weight, value_weight),
        (keys, values, extra),
    )
    key_count = keys.shape[0]

    def body(pair, carry):
        lanes = pl.ds(pl.multiple_of(pair * LANES, LANES), LANES)
        bounded, rows, norms = bound_scores(queries[:, lanes], keys[:, lanes], None)
        largest[pair] = norms
        for side in range(2):
            bounds[2 * pair + side] = rows[side]
            sums[2 * pair + side] = mix(
                bounded[side], side, keys, values, extra, lanes, (0,), key_count
            )
        return carry

    lax.fori_loop(0, HEADS // 2, body, 0, unroll=True)


def attend_kernel(order, *refs):
    refs = list(refs)
    heights, widths = refs[:2]
    del refs[:2]
    near = refs[:6]
    del refs[:6]
    pooled = refs[: len(order) - 2]
    del refs[: len(order) - 2]
    (key_weight, value_weight, queries, tokens, out_weight, out_bias, gain, bias,
     keys, values, extra, attended, middle, normal, to_core, to_far, marks, square,
     sums, totals) = refs
    near_keys, near_values, near_extra, near_sums, near_bounds, near_largest = near
    tasks, rows, width, model = tokens.shape
    me = lax.axis_index("rows")
    height, valid_width = heights[0], widths[0]
    known = near_keys.shape[0]
    keys[0:known, :] = near_keys[...]
    values[0:known, :] = near_values[...]
    extra[0:known, :] = near_extra[...]
    project(
        order[2:], pooled, known, (rows, width), height, valid_width, (key_weight, value_weight),
        (keys, values, extra),
    )
    query_count = queries.shape[0]
    key_count = keys.shape[0]
    block = known
    rest = (key_count - known) // block
    together = max(k for k in (1, 2, 3, 4) if rest % k == 0)
    steps = rest // together

    def body(pair, carry):
        lanes = pl.ds(pl.multiple_of(pair * LANES, LANES), LANES)
        query_pair = queries[:, lanes]
        shape = query_pair.shape
        bounded, bounds, _ = bound_scores(query_pair, keys[known:, lanes], near_largest[pair])

        def some(step):
            starts = [
                pl.multiple_of(known + (step * together + k) * block, block) for k in range(together)
            ]
            return [
                mix(bounded[side], side, keys, values, extra, lanes, starts, block)
                for side in range(2)
            ]

        first = some(0)
        for side in range(2):
            scale = jnp.exp(near_bounds[2 * pair + side] - bounds[side])
            sums[side] = first[side] + near_sums[2 * pair + side] * scale
        if steps > 1:

            def more(step, carry):
                for side, total in enumerate(some(step)):
                    sums[side] += total
                return carry

            lax.fori_loop(1, steps, more, 0)
        for side in range(2):
            totals[side : side + 1, :] = bounds[side]
        at = [(1 - side) * HALF + 1 for side in range(2)]
        least = jnp.minimum(
            jnp.min(sums[0, at[0] : at[0] + 1, :]), jnp.min(sums[1, at[1] : at[1] + 1, :])
        )

        @pl.when(jnp.logical_not(least > 1e-25))
        def _():
            lead = jnp.where(small_lane(shape) == 0, 1.0, 0.0).astype(bf16)
            for side in range(2):
                query = jnp.where(half_mask(shape, side), query_pair, lead)

                def scores_of(step):
                    part = pl.ds(pl.multiple_of(step * LANES, LANES), LANES)
                    half = half_mask((LANES, LANES), side)
                    extras = extra[part, :]
                    value = jnp.where(half, values[part, lanes], extras)
                    return dot(jnp.where(half, keys[part, lanes], extras), query, NT), value

                def highest(step, peak):
                    scores, _ = scores_of(step)
                    return jnp.maximum(peak, jnp.max(scores, axis=0, keepdims=True))

                start = jnp.full((1, query_count), -jnp.inf, f32)
                peak = lax.fori_loop(0, key_count // LANES, highest, start)
                totals[side : side + 1, :] = peak
                sums[side] = jnp.zeros((LANES, query_count), f32)

                def add(step, carry):
                    scores, value = scores_of(step)
                    weights = jnp.exp(scores - totals[side : side + 1, :]).astype(bf16)
                    sums[side] += dot(value, weights, TN)
                    return carry

                lax.fori_loop(0, key_count // LANES, add, 0)

        both = []
        row = lax.broadcasted_iota(jnp.int32, (LANES, query_count), 0)
        small = row & (HALF - 1)
        for side in range(2):
            mixture = sums[side]
            total = mixture[at[side] : at[side] + 1]
            high, middle_part, low = pieces(-(totals[side : side + 1, :] + jnp.log(total)))
            mark = jnp.where(
                small == 0,
                1.0,
                jnp.where(
                    small == 1,
                    high,
                    jnp.where(small == 2, middle_part, jnp.where(small == 3, low, 0.0)),
                ),
            )
            inside = (row < HALF) if side == 0 else (row >= HALF)
            across = jnp.where(inside, mixture / total, mark).T
            marks[2 * pair + side] = jnp.where(
                half_mask(shape, side), query_pair, across.astype(bf16)
            )
            both.append(across)
        chosen = jnp.where(half_mask(shape, 0), both[0], both[1])
        attended[:, lanes] = chosen.astype(bf16)
        return carry

    lax.fori_loop(0, HEADS // 2, body, 0)
    branch = dot(attended[...], out_weight[...]) + out_bias[...].reshape(1, model)
    total = flat(tokens).astype(f32) + branch
    middle[...] = total.reshape(middle.shape)
    normed, _ = normalize(total)
    low = normed * gain[...].reshape(1, model) + bias[...].reshape(1, model)
    normal[...] = low.astype(bf16).reshape(normal.shape)
    core_row, far_row, _, _ = neighbours(rows)
    for task in range(tasks):
        to_core[task, 0] = normal[task, core_row]
        to_far[task, 0] = normal[task, far_row]
    index = lax.broadcasted_iota(jnp.int32, (query_count, 1), 0)
    inside = (me * rows + (index // width) % rows < height) & ((index & (width - 1)) < valid_width)
    square[...] = column_sum(branch * branch * inside.astype(f32))


def put_pieces(grad, first, count, me, held):
    size = grad.shape[0] // PIECES
    for group in range(PIECES):
        piece = grad[group * size : (group + 1) * size]
        slot, owner = divmod(first + group, count)
        store_piece(owner, me, held, slot * size, piece)


def store_piece(owner, me, held, start, piece):
    place = owner ^ me
    place = (place & 1) * (held.shape[0] // 2) + (place >> 1)
    held[place, start : start + piece.shape[0], :] = piece


def part_pieces(held, keep, send):
    half = held.shape[0] // 2
    keep[...] = held[0:half]
    send[...] = held[half:]


def feed_in_kernel(normal, cotangent, up_weight, up_bias, down_weight, lifted, grad_act):
    tasks, rows, width, model = cotangent.shape
    hidden = up_weight.shape[1]
    bias = up_bias[...].reshape(1, hidden)
    fed, grad = flat(normal), flat(cotangent)
    for start in range(0, hidden, model):
        lanes = slice(start, start + model)
        value = (dot(fed, up_weight[:, lanes]) + bias[:, lanes]).astype(bf16)
        lifted[:, :, :, lanes] = value.reshape(tasks, rows, width, model)
        value = dot(grad, down_weight[lanes, :], NT).astype(bf16)
        grad_act[:, :, :, lanes] = value.reshape(tasks, rows, width, model)


def feed_kernel(
    from_core, from_far, lifted, grad_act, up_weight, up_bias, taps,
    active, grad_lifted, grad_band, to_core, to_far, grad_taps, grad_up_bias,
    core_lifted, far_lifted, wide, wide_back, grad_normal,
):
    tasks, rows, width, hidden = lifted.shape
    model = up_weight.shape[0]
    _, has_before, has_after = band_flags()
    lines = rows + 2
    _, _, core_line, far_line = neighbours(rows)
    c1 = 0.7978845608028654
    c2 = c1 * 0.044715

    clear_guards(wide)
    clear_guards(wide_back)
    bias = up_bias[...].reshape(1, hidden)
    for source, weight, target in ((from_core, None, core_lifted), (from_far, far_weight(), far_lifted)):
        value = dot(flat(source), up_weight[...]) + bias
        if weight is not None:
            value = value * weight
        target[...] = value.astype(bf16).reshape(target.shape)

    def across(block, carry):
        lanes = pl.ds(pl.multiple_of(block * LANES, LANES), LANES)
        tap = [[taps[a, b, lanes][None, :] for b in range(3)] for a in range(3)]

        def forth(task, sums9):
            sums9 = list(sums9)
            put_line(wide, task * lines + core_line, core_lifted[task, :, lanes].astype(f32))
            put_line(wide, task * lines + far_line, far_lifted[task, :, lanes].astype(f32))
            for row in range(rows):
                put_line(wide, task * lines + row + 1, lifted[task, row, :, lanes].astype(f32))
            for row in range(rows):
                for start in range(0, width, 16):
                    near = []
                    spread = None
                    for a in range(3):
                        for b in range(3):
                            at = GUARD - 1 + b + start
                            value = wide[0, task * lines + row + a, at : at + 16, :]
                            near.append(value)
                            term = tap[a][b] * value
                            spread = term if spread is None else spread + term
                    squared = spread * spread
                    gate = 0.5 + 0.5 * jnp.tanh(spread * (c1 + c2 * squared))
                    active[task, row, start : start + 16, lanes] = (spread * gate).astype(bf16)
                    slope = gate + spread * (gate - gate * gate) * (2 * c1 + 6 * c2 * squared)
                    grad = grad_act[task, row, start : start + 16, lanes].astype(f32) * slope
                    wide_back[
                        0, task * rows + row, GUARD + start : GUARD + start + 16, :
                    ] = grad
                    for k in range(9):
                        both = near[k] * grad
                        sums9[k] = sums9[k] + (both[0:8] + both[8:16])
            return tuple(sums9)

        zero = jnp.zeros((8, LANES), f32)
        sums9 = lax.fori_loop(0, tasks, forth, (zero,) * 9)
        for k in range(9):
            grad_taps[k // 3, k % 3, lanes] = jnp.sum(sums9[k], axis=0)

        def back(task, total):
            for line in range(lines):
                for start in range(0, width, 16):
                    value = None
                    for a in range(3):
                        if not 0 <= line - a < rows:
                            continue
                        for b in range(3):
                            at = GUARD + 1 - b + start
                            term = tap[a][b] * wide_back[
                                0, task * rows + line - a, at : at + 16, :
                            ]
                            value = term if value is None else value + term
                    if line == 0:
                        value = value * has_before
                    if line == lines - 1:
                        value = value * has_after
                    grad_lifted[task, line, start : start + 16, lanes] = value.astype(bf16)
                    total = total + (value[0:8] + value[8:16])
            return total

        grad_up_bias[0:1, lanes] = column_sum(lax.fori_loop(0, tasks, back, zero))
        return carry

    lax.fori_loop(0, hidden // LANES, across, 0)
    grad = dot(flat(grad_lifted), up_weight[...], NT)
    grad_normal[...] = grad.reshape(grad_normal.shape)
    for task in range(tasks):
        grad_band[task] = grad_normal[task, 1 : rows + 1]
        to_core[task, 0] = grad_normal[task, core_line].astype(bf16)
        to_far[task, 0] = grad_normal[task, far_line].astype(bf16)


def feed_weight_kernel(
    middle_normal, from_core, from_far, active, grad_lifted, cotangent, keep, send, normal, held
):
    tasks, rows, width, model = cotangent.shape
    hidden = active.shape[-1]
    me = lax.axis_index("rows")
    count = lax.axis_size("rows")
    _, _, core_line, far_line = neighbours(rows)
    for task in range(tasks):
        for row in range(rows):
            normal[task, row + 1] = middle_normal[task, row]
        normal[task, core_line] = from_core[task, 0]
        normal[task, far_line] = from_far[task, 0]
    size = hidden // count
    groups = model // size
    columns = hidden // model
    fed, grad_output = flat(normal), flat(cotangent)
    for column in range(columns):
        lanes = slice(column * model, (column + 1) * model)
        grad = grad_lifted[:, :, :, lanes].reshape(-1, model)
        grad_up = dot(fed, grad, TN).astype(bf16)
        act = active[:, :, :, lanes].reshape(-1, model)
        grad_down = dot(act, grad_output, TN).astype(bf16)
        for group in range(groups):
            part = slice(group * size, (group + 1) * size)
            store_piece(group * columns + column, me, held, 0, grad_up[part])
            store_piece(column * groups + group, me, held, size, grad_down[part])
    part_pieces(held, keep, send)


def layer_kernel(
    heights, widths, active, down_weight, down_bias, cotangent, middle, layer_out, sums
):
    tasks, rows, width, model = cotangent.shape
    me = lax.axis_index("rows")
    height, valid_width = heights[0], widths[0]
    zero = jnp.zeros((1, model), f32)
    totals = [zero, zero, zero]
    col = lax.broadcasted_iota(jnp.int32, (width, 1), 0)
    for task in range(tasks):
        branch = dot(flat(active.at[task]), down_weight[...]) + down_bias[...].reshape(1, model)
        for row in range(rows):
            mlp = branch[row * width : (row + 1) * width]
            final = middle[task, row] + mlp
            layer_out[task, row] = final.astype(bf16)
            inside = (col < valid_width) & (me * rows + row < height)
            weight = inside.astype(f32)
            grad = cotangent[task, row].astype(f32)
            for k, value in enumerate((grad, mlp * mlp * weight, final * final * weight)):
                totals[k] = totals[k] + column_sum(value)
    sums[...] = jnp.concatenate([*totals, jnp.zeros((5, model), f32)], axis=0)


def norm_back_kernel(
    grad_band, from_core, from_far, middle, cotangent, gain, out_weight, attended,
    grad_middle, grad_marks, grad_out, sums,
):
    tasks, rows, width, model = cotangent.shape
    scale = gain[...].reshape(1, model)
    parts = []
    odd = (lax.axis_index("rows") & 1).astype(f32)
    for task in range(tasks):
        core = from_core[task, 0].astype(f32)
        far = from_far[task, 0].astype(f32)
        for row in range(rows):
            grad = grad_band[task, row]
            if row == 0:
                grad = grad + core * odd + far * (1.0 - odd)
            if row == rows - 1:
                grad = grad + far * odd + core * (1.0 - odd)
            parts.append(grad)
    grad_input = jnp.concatenate(parts, axis=0)
    normed, inverse = normalize(flat(middle))
    total = flat(cotangent).astype(f32) + normalize_back(grad_input, scale, normed, inverse)
    grad_middle[...] = total.reshape(grad_middle.shape)
    sums[0:1, :] = column_sum(grad_input * normed)
    sums[1:2, :] = column_sum(grad_input)
    sums[2:3, :] = column_sum(total)
    sums[3:8, :] = jnp.zeros((5, model), f32)
    grad_branch = total.astype(bf16)
    mixture = attended[...]
    grad_out[...] = dot(mixture, grad_branch, TN).astype(bf16)
    grad_attended = dot(grad_branch, out_weight[...], NT).astype(bf16)
    shape = (mixture.shape[0], LANES)
    for pair in range(HEADS // 2):
        lanes = slice(pair * LANES, (pair + 1) * LANES)
        grad_two = grad_attended[:, lanes]
        both = grad_two.astype(f32) * mixture[:, lanes].astype(f32)
        for side in range(2):
            half = half_mask(shape, side)
            inner = jnp.sum(jnp.where(half, both, 0.0), axis=-1, keepdims=True)
            grad_marks[2 * pair + side] = jnp.where(half, grad_two, marked(0.0, -inner, shape))


def attend_back_kernel(
    marks, grad_marks, keys, values, extra, grad_queries, grad_keys, grad_values,
    total, query_zero, grad_zero,
):
    key_count = keys.shape[0]
    query_count = grad_marks.shape[1]
    block = min(1024, key_count)
    shape = (query_count, LANES)
    for side in range(2):
        half = half_mask(shape, side)
        zero = jnp.zeros(shape, bf16)
        part = slice(side * query_count, (side + 1) * query_count)
        query_zero[part, :] = jnp.where(half, marks[side], zero)
        grad_zero[part, :] = jnp.where(half, grad_marks[side], zero)

    def body(place, carry):
        part = pl.ds(pl.multiple_of(place * block, block), block)
        key_pair, value_pair, extras = keys[part, :], values[part, :], extra[part, :]
        lows, grads = [], []
        query_part = None
        for side in range(2):
            half = half_mask((block, LANES), side)
            scores = dot(jnp.where(half, key_pair, extras), marks[side], NT)
            grad_prob = dot(jnp.where(half, value_pair, extras), grad_marks[side], NT)
            probability = jnp.exp(scores)
            grad = (probability * grad_prob).astype(bf16)
            grads.append(grad)
            lows.append(probability.astype(bf16))
            one = dot(jnp.where(half, key_pair, jnp.zeros((block, LANES), bf16)), grad, TN)
            query_part = one if query_part is None else query_part + one
        grad_values[part, :] = dot(jnp.concatenate(lows, axis=1), grad_zero[...]).astype(bf16)
        grad_keys[part, :] = dot(jnp.concatenate(grads, axis=1), query_zero[...]).astype(bf16)

        @pl.when(place == 0)
        def _():
            total[...] = query_part

        @pl.when(place > 0)
        def _():
            total[...] += query_part

        return carry

    lax.fori_loop(0, key_count // block, body, 0)
    grad_queries[...] = (total[...] * HALF**-0.5).T.astype(bf16)


def side_by_side(refs):
    return jnp.concatenate([ref[...] for ref in refs], axis=1)


def conv_back_kernel(*refs):
    pairs = HEADS // 2
    grad_queries = refs[:pairs]
    query_weight, grad_conv, to_core, to_far = refs[pairs:]
    tasks, rows = grad_conv.shape[:2]
    grad = dot(side_by_side(grad_queries), query_weight[...], NT).astype(bf16)
    grad_conv[...] = grad.reshape(grad_conv.shape)
    core_row, far_row, _, _ = neighbours(rows)
    for task in range(tasks):
        to_core[task, 0] = grad_conv[task, core_row]
        to_far[task, 0] = grad_conv[task, far_row]


def pool_back_kernel(order, *refs):
    pairs = HEADS // 2
    grad_keys, grad_values = refs[:pairs], refs[pairs : 2 * pairs]
    key_weight, value_weight, keep, send = refs[2 * pairs :]
    cells = keep.shape[1]
    both = jnp.concatenate([key_weight[...], value_weight[...]], axis=1)
    for position, offset in enumerate(order):
        part = slice(position * cells, (position + 1) * cells)
        grads = jnp.concatenate([ref[part, :] for ref in (*grad_keys, *grad_values)], axis=1)
        target = send if offset & 1 else keep
        target[offset >> 1] = dot(grads, both, NT).astype(bf16)


def pair_weights(order, pooled, conv, queries, keys, values):
    cells = pooled[0].shape[0]
    total = None
    for position in range(len(order)):
        part = slice(position * cells, (position + 1) * cells)
        grads = jnp.concatenate([ref[part, :] for ref in (*keys, *values)], axis=1)
        value = dot(pooled[position][...], grads, TN)
        total = value if total is None else total + value
    grad_query = dot(flat(conv), side_by_side(queries), TN)
    return jnp.concatenate([grad_query, total], axis=1).astype(bf16)


def weight_kernel(order, *refs):
    refs = list(refs)
    heights, widths = refs[:2]
    del refs[:2]
    pooled = refs[: len(order)]
    del refs[: len(order)]
    pairs = HEADS // 2
    queries, keys, values = refs[:pairs], refs[pairs : 2 * pairs], refs[2 * pairs : 3 * pairs]
    del refs[: 3 * pairs]
    (pool_keep, pool_send, conv, extended, grad_conv, taps, gain, bias, grad_out, square, back_sums,
     feed_sums, hidden_taps, up_bias, keep, send, wide, rows_of, held) = refs
    tasks, rows, width, model = grad_conv.shape
    count = len(order)
    lines = rows + 2
    me, has_before, has_after = band_flags()
    size = keep.shape[1] - 16
    model_grads = pair_weights(order, pooled, conv, queries, keys, values)
    for which in range(3):
        grad = model_grads[:, which * model : (which + 1) * model]
        put_pieces(grad, which * PIECES, count, me, held)
    put_pieces(grad_out[...], 3 * PIECES, count, me, held)
    pool_sum = jnp.zeros((1, model), f32)
    pool_dot = jnp.zeros((1, model), f32)
    for position, offset in enumerate(order):
        source = pool_send if offset & 1 else pool_keep
        grad = source[offset >> 1].astype(f32)
        pool_sum = pool_sum + column_sum(grad)
        pool_dot = pool_dot + column_sum(grad * pooled[position][...].astype(f32))

    clear_guards(wide)
    for task in range(tasks):
        for line in range(lines):
            put_line(wide, task * lines + line, extended[task, line].astype(f32))

    def across(block, carry):
        lanes = pl.ds(pl.multiple_of(block * LANES, LANES), LANES)

        def one_task(task, sums9):
            sums9 = list(sums9)
            for row in range(rows):
                for start in range(0, width, 16):
                    grad = grad_conv[task, row, start : start + 16, lanes].astype(f32)
                    for k in range(9):
                        at = GUARD - 1 + k % 3 + start
                        both = grad * wide[block, task * lines + row + k // 3, at : at + 16, :]
                        sums9[k] = sums9[k] + (both[0:8] + both[8:16])
            return tuple(sums9)

        sums9 = lax.fori_loop(
            0, tasks, one_task, tuple(jnp.zeros((8, LANES), f32) for _ in range(9))
        )
        for k in range(9):
            rows_of[2 + k : 3 + k, lanes] = column_sum(sums9[k])
        return carry

    lax.fori_loop(0, model // LANES, across, 0)

    shift = bias[...].reshape(1, model)
    zero = jnp.zeros((1, model), f32)
    conv_dot, conv_sum = zero, zero
    for row in range(rows):
        line = grad_conv[0, row].astype(f32)
        for task in range(1, tasks):
            line = line + grad_conv[task, row].astype(f32)
        full = column_sum(line)
        by_col = (full - line[0:1], full, full - line[width - 1 : width])
        for a in range(3):
            for b in range(3):
                value = by_col[b]
                if a == 0 and row == 0:
                    value = value * has_before
                if a == 2 and row == rows - 1:
                    value = value * has_after
                conv_sum = conv_sum + taps[a, b].reshape(1, model) * value
    for k in range(9):
        conv_dot = conv_dot + taps[k // 3, k % 3].reshape(1, model) * rows_of[2 + k : 3 + k, :]
    grad_bias = conv_sum + pool_sum
    grad_gain = (conv_dot + pool_dot - shift * grad_bias) / gain[...].reshape(1, model)
    rows_of[0:1, :] = grad_gain
    rows_of[1:2, :] = grad_bias
    rows_of[11:12, :] = back_sums[2:3, :]
    rows_of[12:14, :] = back_sums[0:2, :]
    rows_of[14:15, :] = feed_sums[0:1, :]
    rows_of[15:16, :] = square[...]
    rows_of[16:18, :] = feed_sums[1:3, :]
    in_rows = jnp.clip(heights[0] - me * rows, 0, rows)
    in_cols = jnp.clip(widths[0], 0, width)
    cells_in = (tasks * in_rows * in_cols).astype(f32)
    rows_of[18:19, :] = jnp.full((1, model), cells_in, f32)
    parts = up_bias.shape[1] // model
    for part in range(parts):
        rows_of[19 + part : 20 + part, :] = up_bias[:, part * model : (part + 1) * model]
        for k in range(9):
            rows_of[19 + parts * (k + 1) + part : 20 + parts * (k + 1) + part, :] = hidden_taps[
                k // 3, k % 3, part * model : (part + 1) * model
            ].reshape(1, model)
    used = 19 + 10 * parts
    rows_of[used:SMALL, :] = jnp.zeros((SMALL - used, model), f32)
    group = SMALL // count
    for owner in range(count):
        value = rows_of[owner * group : (owner + 1) * group, :]
        if group < 8:
            value = jnp.concatenate([value, jnp.zeros((8 - group, model), f32)], axis=0)
        high = value.astype(bf16)
        low = (value - high.astype(f32)).astype(bf16)
        store_piece(owner, me, held, size, jnp.concatenate([high, low], axis=0))
    part_pieces(held, keep, send)


def last_kernel(
    grad_conv, from_core, from_far, taps, tokens, gain, grad_middle, pool, input_grad, wide
):
    tasks, rows, width, model = tokens.shape
    lines = rows + 2
    pooled_rows = rows // 2
    clear_guards(wide)
    _, _, core_line, far_line = neighbours(rows)
    for task in range(tasks):
        put_line(wide, task * lines + core_line, from_core[task, 0].astype(f32))
        put_line(wide, task * lines + far_line, from_far[task, 0].astype(f32) * far_weight())
        for row in range(rows):
            put_line(wide, task * lines + row + 1, grad_conv[task, row].astype(f32))
    pooled = pool[...].reshape(tasks, pooled_rows, width // 2, model)
    spread_matrix = pool_matrix(width)[:, 0:width]

    def body(step, carry):
        task = step // (model // LANES)
        block = step % (model // LANES)
        lanes = pl.ds(pl.multiple_of(block * LANES, LANES), LANES)
        for row in range(rows):
            for start in range(0, width, 16):
                total = jnp.zeros((16, LANES), f32)
                for a in range(3):
                    for b in range(3):
                        at = GUARD + 1 - b + start
                        total = total + taps[a, b, lanes][None, :] * wide[
                            block, task * lines + row + 2 - a, at : at + 16, :
                        ]
                input_grad[task, row, start : start + 16, lanes] = total
        return carry

    lax.fori_loop(0, tasks * (model // LANES), body, 0)
    scale = gain[...].reshape(1, model)
    for task in range(tasks):
        for row in range(rows):
            grad = input_grad[task, row] + dot(spread_matrix, pooled[task, row // 2], TN)
            normed, inverse = normalize(tokens[task, row].astype(f32))
            input_grad[task, row] = grad_middle[task, row] + normalize_back(grad, scale, normed, inverse)


def add_blocks(values):
    total = values[0].astype(f32)
    for other in values[1:]:
        total = total + other.astype(f32)
    return total


def put_sum(out, start, values, small):
    total = add_blocks(values)
    size = total.shape[0]
    if not small:
        out[start : start + size, :] = total.astype(bf16)
        return
    size -= 16
    value = total[size : size + 8] + total[size + 8 : size + 16]
    high = value.astype(bf16)
    low = (value - high.astype(f32)).astype(bf16)
    out[start : start + size, :] = total[0:size].astype(bf16)
    out[start + size : start + size + 16, :] = jnp.concatenate([high, low], axis=0)


def combine(arrays, small):
    blocks, size, model = arrays[0].shape

    def kernel(*refs):
        ins, outs = refs[: len(arrays)], refs[len(arrays) :]
        for block, out in enumerate(outs):
            put_sum(out, 0, [x[block] for x in ins], small)

    return call("combine", kernel, [((size, model), bf16)] * blocks, list(arrays))


def stack(values):
    size, model = values[0].shape

    def kernel(*refs):
        for place, value in enumerate(refs[:-1]):
            refs[-1][place] = value[...]

    return call("stack", kernel, [((len(values), size, model), bf16)], list(values))[0]


def exchange(value, axis, mask):
    count = lax.axis_size(axis)
    return lax.ppermute(value, axis, [(i, i ^ mask) for i in range(count)])


def far_masks():
    return list(range(2, lax.axis_size("rows"), 2))


def once(value, *earlier):
    return lax.optimization_barrier((value, earlier))[0]


def far_rows(value):
    return [exchange(value, "rows", mask) for mask in far_masks()]


def all_images(value):
    return [exchange(value, "batch", mask) for mask in range(1, lax.axis_size("batch"))]


def add_images(own, arrived, small):
    (total,) = combine([x[None] for x in [own, *arrived]], small)
    return total


def unpack_feed_kernel(count, *refs):
    even, odd, grad_up, grad_down = refs
    blocks = [half.at[place] for half in (even, odd) for place in range(count // 2)]
    me = lax.axis_index("rows")
    model, hidden = grad_up.shape
    size = hidden // count
    columns = hidden // model
    for j in range(count):
        owner = blocks_owner(j, count, me)
        block = blocks[j]
        up = block[0:size, :].astype(f32)
        place = owner // columns
        col = owner % columns
        grad_up[
            pl.ds(pl.multiple_of(place * size, size), size),
            pl.ds(pl.multiple_of(col * model, model), model),
        ] = up
        grad_down[pl.ds(pl.multiple_of(owner * size, size), size), :] = block[
            size : 2 * size, :
        ].astype(f32)


def blocks_owner(j, count, me):
    half = count // 2
    offset = 2 * j if j < half else 2 * (j - half) + 1
    return me ^ offset


def unpack_late_kernel(count, *refs):
    blocks = refs[:count]
    (grad_query, grad_key, grad_value, grad_out, norm1_gain, norm1_bias, query_taps, out_bias,
     norm2_gain, norm2_bias, up_bias, hidden_taps, down_bias, stats, weights, rows_of) = refs[count:]
    me = lax.axis_index("rows")
    model = grad_query.shape[0]
    piece = model // PIECES
    size = blocks[0].shape[0] - 16
    group = SMALL // count
    for j in range(count):
        owner = blocks_owner(j, count, me)
        block = blocks[j][...].astype(f32)
        for slot in range(size // piece):
            start = pl.multiple_of((slot * count + owner) * piece, piece)
            weights[pl.ds(start, piece), :] = block[slot * piece : (slot + 1) * piece]
        rows_of[owner] = block[size : size + 8] + block[size + 8 : size + 16]
    for which, out in enumerate((grad_query, grad_key, grad_value, grad_out)):
        out[...] = weights[which * model : (which + 1) * model, :]

    def line(k):
        return rows_of[k // group, k % group, :]

    norm1_gain[...] = line(0)
    norm1_bias[...] = line(1)
    for k in range(9):
        query_taps[k // 3, k % 3, :] = line(2 + k)
    out_bias[...] = line(11)
    norm2_gain[...] = line(12)
    norm2_bias[...] = line(13)
    down_bias[...] = line(14)
    parts = up_bias.shape[0] // model
    for part in range(parts):
        lanes = slice(part * model, (part + 1) * model)
        up_bias[lanes] = line(19 + part)
        for k in range(9):
            hidden_taps[k // 3, k % 3, lanes] = line(19 + parts * (k + 1) + part)
    cells = line(18).reshape(1, model)[:, 0:1]
    row = lax.broadcasted_iota(jnp.int32, (1, LANES), 1)
    value = jnp.zeros((1, LANES), f32)
    for k in range(3):
        total = jnp.sum(line(15 + k).reshape(1, model), axis=-1, keepdims=True)
        value = jnp.where(row == k, jnp.sqrt(total / (cells * model)), value)
    stats[...] = value.reshape(LANES)[0:3]


def local(
    tokens,
    norm1_gain,
    norm1_bias,
    query_taps,
    query_weight,
    key_weight,
    value_weight,
    out_weight,
    out_bias,
    norm2_gain,
    norm2_bias,
    up_weight,
    up_bias,
    hidden_taps,
    down_weight,
    down_bias,
    cotangent,
    heights,
    widths,
):
    shape = tokens.shape
    tokens, cotangent = tokens[0], cotangent[0]
    tasks, rows, width, model = tokens.shape
    hidden = up_weight.shape[1]
    count = lax.axis_size("rows")
    cells = tasks * (rows // 2) * (width // 2)
    key_count = count * cells
    lines = rows + 2
    token_count = tasks * rows * width
    line = (tasks, 1, width, model)

    def swap_lines(lines_out):
        to_core, to_far = lines_out
        across = [p for i in range(1, count, 2) for p in ((i, (i + 1) % count), ((i + 1) % count, i))]
        return exchange(to_core, "rows", 1), lax.ppermute(to_far, "rows", across)

    normal_one, pooled = call(
        "first_norm",
        first_norm_kernel,
        [(tokens.shape, bf16), ((cells, model), bf16)],
        [hbm(x) for x in (tokens, norm1_gain, norm1_bias)],
        limit=8,
    )
    far = far_masks()
    order = [0, 1, *far, *[mask + 1 for mask in far]]
    arrived = far_rows(pooled)
    edge = call("edge", edge_kernel, [(line, bf16), (line, bf16)], [normal_one])
    edge = swap_lines(edge)
    swapped = exchange(pooled, "rows", 1)
    extended, conv, queries = call(
        "query_conv",
        query_kernel,
        [
            ((tasks, lines, width, model), bf16), (tokens.shape, bf16), ((token_count, model), bf16),
        ],
        [normal_one, *edge, hbm(query_taps), hbm(query_weight)],
        scratch=[wide_scratch(tasks * lines, width, model)],
        us=2,
        limit=12,
    )
    near_count = 2 * cells
    near = call(
        "near",
        lambda *refs: near_kernel(order[:2], (rows, width), *refs),
        [
            ((near_count, model), bf16), ((near_count, model), bf16), ((near_count, LANES), bf16),
            ((HEADS, LANES, token_count), f32), ((HEADS, 1, token_count), f32),
            ((HEADS // 2, 1, LANES), f32),
        ],
        [heights, widths, pooled, swapped, hbm(key_weight), hbm(value_weight), queries],
        smem=2,
        us=4,
        limit=20,
    )
    arrived = once(arrived, *near)
    blocks = [pooled, swapped, *arrived, *[exchange(x, "rows", 1) for x in arrived]]

    (keys, values, extra, attended, middle, normal_two, to_core, to_far, marks, square) = call(
        "attend",
        lambda *refs: attend_kernel(order, *refs),
        [
            ((key_count, model), bf16), ((key_count, model), bf16), ((key_count, LANES), bf16),
            ((token_count, model), bf16), (tokens.shape, f32),
            (tokens.shape, bf16), (line, bf16), (line, bf16), ((HEADS, token_count, LANES), bf16), ((1, model), f32),
        ],
        [heights, widths, *near, *blocks[2:], hbm(key_weight), hbm(value_weight), queries,
         *[hbm(x) for x in (tokens, out_weight, out_bias, norm2_gain, norm2_bias)]],
        smem=2,
        scratch=[pltpu.VMEM((2, LANES, token_count), f32), pltpu.VMEM((8, token_count), f32)],
        us=18,
        limit=24,
    )
    next_lines = swap_lines((to_core, to_far))
    band = (tasks, rows, width, hidden)
    lifted, grad_act = call(
        "feed_in",
        feed_in_kernel,
        [(band, bf16), (band, bf16)],
        [normal_two, *[hbm(x) for x in (cotangent, up_weight, up_bias, down_weight)]],
        us=4,
        limit=20,
    )
    next_lines = once(next_lines, grad_act)
    (active, grad_lifted, grad_band, to_core, to_far, grad_hidden_taps, grad_up_bias) = call(
        "feed",
        feed_kernel,
        [
            (band, bf16), ((tasks, lines, width, hidden), bf16), (tokens.shape, f32), (line, bf16),
            (line, bf16), ((3, 3, hidden), f32), ((1, hidden), f32),
        ],
        [*next_lines, lifted, grad_act, *[hbm(x) for x in (up_weight, up_bias, hidden_taps)]],
        scratch=[
            pltpu.VMEM((tasks, width, hidden), bf16),
            pltpu.VMEM((tasks, width, hidden), bf16),
            wide_scratch(tasks * lines, width, LANES),
            wide_scratch(tasks * rows, width, LANES),
            pltpu.VMEM((tasks, lines, width, model), f32),
        ],
        us=24,
        limit=24,
    )
    edge = swap_lines((to_core, to_far))
    feed_keep, feed_send = call(
        "feed_weights",
        feed_weight_kernel,
        [((count // 2, 2 * hidden // count, model), bf16)] * 2,
        [normal_two, *next_lines, active, grad_lifted, hbm(cotangent)],
        scratch=[
            pltpu.VMEM((tasks, lines, width, model), bf16),
            pltpu.VMEM((count, 2 * hidden // count, model), bf16),
        ],
        us=5,
        limit=24,
    )
    edge = once(edge, feed_keep)
    feed_swapped = exchange(once(feed_send, edge), "rows", 1)
    feed_blocks = combine(once([feed_keep, feed_swapped], edge), False)
    feed_arrived = [exchange(feed_blocks[mask >> 1], "rows", mask) for mask in far]
    piece = model // PIECES
    grad_middle, grad_marks, grad_out, back_sums = call(
        "norm_back",
        norm_back_kernel,
        [
            (tokens.shape, f32), ((HEADS, token_count, LANES), bf16), ((model, model), bf16),
            ((8, model), f32),
        ],
        [
            once(grad_band, feed_blocks), *edge,
            middle, *[hbm(x) for x in (cotangent, norm2_gain, out_weight)], attended,
        ],
        us=4,
        limit=20,
    )

    def attend_back(pair, tie):
        inputs = [marks, grad_marks, keys, values, extra]
        inputs = once(inputs, *tie)

        def of_heads(x):
            return pl.BlockSpec((2, x.shape[1], LANES), lambda i: (pair, 0, 0))

        def of_lanes(x):
            return pl.BlockSpec((x.shape[0], LANES), lambda i: (0, pair))

        whole = pl.BlockSpec((key_count, LANES), lambda i: (0, 0))
        outs = [(token_count, LANES), (key_count, LANES), (key_count, LANES)]
        return pl.pallas_call(
            attend_back_kernel,
            name="attend_back",
            grid=(1,),
            out_shape=[jax.ShapeDtypeStruct(shape, bf16) for shape in outs],
            in_specs=[*[of_heads(x) for x in inputs[0:2]], *[of_lanes(x) for x in inputs[2:4]], whole],
            out_specs=[pl.BlockSpec(shape, lambda i: (0, 0)) for shape in outs],
            scratch_shapes=[
                pltpu.VMEM((LANES, token_count), f32),
                pltpu.VMEM((2 * token_count, LANES), bf16),
                pltpu.VMEM((2 * token_count, LANES), bf16),
            ],
            compiler_params=pltpu.CompilerParams(vmem_limit_bytes=20 << 20),
            cost_estimate=cost(11),
        )(*inputs)

    back = [attend_back(0, [])]
    feed_arrived = once(feed_arrived, *back[0])
    feed_own = add_images(feed_blocks[0], feed_arrived, False)
    hop = 1
    while hop < lax.axis_size("batch"):
        feed_arrived = exchange(feed_own, "batch", hop)
        if len(back) < HEADS // 2:
            back.append(attend_back(len(back), [*back[-1], feed_own]))
        feed_arrived = once(feed_arrived, *back[-1])
        feed_own = add_images(feed_own, [feed_arrived], False)
        hop *= 2
    while len(back) < HEADS // 2:
        back.append(attend_back(len(back), back[-1]))
    grads = [part for which in range(3) for part in [x[which] for x in back]]
    pairs = HEADS // 2
    grad_conv, *edge = call(
        "conv_back",
        conv_back_kernel,
        [(tokens.shape, bf16), (line, bf16), (line, bf16)],
        [*once(grads[:pairs], feed_own), query_weight],
    )
    feed_arrived = far_rows(feed_own)
    edge = swap_lines(edge)
    pool_keep, pool_send = call(
        "pool_back",
        lambda *refs: pool_back_kernel(order, *refs),
        [((count // 2, cells, model), bf16)] * 2,
        [*once(grads[pairs:], grad_conv), key_weight, value_weight],
        us=3,
        limit=12,
    )
    layer_out, feed_sums = call(
        "layer",
        layer_kernel,
        [(tokens.shape, bf16), ((8, model), f32)],
        [heights, widths, once(active, pool_keep), *[hbm(x) for x in (down_weight, down_bias, cotangent)], middle],
        smem=2,
        us=3,
        limit=20,
    )
    slots = -(-4 * PIECES // count)
    keep, send = call(
        "weights",
        lambda *refs: weight_kernel(order, *refs),
        [((count // 2, slots * piece + 16, model), bf16)] * 2,
        [
            heights, widths, *blocks, *grads, pool_keep, pool_send, conv, extended, grad_conv,
            query_taps, norm1_gain, norm1_bias, grad_out, square, back_sums, feed_sums,
            grad_hidden_taps, grad_up_bias,
        ],
        smem=2,
        scratch=[
            wide_scratch(tasks * lines, width, model),
            pltpu.VMEM((SMALL, model), f32),
            pltpu.VMEM((count, slots * piece + 16, model), bf16),
        ],
        us=4,
        limit=16,
    )
    feed_arrived, edge = once((feed_arrived, edge), keep)
    send, pool_send = once((send, pool_send), feed_arrived, edge)
    late_swapped = exchange(send, "rows", 1)
    pool_swapped = exchange(pool_send, "rows", 1)
    late_blocks = combine([keep, late_swapped], True)
    late_arrived = [exchange(late_blocks[mask >> 1], "rows", mask) for mask in far]
    pool_blocks = combine([pool_keep, once(pool_swapped, late_blocks)], False)
    feed_even = stack(once([feed_own, *feed_arrived], pool_blocks))
    feed_odd = exchange(feed_even, "rows", 1)
    late_arrived = once(late_arrived, feed_even)
    (late_own,) = combine([x[None] for x in [late_blocks[0], *late_arrived]], True)
    pool_arrived = [exchange(x, "rows", mask) for x, mask in zip(once(pool_blocks[1:], late_own), far)]
    arrived = exchange(late_own, "batch", 1)
    grad_up, grad_down = call(
        "unpack_feed",
        lambda *refs: unpack_feed_kernel(count, *refs),
        [((model, hidden), f32), ((hidden, model), f32)],
        [once(feed_even, late_own), feed_odd],
        us=3,
        limit=12,
    )
    arrived = once(arrived, grad_up)
    hop = 2
    while hop < lax.axis_size("batch"):
        late_own = add_images(late_own, [arrived], True)
        arrived = exchange(late_own, "batch", hop)
        hop *= 2
    pool_arrived = once(pool_arrived, late_own)
    (pool_total,) = combine([x[None] for x in [pool_blocks[0], *pool_arrived]], False)
    (input_grad,) = call(
        "last_norm",
        last_kernel,
        [(tokens.shape, f32)],
        [grad_conv, *edge, query_taps, tokens, norm1_gain, grad_middle, pool_total],
        scratch=[wide_scratch(tasks * lines, width, model)],
        us=5,
        limit=12,
    )
    late_own = add_images(late_own, [once(arrived, input_grad)], True)
    even = [late_own, *far_rows(late_own)]
    odd = [exchange(x, "rows", 1) for x in even]
    vector = ((model,), f32)
    late = call(
        "unpack_late",
        lambda *refs: unpack_late_kernel(count, *refs),
        [((model, model), f32)] * 4
        + [vector, vector, ((3, 3, model), f32), vector, vector, vector, ((hidden,), f32),
           ((3, 3, hidden), f32), vector, ((3,), f32)],
        [*even, *odd],
        scratch=[
            pltpu.VMEM((slots * count * piece, model), f32),
            pltpu.VMEM((count, 8, model), f32),
        ],
        us=2,
        limit=12,
    )
    (grad_query, grad_key, grad_value, grad_out, gain1, bias1, taps1, out_sum, gain2, bias2, up_sum,
     taps2, down_sum, stats) = late
    return (
        layer_out.reshape(shape),
        input_grad.reshape(shape),
        gain1,
        bias1,
        taps1,
        grad_query,
        grad_key,
        grad_value,
        grad_out,
        out_sum,
        gain2,
        bias2,
        grad_up,
        up_sum,
        taps2,
        grad_down,
        down_sum,
        stats,
    )


def solution(mesh):
    band = P("batch", None, "rows", None, None)
    placed = (band, *[P()] * 15, band, P("batch"), P("batch"))
    return jax.shard_map(
        local,
        mesh=mesh,
        in_specs=placed,
        out_specs=(band, band, *[P()] * 16),
        check_vma=False,
    )
```

```python
import jax
import jax.numpy as jnp
from jax import lax
from jax.experimental import pallas as pl
from jax.experimental.pallas import tpu as pltpu
from jax.sharding import PartitionSpec as P

HEADS = 6
LANES = 128
HALF = 64
GUARD = 8
SMALL = 64
PIECES = 8
epsilon = 1e-05
f32 = jnp.float32
bf16 = jnp.bfloat16
NN = (((1,), (0,)), ((), ()))
NT = (((1,), (1,)), ((), ()))
TN = (((0,), (0,)), ((), ()))


def dot(left, right, form=NN):
    return lax.dot_general(left, right, form, preferred_element_type=f32)


def cost(us):
    return pl.CostEstimate(flops=int(us * 1e4), bytes_accessed=int(us * 1e4), transcendentals=0)


def hbm(value):
    return pltpu.with_memory_space_constraint(value, pltpu.HBM)


def in_hbm(shape, dtype):
    return shape, dtype, True


def out_type(shape, dtype, away=False):
    return pltpu.HBM(shape, dtype) if away else jax.ShapeDtypeStruct(shape, dtype)


def call(name, kernel, outs, args, smem=0, scratch=(), us=1, limit=12):
    def whole(shape):
        return pl.BlockSpec(shape, lambda i, k=len(shape): (0,) * k)

    return pl.pallas_call(
        kernel,
        grid=(1,),
        out_shape=tuple(out_type(*x) for x in outs),
        in_specs=[pl.BlockSpec(memory_space=pltpu.SMEM)] * smem
        + [whole(x.shape) for x in args[smem:]],
        out_specs=tuple(whole(x[0]) for x in outs),
        scratch_shapes=list(scratch),
        name=name,
        compiler_params=pltpu.CompilerParams(vmem_limit_bytes=limit << 20),
        cost_estimate=cost(us),
    )(*args)


def normalize(values):
    center = jnp.mean(values, axis=-1, keepdims=True)
    centered = values - center
    inverse = lax.rsqrt(jnp.mean(centered * centered, axis=-1, keepdims=True) + epsilon)
    return centered * inverse, inverse


def normalize_back(grad_output, gain, normed, inverse):
    scaled = grad_output * gain
    return inverse * (
        scaled
        - jnp.mean(scaled, axis=-1, keepdims=True)
        - normed * jnp.mean(scaled * normed, axis=-1, keepdims=True)
    )


def column_sum(values):
    return jnp.sum(values, axis=0, keepdims=True)


def flat(ref):
    value = ref[...]
    return value.reshape(-1, value.shape[-1])


def band_flags():
    me = lax.axis_index("rows")
    count = lax.axis_size("rows")
    return me, (me > 0).astype(f32), (me < count - 1).astype(f32)


def neighbours(rows):
    odd = lax.axis_index("rows") & 1
    even = 1 - odd
    return even * (rows - 1), odd * (rows - 1), even * (rows + 1), odd * (rows + 1)


def far_weight():
    me, has_before, has_after = band_flags()
    return jnp.where((me & 1) == 1, has_after, has_before)


def pool_matrix(width):
    rows = lax.broadcasted_iota(jnp.int32, (width // 2, 2 * width), 0)
    cols = lax.broadcasted_iota(jnp.int32, (width // 2, 2 * width), 1)
    cols = jnp.where(cols >= width, cols - width, cols)
    return jnp.where((cols >> 1) == rows, 0.25, 0.0).astype(bf16)


def first_norm_kernel(tokens, gain, bias, normal, pooled):
    tasks, rows, width, model = tokens.shape
    matrix = pool_matrix(width)
    scale = gain[...].reshape(1, model)
    shift = bias[...].reshape(1, model)
    for task in range(tasks):
        for row in range(0, rows, 2):
            value = tokens[task, row : row + 2].astype(f32).reshape(2 * width, model)
            low = (normalize(value)[0] * scale + shift).astype(bf16)
            normal[task, row : row + 2] = low.reshape(2, width, model)
            start = (task * (rows // 2) + row // 2) * (width // 2)
            pooled[start : start + width // 2, :] = dot(matrix, low).astype(bf16)


def edge_kernel(normal, to_core, to_far):
    tasks, rows = normal.shape[:2]
    core_row, far_row, _, _ = neighbours(rows)
    for task in range(tasks):
        to_core[task, 0] = normal[task, core_row]
        to_far[task, 0] = normal[task, far_row]


def clear_guards(wide):
    blocks, lines, length, lanes = wide.shape
    zero = jnp.zeros((blocks, lines, GUARD, lanes), wide.dtype)
    wide[:, :, 0:GUARD, :] = zero
    wide[:, :, length - GUARD : length, :] = zero


def put_line(wide, line, value):
    for block in range(wide.shape[0]):
        wide[block, line, GUARD : GUARD + value.shape[0], :] = value[
            :, block * LANES : (block + 1) * LANES
        ]


def wide_scratch(lines, width, model):
    return pltpu.VMEM((model // LANES, lines, width + 2 * GUARD, LANES), f32)


def query_kernel(normal, from_core, from_far, taps, weight, extended, conv, queries, wide):
    tasks, rows, width, model = normal.shape
    clear_guards(wide)
    lines = rows + 2
    _, _, core_line, far_line = neighbours(rows)
    for task in range(tasks):
        extended[task, core_line] = from_core[task, 0]
        extended[task, far_line] = (from_far[task, 0].astype(f32) * far_weight()).astype(bf16)
        for row in range(rows):
            extended[task, row + 1] = normal[task, row]
        for line in range(lines):
            put_line(wide, task * lines + line, extended[task, line].astype(f32))

    def body(step, carry):
        task = step // (model // LANES)
        block = step % (model // LANES)
        lanes = pl.ds(pl.multiple_of(block * LANES, LANES), LANES)
        for row in range(rows):
            for start in range(0, width, 16):
                total = jnp.zeros((16, LANES), f32)
                for a in range(3):
                    for b in range(3):
                        at = GUARD - 1 + b + start
                        total = total + taps[a, b, lanes][None, :] * wide[
                            block, task * lines + row + a, at : at + 16, :
                        ]
                conv[task, row, start : start + 16, lanes] = total.astype(bf16)
        return carry

    lax.fori_loop(0, tasks * (model // LANES), body, 0)
    product = dot(flat(conv), weight[...]).astype(bf16)
    scaled = product * jnp.asarray(HALF**-0.5, bf16)
    queries[...] = scaled.reshape(queries.shape)


def half_mask(shape, side):
    lane = lax.broadcasted_iota(jnp.int32, shape, 1)
    return (lane < HALF) if side == 0 else (lane >= HALF)


def small_lane(shape):
    return lax.broadcasted_iota(jnp.int32, shape, 1) & (HALF - 1)


def pieces(value):
    high = value.astype(bf16).astype(f32)
    middle = (value - high).astype(bf16).astype(f32)
    return high, middle, value - high - middle


def marked(lead, value, shape):
    lane = small_lane(shape)
    high, middle, low = pieces(value)
    rest = jnp.where(lane == 1, high, jnp.where(lane == 2, middle, jnp.where(lane == 3, low, 0.0)))
    return jnp.where(lane == 0, lead, rest).astype(bf16)


def project(offsets, blocks, start, shape, height, valid_width, weights, targets):
    rows, width = shape
    pooled_rows = rows // 2
    me = lax.axis_index("rows")
    key_weight, value_weight = weights
    keys, values, extra = targets
    cells = blocks[0].shape[0]
    for position, offset in enumerate(offsets):
        part = slice(start + position * cells, start + (position + 1) * cells)
        block = blocks[position][...]
        keys[part, :] = dot(block, key_weight[...]).astype(bf16)
        values[part, :] = dot(block, value_weight[...]).astype(bf16)
        cell = lax.broadcasted_iota(jnp.int32, (cells, LANES), 0)
        col = cell & (width // 2 - 1)
        row = (cell // (width // 2)) % pooled_rows + (me ^ offset) * pooled_rows
        good = (2 * row < height) & (2 * col < valid_width)
        lane = small_lane((cells, LANES))
        ones = jnp.where(lane < 4, 1.0, 0.0)
        extra[part, :] = jnp.where(lane == 0, jnp.where(good, 0.0, -1e30), ones).astype(bf16)


def bound_scores(query_pair, key_pair, known):
    shape = query_pair.shape
    across = lax.broadcasted_iota(jnp.int32, (LANES, LANES), 0) < HALF
    over = lax.broadcasted_iota(jnp.int32, (LANES, LANES), 1) >= HALF
    swap = jnp.where(across == over, 1.0, 0.0).astype(bf16)
    key_all = key_pair.astype(f32)
    largest = jnp.max(dot((key_all * key_all).astype(bf16), swap), axis=0, keepdims=True)
    if known is not None:
        largest = jnp.maximum(largest, known)
    query_all = query_pair.astype(f32)
    query_norms = dot((query_all * query_all).astype(bf16), swap)
    bound = 1.02 * jnp.sqrt(query_norms * largest)
    small = small_lane(shape)
    mark = jnp.where(small == 0, 1.0, jnp.where(small == 1, -bound, 0.0)).astype(bf16)
    bounded = []
    bounds = []
    for side in range(2):
        query = jnp.where(half_mask(shape, side), query_pair, mark)
        bounded.append(query)
        lane = lax.broadcasted_iota(jnp.int32, (8, LANES), 1)
        chosen = jnp.where(lane == (1 - side) * HALF + 1, 1.0, 0.0).astype(bf16)
        bounds.append(-dot(chosen, query, NT)[0:1])
    return bounded, bounds, largest


def mix(query, side, keys, values, extra, lanes, starts, block):
    total = None
    for start in starts:
        part = pl.ds(start, block)
        half = half_mask((block, LANES), side)
        extras = extra[part, :]
        scores = dot(jnp.where(half, keys[part, lanes], extras), query, NT)
        weights = jnp.exp(scores).astype(bf16)
        mixture = dot(jnp.where(half, values[part, lanes], extras), weights, TN)
        total = mixture if total is None else total + mixture
    return total


def near_project_kernel(
    offsets, shape, heights, widths, first, second, key_weight, value_weight, keys, values, extra
):
    project(
        offsets, (first, second), 0, shape, heights[0], widths[0], (key_weight, value_weight),
        (keys, values, extra),
    )


def near_kernel(keys, values, extra, queries, sums, bounds, largest):
    key_count = keys.shape[0]

    def body(pair, carry):
        lanes = pl.ds(pl.multiple_of(pair * LANES, LANES), LANES)
        bounded, rows, norms = bound_scores(queries[:, lanes], keys[:, lanes], None)
        largest[pair] = norms
        for side in range(2):
            bounds[2 * pair + side] = rows[side]
            sums[2 * pair + side] = mix(
                bounded[side], side, keys, values, extra, lanes, (0,), key_count
            )
        return carry

    lax.fori_loop(0, HEADS // 2, body, 0, unroll=True)


def attend_kernel(order, *refs):
    refs = list(refs)
    heights, widths = refs[:2]
    del refs[:2]
    near = refs[:6]
    del refs[:6]
    pooled = refs[: len(order) - 2]
    del refs[: len(order) - 2]
    (key_weight, value_weight, queries, tokens, out_weight, out_bias, gain, bias,
     keys, values, extra, attended, middle, normal, to_core, to_far, marks, square,
     sums, totals) = refs
    near_keys, near_values, near_extra, near_sums, near_bounds, near_largest = near
    tasks, rows, width, model = tokens.shape
    me = lax.axis_index("rows")
    height, valid_width = heights[0], widths[0]
    known = near_keys.shape[0]
    keys[0:known, :] = near_keys[...]
    values[0:known, :] = near_values[...]
    extra[0:known, :] = near_extra[...]
    project(
        order[2:], pooled, known, (rows, width), height, valid_width, (key_weight, value_weight),
        (keys, values, extra),
    )
    query_count = queries.shape[0]
    key_count = keys.shape[0]
    block = known
    rest = (key_count - known) // block
    together = max(k for k in (1, 2, 3, 4) if rest % k == 0)
    steps = rest // together

    def body(pair, carry):
        lanes = pl.ds(pl.multiple_of(pair * LANES, LANES), LANES)
        query_pair = queries[:, lanes]
        shape = query_pair.shape
        bounded, bounds, _ = bound_scores(query_pair, keys[known:, lanes], near_largest[pair])

        def some(step):
            starts = [
                pl.multiple_of(known + (step * together + k) * block, block) for k in range(together)
            ]
            return [
                mix(bounded[side], side, keys, values, extra, lanes, starts, block)
                for side in range(2)
            ]

        first = some(0)
        for side in range(2):
            scale = jnp.exp(near_bounds[2 * pair + side] - bounds[side])
            sums[side] = first[side] + near_sums[2 * pair + side] * scale
        if steps > 1:

            def more(step, carry):
                for side, total in enumerate(some(step)):
                    sums[side] += total
                return carry

            lax.fori_loop(1, steps, more, 0)
        for side in range(2):
            totals[side : side + 1, :] = bounds[side]
        at = [(1 - side) * HALF + 1 for side in range(2)]
        least = jnp.minimum(
            jnp.min(sums[0, at[0] : at[0] + 1, :]), jnp.min(sums[1, at[1] : at[1] + 1, :])
        )

        @pl.when(jnp.logical_not(least > 1e-25))
        def _():
            lead = jnp.where(small_lane(shape) == 0, 1.0, 0.0).astype(bf16)
            for side in range(2):
                query = jnp.where(half_mask(shape, side), query_pair, lead)

                def scores_of(step):
                    part = pl.ds(pl.multiple_of(step * LANES, LANES), LANES)
                    half = half_mask((LANES, LANES), side)
                    extras = extra[part, :]
                    value = jnp.where(half, values[part, lanes], extras)
                    return dot(jnp.where(half, keys[part, lanes], extras), query, NT), value

                def highest(step, peak):
                    scores, _ = scores_of(step)
                    return jnp.maximum(peak, jnp.max(scores, axis=0, keepdims=True))

                start = jnp.full((1, query_count), -jnp.inf, f32)
                peak = lax.fori_loop(0, key_count // LANES, highest, start)
                totals[side : side + 1, :] = peak
                sums[side] = jnp.zeros((LANES, query_count), f32)

                def add(step, carry):
                    scores, value = scores_of(step)
                    weights = jnp.exp(scores - totals[side : side + 1, :]).astype(bf16)
                    sums[side] += dot(value, weights, TN)
                    return carry

                lax.fori_loop(0, key_count // LANES, add, 0)

        both = []
        row = lax.broadcasted_iota(jnp.int32, (LANES, query_count), 0)
        small = row & (HALF - 1)
        for side in range(2):
            mixture = sums[side]
            total = mixture[at[side] : at[side] + 1]
            high, middle_part, low = pieces(-(totals[side : side + 1, :] + jnp.log(total)))
            mark = jnp.where(
                small == 0,
                1.0,
                jnp.where(
                    small == 1,
                    high,
                    jnp.where(small == 2, middle_part, jnp.where(small == 3, low, 0.0)),
                ),
            )
            inside = (row < HALF) if side == 0 else (row >= HALF)
            across = jnp.where(inside, mixture / total, mark).T
            marks[2 * pair + side] = jnp.where(
                half_mask(shape, side), query_pair, across.astype(bf16)
            )
            both.append(across)
        chosen = jnp.where(half_mask(shape, 0), both[0], both[1])
        attended[:, lanes] = chosen.astype(bf16)
        return carry

    lax.fori_loop(0, HEADS // 2, body, 0)
    branch = dot(attended[...], out_weight[...]) + out_bias[...].reshape(1, model)
    total = flat(tokens).astype(f32) + branch
    middle[...] = total.reshape(middle.shape)
    normed, _ = normalize(total)
    low = normed * gain[...].reshape(1, model) + bias[...].reshape(1, model)
    normal[...] = low.astype(bf16).reshape(normal.shape)
    core_row, far_row, _, _ = neighbours(rows)
    for task in range(tasks):
        to_core[task, 0] = normal[task, core_row]
        to_far[task, 0] = normal[task, far_row]
    index = lax.broadcasted_iota(jnp.int32, (query_count, 1), 0)
    inside = (me * rows + (index // width) % rows < height) & ((index & (width - 1)) < valid_width)
    square[...] = column_sum(branch * branch * inside.astype(f32))


def put_pieces(grad, first, count, me, held):
    size = grad.shape[0] // PIECES
    for group in range(PIECES):
        piece = grad[group * size : (group + 1) * size]
        slot, owner = divmod(first + group, count)
        store_piece(owner, me, held, slot * size, piece)


def store_piece(owner, me, held, start, piece):
    place = owner ^ me
    place = (place & 1) * (held.shape[0] // 2) + (place >> 1)
    held[place, start : start + piece.shape[0], :] = piece


def part_pieces(held, keep, send):
    half = held.shape[0] // 2
    keep[...] = held[0:half]
    send[...] = held[half:]


def feed_in_kernel(normal, cotangent, up_weight, up_bias, down_weight, lifted, grad_act):
    tasks, rows, width, model = cotangent.shape
    hidden = up_weight.shape[1]
    bias = up_bias[...].reshape(1, hidden)
    fed, grad = flat(normal), flat(cotangent)
    for start in range(0, hidden, model):
        lanes = slice(start, start + model)
        value = (dot(fed, up_weight[:, lanes]) + bias[:, lanes]).astype(bf16)
        lifted[:, :, :, lanes] = value.reshape(tasks, rows, width, model)
        value = dot(grad, down_weight[lanes, :], NT).astype(bf16)
        grad_act[:, :, :, lanes] = value.reshape(tasks, rows, width, model)


def feed_kernel(
    from_core, from_far, lifted, grad_act, up_weight, up_bias, taps,
    active, grad_lifted, grad_band, to_core, to_far, grad_taps, grad_up_bias,
    core_lifted, far_lifted, wide, wide_back, grad_normal,
):
    tasks, rows, width, hidden = lifted.shape
    model = up_weight.shape[0]
    _, has_before, has_after = band_flags()
    lines = rows + 2
    _, _, core_line, far_line = neighbours(rows)
    c1 = 0.7978845608028654
    c2 = c1 * 0.044715

    clear_guards(wide)
    clear_guards(wide_back)
    bias = up_bias[...].reshape(1, hidden)
    for source, weight, target in ((from_core, None, core_lifted), (from_far, far_weight(), far_lifted)):
        value = dot(flat(source), up_weight[...]) + bias
        if weight is not None:
            value = value * weight
        target[...] = value.astype(bf16).reshape(target.shape)

    def across(block, carry):
        lanes = pl.ds(pl.multiple_of(block * LANES, LANES), LANES)
        tap = [[taps[a, b, lanes][None, :] for b in range(3)] for a in range(3)]

        def forth(task, sums9):
            sums9 = list(sums9)
            put_line(wide, task * lines + core_line, core_lifted[task, :, lanes].astype(f32))
            put_line(wide, task * lines + far_line, far_lifted[task, :, lanes].astype(f32))
            for row in range(rows):
                put_line(wide, task * lines + row + 1, lifted[task, row, :, lanes].astype(f32))
            for row in range(rows):
                for start in range(0, width, 16):
                    near = []
                    spread = None
                    for a in range(3):
                        for b in range(3):
                            at = GUARD - 1 + b + start
                            value = wide[0, task * lines + row + a, at : at + 16, :]
                            near.append(value)
                            term = tap[a][b] * value
                            spread = term if spread is None else spread + term
                    squared = spread * spread
                    gate = 0.5 + 0.5 * jnp.tanh(spread * (c1 + c2 * squared))
                    active[task, row, start : start + 16, lanes] = (spread * gate).astype(bf16)
                    slope = gate + spread * (gate - gate * gate) * (2 * c1 + 6 * c2 * squared)
                    grad = grad_act[task, row, start : start + 16, lanes].astype(f32) * slope
                    wide_back[
                        0, task * rows + row, GUARD + start : GUARD + start + 16, :
                    ] = grad
                    for k in range(9):
                        both = near[k] * grad
                        sums9[k] = sums9[k] + (both[0:8] + both[8:16])
            return tuple(sums9)

        zero = jnp.zeros((8, LANES), f32)
        sums9 = lax.fori_loop(0, tasks, forth, (zero,) * 9)
        for k in range(9):
            grad_taps[k // 3, k % 3, lanes] = jnp.sum(sums9[k], axis=0)

        def back(task, total):
            for line in range(lines):
                for start in range(0, width, 16):
                    value = None
                    for a in range(3):
                        if not 0 <= line - a < rows:
                            continue
                        for b in range(3):
                            at = GUARD + 1 - b + start
                            term = tap[a][b] * wide_back[
                                0, task * rows + line - a, at : at + 16, :
                            ]
                            value = term if value is None else value + term
                    if line == 0:
                        value = value * has_before
                    if line == lines - 1:
                        value = value * has_after
                    grad_lifted[task, line, start : start + 16, lanes] = value.astype(bf16)
                    total = total + (value[0:8] + value[8:16])
            return total

        grad_up_bias[0:1, lanes] = column_sum(lax.fori_loop(0, tasks, back, zero))
        return carry

    lax.fori_loop(0, hidden // LANES, across, 0)
    grad = dot(flat(grad_lifted), up_weight[...], NT)
    grad_normal[...] = grad.reshape(grad_normal.shape)
    for task in range(tasks):
        grad_band[task] = grad_normal[task, 1 : rows + 1]
        to_core[task, 0] = grad_normal[task, core_line].astype(bf16)
        to_far[task, 0] = grad_normal[task, far_line].astype(bf16)


def feed_weight_kernel(
    middle_normal, from_core, from_far, active, grad_lifted, cotangent, keep, send, normal, held
):
    tasks, rows, width, model = cotangent.shape
    hidden = active.shape[-1]
    me = lax.axis_index("rows")
    count = lax.axis_size("rows")
    _, _, core_line, far_line = neighbours(rows)
    for task in range(tasks):
        for row in range(rows):
            normal[task, row + 1] = middle_normal[task, row]
        normal[task, core_line] = from_core[task, 0]
        normal[task, far_line] = from_far[task, 0]
    size = hidden // count
    groups = model // size
    columns = hidden // model
    fed, grad_output = flat(normal), flat(cotangent)
    for column in range(columns):
        lanes = slice(column * model, (column + 1) * model)
        grad = grad_lifted[:, :, :, lanes].reshape(-1, model)
        grad_up = dot(fed, grad, TN).astype(bf16)
        act = active[:, :, :, lanes].reshape(-1, model)
        grad_down = dot(act, grad_output, TN).astype(bf16)
        for group in range(groups):
            part = slice(group * size, (group + 1) * size)
            store_piece(group * columns + column, me, held, 0, grad_up[part])
            store_piece(column * groups + group, me, held, size, grad_down[part])
    part_pieces(held, keep, send)


def layer_kernel(
    heights, widths, active, down_weight, down_bias, cotangent, middle, layer_out, sums
):
    tasks, rows, width, model = cotangent.shape
    me = lax.axis_index("rows")
    height, valid_width = heights[0], widths[0]
    zero = jnp.zeros((1, model), f32)
    totals = [zero, zero, zero]
    col = lax.broadcasted_iota(jnp.int32, (width, 1), 0)
    for task in range(tasks):
        branch = dot(flat(active.at[task]), down_weight[...]) + down_bias[...].reshape(1, model)
        for row in range(rows):
            mlp = branch[row * width : (row + 1) * width]
            final = middle[task, row] + mlp
            layer_out[task, row] = final.astype(bf16)
            inside = (col < valid_width) & (me * rows + row < height)
            weight = inside.astype(f32)
            grad = cotangent[task, row].astype(f32)
            for k, value in enumerate((grad, mlp * mlp * weight, final * final * weight)):
                totals[k] = totals[k] + column_sum(value)
    sums[...] = jnp.concatenate([*totals, jnp.zeros((5, model), f32)], axis=0)


def norm_back_kernel(
    grad_band, from_core, from_far, middle, cotangent, gain, out_weight, attended,
    grad_middle, grad_marks, grad_low, sums,
):
    tasks, rows, width, model = cotangent.shape
    scale = gain[...].reshape(1, model)
    parts = []
    odd = (lax.axis_index("rows") & 1).astype(f32)
    for task in range(tasks):
        core = from_core[task, 0].astype(f32)
        far = from_far[task, 0].astype(f32)
        for row in range(rows):
            grad = grad_band[task, row]
            if row == 0:
                grad = grad + core * odd + far * (1.0 - odd)
            if row == rows - 1:
                grad = grad + far * odd + core * (1.0 - odd)
            parts.append(grad)
    grad_input = jnp.concatenate(parts, axis=0)
    normed, inverse = normalize(flat(middle))
    total = flat(cotangent).astype(f32) + normalize_back(grad_input, scale, normed, inverse)
    grad_middle[...] = total.reshape(grad_middle.shape)
    sums[0:1, :] = column_sum(grad_input * normed)
    sums[1:2, :] = column_sum(grad_input)
    sums[2:3, :] = column_sum(total)
    sums[3:8, :] = jnp.zeros((5, model), f32)
    grad_branch = total.astype(bf16)
    mixture = attended[...]
    grad_low[...] = grad_branch
    grad_attended = dot(grad_branch, out_weight[...], NT).astype(bf16)
    shape = (mixture.shape[0], LANES)
    for pair in range(HEADS // 2):
        lanes = slice(pair * LANES, (pair + 1) * LANES)
        grad_two = grad_attended[:, lanes]
        both = grad_two.astype(f32) * mixture[:, lanes].astype(f32)
        for side in range(2):
            half = half_mask(shape, side)
            inner = jnp.sum(jnp.where(half, both, 0.0), axis=-1, keepdims=True)
            grad_marks[2 * pair + side] = jnp.where(half, grad_two, marked(0.0, -inner, shape))


def attend_back_kernel(
    marks, grad_marks, keys, values, extra, grad_queries, grad_keys, grad_values,
    total, query_zero, grad_zero,
):
    key_count = keys.shape[0]
    query_count = grad_marks.shape[1]
    block = min(1024, key_count)
    shape = (query_count, LANES)
    for side in range(2):
        half = half_mask(shape, side)
        zero = jnp.zeros(shape, bf16)
        part = slice(side * query_count, (side + 1) * query_count)
        query_zero[part, :] = jnp.where(half, marks[side], zero)
        grad_zero[part, :] = jnp.where(half, grad_marks[side], zero)

    def body(place, carry):
        part = pl.ds(pl.multiple_of(place * block, block), block)
        key_pair, value_pair, extras = keys[part, :], values[part, :], extra[part, :]
        lows, grads = [], []
        query_part = None
        for side in range(2):
            half = half_mask((block, LANES), side)
            scores = dot(jnp.where(half, key_pair, extras), marks[side], NT)
            grad_prob = dot(jnp.where(half, value_pair, extras), grad_marks[side], NT)
            probability = jnp.exp(scores)
            grad = (probability * grad_prob).astype(bf16)
            grads.append(grad)
            lows.append(probability.astype(bf16))
            one = dot(jnp.where(half, key_pair, jnp.zeros((block, LANES), bf16)), grad, TN)
            query_part = one if query_part is None else query_part + one
        grad_values[part, :] = dot(jnp.concatenate(lows, axis=1), grad_zero[...]).astype(bf16)
        grad_keys[part, :] = dot(jnp.concatenate(grads, axis=1), query_zero[...]).astype(bf16)

        @pl.when(place == 0)
        def _():
            total[...] = query_part

        @pl.when(place > 0)
        def _():
            total[...] += query_part

        return carry

    lax.fori_loop(0, key_count // block, body, 0)
    grad_queries[...] = (total[...] * HALF**-0.5).T.astype(bf16)


def side_by_side(refs):
    return jnp.concatenate([ref[...] for ref in refs], axis=1)


def conv_back_kernel(*refs):
    pairs = HEADS // 2
    grad_queries = refs[:pairs]
    query_weight, grad_conv, to_core, to_far = refs[pairs:]
    tasks, rows = grad_conv.shape[:2]
    grad = dot(side_by_side(grad_queries), query_weight[...], NT).astype(bf16)
    grad_conv[...] = grad.reshape(grad_conv.shape)
    core_row, far_row, _, _ = neighbours(rows)
    for task in range(tasks):
        to_core[task, 0] = grad_conv[task, core_row]
        to_far[task, 0] = grad_conv[task, far_row]


def pool_back_kernel(order, *refs):
    pairs = HEADS // 2
    grad_keys, grad_values = refs[:pairs], refs[pairs : 2 * pairs]
    key_weight, value_weight, keep, send = refs[2 * pairs :]
    cells = keep.shape[1]
    both = jnp.concatenate([key_weight[...], value_weight[...]], axis=1)
    for position, offset in enumerate(order):
        part = slice(position * cells, (position + 1) * cells)
        grads = jnp.concatenate([ref[part, :] for ref in (*grad_keys, *grad_values)], axis=1)
        target = send if offset & 1 else keep
        target[offset >> 1] = dot(grads, both, NT).astype(bf16)


def pair_weights(order, pooled, conv, queries, keys, values):
    cells = pooled[0].shape[0]
    total = None
    for position in range(len(order)):
        part = slice(position * cells, (position + 1) * cells)
        grads = jnp.concatenate([ref[part, :] for ref in (*keys, *values)], axis=1)
        value = dot(pooled[position][...], grads, TN)
        total = value if total is None else total + value
    grad_query = dot(flat(conv), side_by_side(queries), TN)
    return jnp.concatenate([grad_query, total], axis=1).astype(bf16)


def weight_kernel(order, *refs):
    refs = list(refs)
    heights, widths = refs[:2]
    del refs[:2]
    pooled = refs[: len(order)]
    del refs[: len(order)]
    pairs = HEADS // 2
    queries, keys, values = refs[:pairs], refs[pairs : 2 * pairs], refs[2 * pairs : 3 * pairs]
    del refs[: 3 * pairs]
    (pool_keep, pool_send, conv, extended, grad_conv, taps, gain, bias, attended, grad_low, square, back_sums,
     feed_sums, hidden_taps, up_bias, keep, send, wide, rows_of, held) = refs
    tasks, rows, width, model = grad_conv.shape
    count = len(order)
    lines = rows + 2
    me, has_before, has_after = band_flags()
    size = keep.shape[1] - 16
    model_grads = pair_weights(order, pooled, conv, queries, keys, values)
    for which in range(3):
        grad = model_grads[:, which * model : (which + 1) * model]
        put_pieces(grad, which * PIECES, count, me, held)
    grad_out = dot(attended[...], grad_low[...], TN)
    put_pieces(grad_out.astype(bf16), 3 * PIECES, count, me, held)
    pool_sum = jnp.zeros((1, model), f32)
    pool_dot = jnp.zeros((1, model), f32)
    for position, offset in enumerate(order):
        source = pool_send if offset & 1 else pool_keep
        grad = source[offset >> 1].astype(f32)
        pool_sum = pool_sum + column_sum(grad)
        pool_dot = pool_dot + column_sum(grad * pooled[position][...].astype(f32))

    clear_guards(wide)
    for task in range(tasks):
        for line in range(lines):
            put_line(wide, task * lines + line, extended[task, line].astype(f32))

    def across(block, carry):
        lanes = pl.ds(pl.multiple_of(block * LANES, LANES), LANES)

        def one_task(task, sums9):
            sums9 = list(sums9)
            for row in range(rows):
                for start in range(0, width, 16):
                    grad = grad_conv[task, row, start : start + 16, lanes].astype(f32)
                    for k in range(9):
                        at = GUARD - 1 + k % 3 + start
                        both = grad * wide[block, task * lines + row + k // 3, at : at + 16, :]
                        sums9[k] = sums9[k] + (both[0:8] + both[8:16])
            return tuple(sums9)

        sums9 = lax.fori_loop(
            0, tasks, one_task, tuple(jnp.zeros((8, LANES), f32) for _ in range(9))
        )
        for k in range(9):
            rows_of[2 + k : 3 + k, lanes] = column_sum(sums9[k])
        return carry

    lax.fori_loop(0, model // LANES, across, 0)

    shift = bias[...].reshape(1, model)
    zero = jnp.zeros((1, model), f32)
    conv_dot, conv_sum = zero, zero
    for row in range(rows):
        line = grad_conv[0, row].astype(f32)
        for task in range(1, tasks):
            line = line + grad_conv[task, row].astype(f32)
        full = column_sum(line)
        by_col = (full - line[0:1], full, full - line[width - 1 : width])
        for a in range(3):
            for b in range(3):
                value = by_col[b]
                if a == 0 and row == 0:
                    value = value * has_before
                if a == 2 and row == rows - 1:
                    value = value * has_after
                conv_sum = conv_sum + taps[a, b].reshape(1, model) * value
    for k in range(9):
        conv_dot = conv_dot + taps[k // 3, k % 3].reshape(1, model) * rows_of[2 + k : 3 + k, :]
    grad_bias = conv_sum + pool_sum
    grad_gain = (conv_dot + pool_dot - shift * grad_bias) / gain[...].reshape(1, model)
    rows_of[0:1, :] = grad_gain
    rows_of[1:2, :] = grad_bias
    rows_of[11:12, :] = back_sums[2:3, :]
    rows_of[12:14, :] = back_sums[0:2, :]
    rows_of[14:15, :] = feed_sums[0:1, :]
    rows_of[15:16, :] = square[...]
    rows_of[16:18, :] = feed_sums[1:3, :]
    in_rows = jnp.clip(heights[0] - me * rows, 0, rows)
    in_cols = jnp.clip(widths[0], 0, width)
    cells_in = (tasks * in_rows * in_cols).astype(f32)
    rows_of[18:19, :] = jnp.full((1, model), cells_in, f32)
    parts = up_bias.shape[1] // model
    for part in range(parts):
        rows_of[19 + part : 20 + part, :] = up_bias[:, part * model : (part + 1) * model]
        for k in range(9):
            rows_of[19 + parts * (k + 1) + part : 20 + parts * (k + 1) + part, :] = hidden_taps[
                k // 3, k % 3, part * model : (part + 1) * model
            ].reshape(1, model)
    used = 19 + 10 * parts
    rows_of[used:SMALL, :] = jnp.zeros((SMALL - used, model), f32)
    group = SMALL // count
    for owner in range(count):
        value = rows_of[owner * group : (owner + 1) * group, :]
        if group < 8:
            value = jnp.concatenate([value, jnp.zeros((8 - group, model), f32)], axis=0)
        high = value.astype(bf16)
        low = (value - high.astype(f32)).astype(bf16)
        store_piece(owner, me, held, size, jnp.concatenate([high, low], axis=0))
    part_pieces(held, keep, send)


def last_kernel(
    grad_conv, from_core, from_far, taps, tokens, gain, grad_middle, pool, input_grad, wide
):
    tasks, rows, width, model = tokens.shape
    lines = rows + 2
    pooled_rows = rows // 2
    clear_guards(wide)
    _, _, core_line, far_line = neighbours(rows)
    for task in range(tasks):
        put_line(wide, task * lines + core_line, from_core[task, 0].astype(f32))
        put_line(wide, task * lines + far_line, from_far[task, 0].astype(f32) * far_weight())
        for row in range(rows):
            put_line(wide, task * lines + row + 1, grad_conv[task, row].astype(f32))
    pooled = pool[...].reshape(tasks, pooled_rows, width // 2, model)
    spread_matrix = pool_matrix(width)[:, 0:width]

    def body(step, carry):
        task = step // (model // LANES)
        block = step % (model // LANES)
        lanes = pl.ds(pl.multiple_of(block * LANES, LANES), LANES)
        for row in range(rows):
            for start in range(0, width, 16):
                total = jnp.zeros((16, LANES), f32)
                for a in range(3):
                    for b in range(3):
                        at = GUARD + 1 - b + start
                        total = total + taps[a, b, lanes][None, :] * wide[
                            block, task * lines + row + 2 - a, at : at + 16, :
                        ]
                input_grad[task, row, start : start + 16, lanes] = total
        return carry

    lax.fori_loop(0, tasks * (model // LANES), body, 0)
    scale = gain[...].reshape(1, model)
    for task in range(tasks):
        for row in range(rows):
            grad = input_grad[task, row] + dot(spread_matrix, pooled[task, row // 2], TN)
            normed, inverse = normalize(tokens[task, row].astype(f32))
            input_grad[task, row] = grad_middle[task, row] + normalize_back(grad, scale, normed, inverse)


def add_blocks(values):
    total = values[0].astype(f32)
    for other in values[1:]:
        total = total + other.astype(f32)
    return total


def put_sum(out, start, values, small):
    total = add_blocks(values)
    size = total.shape[0]
    if not small:
        out[start : start + size, :] = total.astype(bf16)
        return
    size -= 16
    value = total[size : size + 8] + total[size + 8 : size + 16]
    high = value.astype(bf16)
    low = (value - high.astype(f32)).astype(bf16)
    out[start : start + size, :] = total[0:size].astype(bf16)
    out[start + size : start + size + 16, :] = jnp.concatenate([high, low], axis=0)


def combine(arrays, small):
    blocks, size, model = arrays[0].shape

    def kernel(*refs):
        ins, outs = refs[: len(arrays)], refs[len(arrays) :]
        for block, out in enumerate(outs):
            put_sum(out, 0, [x[block] for x in ins], small)

    return call("combine", kernel, [((size, model), bf16)] * blocks, list(arrays))


def stack(values):
    size, model = values[0].shape

    def kernel(*refs):
        for place, value in enumerate(refs[:-1]):
            refs[-1][place] = value[...]

    return call("stack", kernel, [((len(values), size, model), bf16)], list(values))[0]


def exchange(value, axis, mask):
    count = lax.axis_size(axis)
    return lax.ppermute(value, axis, [(i, i ^ mask) for i in range(count)])


def far_masks():
    return list(range(2, lax.axis_size("rows"), 2))


def once(value, *earlier):
    return lax.optimization_barrier((value, earlier))[0]


def far_rows(value):
    return [exchange(value, "rows", mask) for mask in far_masks()]


def all_images(value):
    return [exchange(value, "batch", mask) for mask in range(1, lax.axis_size("batch"))]


def add_images(own, arrived, small):
    (total,) = combine([x[None] for x in [own, *arrived]], small)
    return total


def unpack_feed_kernel(count, *refs):
    even, odd, grad_up, grad_down = refs
    blocks = [half.at[place] for half in (even, odd) for place in range(count // 2)]
    me = lax.axis_index("rows")
    model, hidden = grad_up.shape
    size = hidden // count
    columns = hidden // model
    for j in range(count):
        owner = blocks_owner(j, count, me)
        block = blocks[j]
        up = block[0:size, :].astype(f32)
        place = owner // columns
        col = owner % columns
        grad_up[
            pl.ds(pl.multiple_of(place * size, size), size),
            pl.ds(pl.multiple_of(col * model, model), model),
        ] = up
        grad_down[pl.ds(pl.multiple_of(owner * size, size), size), :] = block[
            size : 2 * size, :
        ].astype(f32)


def blocks_owner(j, count, me):
    half = count // 2
    offset = 2 * j if j < half else 2 * (j - half) + 1
    return me ^ offset


def unpack_late_kernel(count, *refs):
    blocks = refs[:count]
    (grad_query, grad_key, grad_value, grad_out, norm1_gain, norm1_bias, query_taps, out_bias,
     norm2_gain, norm2_bias, up_bias, hidden_taps, down_bias, stats, weights, rows_of) = refs[count:]
    me = lax.axis_index("rows")
    model = grad_query.shape[0]
    piece = model // PIECES
    size = blocks[0].shape[0] - 16
    group = SMALL // count
    for j in range(count):
        owner = blocks_owner(j, count, me)
        block = blocks[j][...].astype(f32)
        for slot in range(size // piece):
            start = pl.multiple_of((slot * count + owner) * piece, piece)
            weights[pl.ds(start, piece), :] = block[slot * piece : (slot + 1) * piece]
        rows_of[owner] = block[size : size + 8] + block[size + 8 : size + 16]
    for which, out in enumerate((grad_query, grad_key, grad_value, grad_out)):
        out[...] = weights[which * model : (which + 1) * model, :]

    def line(k):
        return rows_of[k // group, k % group, :]

    norm1_gain[...] = line(0)
    norm1_bias[...] = line(1)
    for k in range(9):
        query_taps[k // 3, k % 3, :] = line(2 + k)
    out_bias[...] = line(11)
    norm2_gain[...] = line(12)
    norm2_bias[...] = line(13)
    down_bias[...] = line(14)
    parts = up_bias.shape[0] // model
    for part in range(parts):
        lanes = slice(part * model, (part + 1) * model)
        up_bias[lanes] = line(19 + part)
        for k in range(9):
            hidden_taps[k // 3, k % 3, lanes] = line(19 + parts * (k + 1) + part)
    cells = line(18).reshape(1, model)[:, 0:1]
    row = lax.broadcasted_iota(jnp.int32, (1, LANES), 1)
    value = jnp.zeros((1, LANES), f32)
    for k in range(3):
        total = jnp.sum(line(15 + k).reshape(1, model), axis=-1, keepdims=True)
        value = jnp.where(row == k, jnp.sqrt(total / (cells * model)), value)
    stats[...] = value.reshape(LANES)[0:3]


def local(
    tokens,
    norm1_gain,
    norm1_bias,
    query_taps,
    query_weight,
    key_weight,
    value_weight,
    out_weight,
    out_bias,
    norm2_gain,
    norm2_bias,
    up_weight,
    up_bias,
    hidden_taps,
    down_weight,
    down_bias,
    cotangent,
    heights,
    widths,
):
    shape = tokens.shape
    tokens, cotangent = tokens[0], cotangent[0]
    tasks, rows, width, model = tokens.shape
    hidden = up_weight.shape[1]
    count = lax.axis_size("rows")
    cells = tasks * (rows // 2) * (width // 2)
    key_count = count * cells
    lines = rows + 2
    token_count = tasks * rows * width
    line = (tasks, 1, width, model)

    def swap_lines(lines_out):
        to_core, to_far = lines_out
        across = [p for i in range(1, count, 2) for p in ((i, (i + 1) % count), ((i + 1) % count, i))]
        return exchange(to_core, "rows", 1), lax.ppermute(to_far, "rows", across)

    normal_one, pooled = call(
        "first_norm",
        first_norm_kernel,
        [(tokens.shape, bf16), ((cells, model), bf16)],
        [hbm(x) for x in (tokens, norm1_gain, norm1_bias)],
        limit=8,
    )
    far = far_masks()
    order = [0, 1, *far, *[mask + 1 for mask in far]]
    arrived = far_rows(pooled)
    edge = call("edge", edge_kernel, [(line, bf16), (line, bf16)], [normal_one])
    edge = swap_lines(edge)
    swapped = exchange(pooled, "rows", 1)
    near_count = 2 * cells
    near = call(
        "near_project",
        lambda *refs: near_project_kernel(order[:2], (rows, width), *refs),
        [((near_count, model), bf16), ((near_count, model), bf16), ((near_count, LANES), bf16)],
        [heights, widths, pooled, swapped, hbm(key_weight), hbm(value_weight)],
        smem=2,
        limit=12,
    )
    edge = once(edge, *near)
    extended, conv, queries = call(
        "query_conv",
        query_kernel,
        [
            ((tasks, lines, width, model), bf16), (tokens.shape, bf16), ((token_count, model), bf16),
        ],
        [normal_one, *edge, hbm(query_taps), hbm(query_weight)],
        scratch=[wide_scratch(tasks * lines, width, model)],
        us=2,
        limit=12,
    )
    near += call(
        "near",
        near_kernel,
        [
            ((HEADS, LANES, token_count), f32), ((HEADS, 1, token_count), f32),
            ((HEADS // 2, 1, LANES), f32),
        ],
        [*near, queries],
        us=4,
        limit=20,
    )
    arrived = once(arrived, *near)
    blocks = [pooled, swapped, *arrived, *[exchange(x, "rows", 1) for x in arrived]]

    (keys, values, extra, attended, middle, normal_two, to_core, to_far, marks, square) = call(
        "attend",
        lambda *refs: attend_kernel(order, *refs),
        [
            ((key_count, model), bf16), ((key_count, model), bf16), ((key_count, LANES), bf16),
            ((token_count, model), bf16), (tokens.shape, f32),
            (tokens.shape, bf16), (line, bf16), (line, bf16), ((HEADS, token_count, LANES), bf16), ((1, model), f32),
        ],
        [heights, widths, *near, *blocks[2:], hbm(key_weight), hbm(value_weight), queries,
         *[hbm(x) for x in (tokens, out_weight, out_bias, norm2_gain, norm2_bias)]],
        smem=2,
        scratch=[pltpu.VMEM((2, LANES, token_count), f32), pltpu.VMEM((8, token_count), f32)],
        us=18,
        limit=24,
    )
    next_lines = swap_lines((to_core, to_far))
    band = (tasks, rows, width, hidden)
    lifted, grad_act = call(
        "feed_in",
        feed_in_kernel,
        [(band, bf16), (band, bf16)],
        [normal_two, *[hbm(x) for x in (cotangent, up_weight, up_bias, down_weight)]],
        us=4,
        limit=20,
    )
    next_lines = once(next_lines, grad_act)
    (active, grad_lifted, grad_band, to_core, to_far, grad_hidden_taps, grad_up_bias) = call(
        "feed",
        feed_kernel,
        [
            (band, bf16), ((tasks, lines, width, hidden), bf16), (tokens.shape, f32), (line, bf16),
            (line, bf16), ((3, 3, hidden), f32), ((1, hidden), f32),
        ],
        [*next_lines, lifted, grad_act, *[hbm(x) for x in (up_weight, up_bias, hidden_taps)]],
        scratch=[
            pltpu.VMEM((tasks, width, hidden), bf16),
            pltpu.VMEM((tasks, width, hidden), bf16),
            wide_scratch(tasks * lines, width, LANES),
            wide_scratch(tasks * rows, width, LANES),
            pltpu.VMEM((tasks, lines, width, model), f32),
        ],
        us=24,
        limit=24,
    )
    edge = swap_lines((to_core, to_far))
    feed_keep, feed_send = call(
        "feed_weights",
        feed_weight_kernel,
        [((count // 2, 2 * hidden // count, model), bf16)] * 2,
        [normal_two, *next_lines, active, grad_lifted, hbm(cotangent)],
        scratch=[
            pltpu.VMEM((tasks, lines, width, model), bf16),
            pltpu.VMEM((count, 2 * hidden // count, model), bf16),
        ],
        us=5,
        limit=24,
    )
    edge = once(edge, feed_keep)
    feed_swapped = exchange(once(feed_send, edge), "rows", 1)
    piece = model // PIECES
    grad_middle, grad_marks, grad_low, back_sums = call(
        "norm_back",
        norm_back_kernel,
        [
            (tokens.shape, f32), ((HEADS, token_count, LANES), bf16), ((token_count, model), bf16),
            ((8, model), f32),
        ],
        [
            grad_band, *edge,
            middle, *[hbm(x) for x in (cotangent, norm2_gain, out_weight)], attended,
        ],
        us=4,
        limit=20,
    )

    def attend_back(pair, tie):
        inputs = [marks, grad_marks, keys, values, extra]
        inputs = once(inputs, *tie)

        def of_heads(x):
            return pl.BlockSpec((2, x.shape[1], LANES), lambda i: (pair, 0, 0))

        def of_lanes(x):
            return pl.BlockSpec((x.shape[0], LANES), lambda i: (0, pair))

        whole = pl.BlockSpec((key_count, LANES), lambda i: (0, 0))
        outs = [(token_count, LANES), (key_count, LANES), (key_count, LANES)]
        return pl.pallas_call(
            attend_back_kernel,
            name="attend_back",
            grid=(1,),
            out_shape=[jax.ShapeDtypeStruct(shape, bf16) for shape in outs],
            in_specs=[*[of_heads(x) for x in inputs[0:2]], *[of_lanes(x) for x in inputs[2:4]], whole],
            out_specs=[pl.BlockSpec(shape, lambda i: (0, 0)) for shape in outs],
            scratch_shapes=[
                pltpu.VMEM((LANES, token_count), f32),
                pltpu.VMEM((2 * token_count, LANES), bf16),
                pltpu.VMEM((2 * token_count, LANES), bf16),
            ],
            compiler_params=pltpu.CompilerParams(vmem_limit_bytes=20 << 20),
            cost_estimate=cost(11),
        )(*inputs)

    feed_blocks = combine(once([feed_keep, feed_swapped], grad_marks), False)
    feed_arrived = [exchange(feed_blocks[mask >> 1], "rows", mask) for mask in far]
    back = [attend_back(0, feed_blocks)]
    feed_arrived = once(feed_arrived, *back[0])
    feed_own = add_images(feed_blocks[0], feed_arrived, False)
    hop = 1
    while hop < lax.axis_size("batch"):
        feed_arrived = exchange(feed_own, "batch", hop)
        if len(back) < HEADS // 2:
            back.append(attend_back(len(back), [*back[-1], feed_own]))
        feed_arrived = once(feed_arrived, *back[-1])
        feed_own = add_images(feed_own, [feed_arrived], False)
        hop *= 2
    while len(back) < HEADS // 2:
        back.append(attend_back(len(back), back[-1]))
    grads = [part for which in range(3) for part in [x[which] for x in back]]
    pairs = HEADS // 2
    grad_conv, *edge = call(
        "conv_back",
        conv_back_kernel,
        [(tokens.shape, bf16), (line, bf16), (line, bf16)],
        [*once(grads[:pairs], feed_own), query_weight],
    )
    feed_arrived = far_rows(feed_own)
    edge = swap_lines(edge)
    pool_keep, pool_send = call(
        "pool_back",
        lambda *refs: pool_back_kernel(order, *refs),
        [((count // 2, cells, model), bf16)] * 2,
        [*once(grads[pairs:], grad_conv), key_weight, value_weight],
        us=3,
        limit=12,
    )
    layer_out, feed_sums = call(
        "layer",
        layer_kernel,
        [(tokens.shape, bf16), ((8, model), f32)],
        [heights, widths, once(active, pool_keep), *[hbm(x) for x in (down_weight, down_bias, cotangent)], middle],
        smem=2,
        us=3,
        limit=20,
    )
    slots = -(-4 * PIECES // count)
    keep, send = call(
        "weights",
        lambda *refs: weight_kernel(order, *refs),
        [((count // 2, slots * piece + 16, model), bf16)] * 2,
        [
            heights, widths, *blocks, *grads, pool_keep, pool_send, conv, extended, grad_conv,
            query_taps, norm1_gain, norm1_bias, attended, grad_low, square, back_sums, feed_sums,
            grad_hidden_taps, grad_up_bias,
        ],
        smem=2,
        scratch=[
            wide_scratch(tasks * lines, width, model),
            pltpu.VMEM((SMALL, model), f32),
            pltpu.VMEM((count, slots * piece + 16, model), bf16),
        ],
        us=4,
        limit=16,
    )
    feed_arrived, edge = once((feed_arrived, edge), keep)
    send, pool_send = once((send, pool_send), feed_arrived, edge)
    late_swapped = exchange(send, "rows", 1)
    pool_swapped = exchange(pool_send, "rows", 1)
    late_blocks = combine([keep, late_swapped], True)
    late_arrived = [exchange(late_blocks[mask >> 1], "rows", mask) for mask in far]
    pool_blocks = combine([pool_keep, once(pool_swapped, late_blocks)], False)
    feed_even = stack(once([feed_own, *feed_arrived], pool_blocks))
    feed_odd = exchange(feed_even, "rows", 1)
    late_arrived = once(late_arrived, feed_even)
    (late_own,) = combine([x[None] for x in [late_blocks[0], *late_arrived]], True)
    pool_arrived = [exchange(x, "rows", mask) for x, mask in zip(once(pool_blocks[1:], late_own), far)]
    arrived = exchange(late_own, "batch", 1)
    grad_up, grad_down = call(
        "unpack_feed",
        lambda *refs: unpack_feed_kernel(count, *refs),
        [((model, hidden), f32), ((hidden, model), f32)],
        [once(feed_even, late_own), feed_odd],
        us=3,
        limit=12,
    )
    arrived = once(arrived, grad_up)
    hop = 2
    while hop < lax.axis_size("batch"):
        late_own = add_images(late_own, [arrived], True)
        arrived = exchange(late_own, "batch", hop)
        hop *= 2
    pool_arrived = once(pool_arrived, late_own)
    (pool_total,) = combine([x[None] for x in [pool_blocks[0], *pool_arrived]], False)
    (input_grad,) = call(
        "last_norm",
        last_kernel,
        [(tokens.shape, f32)],
        [grad_conv, *edge, query_taps, tokens, norm1_gain, grad_middle, pool_total],
        scratch=[wide_scratch(tasks * lines, width, model)],
        us=5,
        limit=12,
    )
    late_own = add_images(late_own, [once(arrived, input_grad)], True)
    even = [late_own, *far_rows(late_own)]
    odd = [exchange(x, "rows", 1) for x in even]
    vector = ((model,), f32)
    late = call(
        "unpack_late",
        lambda *refs: unpack_late_kernel(count, *refs),
        [((model, model), f32)] * 4
        + [vector, vector, ((3, 3, model), f32), vector, vector, vector, ((hidden,), f32),
           ((3, 3, hidden), f32), vector, ((3,), f32)],
        [*even, *odd],
        scratch=[
            pltpu.VMEM((slots * count * piece, model), f32),
            pltpu.VMEM((count, 8, model), f32),
        ],
        us=2,
        limit=12,
    )
    (grad_query, grad_key, grad_value, grad_out, gain1, bias1, taps1, out_sum, gain2, bias2, up_sum,
     taps2, down_sum, stats) = late
    return (
        layer_out.reshape(shape),
        input_grad.reshape(shape),
        gain1,
        bias1,
        taps1,
        grad_query,
        grad_key,
        grad_value,
        grad_out,
        out_sum,
        gain2,
        bias2,
        grad_up,
        up_sum,
        taps2,
        grad_down,
        down_sum,
        stats,
    )


def solution(mesh):
    band = P("batch", None, "rows", None, None)
    placed = (band, *[P()] * 15, band, P("batch"), P("batch"))
    return jax.shard_map(
        local,
        mesh=mesh,
        in_specs=placed,
        out_specs=(band, band, *[P()] * 16),
        check_vma=False,
    )
```

```python
import jax
import jax.numpy as jnp
from jax import lax
from jax.experimental import pallas as pl
from jax.experimental.pallas import tpu as pltpu
from jax.sharding import PartitionSpec as P

HEADS = 6
LANES = 128
HALF = 64
GUARD = 8
SMALL = 64
PIECES = 8
epsilon = 1e-05
f32 = jnp.float32
bf16 = jnp.bfloat16
NN = (((1,), (0,)), ((), ()))
NT = (((1,), (1,)), ((), ()))
TN = (((0,), (0,)), ((), ()))


def dot(left, right, form=NN):
    return lax.dot_general(left, right, form, preferred_element_type=f32)


def cost(us):
    return pl.CostEstimate(flops=int(us * 1e4), bytes_accessed=int(us * 1e4), transcendentals=0)


def hbm(value):
    return pltpu.with_memory_space_constraint(value, pltpu.HBM)


def in_hbm(shape, dtype):
    return shape, dtype, True


def out_type(shape, dtype, away=False):
    return pltpu.HBM(shape, dtype) if away else jax.ShapeDtypeStruct(shape, dtype)


def call(name, kernel, outs, args, smem=0, scratch=(), us=1, limit=12):
    def whole(shape):
        return pl.BlockSpec(shape, lambda i, k=len(shape): (0,) * k)

    return pl.pallas_call(
        kernel,
        grid=(1,),
        out_shape=tuple(out_type(*x) for x in outs),
        in_specs=[pl.BlockSpec(memory_space=pltpu.SMEM)] * smem
        + [whole(x.shape) for x in args[smem:]],
        out_specs=tuple(whole(x[0]) for x in outs),
        scratch_shapes=list(scratch),
        name=name,
        compiler_params=pltpu.CompilerParams(vmem_limit_bytes=limit << 20),
        cost_estimate=cost(us),
    )(*args)


def normalize(values):
    center = jnp.mean(values, axis=-1, keepdims=True)
    centered = values - center
    inverse = lax.rsqrt(jnp.mean(centered * centered, axis=-1, keepdims=True) + epsilon)
    return centered * inverse, inverse


def normalize_back(grad_output, gain, normed, inverse):
    scaled = grad_output * gain
    return inverse * (
        scaled
        - jnp.mean(scaled, axis=-1, keepdims=True)
        - normed * jnp.mean(scaled * normed, axis=-1, keepdims=True)
    )


def column_sum(values):
    return jnp.sum(values, axis=0, keepdims=True)


def one(ref):
    return ref[...].reshape(1, 1)


def flat(ref):
    value = ref[...]
    return value.reshape(-1, value.shape[-1])


def band_flags():
    me = lax.axis_index("rows")
    count = lax.axis_size("rows")
    return me, (me > 0).astype(f32), (me < count - 1).astype(f32)


def neighbours(rows):
    odd = lax.axis_index("rows") & 1
    even = 1 - odd
    return even * (rows - 1), odd * (rows - 1), even * (rows + 1), odd * (rows + 1)


def far_weight():
    me, has_before, has_after = band_flags()
    return jnp.where((me & 1) == 1, has_after, has_before)


def pool_matrix(width):
    rows = lax.broadcasted_iota(jnp.int32, (width // 2, 2 * width), 0)
    cols = lax.broadcasted_iota(jnp.int32, (width // 2, 2 * width), 1)
    cols = jnp.where(cols >= width, cols - width, cols)
    return jnp.where((cols >> 1) == rows, 0.25, 0.0).astype(bf16)


def first_norm_kernel(tokens, gain, bias, normal, pooled):
    tasks, rows, width, model = tokens.shape
    matrix = pool_matrix(width)
    scale = gain[...].reshape(1, model)
    shift = bias[...].reshape(1, model)
    for task in range(tasks):
        for row in range(0, rows, 2):
            value = tokens[task, row : row + 2].astype(f32).reshape(2 * width, model)
            low = (normalize(value)[0] * scale + shift).astype(bf16)
            normal[task, row : row + 2] = low.reshape(2, width, model)
            start = (task * (rows // 2) + row // 2) * (width // 2)
            pooled[start : start + width // 2, :] = dot(matrix, low).astype(bf16)


def edge_kernel(normal, to_core, to_far):
    tasks, rows = normal.shape[:2]
    core_row, far_row, _, _ = neighbours(rows)
    for task in range(tasks):
        to_core[task, 0] = normal[task, core_row]
        to_far[task, 0] = normal[task, far_row]


def clear_guards(wide):
    blocks, lines, length, lanes = wide.shape
    zero = jnp.zeros((blocks, lines, GUARD, lanes), wide.dtype)
    wide[:, :, 0:GUARD, :] = zero
    wide[:, :, length - GUARD : length, :] = zero


def put_line(wide, line, value):
    for block in range(wide.shape[0]):
        wide[block, line, GUARD : GUARD + value.shape[0], :] = value[
            :, block * LANES : (block + 1) * LANES
        ]


def wide_scratch(lines, width, model):
    return pltpu.VMEM((model // LANES, lines, width + 2 * GUARD, LANES), f32)


def query_kernel(normal, from_core, from_far, taps, weight, extended, conv, queries, wide):
    tasks, rows, width, model = normal.shape
    clear_guards(wide)
    lines = rows + 2
    _, _, core_line, far_line = neighbours(rows)
    for task in range(tasks):
        extended[task, core_line] = from_core[task, 0]
        extended[task, far_line] = (from_far[task, 0].astype(f32) * far_weight()).astype(bf16)
        for row in range(rows):
            extended[task, row + 1] = normal[task, row]
        for line in range(lines):
            put_line(wide, task * lines + line, extended[task, line].astype(f32))

    def body(step, carry):
        task = step // (model // LANES)
        block = step % (model // LANES)
        lanes = pl.ds(pl.multiple_of(block * LANES, LANES), LANES)
        for row in range(rows):
            for start in range(0, width, 16):
                total = jnp.zeros((16, LANES), f32)
                for a in range(3):
                    for b in range(3):
                        at = GUARD - 1 + b + start
                        total = total + taps[a, b, lanes][None, :] * wide[
                            block, task * lines + row + a, at : at + 16, :
                        ]
                conv[task, row, start : start + 16, lanes] = total.astype(bf16)
        return carry

    lax.fori_loop(0, tasks * (model // LANES), body, 0)
    product = dot(flat(conv), weight[...]).astype(bf16)
    scaled = product * jnp.asarray(HALF**-0.5, bf16)
    queries[...] = scaled.reshape(queries.shape)


def half_mask(shape, side):
    lane = lax.broadcasted_iota(jnp.int32, shape, 1)
    return (lane < HALF) if side == 0 else (lane >= HALF)


def small_lane(shape):
    return lax.broadcasted_iota(jnp.int32, shape, 1) & (HALF - 1)


def pieces(value):
    high = value.astype(bf16).astype(f32)
    middle = (value - high).astype(bf16).astype(f32)
    return high, middle, value - high - middle


def marked(lead, value, shape):
    lane = small_lane(shape)
    high, middle, low = pieces(value)
    rest = jnp.where(lane == 1, high, jnp.where(lane == 2, middle, jnp.where(lane == 3, low, 0.0)))
    return jnp.where(lane == 0, lead, rest).astype(bf16)


def project(offsets, blocks, start, shape, height, valid_width, weights, targets):
    rows, width = shape
    pooled_rows = rows // 2
    me = lax.axis_index("rows")
    key_weight, value_weight = weights
    keys, values, extra = targets
    cells = blocks[0].shape[0]
    for position, offset in enumerate(offsets):
        part = slice(start + position * cells, start + (position + 1) * cells)
        block = blocks[position][...]
        keys[part, :] = dot(block, key_weight[...]).astype(bf16)
        values[part, :] = dot(block, value_weight[...]).astype(bf16)
        cell = lax.broadcasted_iota(jnp.int32, (cells, LANES), 0)
        col = cell & (width // 2 - 1)
        row = (cell // (width // 2)) % pooled_rows + (me ^ offset) * pooled_rows
        good = (2 * row < height) & (2 * col < valid_width)
        lane = small_lane((cells, LANES))
        ones = jnp.where(lane < 4, 1.0, 0.0)
        extra[part, :] = jnp.where(lane == 0, jnp.where(good, 0.0, -1e30), ones).astype(bf16)


def bound_scores(query_pair, key_pair, known):
    shape = query_pair.shape
    across = lax.broadcasted_iota(jnp.int32, (LANES, LANES), 0) < HALF
    over = lax.broadcasted_iota(jnp.int32, (LANES, LANES), 1) >= HALF
    swap = jnp.where(across == over, 1.0, 0.0).astype(bf16)
    key_all = key_pair.astype(f32)
    largest = jnp.max(dot((key_all * key_all).astype(bf16), swap), axis=0, keepdims=True)
    if known is not None:
        largest = jnp.maximum(largest, known)
    query_all = query_pair.astype(f32)
    query_norms = dot((query_all * query_all).astype(bf16), swap)
    bound = 1.02 * jnp.sqrt(query_norms * largest)
    small = small_lane(shape)
    mark = jnp.where(small == 0, 1.0, jnp.where(small == 1, -bound, 0.0)).astype(bf16)
    bounded = []
    bounds = []
    for side in range(2):
        query = jnp.where(half_mask(shape, side), query_pair, mark)
        bounded.append(query)
        lane = lax.broadcasted_iota(jnp.int32, (8, LANES), 1)
        chosen = jnp.where(lane == (1 - side) * HALF + 1, 1.0, 0.0).astype(bf16)
        bounds.append(-dot(chosen, query, NT)[0:1])
    return bounded, bounds, largest


def mix(query, side, keys, values, extra, lanes, starts, block):
    total = None
    for start in starts:
        part = pl.ds(start, block)
        half = half_mask((block, LANES), side)
        extras = extra[part, :]
        scores = dot(jnp.where(half, keys[part, lanes], extras), query, NT)
        weights = jnp.exp(scores).astype(bf16)
        mixture = dot(jnp.where(half, values[part, lanes], extras), weights, TN)
        total = mixture if total is None else total + mixture
    return total


def near_project_kernel(
    offsets, shape, heights, widths, first, second, key_weight, value_weight, keys, values, extra
):
    project(
        offsets, (first, second), 0, shape, one(heights), one(widths), (key_weight, value_weight),
        (keys, values, extra),
    )


def near_kernel(keys, values, extra, queries, sums, bounds, largest):
    key_count = keys.shape[0]

    def body(pair, carry):
        lanes = pl.ds(pl.multiple_of(pair * LANES, LANES), LANES)
        bounded, rows, norms = bound_scores(queries[:, lanes], keys[:, lanes], None)
        largest[pair] = norms
        for side in range(2):
            bounds[2 * pair + side] = rows[side]
            sums[2 * pair + side] = mix(
                bounded[side], side, keys, values, extra, lanes, (0,), key_count
            )
        return carry

    lax.fori_loop(0, HEADS // 2, body, 0, unroll=True)


def attend_kernel(order, *refs):
    refs = list(refs)
    heights, widths = refs[:2]
    del refs[:2]
    near = refs[:6]
    del refs[:6]
    pooled = refs[: len(order) - 2]
    del refs[: len(order) - 2]
    (key_weight, value_weight, queries, tokens, out_weight, out_bias, gain, bias,
     keys, values, extra, attended, middle, normal, to_core, to_far, marks, square,
     sums, totals) = refs
    near_keys, near_values, near_extra, near_sums, near_bounds, near_largest = near
    tasks, rows, width, model = tokens.shape
    me = lax.axis_index("rows")
    height, valid_width = one(heights), one(widths)
    known = near_keys.shape[0]
    keys[0:known, :] = near_keys[...]
    values[0:known, :] = near_values[...]
    extra[0:known, :] = near_extra[...]
    project(
        order[2:], pooled, known, (rows, width), height, valid_width, (key_weight, value_weight),
        (keys, values, extra),
    )
    query_count = queries.shape[0]
    key_count = keys.shape[0]
    block = known
    rest = (key_count - known) // block
    together = max(k for k in (1, 2, 3, 4) if rest % k == 0)
    steps = rest // together

    def body(pair, carry):
        lanes = pl.ds(pl.multiple_of(pair * LANES, LANES), LANES)
        query_pair = queries[:, lanes]
        shape = query_pair.shape
        bounded, bounds, _ = bound_scores(query_pair, keys[known:, lanes], near_largest[pair])

        def some(step):
            starts = [
                pl.multiple_of(known + (step * together + k) * block, block) for k in range(together)
            ]
            return [
                mix(bounded[side], side, keys, values, extra, lanes, starts, block)
                for side in range(2)
            ]

        first = some(0)
        for side in range(2):
            scale = jnp.exp(near_bounds[2 * pair + side] - bounds[side])
            sums[side] = first[side] + near_sums[2 * pair + side] * scale
        if steps > 1:

            def more(step, carry):
                for side, total in enumerate(some(step)):
                    sums[side] += total
                return carry

            lax.fori_loop(1, steps, more, 0)
        for side in range(2):
            totals[side : side + 1, :] = bounds[side]
        at = [(1 - side) * HALF + 1 for side in range(2)]
        least = jnp.minimum(
            jnp.min(sums[0, at[0] : at[0] + 1, :]), jnp.min(sums[1, at[1] : at[1] + 1, :])
        )

        @pl.when(jnp.logical_not(least > 1e-25))
        def _():
            lead = jnp.where(small_lane(shape) == 0, 1.0, 0.0).astype(bf16)
            for side in range(2):
                query = jnp.where(half_mask(shape, side), query_pair, lead)

                def scores_of(step):
                    part = pl.ds(pl.multiple_of(step * LANES, LANES), LANES)
                    half = half_mask((LANES, LANES), side)
                    extras = extra[part, :]
                    value = jnp.where(half, values[part, lanes], extras)
                    return dot(jnp.where(half, keys[part, lanes], extras), query, NT), value

                def highest(step, peak):
                    scores, _ = scores_of(step)
                    return jnp.maximum(peak, jnp.max(scores, axis=0, keepdims=True))

                start = jnp.full((1, query_count), -jnp.inf, f32)
                peak = lax.fori_loop(0, key_count // LANES, highest, start)
                totals[side : side + 1, :] = peak
                sums[side] = jnp.zeros((LANES, query_count), f32)

                def add(step, carry):
                    scores, value = scores_of(step)
                    weights = jnp.exp(scores - totals[side : side + 1, :]).astype(bf16)
                    sums[side] += dot(value, weights, TN)
                    return carry

                lax.fori_loop(0, key_count // LANES, add, 0)

        both = []
        row = lax.broadcasted_iota(jnp.int32, (LANES, query_count), 0)
        small = row & (HALF - 1)
        for side in range(2):
            mixture = sums[side]
            total = mixture[at[side] : at[side] + 1]
            high, middle_part, low = pieces(-(totals[side : side + 1, :] + jnp.log(total)))
            mark = jnp.where(
                small == 0,
                1.0,
                jnp.where(
                    small == 1,
                    high,
                    jnp.where(small == 2, middle_part, jnp.where(small == 3, low, 0.0)),
                ),
            )
            inside = (row < HALF) if side == 0 else (row >= HALF)
            across = jnp.where(inside, mixture / total, mark).T
            marks[2 * pair + side] = jnp.where(
                half_mask(shape, side), query_pair, across.astype(bf16)
            )
            both.append(across)
        chosen = jnp.where(half_mask(shape, 0), both[0], both[1])
        attended[:, lanes] = chosen.astype(bf16)
        return carry

    lax.fori_loop(0, HEADS // 2, body, 0)
    branch = dot(attended[...], out_weight[...]) + out_bias[...].reshape(1, model)
    total = flat(tokens).astype(f32) + branch
    middle[...] = total.reshape(middle.shape)
    normed, _ = normalize(total)
    low = normed * gain[...].reshape(1, model) + bias[...].reshape(1, model)
    normal[...] = low.astype(bf16).reshape(normal.shape)
    core_row, far_row, _, _ = neighbours(rows)
    for task in range(tasks):
        to_core[task, 0] = normal[task, core_row]
        to_far[task, 0] = normal[task, far_row]
    index = lax.broadcasted_iota(jnp.int32, (query_count, 1), 0)
    inside = (me * rows + (index // width) % rows < height) & ((index & (width - 1)) < valid_width)
    square[...] = column_sum(branch * branch * inside.astype(f32))


def put_pieces(grad, first, count, me, held):
    size = grad.shape[0] // PIECES
    for group in range(PIECES):
        piece = grad[group * size : (group + 1) * size]
        slot, owner = divmod(first + group, count)
        store_piece(owner, me, held, slot * size, piece)


def store_piece(owner, me, held, start, piece):
    place = owner ^ me
    place = (place & 1) * (held.shape[0] // 2) + (place >> 1)
    held[place, start : start + piece.shape[0], :] = piece


def part_pieces(held, keep, send):
    half = held.shape[0] // 2
    keep[...] = held[0:half]
    send[...] = held[half:]


def feed_in_kernel(normal, cotangent, up_weight, up_bias, down_weight, lifted, grad_act):
    tasks, rows, width, model = cotangent.shape
    hidden = up_weight.shape[1]
    bias = up_bias[...].reshape(1, hidden)
    fed, grad = flat(normal), flat(cotangent)
    for start in range(0, hidden, model):
        lanes = slice(start, start + model)
        value = (dot(fed, up_weight[:, lanes]) + bias[:, lanes]).astype(bf16)
        lifted[:, :, :, lanes] = value.reshape(tasks, rows, width, model)
        value = dot(grad, down_weight[lanes, :], NT).astype(bf16)
        grad_act[:, :, :, lanes] = value.reshape(tasks, rows, width, model)


def feed_kernel(
    from_core, from_far, lifted, grad_act, up_weight, up_bias, taps,
    active, grad_lifted, grad_band, to_core, to_far, grad_taps, grad_up_bias,
    core_lifted, far_lifted, wide, wide_back, grad_normal,
):
    tasks, rows, width, hidden = lifted.shape
    model = up_weight.shape[0]
    _, has_before, has_after = band_flags()
    lines = rows + 2
    _, _, core_line, far_line = neighbours(rows)
    c1 = 0.7978845608028654
    c2 = c1 * 0.044715

    clear_guards(wide)
    clear_guards(wide_back)
    bias = up_bias[...].reshape(1, hidden)
    for source, weight, target in ((from_core, None, core_lifted), (from_far, far_weight(), far_lifted)):
        value = dot(flat(source), up_weight[...]) + bias
        if weight is not None:
            value = value * weight
        target[...] = value.astype(bf16).reshape(target.shape)

    def across(block, carry):
        lanes = pl.ds(pl.multiple_of(block * LANES, LANES), LANES)
        tap = [[taps[a, b, lanes][None, :] for b in range(3)] for a in range(3)]

        def forth(task, sums9):
            sums9 = list(sums9)
            put_line(wide, task * lines + core_line, core_lifted[task, :, lanes].astype(f32))
            put_line(wide, task * lines + far_line, far_lifted[task, :, lanes].astype(f32))
            for row in range(rows):
                put_line(wide, task * lines + row + 1, lifted[task, row, :, lanes].astype(f32))
            for row in range(rows):
                for start in range(0, width, 16):
                    near = []
                    spread = None
                    for a in range(3):
                        for b in range(3):
                            at = GUARD - 1 + b + start
                            value = wide[0, task * lines + row + a, at : at + 16, :]
                            near.append(value)
                            term = tap[a][b] * value
                            spread = term if spread is None else spread + term
                    squared = spread * spread
                    gate = 0.5 + 0.5 * jnp.tanh(spread * (c1 + c2 * squared))
                    active[task, row, start : start + 16, lanes] = (spread * gate).astype(bf16)
                    slope = gate + spread * (gate - gate * gate) * (2 * c1 + 6 * c2 * squared)
                    grad = grad_act[task, row, start : start + 16, lanes].astype(f32) * slope
                    wide_back[
                        0, task * rows + row, GUARD + start : GUARD + start + 16, :
                    ] = grad
                    for k in range(9):
                        both = near[k] * grad
                        sums9[k] = sums9[k] + (both[0:8] + both[8:16])
            return tuple(sums9)

        zero = jnp.zeros((8, LANES), f32)
        sums9 = lax.fori_loop(0, tasks, forth, (zero,) * 9)
        for k in range(9):
            grad_taps[k // 3, k % 3, lanes] = jnp.sum(sums9[k], axis=0)

        def back(task, total):
            for line in range(lines):
                for start in range(0, width, 16):
                    value = None
                    for a in range(3):
                        if not 0 <= line - a < rows:
                            continue
                        for b in range(3):
                            at = GUARD + 1 - b + start
                            term = tap[a][b] * wide_back[
                                0, task * rows + line - a, at : at + 16, :
                            ]
                            value = term if value is None else value + term
                    if line == 0:
                        value = value * has_before
                    if line == lines - 1:
                        value = value * has_after
                    grad_lifted[task, line, start : start + 16, lanes] = value.astype(bf16)
                    total = total + (value[0:8] + value[8:16])
            return total

        grad_up_bias[0:1, lanes] = column_sum(lax.fori_loop(0, tasks, back, zero))
        return carry

    lax.fori_loop(0, hidden // LANES, across, 0)
    grad = dot(flat(grad_lifted), up_weight[...], NT)
    grad_normal[...] = grad.reshape(grad_normal.shape)
    for task in range(tasks):
        grad_band[task] = grad_normal[task, 1 : rows + 1]
        to_core[task, 0] = grad_normal[task, core_line].astype(bf16)
        to_far[task, 0] = grad_normal[task, far_line].astype(bf16)


def feed_weight_kernel(
    middle_normal, from_core, from_far, active, grad_lifted, cotangent, keep, send, normal, held
):
    tasks, rows, width, model = cotangent.shape
    hidden = active.shape[-1]
    me = lax.axis_index("rows")
    count = lax.axis_size("rows")
    _, _, core_line, far_line = neighbours(rows)
    for task in range(tasks):
        for row in range(rows):
            normal[task, row + 1] = middle_normal[task, row]
        normal[task, core_line] = from_core[task, 0]
        normal[task, far_line] = from_far[task, 0]
    size = hidden // count
    groups = model // size
    columns = hidden // model
    fed, grad_output = flat(normal), flat(cotangent)
    for column in range(columns):
        lanes = slice(column * model, (column + 1) * model)
        grad = grad_lifted[:, :, :, lanes].reshape(-1, model)
        grad_up = dot(fed, grad, TN).astype(bf16)
        act = active[:, :, :, lanes].reshape(-1, model)
        grad_down = dot(act, grad_output, TN).astype(bf16)
        for group in range(groups):
            part = slice(group * size, (group + 1) * size)
            store_piece(group * columns + column, me, held, 0, grad_up[part])
            store_piece(column * groups + group, me, held, size, grad_down[part])
    part_pieces(held, keep, send)


def layer_kernel(
    heights, widths, active, down_weight, down_bias, cotangent, middle, layer_out, sums
):
    tasks, rows, width, model = cotangent.shape
    me = lax.axis_index("rows")
    height, valid_width = one(heights), one(widths)
    zero = jnp.zeros((1, model), f32)
    totals = [zero, zero, zero]
    col = lax.broadcasted_iota(jnp.int32, (width, 1), 0)
    for task in range(tasks):
        branch = dot(flat(active.at[task]), down_weight[...]) + down_bias[...].reshape(1, model)
        for row in range(rows):
            mlp = branch[row * width : (row + 1) * width]
            final = middle[task, row] + mlp
            layer_out[task, row] = final.astype(bf16)
            weight = (col < valid_width).astype(f32) * (me * rows + row < height).astype(f32)
            grad = cotangent[task, row].astype(f32)
            for k, value in enumerate((grad, mlp * mlp * weight, final * final * weight)):
                totals[k] = totals[k] + column_sum(value)
    sums[...] = jnp.concatenate([*totals, jnp.zeros((5, model), f32)], axis=0)


def norm_back_kernel(
    grad_band, from_core, from_far, middle, cotangent, gain, out_weight, attended,
    grad_middle, grad_marks, grad_low, sums,
):
    tasks, rows, width, model = cotangent.shape
    scale = gain[...].reshape(1, model)
    parts = []
    odd = (lax.axis_index("rows") & 1).astype(f32)
    for task in range(tasks):
        core = from_core[task, 0].astype(f32)
        far = from_far[task, 0].astype(f32)
        for row in range(rows):
            grad = grad_band[task, row]
            if row == 0:
                grad = grad + core * odd + far * (1.0 - odd)
            if row == rows - 1:
                grad = grad + far * odd + core * (1.0 - odd)
            parts.append(grad)
    grad_input = jnp.concatenate(parts, axis=0)
    normed, inverse = normalize(flat(middle))
    total = flat(cotangent).astype(f32) + normalize_back(grad_input, scale, normed, inverse)
    grad_middle[...] = total.reshape(grad_middle.shape)
    sums[0:1, :] = column_sum(grad_input * normed)
    sums[1:2, :] = column_sum(grad_input)
    sums[2:3, :] = column_sum(total)
    sums[3:8, :] = jnp.zeros((5, model), f32)
    grad_branch = total.astype(bf16)
    mixture = attended[...]
    grad_low[...] = grad_branch
    grad_attended = dot(grad_branch, out_weight[...], NT).astype(bf16)
    shape = (mixture.shape[0], LANES)
    for pair in range(HEADS // 2):
        lanes = slice(pair * LANES, (pair + 1) * LANES)
        grad_two = grad_attended[:, lanes]
        both = grad_two.astype(f32) * mixture[:, lanes].astype(f32)
        for side in range(2):
            half = half_mask(shape, side)
            inner = jnp.sum(jnp.where(half, both, 0.0), axis=-1, keepdims=True)
            grad_marks[2 * pair + side] = jnp.where(half, grad_two, marked(0.0, -inner, shape))


def attend_back_kernel(
    marks, grad_marks, keys, values, extra, grad_queries, grad_keys, grad_values,
    total, query_zero, grad_zero,
):
    key_count = keys.shape[0]
    query_count = grad_marks.shape[1]
    block = min(1024, key_count)
    shape = (query_count, LANES)
    for side in range(2):
        half = half_mask(shape, side)
        zero = jnp.zeros(shape, bf16)
        part = slice(side * query_count, (side + 1) * query_count)
        query_zero[part, :] = jnp.where(half, marks[side], zero)
        grad_zero[part, :] = jnp.where(half, grad_marks[side], zero)

    def body(place, carry):
        part = pl.ds(pl.multiple_of(place * block, block), block)
        key_pair, value_pair, extras = keys[part, :], values[part, :], extra[part, :]
        lows, grads = [], []
        query_part = None
        for side in range(2):
            half = half_mask((block, LANES), side)
            scores = dot(jnp.where(half, key_pair, extras), marks[side], NT)
            grad_prob = dot(jnp.where(half, value_pair, extras), grad_marks[side], NT)
            probability = jnp.exp(scores)
            grad = (probability * grad_prob).astype(bf16)
            grads.append(grad)
            lows.append(probability.astype(bf16))
            one = dot(jnp.where(half, key_pair, jnp.zeros((block, LANES), bf16)), grad, TN)
            query_part = one if query_part is None else query_part + one
        grad_values[part, :] = dot(jnp.concatenate(lows, axis=1), grad_zero[...]).astype(bf16)
        grad_keys[part, :] = dot(jnp.concatenate(grads, axis=1), query_zero[...]).astype(bf16)

        @pl.when(place == 0)
        def _():
            total[...] = query_part

        @pl.when(place > 0)
        def _():
            total[...] += query_part

        return carry

    lax.fori_loop(0, key_count // block, body, 0)
    grad_queries[...] = (total[...] * HALF**-0.5).T.astype(bf16)


def side_by_side(refs):
    return jnp.concatenate([ref[...] for ref in refs], axis=1)


def conv_back_kernel(*refs):
    pairs = HEADS // 2
    grad_queries = refs[:pairs]
    query_weight, grad_conv, to_core, to_far = refs[pairs:]
    tasks, rows = grad_conv.shape[:2]
    grad = dot(side_by_side(grad_queries), query_weight[...], NT).astype(bf16)
    grad_conv[...] = grad.reshape(grad_conv.shape)
    core_row, far_row, _, _ = neighbours(rows)
    for task in range(tasks):
        to_core[task, 0] = grad_conv[task, core_row]
        to_far[task, 0] = grad_conv[task, far_row]


def pool_back_kernel(order, *refs):
    pairs = HEADS // 2
    grad_keys, grad_values = refs[:pairs], refs[pairs : 2 * pairs]
    key_weight, value_weight, keep, send = refs[2 * pairs :]
    cells = keep.shape[1]
    both = jnp.concatenate([key_weight[...], value_weight[...]], axis=1)
    for position, offset in enumerate(order):
        part = slice(position * cells, (position + 1) * cells)
        grads = jnp.concatenate([ref[part, :] for ref in (*grad_keys, *grad_values)], axis=1)
        target = send if offset & 1 else keep
        target[offset >> 1] = dot(grads, both, NT).astype(bf16)


def pair_weights(order, pooled, conv, queries, keys, values):
    cells = pooled[0].shape[0]
    total = None
    for position in range(len(order)):
        part = slice(position * cells, (position + 1) * cells)
        grads = jnp.concatenate([ref[part, :] for ref in (*keys, *values)], axis=1)
        value = dot(pooled[position][...], grads, TN)
        total = value if total is None else total + value
    grad_query = dot(flat(conv), side_by_side(queries), TN)
    return jnp.concatenate([grad_query, total], axis=1).astype(bf16)


def weight_kernel(order, *refs):
    refs = list(refs)
    heights, widths = refs[:2]
    del refs[:2]
    pooled = refs[: len(order)]
    del refs[: len(order)]
    pairs = HEADS // 2
    queries, keys, values = refs[:pairs], refs[pairs : 2 * pairs], refs[2 * pairs : 3 * pairs]
    del refs[: 3 * pairs]
    (pool_keep, pool_send, conv, extended, grad_conv, taps, gain, bias, attended, grad_low, square, back_sums,
     feed_sums, hidden_taps, up_bias, keep, send, wide, rows_of, held) = refs
    tasks, rows, width, model = grad_conv.shape
    count = len(order)
    lines = rows + 2
    me, has_before, has_after = band_flags()
    size = keep.shape[1] - 16
    model_grads = pair_weights(order, pooled, conv, queries, keys, values)
    for which in range(3):
        grad = model_grads[:, which * model : (which + 1) * model]
        put_pieces(grad, which * PIECES, count, me, held)
    grad_out = dot(attended[...], grad_low[...], TN)
    put_pieces(grad_out.astype(bf16), 3 * PIECES, count, me, held)
    pool_sum = jnp.zeros((1, model), f32)
    pool_dot = jnp.zeros((1, model), f32)
    for position, offset in enumerate(order):
        source = pool_send if offset & 1 else pool_keep
        grad = source[offset >> 1].astype(f32)
        pool_sum = pool_sum + column_sum(grad)
        pool_dot = pool_dot + column_sum(grad * pooled[position][...].astype(f32))

    clear_guards(wide)
    for task in range(tasks):
        for line in range(lines):
            put_line(wide, task * lines + line, extended[task, line].astype(f32))

    def across(block, carry):
        lanes = pl.ds(pl.multiple_of(block * LANES, LANES), LANES)

        def one_task(task, sums9):
            sums9 = list(sums9)
            for row in range(rows):
                for start in range(0, width, 16):
                    grad = grad_conv[task, row, start : start + 16, lanes].astype(f32)
                    for k in range(9):
                        at = GUARD - 1 + k % 3 + start
                        both = grad * wide[block, task * lines + row + k // 3, at : at + 16, :]
                        sums9[k] = sums9[k] + (both[0:8] + both[8:16])
            return tuple(sums9)

        sums9 = lax.fori_loop(
            0, tasks, one_task, tuple(jnp.zeros((8, LANES), f32) for _ in range(9))
        )
        for k in range(9):
            rows_of[2 + k : 3 + k, lanes] = column_sum(sums9[k])
        return carry

    lax.fori_loop(0, model // LANES, across, 0)

    shift = bias[...].reshape(1, model)
    zero = jnp.zeros((1, model), f32)
    conv_dot, conv_sum = zero, zero
    for row in range(rows):
        line = grad_conv[0, row].astype(f32)
        for task in range(1, tasks):
            line = line + grad_conv[task, row].astype(f32)
        full = column_sum(line)
        by_col = (full - line[0:1], full, full - line[width - 1 : width])
        for a in range(3):
            for b in range(3):
                value = by_col[b]
                if a == 0 and row == 0:
                    value = value * has_before
                if a == 2 and row == rows - 1:
                    value = value * has_after
                conv_sum = conv_sum + taps[a, b].reshape(1, model) * value
    for k in range(9):
        conv_dot = conv_dot + taps[k // 3, k % 3].reshape(1, model) * rows_of[2 + k : 3 + k, :]
    grad_bias = conv_sum + pool_sum
    grad_gain = (conv_dot + pool_dot - shift * grad_bias) / gain[...].reshape(1, model)
    rows_of[0:1, :] = grad_gain
    rows_of[1:2, :] = grad_bias
    rows_of[11:12, :] = back_sums[2:3, :]
    rows_of[12:14, :] = back_sums[0:2, :]
    rows_of[14:15, :] = feed_sums[0:1, :]
    rows_of[15:16, :] = square[...]
    rows_of[16:18, :] = feed_sums[1:3, :]
    in_rows = jnp.minimum(jnp.maximum(one(heights) - me * rows, 0), rows)
    in_cols = jnp.minimum(jnp.maximum(one(widths), 0), width)
    cells_in = (tasks * in_rows * in_cols).astype(f32)
    rows_of[18:19, :] = jnp.broadcast_to(cells_in, (1, model))
    parts = up_bias.shape[1] // model
    for part in range(parts):
        rows_of[19 + part : 20 + part, :] = up_bias[:, part * model : (part + 1) * model]
        for k in range(9):
            rows_of[19 + parts * (k + 1) + part : 20 + parts * (k + 1) + part, :] = hidden_taps[
                k // 3, k % 3, part * model : (part + 1) * model
            ].reshape(1, model)
    used = 19 + 10 * parts
    rows_of[used:SMALL, :] = jnp.zeros((SMALL - used, model), f32)
    group = SMALL // count
    for owner in range(count):
        value = rows_of[owner * group : (owner + 1) * group, :]
        if group < 8:
            value = jnp.concatenate([value, jnp.zeros((8 - group, model), f32)], axis=0)
        high = value.astype(bf16)
        low = (value - high.astype(f32)).astype(bf16)
        store_piece(owner, me, held, size, jnp.concatenate([high, low], axis=0))
    part_pieces(held, keep, send)


def last_kernel(
    grad_conv, from_core, from_far, taps, tokens, gain, grad_middle, pool, input_grad, wide
):
    tasks, rows, width, model = tokens.shape
    lines = rows + 2
    pooled_rows = rows // 2
    clear_guards(wide)
    _, _, core_line, far_line = neighbours(rows)
    for task in range(tasks):
        put_line(wide, task * lines + core_line, from_core[task, 0].astype(f32))
        put_line(wide, task * lines + far_line, from_far[task, 0].astype(f32) * far_weight())
        for row in range(rows):
            put_line(wide, task * lines + row + 1, grad_conv[task, row].astype(f32))
    pooled = pool[...].reshape(tasks, pooled_rows, width // 2, model)
    spread_matrix = pool_matrix(width)[:, 0:width]

    def body(step, carry):
        task = step // (model // LANES)
        block = step % (model // LANES)
        lanes = pl.ds(pl.multiple_of(block * LANES, LANES), LANES)
        for row in range(rows):
            for start in range(0, width, 16):
                total = jnp.zeros((16, LANES), f32)
                for a in range(3):
                    for b in range(3):
                        at = GUARD + 1 - b + start
                        total = total + taps[a, b, lanes][None, :] * wide[
                            block, task * lines + row + 2 - a, at : at + 16, :
                        ]
                input_grad[task, row, start : start + 16, lanes] = total
        return carry

    lax.fori_loop(0, tasks * (model // LANES), body, 0)
    scale = gain[...].reshape(1, model)
    for task in range(tasks):
        for row in range(rows):
            grad = input_grad[task, row] + dot(spread_matrix, pooled[task, row // 2], TN)
            normed, inverse = normalize(tokens[task, row].astype(f32))
            input_grad[task, row] = grad_middle[task, row] + normalize_back(grad, scale, normed, inverse)


def add_blocks(values):
    total = values[0].astype(f32)
    for other in values[1:]:
        total = total + other.astype(f32)
    return total


def put_sum(out, start, values, small):
    total = add_blocks(values)
    size = total.shape[0]
    if not small:
        out[start : start + size, :] = total.astype(bf16)
        return
    size -= 16
    value = total[size : size + 8] + total[size + 8 : size + 16]
    high = value.astype(bf16)
    low = (value - high.astype(f32)).astype(bf16)
    out[start : start + size, :] = total[0:size].astype(bf16)
    out[start + size : start + size + 16, :] = jnp.concatenate([high, low], axis=0)


def combine(arrays, small):
    blocks, size, model = arrays[0].shape

    def kernel(*refs):
        ins, outs = refs[: len(arrays)], refs[len(arrays) :]
        for block, out in enumerate(outs):
            put_sum(out, 0, [x[block] for x in ins], small)

    return call("combine", kernel, [((size, model), bf16)] * blocks, list(arrays))


def stack(values):
    size, model = values[0].shape

    def kernel(*refs):
        for place, value in enumerate(refs[:-1]):
            refs[-1][place] = value[...]

    return call("stack", kernel, [((len(values), size, model), bf16)], list(values))[0]


def exchange(value, axis, mask):
    count = lax.axis_size(axis)
    return lax.ppermute(value, axis, [(i, i ^ mask) for i in range(count)])


def far_masks():
    return list(range(2, lax.axis_size("rows"), 2))


def once(value, *earlier):
    return lax.optimization_barrier((value, earlier))[0]


def far_rows(value):
    return [exchange(value, "rows", mask) for mask in far_masks()]


def all_images(value):
    return [exchange(value, "batch", mask) for mask in range(1, lax.axis_size("batch"))]


def add_images(own, arrived, small):
    (total,) = combine([x[None] for x in [own, *arrived]], small)
    return total


def unpack_feed_kernel(count, *refs):
    even, odd, grad_up, grad_down = refs
    blocks = [half.at[place] for half in (even, odd) for place in range(count // 2)]
    me = lax.axis_index("rows")
    model, hidden = grad_up.shape
    size = hidden // count
    columns = hidden // model
    for j in range(count):
        owner = blocks_owner(j, count, me)
        block = blocks[j]
        up = block[0:size, :].astype(f32)
        place = owner // columns
        col = owner % columns
        grad_up[
            pl.ds(pl.multiple_of(place * size, size), size),
            pl.ds(pl.multiple_of(col * model, model), model),
        ] = up
        grad_down[pl.ds(pl.multiple_of(owner * size, size), size), :] = block[
            size : 2 * size, :
        ].astype(f32)


def blocks_owner(j, count, me):
    half = count // 2
    offset = 2 * j if j < half else 2 * (j - half) + 1
    return me ^ offset


def unpack_late_kernel(count, *refs):
    blocks = refs[:count]
    (grad_query, grad_key, grad_value, grad_out, norm1_gain, norm1_bias, query_taps, out_bias,
     norm2_gain, norm2_bias, up_bias, hidden_taps, down_bias, stats, weights, rows_of) = refs[count:]
    me = lax.axis_index("rows")
    model = grad_query.shape[0]
    piece = model // PIECES
    size = blocks[0].shape[0] - 16
    group = SMALL // count
    for j in range(count):
        owner = blocks_owner(j, count, me)
        block = blocks[j][...].astype(f32)
        for slot in range(size // piece):
            start = pl.multiple_of((slot * count + owner) * piece, piece)
            weights[pl.ds(start, piece), :] = block[slot * piece : (slot + 1) * piece]
        rows_of[owner] = block[size : size + 8] + block[size + 8 : size + 16]
    for which, out in enumerate((grad_query, grad_key, grad_value, grad_out)):
        out[...] = weights[which * model : (which + 1) * model, :]

    def line(k):
        return rows_of[k // group, k % group, :]

    norm1_gain[...] = line(0)
    norm1_bias[...] = line(1)
    for k in range(9):
        query_taps[k // 3, k % 3, :] = line(2 + k)
    out_bias[...] = line(11)
    norm2_gain[...] = line(12)
    norm2_bias[...] = line(13)
    down_bias[...] = line(14)
    parts = up_bias.shape[0] // model
    for part in range(parts):
        lanes = slice(part * model, (part + 1) * model)
        up_bias[lanes] = line(19 + part)
        for k in range(9):
            hidden_taps[k // 3, k % 3, lanes] = line(19 + parts * (k + 1) + part)
    cells = line(18).reshape(1, model)[:, 0:1]
    row = lax.broadcasted_iota(jnp.int32, (1, LANES), 1)
    value = jnp.zeros((1, LANES), f32)
    for k in range(3):
        total = jnp.sum(line(15 + k).reshape(1, model), axis=-1, keepdims=True)
        value = jnp.where(row == k, jnp.sqrt(total / (cells * model)), value)
    stats[...] = value.reshape(LANES)[0:3]


def local(
    tokens,
    norm1_gain,
    norm1_bias,
    query_taps,
    query_weight,
    key_weight,
    value_weight,
    out_weight,
    out_bias,
    norm2_gain,
    norm2_bias,
    up_weight,
    up_bias,
    hidden_taps,
    down_weight,
    down_bias,
    cotangent,
    heights,
    widths,
):
    shape = tokens.shape
    tokens, cotangent = tokens[0], cotangent[0]
    tasks, rows, width, model = tokens.shape
    hidden = up_weight.shape[1]
    count = lax.axis_size("rows")
    cells = tasks * (rows // 2) * (width // 2)
    key_count = count * cells
    lines = rows + 2
    token_count = tasks * rows * width
    line = (tasks, 1, width, model)

    def swap_lines(lines_out):
        to_core, to_far = lines_out
        across = [p for i in range(1, count, 2) for p in ((i, (i + 1) % count), ((i + 1) % count, i))]
        return exchange(to_core, "rows", 1), lax.ppermute(to_far, "rows", across)

    normal_one, pooled = call(
        "first_norm",
        first_norm_kernel,
        [(tokens.shape, bf16), ((cells, model), bf16)],
        [hbm(x) for x in (tokens, norm1_gain, norm1_bias)],
        limit=8,
    )
    far = far_masks()
    order = [0, 1, *far, *[mask + 1 for mask in far]]
    arrived = far_rows(pooled)
    edge = call("edge", edge_kernel, [(line, bf16), (line, bf16)], [normal_one])
    edge = swap_lines(edge)
    swapped = exchange(pooled, "rows", 1)
    near_count = 2 * cells
    near = call(
        "near_project",
        lambda *refs: near_project_kernel(order[:2], (rows, width), *refs),
        [((near_count, model), bf16), ((near_count, model), bf16), ((near_count, LANES), bf16)],
        [heights, widths, pooled, swapped, hbm(key_weight), hbm(value_weight)],
        limit=12,
    )
    edge = once(edge, *near)
    extended, conv, queries = call(
        "query_conv",
        query_kernel,
        [
            ((tasks, lines, width, model), bf16), (tokens.shape, bf16), ((token_count, model), bf16),
        ],
        [normal_one, *edge, hbm(query_taps), hbm(query_weight)],
        scratch=[wide_scratch(tasks * lines, width, model)],
        us=2,
        limit=12,
    )
    near += call(
        "near",
        near_kernel,
        [
            ((HEADS, LANES, token_count), f32), ((HEADS, 1, token_count), f32),
            ((HEADS // 2, 1, LANES), f32),
        ],
        [*near, queries],
        us=4,
        limit=20,
    )
    arrived = once(arrived, *near)
    blocks = [pooled, swapped, *arrived, *[exchange(x, "rows", 1) for x in arrived]]

    (keys, values, extra, attended, middle, normal_two, to_core, to_far, marks, square) = call(
        "attend",
        lambda *refs: attend_kernel(order, *refs),
        [
            ((key_count, model), bf16), ((key_count, model), bf16), ((key_count, LANES), bf16),
            ((token_count, model), bf16), (tokens.shape, f32),
            (tokens.shape, bf16), (line, bf16), (line, bf16), ((HEADS, token_count, LANES), bf16), ((1, model), f32),
        ],
        [heights, widths, *near, *blocks[2:], hbm(key_weight), hbm(value_weight), queries,
         *[hbm(x) for x in (tokens, out_weight, out_bias, norm2_gain, norm2_bias)]],
        scratch=[pltpu.VMEM((2, LANES, token_count), f32), pltpu.VMEM((8, token_count), f32)],
        us=18,
        limit=24,
    )
    next_lines = swap_lines((to_core, to_far))
    band = (tasks, rows, width, hidden)
    lifted, grad_act = call(
        "feed_in",
        feed_in_kernel,
        [(band, bf16), (band, bf16)],
        [normal_two, *[hbm(x) for x in (cotangent, up_weight, up_bias, down_weight)]],
        us=4,
        limit=20,
    )
    next_lines = once(next_lines, grad_act)
    (active, grad_lifted, grad_band, to_core, to_far, grad_hidden_taps, grad_up_bias) = call(
        "feed",
        feed_kernel,
        [
            (band, bf16), ((tasks, lines, width, hidden), bf16), (tokens.shape, f32), (line, bf16),
            (line, bf16), ((3, 3, hidden), f32), ((1, hidden), f32),
        ],
        [*next_lines, lifted, grad_act, *[hbm(x) for x in (up_weight, up_bias, hidden_taps)]],
        scratch=[
            pltpu.VMEM((tasks, width, hidden), bf16),
            pltpu.VMEM((tasks, width, hidden), bf16),
            wide_scratch(tasks * lines, width, LANES),
            wide_scratch(tasks * rows, width, LANES),
            pltpu.VMEM((tasks, lines, width, model), f32),
        ],
        us=24,
        limit=24,
    )
    edge = swap_lines((to_core, to_far))
    feed_keep, feed_send = call(
        "feed_weights",
        feed_weight_kernel,
        [((count // 2, 2 * hidden // count, model), bf16)] * 2,
        [normal_two, *next_lines, active, grad_lifted, hbm(cotangent)],
        scratch=[
            pltpu.VMEM((tasks, lines, width, model), bf16),
            pltpu.VMEM((count, 2 * hidden // count, model), bf16),
        ],
        us=5,
        limit=24,
    )
    edge = once(edge, feed_keep)
    feed_swapped = exchange(once(feed_send, edge), "rows", 1)
    piece = model // PIECES
    grad_middle, grad_marks, grad_low, back_sums = call(
        "norm_back",
        norm_back_kernel,
        [
            (tokens.shape, f32), ((HEADS, token_count, LANES), bf16), ((token_count, model), bf16),
            ((8, model), f32),
        ],
        [
            grad_band, *edge,
            middle, *[hbm(x) for x in (cotangent, norm2_gain, out_weight)], attended,
        ],
        us=4,
        limit=20,
    )

    def attend_back(pair, tie):
        inputs = [marks, grad_marks, keys, values, extra]
        inputs = once(inputs, *tie)

        def of_heads(x):
            return pl.BlockSpec((2, x.shape[1], LANES), lambda i: (pair, 0, 0))

        def of_lanes(x):
            return pl.BlockSpec((x.shape[0], LANES), lambda i: (0, pair))

        whole = pl.BlockSpec((key_count, LANES), lambda i: (0, 0))
        outs = [(token_count, LANES), (key_count, LANES), (key_count, LANES)]
        return pl.pallas_call(
            attend_back_kernel,
            name="attend_back",
            grid=(1,),
            out_shape=[jax.ShapeDtypeStruct(shape, bf16) for shape in outs],
            in_specs=[*[of_heads(x) for x in inputs[0:2]], *[of_lanes(x) for x in inputs[2:4]], whole],
            out_specs=[pl.BlockSpec(shape, lambda i: (0, 0)) for shape in outs],
            scratch_shapes=[
                pltpu.VMEM((LANES, token_count), f32),
                pltpu.VMEM((2 * token_count, LANES), bf16),
                pltpu.VMEM((2 * token_count, LANES), bf16),
            ],
            compiler_params=pltpu.CompilerParams(vmem_limit_bytes=20 << 20),
            cost_estimate=cost(11),
        )(*inputs)

    feed_blocks = combine(once([feed_keep, feed_swapped], grad_marks), False)
    feed_arrived = [exchange(feed_blocks[mask >> 1], "rows", mask) for mask in far]
    back = [attend_back(0, feed_blocks)]
    feed_arrived = once(feed_arrived, *back[0])
    feed_own = add_images(feed_blocks[0], feed_arrived, False)
    hop = 1
    while hop < lax.axis_size("batch"):
        feed_arrived = exchange(feed_own, "batch", hop)
        if len(back) < HEADS // 2:
            back.append(attend_back(len(back), [*back[-1], feed_own]))
        feed_arrived = once(feed_arrived, *back[-1])
        feed_own = add_images(feed_own, [feed_arrived], False)
        hop *= 2
    while len(back) < HEADS // 2:
        back.append(attend_back(len(back), back[-1]))
    grads = [part for which in range(3) for part in [x[which] for x in back]]
    pairs = HEADS // 2
    grad_conv, *edge = call(
        "conv_back",
        conv_back_kernel,
        [(tokens.shape, bf16), (line, bf16), (line, bf16)],
        [*once(grads[:pairs], feed_own), query_weight],
    )
    feed_arrived = far_rows(feed_own)
    edge = swap_lines(edge)
    pool_keep, pool_send = call(
        "pool_back",
        lambda *refs: pool_back_kernel(order, *refs),
        [((count // 2, cells, model), bf16)] * 2,
        [*once(grads[pairs:], grad_conv), key_weight, value_weight],
        us=3,
        limit=12,
    )
    layer_out, feed_sums = call(
        "layer",
        layer_kernel,
        [(tokens.shape, bf16), ((8, model), f32)],
        [heights, widths, once(active, pool_keep), *[hbm(x) for x in (down_weight, down_bias, cotangent)], middle],
        us=3,
        limit=20,
    )
    slots = -(-4 * PIECES // count)
    keep, send = call(
        "weights",
        lambda *refs: weight_kernel(order, *refs),
        [((count // 2, slots * piece + 16, model), bf16)] * 2,
        [
            heights, widths, *blocks, *grads, pool_keep, pool_send, conv, extended, grad_conv,
            query_taps, norm1_gain, norm1_bias, attended, grad_low, square, back_sums, feed_sums,
            grad_hidden_taps, grad_up_bias,
        ],
        scratch=[
            wide_scratch(tasks * lines, width, model),
            pltpu.VMEM((SMALL, model), f32),
            pltpu.VMEM((count, slots * piece + 16, model), bf16),
        ],
        us=4,
        limit=16,
    )
    feed_arrived, edge = once((feed_arrived, edge), keep)
    send, pool_send = once((send, pool_send), feed_arrived, edge)
    late_swapped = exchange(send, "rows", 1)
    pool_swapped = exchange(pool_send, "rows", 1)
    late_blocks = combine([keep, late_swapped], True)
    late_arrived = [exchange(late_blocks[mask >> 1], "rows", mask) for mask in far]
    pool_blocks = combine([pool_keep, once(pool_swapped, late_blocks)], False)
    feed_even = stack(once([feed_own, *feed_arrived], pool_blocks))
    feed_odd = exchange(feed_even, "rows", 1)
    late_arrived = once(late_arrived, feed_even)
    (late_own,) = combine([x[None] for x in [late_blocks[0], *late_arrived]], True)
    pool_arrived = [exchange(x, "rows", mask) for x, mask in zip(once(pool_blocks[1:], late_own), far)]
    arrived = exchange(late_own, "batch", 1)
    grad_up, grad_down = call(
        "unpack_feed",
        lambda *refs: unpack_feed_kernel(count, *refs),
        [((model, hidden), f32), ((hidden, model), f32)],
        [once(feed_even, late_own), feed_odd],
        us=3,
        limit=12,
    )
    arrived = once(arrived, grad_up)
    hop = 2
    while hop < lax.axis_size("batch"):
        late_own = add_images(late_own, [arrived], True)
        arrived = exchange(late_own, "batch", hop)
        hop *= 2
    pool_arrived = once(pool_arrived, late_own)
    (pool_total,) = combine([x[None] for x in [pool_blocks[0], *pool_arrived]], False)
    (input_grad,) = call(
        "last_norm",
        last_kernel,
        [(tokens.shape, f32)],
        [grad_conv, *edge, query_taps, tokens, norm1_gain, grad_middle, pool_total],
        scratch=[wide_scratch(tasks * lines, width, model)],
        us=5,
        limit=12,
    )
    late_own = add_images(late_own, [once(arrived, input_grad)], True)
    even = [late_own, *far_rows(late_own)]
    odd = [exchange(x, "rows", 1) for x in even]
    vector = ((model,), f32)
    late = call(
        "unpack_late",
        lambda *refs: unpack_late_kernel(count, *refs),
        [((model, model), f32)] * 4
        + [vector, vector, ((3, 3, model), f32), vector, vector, vector, ((hidden,), f32),
           ((3, 3, hidden), f32), vector, ((3,), f32)],
        [*even, *odd],
        scratch=[
            pltpu.VMEM((slots * count * piece, model), f32),
            pltpu.VMEM((count, 8, model), f32),
        ],
        us=2,
        limit=12,
    )
    (grad_query, grad_key, grad_value, grad_out, gain1, bias1, taps1, out_sum, gain2, bias2, up_sum,
     taps2, down_sum, stats) = late
    return (
        layer_out.reshape(shape),
        input_grad.reshape(shape),
        gain1,
        bias1,
        taps1,
        grad_query,
        grad_key,
        grad_value,
        grad_out,
        out_sum,
        gain2,
        bias2,
        grad_up,
        up_sum,
        taps2,
        grad_down,
        down_sum,
        stats,
    )


def solution(mesh):
    band = P("batch", None, "rows", None, None)
    placed = (band, *[P()] * 15, band, P("batch"), P("batch"))
    return jax.shard_map(
        local,
        mesh=mesh,
        in_specs=placed,
        out_specs=(band, band, *[P()] * 16),
        check_vma=False,
    )
```
